32 devices in a mesh: dp: 16 (over z, x, core), tensor: 2 (over y).
Axes of the slice: x: 2, y: 2, z: 4, core: 2. Of those that a mesh axis runs over, the one named last changes fastest.
Arguments:
- tokens: bfloat16 [16384, 1024], P(('dp', 'tensor')), may hold values from -6 to 6
- lengths: int32 [16, 4], P('dp'), may hold values from 1 to 512, 1024 in all within a row
- norm_gain: float32 [1024], replicated, may hold values from 0.5 to 1.5
- zx_weight: bfloat16 [1024, 2, 2048], P('dp', None, 'tensor'), may hold values from -0.1875 to 0.1875
- bc_weight: bfloat16 [1024, 256], P('dp'), may hold values from -0.1875 to 0.1875
- dt_weight: bfloat16 [1024, 32], P('dp', 'tensor'), may hold values from -0.1875 to 0.1875
- conv_inner: float32 [4, 2048], P(None, 'tensor'), may hold values from -3 to 3
- bias_inner: float32 [2048], P('tensor'), may hold values from -3 to 3
- conv_shared: float32 [4, 256], replicated, may hold values from -3 to 3
- bias_shared: float32 [256], replicated, may hold values from -3 to 3
- step_bias: float32 [32], P('tensor'), may hold values from -6.9 to -2.3
- log_rate: float32 [32], P('tensor'), may hold values from 0 to 2.77
- skip_gain: float32 [32], P('tensor'), may hold values from 0.5 to 1.5
- gate_gain: float32 [2048], P('tensor'), may hold values from 0.5 to 1.5
- out_weight: bfloat16 [1024, 2048], P('dp', 'tensor'), may hold values from -0.125 to 0.125
- cotangent: bfloat16 [16384, 1024], P(('dp', 'tensor')), may hold values from -6 to 6
Outputs:
- block_out: bfloat16 [16384, 1024], P(('dp', 'tensor'))
- grad_tokens: bfloat16 [16384, 1024], P(('dp', 'tensor'))
- grad_norm_gain: float32 [1024], replicated
- grad_zx_weight: float32 [1024, 2, 2048], P('dp', None, 'tensor')
- grad_bc_weight: float32 [1024, 256], P('dp')
- grad_dt_weight: float32 [1024, 32], P('dp', 'tensor')
- grad_conv_inner: float32 [4, 2048], P(None, 'tensor')
- grad_bias_inner: float32 [2048], P('tensor')
- grad_conv_shared: float32 [4, 256], replicated
- grad_bias_shared: float32 [256], replicated
- grad_step_bias: float32 [32], P('tensor')
- grad_log_rate: float32 [32], P('tensor')
- grad_skip_gain: float32 [32], P('tensor')
- grad_gate_gain: float32 [2048], P('tensor')
- grad_out_weight: float32 [1024, 2048], P('dp', 'tensor')
The draws below stay inside these ranges and needn't reach their ends.
Inputs may be any that keep to these rules, and one draw needn't show every extreme that they name: `lengths`: each row lists the 4 sequences packed in order into the 1024 rows of one index of dp; a row sums to 1024 and its longest entry is 512.
All inputs are finite; a program needn't handle non-finite values.
Results may differ from the reference program's by a relative error of at most 0.014.
Values may be sent and summed in bfloat16 or wider, within the bound.
No kernel may reach another device: no remote copies, remote signals or barrier semaphores. Data moves between devices by JAX's collectives and lax.ppermute only.
A program may use at most 192 MiB of HBM per device.

```python
import math
from functools import partial
import jax
import jax.numpy as jnp
import numpy as np
from jax import lax

D = 1024
HEADS = 32
STATE = 128
CONV = 4
SPAN = 256
INNER = 2048
TOK_G = 1024
TOKENS = 16384
MAXLEN = 512
NSEQ = 4
N_DP = 16


def level_of(own_key, dims, split, least, top_value):
    level, own = 1.0, jax.random.fold_in(own_key, 6)
    for dim, blocks in split:
        heights = jnp.exp(jax.random.uniform(jax.random.fold_in(own, dim), (blocks,), jnp.float32, least / len(split), top_value / len(split)))
        level = level * jnp.repeat(heights, dims[dim] // blocks).reshape([-1 if axis == dim else 1 for axis in range(len(dims))])
    return level


def profile(amount, total, reach, lean):
    loads = [(1 << 20) // math.isqrt(standing ** lean) + 1 for standing in range(2, amount + 1)]
    spare, holding = total - reach - (amount - 1), [1] * (amount - 1)
    while spare > 0:
        movable = [i for i in range(amount - 1) if holding[i] < reach]
        mass, remaining = sum([loads[i] for i in movable]), spare
        for i in movable:
            addition = min(reach - holding[i], max(1, remaining * loads[i] // mass), spare)
            holding[i] = holding[i] + addition
            spare = spare - addition
    return np.array([reach] + holding)


def ragged_sizes(stream_key, count, total, reach, skew):
    if count == 2:
        one = jax.random.randint(stream_key, (), max(1, total - reach), min(reach, total - 1) + 1)
        return jnp.stack([one, total - one])
    sizes = jnp.asarray(profile(count, total, reach, skew), jnp.int32)
    pairs = (count - 1) // 2
    giver, receiver = sizes[1:1 + 2 * pairs:2], sizes[2:2 + 2 * pairs:2]
    room = jnp.minimum(giver - 1, reach - receiver)
    passed = jax.random.randint(jax.random.fold_in(stream_key, 1), (pairs,), 0, 1 << 20) % (room + 1)
    sizes = sizes.at[1:1 + 2 * pairs:2].set(giver - passed).at[2:2 + 2 * pairs:2].set(receiver + passed)
    return sizes[jax.random.permutation(jax.random.fold_in(stream_key, 2), count)]


def scatter_about(rng, shape, scale, limit, shards=(), kind=jnp.bfloat16):
    values = scale * jax.random.normal(rng, shape, jnp.float32)
    if shards:
        values = values * level_of(rng, shape, shards, -0.22, 0.18)
    return jnp.clip(values, -limit, limit).astype(kind)


def setup_inputs(seed: int = 0) -> dict:
    keys = jax.random.split(jax.random.key(seed), 17)
    tokens = scatter_about(keys[0], (TOKENS, D), 1.0, 6.0, ((0, 32),))
    lengths = jax.vmap(lambda own: ragged_sizes(own, NSEQ, TOK_G, MAXLEN, 2))(jax.random.split(keys[1], N_DP)).reshape((N_DP, NSEQ)).astype(jnp.int32)
    norm_gain = jnp.clip(1.0 + 0.1 * jax.random.normal(keys[2], (D,), jnp.float32), 0.5, 1.5)
    zx_weight = scatter_about(keys[3], (D, 2, INNER), D ** -0.5, 0.1875, ((0, 16), (2, 2)))
    bc_weight = scatter_about(keys[4], (D, 2 * STATE), D ** -0.5, 0.1875, ((0, 16),))
    dt_weight = scatter_about(keys[5], (D, HEADS), D ** -0.5, 0.1875, ((0, 16), (1, 2)))
    conv_inner = scatter_about(keys[6], (CONV, INNER), CONV ** -0.5, 3.0, ((1, 2),), jnp.float32)
    bias_inner = scatter_about(keys[7], (INNER,), 0.5, 3.0, ((0, 2),), jnp.float32)
    conv_shared = scatter_about(keys[8], (CONV, 2 * STATE), CONV ** -0.5, 3.0, (), jnp.float32)
    bias_shared = scatter_about(keys[9], (2 * STATE,), 0.5, 3.0, (), jnp.float32)
    step_bias = jnp.clip(-6.9 + 4.6000001430511475 * jax.random.uniform(keys[10], (HEADS,), jnp.float32) ** level_of(keys[10], (HEADS,), ((0, 2),), -0.2, 0.2), -6.9, -2.3)
    log_rate = jnp.clip(2.77 * jax.random.uniform(keys[11], (HEADS,), jnp.float32) ** level_of(keys[11], (HEADS,), ((0, 2),), -0.2, 0.2), 0.0, 2.77)
    skip_gain = jnp.clip(0.5 + 1.0 * jax.random.uniform(keys[12], (HEADS,), jnp.float32) ** level_of(keys[12], (HEADS,), ((0, 2),), -0.2, 0.2), 0.5, 1.5)
    gate_gain = jnp.clip(1.0 + 0.1 * jax.random.normal(keys[13], (INNER,), jnp.float32), 0.5, 1.5)
    out_weight = scatter_about(keys[14], (D, INNER), INNER ** -0.5, 0.125, ((0, 16), (1, 2)))
    cotangent = scatter_about(keys[15], (TOKENS, D), 1.0, 6.0, ((0, 32),))
    return {"tokens": tokens, "lengths": lengths, "norm_gain": norm_gain, "zx_weight": zx_weight, "bc_weight": bc_weight, "dt_weight": dt_weight, "conv_inner": conv_inner, "bias_inner": bias_inner, "conv_shared": conv_shared, "bias_shared": bias_shared, "step_bias": step_bias, "log_rate": log_rate, "skip_gain": skip_gain, "gate_gain": gate_gain, "out_weight": out_weight, "cotangent": cotangent}


EPSILON = 1e-05
PRECISE = lax.Precision.HIGHEST

@jax.custom_vjp
def low(v):
    return lax.optimization_barrier(v.astype(jnp.bfloat16)).astype(jnp.float32)

@jax.custom_vjp
def low_back(v):
    return v

def low_keep(v):
    return (low(v), None)

def low_pass(kept, grad):
    return (grad,)

def back_keep(v):
    return (v, None)

def back_low(kept, grad):
    return (low(grad),)
low.defvjp(low_keep, low_pass)
low_back.defvjp(back_keep, back_low)

def segment_ids(seq_lengths, row_total):
    sequence_ends = jnp.cumsum(seq_lengths.astype(jnp.int32))
    position = jnp.arange(row_total, dtype=jnp.int32)
    return lax.optimization_barrier(jnp.sum((position[:, None] >= sequence_ends[None, :]).astype(jnp.int32), axis=1))

def causal_conv(values, weights, conv_bias, segment):
    taps = weights.shape[0]
    summed = conv_bias[None, :] + weights[taps - 1][None, :] * values
    for offset in range(1, taps):
        shifted = jnp.pad(values, ((offset, 0), (0, 0)))[:-offset]
        earlier = jnp.pad(segment, (offset, 0), constant_values=-1)[:-offset]
        keep_mask = (earlier == segment).astype(values.dtype)
        summed = summed + weights[taps - 1 - offset][None, :] * shifted * keep_mask[:, None]
    return summed

def state_space(head_input, step_size, decay_rate, input_map, output_map, segment, span_length):
    row_total, head_count, head_size = head_input.shape
    span_count = row_total // span_length
    state_width = input_map.shape[1]
    log_decay = (step_size * decay_rate[None, :]).reshape(span_count, span_length, head_count)
    running = jnp.cumsum(log_decay, axis=1)
    scaled_input = (head_input * step_size[:, :, None]).reshape(span_count, span_length, head_count, head_size)
    in_spans = input_map.reshape(span_count, span_length, state_width)
    out_spans = output_map.reshape(span_count, span_length, state_width)
    segment_spans = segment.reshape(span_count, span_length)
    before = jnp.concatenate([jnp.full((1,), -1, jnp.int32), segment_spans[:-1, -1].astype(jnp.int32)])
    carried = (segment_spans == before[:, None]).astype(head_input.dtype)
    position = jnp.arange(span_length, dtype=jnp.int32)
    causal = position[:, None] >= position[None, :]
    same_doc = (segment_spans[:, :, None] == segment_spans[:, None, :]) & causal[None]
    running_heads = jnp.transpose(running, (0, 2, 1))
    log_gap = running_heads[:, :, :, None] - running_heads[:, :, None, :]
    same_mask = same_doc[:, None]
    decays = jnp.where(same_mask, jnp.exp(jnp.where(same_mask, log_gap, 0.0)), 0.0)
    scores = jnp.einsum('cin,cjn->cij', out_spans, in_spans, precision=PRECISE)
    intra_out = jnp.einsum('chij,cjhp->cihp', decays * scores[:, None], scaled_input, precision=PRECISE)
    last_match = (segment_spans == segment_spans[:, -1:]).astype(head_input.dtype)
    end_decay = jnp.exp(running[:, -1:, :] - running) * last_match[:, :, None]
    local_state = jnp.einsum('cjh,cjhp,cjn->chpn', end_decay, scaled_input, in_spans, precision=PRECISE)
    through = jnp.exp(running[:, -1, :]) * carried[:, -1:]

    def advance(carry_state, span_item):
        factor, addend = span_item
        return (factor[:, None, None] * carry_state + addend, carry_state)
    initial = jnp.zeros((head_count, head_size, state_width), head_input.dtype)
    unused, entering = lax.scan(advance, initial, (through, local_state))
    entry_decay = jnp.exp(running) * carried[:, :, None]
    inter_out = jnp.einsum('cin,chpn->cihp', out_spans, entering, precision=PRECISE) * entry_decay[:, :, :, None]
    return (intra_out + inter_out).reshape(row_total, head_count, head_size)

def mixer(segment, span_length, gate_proj, inner_proj, shared_proj, step_proj, conv_inner, bias_inner, conv_shared, bias_shared, step_bias, log_rate, skip_gain):
    row_total = inner_proj.shape[0]
    head_count = step_proj.shape[1]
    conv_out = jax.nn.silu(causal_conv(inner_proj, conv_inner, bias_inner, segment))
    shared_conv = jax.nn.silu(causal_conv(shared_proj, conv_shared, bias_shared, segment))
    half_width = shared_conv.shape[1] // 2
    step_size = jax.nn.softplus(step_proj + step_bias[None, :])
    head_input = conv_out.reshape(row_total, head_count, -1)
    ssm_out = state_space(head_input, step_size, -jnp.exp(log_rate), shared_conv[:, :half_width], shared_conv[:, half_width:], segment, span_length)
    ssm_out = ssm_out + skip_gain[None, :, None] * head_input
    return ssm_out.reshape(row_total, -1) * jax.nn.silu(gate_proj)

def matmul(left, right):
    return jnp.dot(left, right, precision=PRECISE)

def block(segment, inputs, norm_gain, zx_weight, bc_weight, dt_weight, conv_inner, bias_inner, conv_shared, bias_shared, step_bias, log_rate, skip_gain, gate_gain, out_weight):
    norm_scale = lax.rsqrt(lax.optimization_barrier(jnp.mean(inputs * inputs, axis=1, keepdims=True)) + EPSILON)
    normed = low(inputs * norm_scale * norm_gain[None, :])
    gate_proj = low_back(matmul(normed, zx_weight[:, 0, :]))
    inner_proj = low_back(matmul(normed, zx_weight[:, 1, :]))
    shared_proj = low_back(matmul(normed, bc_weight))
    step_proj = low_back(matmul(normed, dt_weight))
    gated_out = mixer(segment, SPAN, gate_proj, inner_proj, shared_proj, step_proj, conv_inner, bias_inner, conv_shared, bias_shared, step_bias, log_rate, skip_gain)
    gate_scale = lax.rsqrt(lax.optimization_barrier(jnp.mean(gated_out * gated_out, axis=1, keepdims=True)) + EPSILON)
    scaled_out = low(gated_out * gate_scale * gate_gain[None, :])
    return inputs + matmul(scaled_out, out_weight.T)

def reference(tokens, lengths, norm_gain, zx_weight, bc_weight, dt_weight, conv_inner, bias_inner, conv_shared, bias_shared, step_bias, log_rate, skip_gain, gate_gain, out_weight, cotangent):
    parameters = tuple((p.astype(jnp.float32) for p in (norm_gain, zx_weight, bc_weight, dt_weight, conv_inner, bias_inner, conv_shared, bias_shared, step_bias, log_rate, skip_gain, gate_gain, out_weight)))
    inputs_all = tokens.astype(jnp.float32).reshape(N_DP, TOK_G, D)
    upstream_all = cotangent.astype(jnp.float32).reshape(N_DP, TOK_G, D)

    def one_group(totals, group_item):
        group_in, group_up, seq_lengths = group_item
        segment = segment_ids(seq_lengths, TOK_G)
        result, pullback = jax.vjp(partial(block, segment), group_in, *parameters)
        gradients = pullback(group_up)
        totals = tuple((a + b for a, b in zip(totals, gradients[1:])))
        return (totals, (result, gradients[0]))
    initial = tuple((jnp.zeros_like(p) for p in parameters))
    totals, (results, input_grads) = lax.scan(one_group, initial, (inputs_all, upstream_all, lengths))
    block_out = results.reshape(TOKENS, D).astype(jnp.bfloat16)
    grad_tokens = input_grads.reshape(TOKENS, D).astype(jnp.bfloat16)
    return (block_out, grad_tokens, totals[0], totals[1], totals[2], totals[3], totals[4], totals[5], totals[6], totals[7], totals[8], totals[9], totals[10], totals[11], totals[12])
```

```python
from functools import partial

import jax
import jax.numpy as jnp
from jax import lax
from jax.experimental import pallas as pl
from jax.experimental.pallas import tpu as pltpu
from jax.sharding import PartitionSpec as P

EPSILON = 1e-05
SPAN = 256
LANES = 128
TAIL = 8
TAPS = 4
MASKED = -1e30
f32 = jnp.float32
bf16 = jnp.bfloat16
LIMIT = 60 * 1024 * 1024


def mm(left, right, dims):
    return lax.dot_general(left, right, ((dims[0], dims[1]), ((), ())), preferred_element_type=f32)


NN = ((1,), (0,))
NT = ((1,), (1,))
TN = ((0,), (0,))


def halves(value, axis):
    high = value.astype(bf16)
    low = (value - high.astype(f32)).astype(bf16)
    return jnp.concatenate([high, low], axis=axis)


def sigmoid(value):
    return 1.0 / (1.0 + jnp.exp(-value))


def softplus(value):
    return jnp.maximum(value, 0.0) + jnp.log1p(jnp.exp(-jnp.abs(value)))


def segment_at(ends, position):
    total = jnp.zeros(position.shape, jnp.int32)
    for end in ends:
        total = total + (position >= end).astype(jnp.int32)
    return total


def sequence_ends(lengths_ref):
    ends, total = [], 0
    for i in range(lengths_ref.shape[1]):
        total = total + lengths_ref[0, i]
        ends.append(total)
    return ends


def step_parts(step_raw, rate, ends, base):
    rows = step_raw.shape[0]
    step = softplus(step_raw)
    row = lax.broadcasted_iota(jnp.int32, (rows, rows), 0)
    col = lax.broadcasted_iota(jnp.int32, (rows, rows), 1)
    lower = (row >= col).astype(f32).astype(bf16)
    split = mm(lower, halves(step * rate, 1), NN)
    running = split[:, :LANES] + split[:, LANES:]
    position = base + lax.broadcasted_iota(jnp.int32, (rows, 1), 0)
    segment = segment_at(ends, position)
    before = segment_at(ends, jnp.full((1, 1), base - 1, jnp.int32))
    last = segment_at(ends, jnp.full((1, 1), base + rows - 1, jnp.int32))
    carried = ((segment == before) & (position >= rows)).astype(f32)
    matched = (segment == last).astype(f32)
    entry = jnp.exp(running) * carried
    leave = jnp.exp(running[rows - 1 :, :] - running) * matched
    return step, running, entry, leave, lower, segment, row, col


def same_rows(ends, base, rows):
    across = segment_at(ends, base + lax.broadcasted_iota(jnp.int32, (1, rows), 1))
    down = segment_at(ends, base + lax.broadcasted_iota(jnp.int32, (rows, 1), 0))
    return down == across


def forward_kernel(
    lengths_ref, normed_ref, weight_ref, conv_inner_ref, bias_inner_ref,
    conv_shared_ref, bias_shared_ref, step_bias_ref, rate_ref, skip_ref, spread_ref,
    ssm_ref, inner_ref, pre_inner_ref, shared_ref, pre_shared_ref, step_ref, entering_ref,
    inner_tail, shared_tail, state,
):
    block = pl.program_id(0)
    rows = normed_ref.shape[0]
    channels = conv_inner_ref.shape[1]
    base = block * rows
    ends = sequence_ends(lengths_ref)

    @pl.when(block == 0)
    def _():
        inner_tail[0:TAIL, :] = jnp.zeros((TAIL, channels), f32)
        shared_tail[0:TAIL, :] = jnp.zeros((TAIL, shared_tail.shape[1]), f32)
        state[...] = jnp.zeros_like(state)

    @pl.when(block > 0)
    def _():
        inner_tail[0:TAIL, :] = inner_tail[rows : rows + TAIL, :]
        shared_tail[0:TAIL, :] = shared_tail[rows : rows + TAIL, :]

    normed = normed_ref[...]
    small = mm(normed, weight_ref[:, channels:], NN)
    width = conv_shared_ref.shape[1]
    shared_proj = small[:, :width]
    shared_tail[TAIL : TAIL + rows, :] = shared_proj
    shared_ref[...] = shared_proj
    step_raw = small[:, width:] + step_bias_ref[...]
    step_ref[...] = step_raw
    inner_proj = mm(normed, weight_ref[:, :channels], NN)
    inner_tail[TAIL : TAIL + rows, :] = inner_proj
    inner_ref[...] = inner_proj

    step, running, entry, leave, lower, segment, row, col = step_parts(
        step_raw, rate_ref[...], ends, base
    )
    position = base + lax.broadcasted_iota(jnp.int32, (rows, 1), 0)
    keeps = [
        ((segment_at(ends, position - k) == segment) & (position >= k)).astype(f32)
        for k in range(1, TAPS)
    ]

    def conv(tail, taps_ref, bias_ref, lo, hi):
        total = bias_ref[:, lo:hi] + taps_ref[TAPS - 1 : TAPS, lo:hi] * tail[TAIL : TAIL + rows, lo:hi]
        for k in range(1, TAPS):
            shifted = tail[TAIL - k : TAIL - k + rows, lo:hi]
            total = total + taps_ref[TAPS - 1 - k : TAPS - k, lo:hi] * (shifted * keeps[k - 1])
        return total

    pre_shared = conv(shared_tail, conv_shared_ref, bias_shared_ref, 0, width)
    pre_shared_ref[...] = pre_shared
    shared = pre_shared * sigmoid(pre_shared)
    in_map = shared[:, : width // 2].astype(bf16)
    out_map = shared[:, width // 2 :].astype(bf16)
    scores = mm(out_map, in_map, NT)
    allowed = jnp.where((row >= col) & same_rows(ends, base, rows), 0.0, MASKED)
    running_t = jnp.transpose(running)
    step2, entry2, leave2 = halves(step, 1), halves(entry, 1), halves(leave, 1)
    lane = lax.broadcasted_iota(jnp.int32, (rows, LANES), 1)
    for pair in range(channels // LANES):
        lo, hi = pair * LANES, (pair + 1) * LANES
        pre = conv(inner_tail, conv_inner_ref, bias_inner_ref, lo, hi)
        pre_inner_ref[:, lo:hi] = pre
        head_in = pre * sigmoid(pre)
        spread = spread_ref[:, lo:hi]
        scaled = head_in * mm(step2, spread, NN)
        scaled_low = scaled.astype(bf16)
        entry_wide = mm(entry2, spread, NN)
        leave_wide = mm(leave2, spread, NN)
        held = state[:, lo:hi]
        entering_ref[0, :, lo:hi] = held
        carried_out = mm(out_map, held.astype(bf16), NN) * entry_wide
        parts = []
        for side in range(2):
            head = 2 * pair + side
            gap = running[:, head : head + 1] - running_t[head : head + 1, :]
            mixed = (scores * jnp.exp(gap + allowed)).astype(bf16)
            parts.append(mm(mixed, scaled_low, NN))
        intra = jnp.where(lane < LANES // 2, parts[0], parts[1])
        ssm_ref[:, lo:hi] = carried_out + intra + skip_ref[:, lo:hi] * head_in
        added = mm(in_map, (scaled * leave_wide).astype(bf16), TN)
        state[:, lo:hi] = held * entry_wide[rows - 1 :, :] + added


def full(shape):
    return pl.BlockSpec(shape, lambda *_: (0,) * len(shape))


def mixer_forward(
    lengths, normed, weight, conv_inner, bias_inner, conv_shared, bias_shared,
    step_bias, rate, skip, spread, span,
):
    rows, model = normed.shape
    channels = conv_inner.shape[1]
    width = conv_shared.shape[1]
    blocks = rows // span
    by_row = lambda cols: pl.BlockSpec((span, cols), lambda i: (i, 0))
    shape = lambda cols: jax.ShapeDtypeStruct((rows, cols), f32)
    states = width // 2
    return pl.pallas_call(
        forward_kernel,
        grid=(blocks,),
        in_specs=[
            pl.BlockSpec(memory_space=pltpu.SMEM),
            by_row(model),
            full(weight.shape),
            full(conv_inner.shape),
            full(bias_inner.shape),
            full(conv_shared.shape),
            full(bias_shared.shape),
            full(step_bias.shape),
            full(rate.shape),
            full(skip.shape),
            full(spread.shape),
        ],
        out_specs=[
            by_row(channels), by_row(channels), by_row(channels), by_row(width), by_row(width),
            by_row(LANES), pl.BlockSpec((1, states, channels), lambda i: (i, 0, 0)),
        ],
        out_shape=[
            shape(channels), shape(channels), shape(channels), shape(width), shape(width),
            shape(LANES), jax.ShapeDtypeStruct((blocks, states, channels), f32),
        ],
        scratch_shapes=[
            pltpu.VMEM((TAIL + span, channels), f32),
            pltpu.VMEM((TAIL + span, width), f32),
            pltpu.VMEM((states, channels), f32),
        ],
        compiler_params=pltpu.CompilerParams(
            dimension_semantics=("arbitrary",), vmem_limit_bytes=LIMIT
        ),
        name="mixer_forward",
    )(
        lengths, normed, weight, conv_inner, bias_inner, conv_shared, bias_shared,
        step_bias, rate, skip, spread,
    )


def backward_kernel(
    lengths_ref, upstream_ref, ssm_ref, inner_ref, pre_inner_ref, shared_ref, pre_shared_ref,
    step_ref, entering_ref, conv_inner_ref, conv_shared_ref, rate_ref, skip_ref, spread_ref,
    gain_sum_ref, grad_inner_ref, grad_small_ref, sums_ref, inner_head, shared_head, adjoint,
):
    turn = pl.program_id(0)
    block = pl.num_programs(0) - 1 - turn
    rows, channels = upstream_ref.shape
    width = conv_shared_ref.shape[1]
    base = block * rows
    total_rows = pl.num_programs(0) * rows
    ends = sequence_ends(lengths_ref)

    @pl.when(turn == 0)
    def _():
        inner_head[rows : rows + TAIL, :] = jnp.zeros((TAIL, channels), f32)
        shared_head[rows : rows + TAIL, :] = jnp.zeros((TAIL, width), f32)
        adjoint[...] = jnp.zeros_like(adjoint)
        sums_ref[...] = jnp.zeros_like(sums_ref)
        sums_ref[TAIL - 1 : TAIL, :channels] = gain_sum_ref[0:1, :]

    @pl.when(turn > 0)
    def _():
        inner_head[rows : rows + TAIL, :] = inner_head[0:TAIL, :]
        shared_head[rows : rows + TAIL, :] = shared_head[0:TAIL, :]

    step_raw = step_ref[...]
    rate = rate_ref[...]
    step, running, entry, leave, lower, segment, row, col = step_parts(step_raw, rate, ends, base)
    position = base + lax.broadcasted_iota(jnp.int32, (rows, 1), 0)
    keeps = [
        ((segment_at(ends, position + k) == segment) & (position + k < total_rows)).astype(f32)
        for k in range(1, TAPS)
    ]
    pre_shared = pre_shared_ref[...]
    shared_gate = sigmoid(pre_shared)
    shared = pre_shared * shared_gate
    half = width // 2
    in_map = shared[:, :half].astype(bf16)
    out_map = shared[:, half:].astype(bf16)
    scores_t = mm(in_map, out_map, NT)
    allowed_t = jnp.where((col >= row) & same_rows(ends, base, rows), 0.0, MASKED)
    running_t = jnp.transpose(running)
    step2, entry2, leave2 = halves(step, 1), halves(entry, 1), halves(leave, 1)
    lane = lax.broadcasted_iota(jnp.int32, (rows, LANES), 1)
    first_half = lane < LANES // 2
    grad_scores_t = jnp.zeros((rows, rows), f32)
    grad_in = jnp.zeros((rows, half), f32)
    grad_out = jnp.zeros((rows, half), f32)
    by_head = jnp.zeros((rows, LANES), f32)
    step_terms = jnp.zeros((rows, LANES), f32)
    leaving = jnp.zeros((TAIL, LANES), f32)
    for pair in range(channels // LANES):
        lo, hi = pair * LANES, (pair + 1) * LANES
        spread = spread_ref[:, lo:hi]
        step_wide = mm(step2, spread, NN)
        entry_wide = mm(entry2, spread, NN)
        leave_wide = mm(leave2, spread, NN)
        pre = pre_inner_ref[:, lo:hi]
        gate = sigmoid(pre)
        head_in = pre * gate
        skip = skip_ref[:, lo:hi]
        upstream = upstream_ref[:, lo:hi]
        upstream_low = upstream.astype(bf16)
        upstream_back = upstream_low.astype(f32)
        scaled = head_in * step_wide
        scaled_low = scaled.astype(bf16)
        scaled_back = scaled_low.astype(f32)
        held = entering_ref[0, :, lo:hi]
        held_low = held.astype(bf16)
        ahead = adjoint[:, lo:hi]
        ahead_low = ahead.astype(bf16)
        entry_up = (upstream_back * entry_wide).astype(bf16)
        grad_out = grad_out + mm(entry_up, held_low, NT)
        grad_in = grad_in + mm((scaled * leave_wide).astype(bf16), ahead_low, NT)
        grad_scaled = mm(in_map, ahead_low, NN) * leave_wide
        through = entry_wide[rows - 1 :, :]
        tail_terms = jnp.sum(scaled_back * grad_scaled, axis=0, keepdims=True) + through * jnp.sum(
            ahead * held, axis=0, keepdims=True
        )
        adjoint[:, lo:hi] = ahead * through + mm(out_map, entry_up, TN)
        parts = []
        for side in range(2):
            head = 2 * pair + side
            gap = running_t[head : head + 1, :] - running[:, head : head + 1]
            decay = jnp.exp(gap + allowed_t)
            mixed = (scores_t * decay).astype(bf16)
            parts.append(mm(mixed, upstream_low, NN))
            mine = first_half if side == 0 else jnp.logical_not(first_half)
            chosen = jnp.where(mine, scaled_back, 0.0).astype(bf16)
            grad_scores_t = grad_scores_t + mm(chosen, upstream_low, NT) * decay
        grad_scaled = grad_scaled + jnp.where(first_half, parts[0], parts[1])
        spread_one = spread[:LANES, :]
        spread_both = jnp.concatenate([spread_one, spread_one], axis=1)
        balance = upstream_back * (ssm_ref[:, lo:hi] - skip * head_in) - scaled_back * grad_scaled
        by_head = by_head + mm(halves(balance, 1), spread_both, NT)
        step_terms = step_terms + mm(halves(head_in * grad_scaled, 1), spread_both, NT)
        skip_terms = jnp.sum(upstream * head_in, axis=0, keepdims=True)
        edge = jnp.concatenate([tail_terms, skip_terms, jnp.zeros((TAIL - 2, LANES), f32)], axis=0)
        leaving = leaving + mm(halves(edge, 1), spread_both, NT)
        grad_pre = (grad_scaled * step_wide + skip * upstream) * (gate * (1.0 + pre * (1.0 - gate)))
        inner_head[0:rows, lo:hi] = grad_pre
        inner_proj = inner_ref[:, lo:hi]
        grad_proj = conv_inner_ref[TAPS - 1 : TAPS, lo:hi] * grad_pre
        sums = [None] * TAPS
        sums[TAPS - 1] = jnp.sum(grad_pre * inner_proj, axis=0, keepdims=True)
        for k in range(1, TAPS):
            moved = inner_head[k : k + rows, lo:hi] * keeps[k - 1]
            grad_proj = grad_proj + conv_inner_ref[TAPS - 1 - k : TAPS - k, lo:hi] * moved
            sums[TAPS - 1 - k] = jnp.sum(moved * inner_proj, axis=0, keepdims=True)
        grad_inner_ref[:, lo:hi] = grad_proj.astype(bf16)
        sums.append(jnp.sum(grad_pre, axis=0, keepdims=True))
        sums.append(jnp.zeros((TAIL - len(sums), LANES), f32))
        sums_ref[:, lo:hi] += jnp.concatenate(sums, axis=0)
    grad_scores_low = grad_scores_t.astype(bf16)
    grad_out = grad_out + mm(grad_scores_low, in_map, TN)
    grad_in = grad_in + mm(grad_scores_low, out_map, NN)
    grad_shared = jnp.concatenate([grad_in, grad_out], axis=1)
    grad_pre = grad_shared * (shared_gate * (1.0 + pre_shared * (1.0 - shared_gate)))
    shared_head[0:rows, :] = grad_pre
    shared_proj = shared_ref[...]
    grad_proj = conv_shared_ref[TAPS - 1 : TAPS, :] * grad_pre
    sums = [None] * TAPS
    sums[TAPS - 1] = jnp.sum(grad_pre * shared_proj, axis=0, keepdims=True)
    for k in range(1, TAPS):
        moved = shared_head[k : k + rows, :] * keeps[k - 1]
        grad_proj = grad_proj + conv_shared_ref[TAPS - 1 - k : TAPS - k, :] * moved
        sums[TAPS - 1 - k] = jnp.sum(moved * shared_proj, axis=0, keepdims=True)
    sums.append(jnp.sum(grad_pre, axis=0, keepdims=True))
    sums.append(jnp.zeros((TAIL - len(sums), width), f32))
    sums_ref[:, channels : channels + width] += jnp.concatenate(sums, axis=0)
    split = mm(lower, halves(by_head, 1), TN)
    grad_log = split[:, :LANES] + split[:, LANES:] + leaving[0:1, :]
    grad_step = (step_terms + rate * grad_log) * sigmoid(step_raw)
    grad_small_ref[...] = jnp.concatenate([grad_proj, grad_step], axis=1).astype(bf16)
    sums_ref[:, channels + width :] += jnp.concatenate(
        [
            jnp.sum(grad_step, axis=0, keepdims=True),
            rate * jnp.sum(step * grad_log, axis=0, keepdims=True),
            leaving[1:2, :],
            jnp.zeros((TAIL - 3, LANES), f32),
        ],
        axis=0,
    )


def mixer_backward(
    lengths, upstream, saved, conv_inner, conv_shared, rate, skip, spread, gain_sum, span
):
    ssm, inner, pre_inner, shared, pre_shared, step_raw, entering = saved
    rows, channels = upstream.shape
    width = conv_shared.shape[1]
    blocks = rows // span
    states = width // 2
    by_row = lambda cols: pl.BlockSpec((span, cols), lambda i: (blocks - 1 - i, 0))
    return pl.pallas_call(
        backward_kernel,
        grid=(blocks,),
        in_specs=[
            pl.BlockSpec(memory_space=pltpu.SMEM),
            by_row(channels), by_row(channels), by_row(channels), by_row(channels),
            by_row(width), by_row(width), by_row(LANES),
            pl.BlockSpec((1, states, channels), lambda i: (blocks - 1 - i, 0, 0)),
            full(conv_inner.shape),
            full(conv_shared.shape),
            full(rate.shape),
            full(skip.shape),
            full(spread.shape),
            full(gain_sum.shape),
        ],
        out_specs=[
            by_row(channels), by_row(width + LANES), full((TAIL, channels + width + LANES)),
        ],
        out_shape=[
            jax.ShapeDtypeStruct((rows, channels), bf16),
            jax.ShapeDtypeStruct((rows, width + LANES), bf16),
            jax.ShapeDtypeStruct((TAIL, channels + width + LANES), f32),
        ],
        scratch_shapes=[
            pltpu.VMEM((TAIL + span, channels), f32),
            pltpu.VMEM((TAIL + span, width), f32),
            pltpu.VMEM((states, channels), f32),
        ],
        compiler_params=pltpu.CompilerParams(
            dimension_semantics=("arbitrary",), vmem_limit_bytes=LIMIT
        ),
        name="mixer_backward",
    )(
        lengths, upstream, ssm, inner, pre_inner, shared, pre_shared, step_raw, entering,
        conv_inner, conv_shared, rate, skip, spread, gain_sum,
    )


def gate_kernel(normed_ref, gate_w_ref, upstream_ref, out_w_ref, gain_ref, ssm_ref,
                gate_ref, grad_ref, sums_ref):
    rows = normed_ref.shape[0]
    gate = mm(normed_ref[...], gate_w_ref[...], NN)
    grad = mm(upstream_ref[...], out_w_ref[...], NN)
    gate_ref[...] = gate
    grad_ref[...] = grad
    gated = ssm_ref[...] * (gate * sigmoid(gate))
    square = jnp.sum(gated * gated, axis=1, keepdims=True)
    cross = jnp.sum(grad * gain_ref[...] * gated, axis=1, keepdims=True)
    lane = lax.broadcasted_iota(jnp.int32, (rows, LANES), 1)
    both = jnp.where(lane == 0, square, jnp.where(lane == 1, cross, 0.0))
    sums_ref[...] = jnp.transpose(both)[0:TAIL, :]


def gate_forward(normed, upstream, weight, gain, ssm, span):
    rows, model = normed.shape
    channels = ssm.shape[1]
    by_row = lambda cols: pl.BlockSpec((span, cols), lambda i: (i, 0))
    return pl.pallas_call(
        gate_kernel,
        grid=(rows // span,),
        in_specs=[
            by_row(model), pl.BlockSpec((model, channels), lambda i: (0, 0)), by_row(model),
            pl.BlockSpec((model, channels), lambda i: (0, 1)), full(gain.shape), by_row(channels),
        ],
        out_specs=[by_row(channels), by_row(channels), pl.BlockSpec((TAIL, span), lambda i: (0, i))],
        out_shape=[
            jax.ShapeDtypeStruct((rows, channels), f32),
            jax.ShapeDtypeStruct((rows, channels), f32),
            jax.ShapeDtypeStruct((TAIL, rows), f32),
        ],
        compiler_params=pltpu.CompilerParams(
            dimension_semantics=("arbitrary",), vmem_limit_bytes=LIMIT
        ),
        name="gate_forward",
    )(normed, weight, upstream, weight, gain, ssm)


def norm_kernel(full_inner, sums_ref, gate_ref, grad_ref, ssm_ref, gain_ref,
                scaled_ref, grad_gate_ref, grad_ssm_ref, gain_sum_ref):
    rows, channels = gate_ref.shape

    @pl.when(pl.program_id(0) == 0)
    def _():
        gain_sum_ref[...] = jnp.zeros_like(gain_sum_ref)

    padded = jnp.concatenate([sums_ref[...], jnp.zeros((LANES - TAIL, rows), f32)], axis=0)
    sums = jnp.transpose(padded)
    scale = lax.rsqrt(sums[:, 0:1] / full_inner + EPSILON)
    pull = scale * scale * scale * (sums[:, 1:2] / full_inner)
    for lo in range(0, channels, LANES):
        hi = lo + LANES
        gain = gain_ref[:, lo:hi]
        gate, grad, ssm = gate_ref[:, lo:hi], grad_ref[:, lo:hi], ssm_ref[:, lo:hi]
        sig = sigmoid(gate)
        silu = gate * sig
        gated = ssm * silu
        normal = gated * scale
        scaled_ref[:, lo:hi] = (normal * gain).astype(bf16)
        gain_sum_ref[:, lo:hi] += jnp.broadcast_to(
            jnp.sum(grad * normal, axis=0, keepdims=True), (TAIL, LANES)
        )
        grad_gated = scale * (grad * gain) - gated * pull
        grad_ssm_ref[:, lo:hi] = grad_gated * silu
        grad_gate_ref[:, lo:hi] = (grad_gated * ssm * (sig * (1.0 + gate * (1.0 - sig)))).astype(bf16)


def gate_norm(sums, gate, grad, ssm, gain, full_inner, span):
    rows, channels = gate.shape
    by_row = lambda cols: pl.BlockSpec((span, cols), lambda i: (i, 0))
    return pl.pallas_call(
        partial(norm_kernel, float(full_inner)),
        grid=(rows // span,),
        in_specs=[
            pl.BlockSpec((TAIL, span), lambda i: (0, i)), by_row(channels), by_row(channels),
            by_row(channels), full(gain.shape),
        ],
        out_specs=[by_row(channels), by_row(channels), by_row(channels), full((TAIL, channels))],
        out_shape=[
            jax.ShapeDtypeStruct((rows, channels), bf16),
            jax.ShapeDtypeStruct((rows, channels), bf16),
            jax.ShapeDtypeStruct((rows, channels), f32),
            jax.ShapeDtypeStruct((TAIL, channels), f32),
        ],
        compiler_params=pltpu.CompilerParams(
            dimension_semantics=("arbitrary",), vmem_limit_bytes=LIMIT
        ),
        name="gate_norm",
    )(sums, gate, grad, ssm, gain)


def lanes_of(vector):
    return jnp.pad(vector, (0, LANES - vector.shape[0]))[None, :]


def spread_map(heads, channels):
    size = channels // heads
    row = lax.broadcasted_iota(jnp.int32, (2 * LANES, channels), 0) % LANES
    col = lax.broadcasted_iota(jnp.int32, (2 * LANES, channels), 1) // size
    return (row == col).astype(bf16)


def input_kernel(grad_gate_ref, grad_inner_ref, grad_small_ref, gate_w_ref, weight_ref, normed_ref,
                 gain_ref, sums_ref, terms_ref, packed_ref):
    channels = grad_inner_ref.shape[1]
    known = sums_ref.shape[1]
    terms = mm(grad_gate_ref[...], gate_w_ref[...], NT)
    terms = terms + mm(grad_inner_ref[...], weight_ref[:, :channels], NT)
    terms = terms + mm(grad_small_ref[...], weight_ref[:, channels:], NT)
    terms_ref[...] = terms.astype(bf16)

    @pl.when(pl.program_id(0) == 0)
    def _():
        packed_ref[:, :known] = sums_ref[...]
        packed_ref[:, known:] = jnp.zeros((TAIL, packed_ref.shape[1] - known), f32)

    total = jnp.sum(terms * normed_ref[...].astype(f32), axis=0, keepdims=True) / gain_ref[...]
    packed_ref[0:1, known:] += total


def input_terms(grad_gate, grad_inner, grad_small, weight_late, weight, normed, gain, sums, span):
    rows, model = normed.shape
    channels = grad_inner.shape[1]
    known = sums.shape[1]
    by_row = lambda cols: pl.BlockSpec((span, cols), lambda i: (i, 0))
    return pl.pallas_call(
        input_kernel,
        grid=(rows // span,),
        in_specs=[
            by_row(channels), by_row(channels), by_row(grad_small.shape[1]),
            pl.BlockSpec((model, channels), lambda i: (0, 0)), full(weight.shape), by_row(model),
            full(gain.shape), full(sums.shape),
        ],
        out_specs=[by_row(model), full((TAIL, known + model))],
        out_shape=[
            jax.ShapeDtypeStruct((rows, model), bf16),
            jax.ShapeDtypeStruct((TAIL, known + model), f32),
        ],
        compiler_params=pltpu.CompilerParams(
            dimension_semantics=("arbitrary",), vmem_limit_bytes=LIMIT
        ),
        name="input_terms",
    )(grad_gate, grad_inner, grad_small, weight_late, weight, normed, gain, sums)


def dp_send(value, bit):
    size = lax.axis_size("dp")
    return lax.ppermute(value, "dp", [(i, i ^ bit) for i in range(size)])


def chip_bits():
    return [4 * k for k in range(1, lax.axis_size("dp") // 4)]


def choose(stacked, index, axis):
    return lax.dynamic_index_in_dim(stacked, index, axis, keepdims=False)


def gather_dp(shard):
    me = lax.axis_index("dp")
    rows, cols = shard.shape
    bits = chip_bits()
    pieces = [shard] + [dp_send(shard, bit) for bit in bits]
    count = len(pieces)
    place = me // 4
    stacked = jnp.zeros((count, rows, cols), shard.dtype)
    for k, piece in enumerate(pieces):
        stacked = lax.dynamic_update_index_in_dim(stacked, piece, place ^ k, 0)
    other = dp_send(stacked, 2)
    upper = (me // 2) % 2 == 1
    both = jnp.stack([jnp.where(upper, other, stacked), jnp.where(upper, stacked, other)], axis=1)
    other = dp_send(both, 1)
    upper = me % 2 == 1
    whole = jnp.stack([jnp.where(upper, other, both), jnp.where(upper, both, other)], axis=2)
    return whole.reshape(4 * count * rows, cols)


def scatter_dp(grads):
    me = lax.axis_index("dp")
    bits = chip_bits()
    count = len(bits) + 1
    parts = [g.reshape(count, 2, 2, -1, g.shape[1]) for g in grads]
    for axis, bit in ((2, 1), (1, 2)):
        mine = (me // bit) % 2
        got = [dp_send(choose(p, 1 - mine, axis), bit) for p in parts]
        parts = [choose(p, mine, axis).astype(f32) + g.astype(f32) for p, g in zip(parts, got)]
        if bit == 1:
            parts = [p.astype(bf16) for p in parts]
    place = me // 4
    sends = [p.astype(bf16) for p in parts]
    totals = [choose(p, place, 0) for p in parts]
    got = [
        [dp_send(choose(p, place ^ (k + 1), 0), bit) for k, bit in enumerate(bits)] for p in sends
    ]
    for i in range(len(totals)):
        for piece in got[i]:
            totals[i] = totals[i] + piece.astype(f32)
    return totals


def tensor_swap(value):
    return lax.ppermute(value, "tensor", [(0, 1), (1, 0)])


def sum_dp(value):
    value = value + dp_send(value, 1)
    value = value + dp_send(value, 2)
    bits = chip_bits()
    pieces = [value] + [dp_send(value, bit) for bit in bits]
    while len(pieces) > 1:
        pieces = [a + b for a, b in zip(pieces[0::2], pieces[1::2])]
    return pieces[0]


def both_halves(own, size):
    if size != 2:
        return lax.all_gather(own, "tensor", axis=0, tiled=True)
    other = tensor_swap(own)
    upper = lax.axis_index("tensor") == 1
    return jnp.concatenate([jnp.where(upper, other, own), jnp.where(upper, own, other)], axis=0)


def own_half(value, size):
    if size != 2:
        return lax.psum_scatter(value, "tensor", scatter_dimension=0, tiled=True).astype(f32)
    me = lax.axis_index("tensor")
    halved = value.reshape(2, -1, value.shape[1])
    got = tensor_swap(choose(halved, 1 - me, 0))
    return choose(halved, me, 0).astype(f32) + got.astype(f32)


def across(left, right):
    return lax.dot_general(
        left, right, (((0,), (0,)), ((), ())), preferred_element_type=f32
    ).astype(bf16)


def shards(
    tokens, lengths, norm_gain, zx_weight, bc_weight, dt_weight, conv_inner, bias_inner,
    conv_shared, bias_shared, step_bias, log_rate, skip_gain, gate_gain, out_weight, cotangent,
):
    size = lax.axis_size("tensor")
    channels = zx_weight.shape[2]
    heads = step_bias.shape[0]
    width = bc_weight.shape[1]
    inputs = tokens.astype(f32)
    norm_scale = lax.rsqrt(jnp.mean(inputs * inputs, axis=1, keepdims=True) + EPSILON)
    normed_rows = (inputs * norm_scale * norm_gain[None, :]).astype(bf16)
    step_weight = jnp.pad(dt_weight, ((0, 0), (0, LANES - heads)))
    early = jnp.concatenate([zx_weight[:, 1, :], bc_weight, step_weight], axis=1)
    late = jnp.concatenate([zx_weight[:, 0, :], out_weight], axis=1)
    normed = both_halves(normed_rows, size)
    weight = gather_dp(early)
    weight_late = lax.all_gather(late, "dp", axis=0, tiled=True)
    upstream = both_halves(cotangent, size)
    spread = spread_map(heads, channels)
    rate = lanes_of(-jnp.exp(log_rate))
    skip = jnp.repeat(skip_gain, channels // heads)[None, :]
    saved = mixer_forward(
        lengths, normed, weight, conv_inner, bias_inner[None, :], conv_shared,
        bias_shared[None, :], lanes_of(step_bias), rate, skip, spread, SPAN,
    )
    gain = gate_gain[None, :]
    gate, grad, sums = gate_forward(normed, upstream, weight_late, gain, saved[0], SPAN)
    sums = lax.psum(sums, "tensor")
    scaled_out, grad_gate, grad_ssm, gain_sum = gate_norm(
        sums, gate, grad, saved[0], gain, channels * size, SPAN
    )
    branch = lax.dot_general(
        scaled_out, weight_late[:, channels:], (((1,), (1,)), ((), ())), preferred_element_type=f32
    ).astype(bf16)
    block_out = (inputs + own_half(branch, size)).astype(bf16)
    first = jnp.concatenate([across(normed, grad_gate), across(upstream, scaled_out)], axis=1)
    first = lax.psum_scatter(first, "dp", scatter_dimension=0, tiled=True)
    grad_inner, grad_small, sums = mixer_backward(
        lengths, grad_ssm, saved, conv_inner, conv_shared, rate, skip, spread, gain_sum, SPAN
    )
    grads = [across(normed, grad_inner), across(normed, grad_small)]
    terms, packed = input_terms(
        grad_gate, grad_inner, grad_small, weight_late, weight, normed, norm_gain[None, :], sums,
        SPAN,
    )
    part_inner, part_small = scatter_dp(grads)
    packed = sum_dp(packed)
    grad_normed = own_half(terms, size)
    packed_all = lax.psum(packed, "tensor")
    part_shared = lax.psum(part_small[:, :width].astype(bf16), "tensor").astype(f32)
    scaled_grad = grad_normed * norm_gain[None, :]
    grad_inputs = norm_scale * scaled_grad - inputs * norm_scale**3 * jnp.mean(
        scaled_grad * inputs, axis=1, keepdims=True
    )
    grad_tokens = (cotangent.astype(f32) + grad_inputs).astype(bf16)
    part_in = jnp.stack([first[:, :channels].astype(f32), part_inner], axis=1)
    at_step = channels + width
    at_norm = at_step + LANES
    return (
        block_out,
        grad_tokens,
        packed_all[0, at_norm:],
        part_in,
        part_shared,
        part_small[:, width : width + heads],
        packed[:TAPS, :channels],
        packed[TAPS, :channels],
        packed_all[:TAPS, channels:at_step],
        packed_all[TAPS, channels:at_step],
        packed[0, at_step : at_step + heads],
        packed[1, at_step : at_step + heads],
        packed[2, at_step : at_step + heads],
        packed[TAIL - 1, :channels],
        first[:, channels:].astype(f32),
    )


def solution(mesh):
    return jax.shard_map(
        shards,
        mesh=mesh,
        in_specs=(
            P(("dp", "tensor"), None),
            P("dp", None),
            P(),
            P("dp", None, "tensor"),
            P("dp", None),
            P("dp", "tensor"),
            P(None, "tensor"),
            P("tensor"),
            P(),
            P(),
            P("tensor"),
            P("tensor"),
            P("tensor"),
            P("tensor"),
            P("dp", "tensor"),
            P(("dp", "tensor"), None),
        ),
        out_specs=(
            P(("dp", "tensor"), None),
            P(("dp", "tensor"), None),
            P(),
            P("dp", None, "tensor"),
            P("dp", None),
            P("dp", "tensor"),
            P(None, "tensor"),
            P("tensor"),
            P(),
            P(),
            P("tensor"),
            P("tensor"),
            P("tensor"),
            P("tensor"),
            P("dp", "tensor"),
        ),
        check_vma=False,
    )
```

```python
from functools import partial

import jax
import jax.numpy as jnp
from jax import lax
from jax.experimental import pallas as pl
from jax.experimental.pallas import tpu as pltpu
from jax.sharding import PartitionSpec as P

EPSILON = 1e-05
SPAN = 256
LANES = 128
TAIL = 8
TAPS = 4
MASKED = -1e30
f32 = jnp.float32
bf16 = jnp.bfloat16
LIMIT = 60 * 1024 * 1024


def mm(left, right, dims):
    return lax.dot_general(left, right, ((dims[0], dims[1]), ((), ())), preferred_element_type=f32)


NN = ((1,), (0,))
NT = ((1,), (1,))
TN = ((0,), (0,))


def halves(value, axis):
    high = value.astype(bf16)
    low = (value - high.astype(f32)).astype(bf16)
    return jnp.concatenate([high, low], axis=axis)


def sigmoid(value):
    return 1.0 / (1.0 + jnp.exp(-value))


def softplus(value):
    return jnp.maximum(value, 0.0) + jnp.log1p(jnp.exp(-jnp.abs(value)))


def segment_at(ends, position):
    total = jnp.zeros(position.shape, jnp.int32)
    for end in ends:
        total = total + (position >= end).astype(jnp.int32)
    return total


def sequence_ends(lengths_ref):
    ends, total = [], 0
    for i in range(lengths_ref.shape[1]):
        total = total + lengths_ref[0, i]
        ends.append(total)
    return ends


def step_parts(step_raw, rate, ends, base):
    rows = step_raw.shape[0]
    step = softplus(step_raw)
    row = lax.broadcasted_iota(jnp.int32, (rows, rows), 0)
    col = lax.broadcasted_iota(jnp.int32, (rows, rows), 1)
    lower = (row >= col).astype(f32).astype(bf16)
    split = mm(lower, halves(step * rate, 1), NN)
    running = split[:, :LANES] + split[:, LANES:]
    position = base + lax.broadcasted_iota(jnp.int32, (rows, 1), 0)
    segment = segment_at(ends, position)
    before = segment_at(ends, jnp.full((1, 1), base - 1, jnp.int32))
    last = segment_at(ends, jnp.full((1, 1), base + rows - 1, jnp.int32))
    carried = ((segment == before) & (position >= rows)).astype(f32)
    matched = (segment == last).astype(f32)
    entry = jnp.exp(running) * carried
    leave = jnp.exp(running[rows - 1 :, :] - running) * matched
    return step, running, entry, leave, lower, segment, row, col


def same_rows(ends, base, rows):
    across = segment_at(ends, base + lax.broadcasted_iota(jnp.int32, (1, rows), 1))
    down = segment_at(ends, base + lax.broadcasted_iota(jnp.int32, (rows, 1), 0))
    return down == across


def forward_kernel(
    lengths_ref, normed_ref, weight_ref, conv_inner_ref, bias_inner_ref,
    conv_shared_ref, bias_shared_ref, step_bias_ref, rate_ref, skip_ref, spread_ref,
    ssm_ref, inner_ref, pre_inner_ref, shared_ref, pre_shared_ref, step_ref, entering_ref,
    inner_tail, shared_tail, state,
):
    block = pl.program_id(0)
    rows = normed_ref.shape[0]
    channels = conv_inner_ref.shape[1]
    base = block * rows
    ends = sequence_ends(lengths_ref)

    @pl.when(block == 0)
    def _():
        inner_tail[0:TAIL, :] = jnp.zeros((TAIL, channels), f32)
        shared_tail[0:TAIL, :] = jnp.zeros((TAIL, shared_tail.shape[1]), f32)
        state[...] = jnp.zeros_like(state)

    @pl.when(block > 0)
    def _():
        inner_tail[0:TAIL, :] = inner_tail[rows : rows + TAIL, :]
        shared_tail[0:TAIL, :] = shared_tail[rows : rows + TAIL, :]

    normed = normed_ref[...]
    small = mm(normed, weight_ref[:, channels:], NN)
    width = conv_shared_ref.shape[1]
    shared_proj = small[:, :width]
    shared_tail[TAIL : TAIL + rows, :] = shared_proj
    shared_ref[...] = shared_proj
    step_raw = small[:, width:] + step_bias_ref[...]
    step_ref[...] = step_raw
    inner_proj = mm(normed, weight_ref[:, :channels], NN)
    inner_tail[TAIL : TAIL + rows, :] = inner_proj
    inner_ref[...] = inner_proj

    step, running, entry, leave, lower, segment, row, col = step_parts(
        step_raw, rate_ref[...], ends, base
    )
    position = base + lax.broadcasted_iota(jnp.int32, (rows, 1), 0)
    keeps = [
        ((segment_at(ends, position - k) == segment) & (position >= k)).astype(f32)
        for k in range(1, TAPS)
    ]

    def conv(tail, taps_ref, bias_ref, lo, hi):
        total = bias_ref[:, lo:hi] + taps_ref[TAPS - 1 : TAPS, lo:hi] * tail[TAIL : TAIL + rows, lo:hi]
        for k in range(1, TAPS):
            shifted = tail[TAIL - k : TAIL - k + rows, lo:hi]
            total = total + taps_ref[TAPS - 1 - k : TAPS - k, lo:hi] * (shifted * keeps[k - 1])
        return total

    pre_shared = conv(shared_tail, conv_shared_ref, bias_shared_ref, 0, width)
    pre_shared_ref[...] = pre_shared
    shared = pre_shared * sigmoid(pre_shared)
    in_map = shared[:, : width // 2].astype(bf16)
    out_map = shared[:, width // 2 :].astype(bf16)
    scores = mm(out_map, in_map, NT)
    allowed = jnp.where((row >= col) & same_rows(ends, base, rows), 0.0, MASKED)
    running_t = jnp.transpose(running)
    step2, entry2, leave2 = halves(step, 1), halves(entry, 1), halves(leave, 1)
    lane = lax.broadcasted_iota(jnp.int32, (rows, LANES), 1)
    for pair in range(channels // LANES):
        lo, hi = pair * LANES, (pair + 1) * LANES
        pre = conv(inner_tail, conv_inner_ref, bias_inner_ref, lo, hi)
        pre_inner_ref[:, lo:hi] = pre
        head_in = pre * sigmoid(pre)
        spread = spread_ref[:, lo:hi]
        scaled = head_in * mm(step2, spread, NN)
        scaled_low = scaled.astype(bf16)
        entry_wide = mm(entry2, spread, NN)
        leave_wide = mm(leave2, spread, NN)
        held = state[:, lo:hi]
        entering_ref[0, :, lo:hi] = held
        carried_out = mm(out_map, held.astype(bf16), NN) * entry_wide
        parts = []
        for side in range(2):
            head = 2 * pair + side
            gap = running[:, head : head + 1] - running_t[head : head + 1, :]
            mixed = (scores * jnp.exp(gap + allowed)).astype(bf16)
            parts.append(mm(mixed, scaled_low, NN))
        intra = jnp.where(lane < LANES // 2, parts[0], parts[1])
        ssm_ref[:, lo:hi] = carried_out + intra + skip_ref[:, lo:hi] * head_in
        added = mm(in_map, (scaled * leave_wide).astype(bf16), TN)
        state[:, lo:hi] = held * entry_wide[rows - 1 :, :] + added


def full(shape):
    return pl.BlockSpec(shape, lambda *_: (0,) * len(shape))


def mixer_forward(
    lengths, normed, weight, conv_inner, bias_inner, conv_shared, bias_shared,
    step_bias, rate, skip, spread, span,
):
    rows, model = normed.shape
    channels = conv_inner.shape[1]
    width = conv_shared.shape[1]
    blocks = rows // span
    by_row = lambda cols: pl.BlockSpec((span, cols), lambda i: (i, 0))
    shape = lambda cols: jax.ShapeDtypeStruct((rows, cols), f32)
    states = width // 2
    return pl.pallas_call(
        forward_kernel,
        grid=(blocks,),
        in_specs=[
            pl.BlockSpec(memory_space=pltpu.SMEM),
            by_row(model),
            full(weight.shape),
            full(conv_inner.shape),
            full(bias_inner.shape),
            full(conv_shared.shape),
            full(bias_shared.shape),
            full(step_bias.shape),
            full(rate.shape),
            full(skip.shape),
            full(spread.shape),
        ],
        out_specs=[
            by_row(channels), by_row(channels), by_row(channels), by_row(width), by_row(width),
            by_row(LANES), pl.BlockSpec((1, states, channels), lambda i: (i, 0, 0)),
        ],
        out_shape=[
            shape(channels), shape(channels), shape(channels), shape(width), shape(width),
            shape(LANES), jax.ShapeDtypeStruct((blocks, states, channels), f32),
        ],
        scratch_shapes=[
            pltpu.VMEM((TAIL + span, channels), f32),
            pltpu.VMEM((TAIL + span, width), f32),
            pltpu.VMEM((states, channels), f32),
        ],
        compiler_params=pltpu.CompilerParams(
            dimension_semantics=("arbitrary",), vmem_limit_bytes=LIMIT
        ),
        name="mixer_forward",
    )(
        lengths, normed, weight, conv_inner, bias_inner, conv_shared, bias_shared,
        step_bias, rate, skip, spread,
    )


def backward_kernel(
    first_block, total_rows, lengths_ref, upstream_ref, ssm_ref, inner_ref, pre_inner_ref, shared_ref, pre_shared_ref,
    step_ref, entering_ref, conv_inner_ref, conv_shared_ref, rate_ref, skip_ref, spread_ref,
    sums_in_ref, inner_in_ref, shared_in_ref, adjoint_in_ref,
    grads_ref, sums_ref, inner_out_ref, shared_out_ref, adjoint, inner_head, shared_head,
):
    turn = pl.program_id(0)
    block = first_block + pl.num_programs(0) - 1 - turn
    rows, channels = upstream_ref.shape
    width = conv_shared_ref.shape[1]
    base = block * rows
    ends = sequence_ends(lengths_ref)

    @pl.when(turn == 0)
    def _():
        inner_head[rows : rows + TAIL, :] = inner_in_ref[...]
        shared_head[rows : rows + TAIL, :] = shared_in_ref[...]
        adjoint[...] = adjoint_in_ref[...]
        sums_ref[...] = sums_in_ref[...]

    @pl.when(turn > 0)
    def _():
        inner_head[rows : rows + TAIL, :] = inner_head[0:TAIL, :]
        shared_head[rows : rows + TAIL, :] = shared_head[0:TAIL, :]

    step_raw = step_ref[...]
    rate = rate_ref[...]
    step, running, entry, leave, lower, segment, row, col = step_parts(step_raw, rate, ends, base)
    position = base + lax.broadcasted_iota(jnp.int32, (rows, 1), 0)
    keeps = [
        ((segment_at(ends, position + k) == segment) & (position + k < total_rows)).astype(f32)
        for k in range(1, TAPS)
    ]
    pre_shared = pre_shared_ref[...]
    shared_gate = sigmoid(pre_shared)
    shared = pre_shared * shared_gate
    half = width // 2
    in_map = shared[:, :half].astype(bf16)
    out_map = shared[:, half:].astype(bf16)
    scores_t = mm(in_map, out_map, NT)
    allowed_t = jnp.where((col >= row) & same_rows(ends, base, rows), 0.0, MASKED)
    running_t = jnp.transpose(running)
    step2, entry2, leave2 = halves(step, 1), halves(entry, 1), halves(leave, 1)
    lane = lax.broadcasted_iota(jnp.int32, (rows, LANES), 1)
    first_half = lane < LANES // 2
    grad_scores_t = jnp.zeros((rows, rows), f32)
    grad_in = jnp.zeros((rows, half), f32)
    grad_out = jnp.zeros((rows, half), f32)
    by_head = jnp.zeros((rows, LANES), f32)
    step_terms = jnp.zeros((rows, LANES), f32)
    leaving = jnp.zeros((TAIL, LANES), f32)
    for pair in range(channels // LANES):
        lo, hi = pair * LANES, (pair + 1) * LANES
        spread = spread_ref[:, lo:hi]
        step_wide = mm(step2, spread, NN)
        entry_wide = mm(entry2, spread, NN)
        leave_wide = mm(leave2, spread, NN)
        pre = pre_inner_ref[:, lo:hi]
        gate = sigmoid(pre)
        head_in = pre * gate
        skip = skip_ref[:, lo:hi]
        upstream = upstream_ref[:, lo:hi]
        upstream_low = upstream.astype(bf16)
        upstream_back = upstream_low.astype(f32)
        scaled = head_in * step_wide
        scaled_low = scaled.astype(bf16)
        scaled_back = scaled_low.astype(f32)
        held = entering_ref[0, :, lo:hi]
        held_low = held.astype(bf16)
        ahead = adjoint[:, lo:hi]
        ahead_low = ahead.astype(bf16)
        entry_up = (upstream_back * entry_wide).astype(bf16)
        grad_out = grad_out + mm(entry_up, held_low, NT)
        grad_in = grad_in + mm((scaled * leave_wide).astype(bf16), ahead_low, NT)
        grad_scaled = mm(in_map, ahead_low, NN) * leave_wide
        through = entry_wide[rows - 1 :, :]
        tail_terms = jnp.sum(scaled_back * grad_scaled, axis=0, keepdims=True) + through * jnp.sum(
            ahead * held, axis=0, keepdims=True
        )
        adjoint[:, lo:hi] = ahead * through + mm(out_map, entry_up, TN)
        parts = []
        for side in range(2):
            head = 2 * pair + side
            gap = running_t[head : head + 1, :] - running[:, head : head + 1]
            decay = jnp.exp(gap + allowed_t)
            mixed = (scores_t * decay).astype(bf16)
            parts.append(mm(mixed, upstream_low, NN))
            mine = first_half if side == 0 else jnp.logical_not(first_half)
            chosen = jnp.where(mine, scaled_back, 0.0).astype(bf16)
            grad_scores_t = grad_scores_t + mm(chosen, upstream_low, NT) * decay
        grad_scaled = grad_scaled + jnp.where(first_half, parts[0], parts[1])
        spread_one = spread[:LANES, :]
        spread_both = jnp.concatenate([spread_one, spread_one], axis=1)
        balance = upstream_back * (ssm_ref[:, lo:hi] - skip * head_in) - scaled_back * grad_scaled
        by_head = by_head + mm(halves(balance, 1), spread_both, NT)
        step_terms = step_terms + mm(halves(head_in * grad_scaled, 1), spread_both, NT)
        skip_terms = jnp.sum(upstream * head_in, axis=0, keepdims=True)
        edge = jnp.concatenate([tail_terms, skip_terms, jnp.zeros((TAIL - 2, LANES), f32)], axis=0)
        leaving = leaving + mm(halves(edge, 1), spread_both, NT)
        grad_pre = (grad_scaled * step_wide + skip * upstream) * (gate * (1.0 + pre * (1.0 - gate)))
        inner_head[0:rows, lo:hi] = grad_pre
        inner_proj = inner_ref[:, lo:hi]
        grad_proj = conv_inner_ref[TAPS - 1 : TAPS, lo:hi] * grad_pre
        sums = [None] * TAPS
        sums[TAPS - 1] = jnp.sum(grad_pre * inner_proj, axis=0, keepdims=True)
        for k in range(1, TAPS):
            moved = inner_head[k : k + rows, lo:hi] * keeps[k - 1]
            grad_proj = grad_proj + conv_inner_ref[TAPS - 1 - k : TAPS - k, lo:hi] * moved
            sums[TAPS - 1 - k] = jnp.sum(moved * inner_proj, axis=0, keepdims=True)
        grads_ref[:, lo:hi] = grad_proj.astype(bf16)
        sums.append(jnp.sum(grad_pre, axis=0, keepdims=True))
        sums.append(jnp.zeros((TAIL - len(sums), LANES), f32))
        sums_ref[:, lo:hi] += jnp.concatenate(sums, axis=0)
    grad_scores_low = grad_scores_t.astype(bf16)
    grad_out = grad_out + mm(grad_scores_low, in_map, TN)
    grad_in = grad_in + mm(grad_scores_low, out_map, NN)
    grad_shared = jnp.concatenate([grad_in, grad_out], axis=1)
    grad_pre = grad_shared * (shared_gate * (1.0 + pre_shared * (1.0 - shared_gate)))
    shared_head[0:rows, :] = grad_pre
    shared_proj = shared_ref[...]
    grad_proj = conv_shared_ref[TAPS - 1 : TAPS, :] * grad_pre
    sums = [None] * TAPS
    sums[TAPS - 1] = jnp.sum(grad_pre * shared_proj, axis=0, keepdims=True)
    for k in range(1, TAPS):
        moved = shared_head[k : k + rows, :] * keeps[k - 1]
        grad_proj = grad_proj + conv_shared_ref[TAPS - 1 - k : TAPS - k, :] * moved
        sums[TAPS - 1 - k] = jnp.sum(moved * shared_proj, axis=0, keepdims=True)
    sums.append(jnp.sum(grad_pre, axis=0, keepdims=True))
    sums.append(jnp.zeros((TAIL - len(sums), width), f32))
    sums_ref[:, channels : channels + width] += jnp.concatenate(sums, axis=0)
    split = mm(lower, halves(by_head, 1), TN)
    grad_log = split[:, :LANES] + split[:, LANES:] + leaving[0:1, :]
    grad_step = (step_terms + rate * grad_log) * sigmoid(step_raw)
    grads_ref[:, channels : channels + width] = grad_proj.astype(bf16)
    grads_ref[:, channels + width :] = grad_step.astype(bf16)
    sums_ref[:, channels + width :] += jnp.concatenate(
        [
            jnp.sum(grad_step, axis=0, keepdims=True),
            rate * jnp.sum(step * grad_log, axis=0, keepdims=True),
            leaving[1:2, :],
            jnp.zeros((TAIL - 3, LANES), f32),
        ],
        axis=0,
    )

    @pl.when(turn == pl.num_programs(0) - 1)
    def _():
        inner_out_ref[...] = inner_head[0:TAIL, :]
        shared_out_ref[...] = shared_head[0:TAIL, :]


def mixer_backward(
    lengths, upstream, saved, conv_inner, conv_shared, rate, skip, spread, carry, blocks, span
):
    ssm, inner, pre_inner, shared, pre_shared, step_raw, entering = saved
    rows, channels = upstream.shape
    width = conv_shared.shape[1]
    states = width // 2
    begin, end = blocks
    known = channels + width + LANES
    by_row = lambda cols: pl.BlockSpec((span, cols), lambda i: (end - 1 - i, 0))
    small = ((TAIL, known), (TAIL, channels), (TAIL, width), (states, channels))
    results = pl.pallas_call(
        partial(backward_kernel, begin, rows),
        grid=(end - begin,),
        in_specs=[
            pl.BlockSpec(memory_space=pltpu.SMEM),
            by_row(channels), by_row(channels), by_row(channels), by_row(channels),
            by_row(width), by_row(width), by_row(LANES),
            pl.BlockSpec((1, states, channels), lambda i: (end - 1 - i, 0, 0)),
            full(conv_inner.shape),
            full(conv_shared.shape),
            full(rate.shape),
            full(skip.shape),
            full(spread.shape),
            *[full(shape) for shape in small],
        ],
        out_specs=[
            pl.BlockSpec((span, known), lambda i: (end - begin - 1 - i, 0)),
            *[full(shape) for shape in small],
        ],
        out_shape=[
            jax.ShapeDtypeStruct(((end - begin) * span, known), bf16),
            *[jax.ShapeDtypeStruct(shape, f32) for shape in small],
        ],
        scratch_shapes=[
            pltpu.VMEM((TAIL + span, channels), f32),
            pltpu.VMEM((TAIL + span, width), f32),
        ],
        compiler_params=pltpu.CompilerParams(
            dimension_semantics=("arbitrary",), vmem_limit_bytes=LIMIT
        ),
        name="mixer_backward",
    )(
        lengths, upstream, ssm, inner, pre_inner, shared, pre_shared, step_raw, entering,
        conv_inner, conv_shared, rate, skip, spread, *carry,
    )
    return results[0], tuple(results[1:])


def product_kernel(normed_ref, *refs):
    grads, out_ref = refs[:-1], refs[-1]
    total, at = 0.0, 0
    for ref in grads:
        rows = ref.shape[0]
        total = total + mm(normed_ref[at : at + rows, :], ref[...], TN)
        at += rows
    out_ref[...] = total.astype(bf16)


def weight_products(normed, grads):
    known = grads[0].shape[1]
    return pl.pallas_call(
        product_kernel,
        out_shape=jax.ShapeDtypeStruct((normed.shape[1], known), bf16),
        compiler_params=pltpu.CompilerParams(vmem_limit_bytes=LIMIT),
        name="weight_products",
    )(normed, *grads)


def gate_kernel(normed_ref, gate_w_ref, upstream_ref, out_w_ref, gain_ref, ssm_ref,
                gate_ref, grad_ref, sums_ref):
    rows = normed_ref.shape[0]
    gate = mm(normed_ref[...], gate_w_ref[...], NN)
    grad = mm(upstream_ref[...], out_w_ref[...], NN)
    gate_ref[...] = gate
    grad_ref[...] = grad
    gated = ssm_ref[...] * (gate * sigmoid(gate))
    square = jnp.sum(gated * gated, axis=1, keepdims=True)
    cross = jnp.sum(grad * gain_ref[...] * gated, axis=1, keepdims=True)
    lane = lax.broadcasted_iota(jnp.int32, (rows, LANES), 1)
    both = jnp.where(lane == 0, square, jnp.where(lane == 1, cross, 0.0))
    sums_ref[...] = jnp.transpose(both)[0:TAIL, :]


def gate_forward(normed, upstream, weight, gain, ssm, span):
    rows, model = normed.shape
    channels = ssm.shape[1]
    by_row = lambda cols: pl.BlockSpec((span, cols), lambda i: (i, 0))
    return pl.pallas_call(
        gate_kernel,
        grid=(rows // span,),
        in_specs=[
            by_row(model), pl.BlockSpec((model, channels), lambda i: (0, 0)), by_row(model),
            pl.BlockSpec((model, channels), lambda i: (0, 1)), full(gain.shape), by_row(channels),
        ],
        out_specs=[by_row(channels), by_row(channels), pl.BlockSpec((TAIL, span), lambda i: (0, i))],
        out_shape=[
            jax.ShapeDtypeStruct((rows, channels), f32),
            jax.ShapeDtypeStruct((rows, channels), f32),
            jax.ShapeDtypeStruct((TAIL, rows), f32),
        ],
        compiler_params=pltpu.CompilerParams(
            dimension_semantics=("arbitrary",), vmem_limit_bytes=LIMIT
        ),
        name="gate_forward",
    )(normed, weight, upstream, weight, gain, ssm)


def norm_kernel(full_inner, sums_ref, gate_ref, grad_ref, ssm_ref, gain_ref, normed_ref,
                upstream_ref, out_w_ref, grad_gate_ref, grad_ssm_ref, gain_sum_ref, branch_ref,
                products_ref, scaled, totals):
    rows, channels = gate_ref.shape

    @pl.when(pl.program_id(0) == 0)
    def _():
        gain_sum_ref[...] = jnp.zeros_like(gain_sum_ref)
        totals[...] = jnp.zeros_like(totals)

    padded = jnp.concatenate([sums_ref[...], jnp.zeros((LANES - TAIL, rows), f32)], axis=0)
    sums = jnp.transpose(padded)
    scale = lax.rsqrt(sums[:, 0:1] / full_inner + EPSILON)
    pull = scale * scale * scale * (sums[:, 1:2] / full_inner)
    for lo in range(0, channels, LANES):
        hi = lo + LANES
        gain = gain_ref[:, lo:hi]
        gate, grad, ssm = gate_ref[:, lo:hi], grad_ref[:, lo:hi], ssm_ref[:, lo:hi]
        sig = sigmoid(gate)
        silu = gate * sig
        gated = ssm * silu
        normal = gated * scale
        scaled[:, lo:hi] = (normal * gain).astype(bf16)
        gain_sum_ref[:, lo:hi] += jnp.broadcast_to(
            jnp.sum(grad * normal, axis=0, keepdims=True), (TAIL, LANES)
        )
        grad_gated = scale * (grad * gain) - gated * pull
        grad_ssm_ref[:, lo:hi] = grad_gated * silu
        grad_gate_ref[:, lo:hi] = (grad_gated * ssm * (sig * (1.0 + gate * (1.0 - sig)))).astype(bf16)
    scaled_out = scaled[...]
    branch_ref[...] = mm(scaled_out, out_w_ref[...], NT).astype(bf16)
    totals[:, :channels] += mm(normed_ref[...], grad_gate_ref[...], TN)
    totals[:, channels:] += mm(upstream_ref[...], scaled_out, TN)

    @pl.when(pl.program_id(0) == pl.num_programs(0) - 1)
    def _():
        products_ref[...] = totals[...].astype(bf16)


def gate_norm(sums, gate, grad, ssm, gain, normed, upstream, weight, full_inner, span):
    rows, channels = gate.shape
    model = normed.shape[1]
    by_row = lambda cols: pl.BlockSpec((span, cols), lambda i: (i, 0))
    return pl.pallas_call(
        partial(norm_kernel, float(full_inner)),
        grid=(rows // span,),
        in_specs=[
            pl.BlockSpec((TAIL, span), lambda i: (0, i)), by_row(channels), by_row(channels),
            by_row(channels), full(gain.shape), by_row(model), by_row(model),
            pl.BlockSpec((model, channels), lambda i: (0, 1)),
        ],
        out_specs=[
            by_row(channels), by_row(channels), full((TAIL, channels)), by_row(model),
            full((model, 2 * channels)),
        ],
        out_shape=[
            jax.ShapeDtypeStruct((rows, channels), bf16),
            jax.ShapeDtypeStruct((rows, channels), f32),
            jax.ShapeDtypeStruct((TAIL, channels), f32),
            jax.ShapeDtypeStruct((rows, model), bf16),
            jax.ShapeDtypeStruct((model, 2 * channels), bf16),
        ],
        scratch_shapes=[
            pltpu.VMEM((span, channels), bf16),
            pltpu.VMEM((model, 2 * channels), f32),
        ],
        compiler_params=pltpu.CompilerParams(
            dimension_semantics=("arbitrary",), vmem_limit_bytes=LIMIT
        ),
        name="gate_norm",
    )(sums, gate, grad, ssm, gain, normed, upstream, weight)


def lanes_of(vector):
    return jnp.pad(vector, (0, LANES - vector.shape[0]))[None, :]


def spread_map(heads, channels):
    size = channels // heads
    row = lax.broadcasted_iota(jnp.int32, (2 * LANES, channels), 0) % LANES
    col = lax.broadcasted_iota(jnp.int32, (2 * LANES, channels), 1) // size
    return (row == col).astype(bf16)


def input_kernel(grad_gate_ref, grads_ref, gate_w_ref, weight_ref, normed_ref, gain_ref, sums_ref,
                 before_ref, terms_ref, packed_ref):
    known = sums_ref.shape[1]
    terms = mm(grad_gate_ref[...], gate_w_ref[...], NT)
    terms = terms + mm(grads_ref[...], weight_ref[...], NT)
    terms_ref[...] = terms.astype(bf16)

    @pl.when(pl.program_id(0) == 0)
    def _():
        packed_ref[:, :known] = sums_ref[...]
        packed_ref[:, known:] = before_ref[:, known:]

    total = jnp.sum(terms * normed_ref[...].astype(f32), axis=0, keepdims=True) / gain_ref[...]
    packed_ref[0:1, known:] += total


def input_terms(grad_gate, grads, weight_late, weight, normed, gain, sums, before, begin, span):
    model = normed.shape[1]
    channels = grad_gate.shape[1]
    rows, known = grads.shape
    by_row = lambda cols: pl.BlockSpec((span, cols), lambda i: (i + begin, 0))
    here = lambda cols: pl.BlockSpec((span, cols), lambda i: (i, 0))
    return pl.pallas_call(
        input_kernel,
        grid=(rows // span,),
        in_specs=[
            by_row(channels), here(known), pl.BlockSpec((model, channels), lambda i: (0, 0)),
            full(weight.shape), by_row(model), full(gain.shape), full(sums.shape),
            full(before.shape),
        ],
        out_specs=[here(model), full((TAIL, known + model))],
        out_shape=[
            jax.ShapeDtypeStruct((rows, model), bf16),
            jax.ShapeDtypeStruct((TAIL, known + model), f32),
        ],
        compiler_params=pltpu.CompilerParams(
            dimension_semantics=("arbitrary",), vmem_limit_bytes=LIMIT
        ),
        name="input_terms",
    )(grad_gate, grads, weight_late, weight, normed, gain, sums, before)


def dp_send(value, bit):
    size = lax.axis_size("dp")
    return lax.ppermute(value, "dp", [(i, i ^ bit) for i in range(size)])


def chip_bits():
    return [4 * k for k in range(1, lax.axis_size("dp") // 4)]


def choose(stacked, index, axis):
    return lax.dynamic_index_in_dim(stacked, index, axis, keepdims=False)


def interleave(mine, other, upper, axis):
    return jnp.stack([jnp.where(upper, other, mine), jnp.where(upper, mine, other)], axis=axis)


def gather_long(shard):
    me = lax.axis_index("dp")
    rows, cols = shard.shape
    pieces = [shard] + [dp_send(shard, bit) for bit in chip_bits()]
    stacked = jnp.zeros((len(pieces), rows, cols), shard.dtype)
    for k, piece in enumerate(pieces):
        stacked = lax.dynamic_update_index_in_dim(stacked, piece, (me // 4) ^ k, 0)
    return stacked


def gather_x(stacked):
    return interleave(stacked, dp_send(stacked, 2), (lax.axis_index("dp") // 2) % 2 == 1, 1)


def gather_cores(chips):
    whole = interleave(chips, dp_send(chips, 1), lax.axis_index("dp") % 2 == 1, 2)
    return whole.reshape(-1, chips.shape[-1])


def fold(parts, bit, axis):
    mine = (lax.axis_index("dp") // bit) % 2
    got = dp_send(choose(parts, 1 - mine, axis), bit)
    return choose(parts, mine, axis).astype(f32) + got.astype(f32)


def fold_chips(parts):
    place = lax.axis_index("dp") // 4
    sends = parts.astype(bf16)
    total = choose(parts, place, 0)
    got = [dp_send(choose(sends, place ^ (bit // 4), 0), bit) for bit in chip_bits()]
    for piece in got:
        total = total + piece.astype(f32)
    return total


def tensor_swap(value):
    return lax.ppermute(value, "tensor", [(0, 1), (1, 0)])


def sum_dp(value):
    value = value + dp_send(value, 1)
    value = value + dp_send(value, 2)
    bits = chip_bits()
    pieces = [value] + [dp_send(value, bit) for bit in bits]
    while len(pieces) > 1:
        pieces = [a + b for a, b in zip(pieces[0::2], pieces[1::2])]
    return pieces[0]


def gather_other(own, size):
    if size != 2:
        return lax.all_gather(own, "tensor", axis=0, tiled=True)
    return tensor_swap(own)


def join_halves(own, other, size):
    if size != 2:
        return other
    upper = lax.axis_index("tensor") == 1
    return jnp.concatenate([jnp.where(upper, other, own), jnp.where(upper, own, other)], axis=0)


def join_pieces(own, top, bottom, size):
    if size != 2:
        top = top.reshape(size, -1, own.shape[1])
        bottom = bottom.reshape(size, -1, own.shape[1])
        return jnp.concatenate([top, bottom], axis=1).reshape(-1, own.shape[1])
    return join_halves(own, jnp.concatenate([top, bottom], axis=0), size)


def pick_half(lower, upper, size):
    if size != 2:
        return lower
    return jnp.where(lax.axis_index("tensor") == 0, lower, upper)


def sum_quarters(quarters, other0, other1, size):
    if size != 2:
        whole = jnp.concatenate(quarters, axis=0)
        return lax.psum_scatter(whole, "tensor", scatter_dimension=0, tiled=True).astype(f32)
    first = lax.axis_index("tensor") == 0
    top = jnp.where(first, quarters[0], quarters[2]).astype(f32) + other0.astype(f32)
    bottom = jnp.where(first, quarters[1], quarters[3]).astype(f32) + other1.astype(f32)
    return jnp.concatenate([top, bottom], axis=0)


def tensor_sum(value, size):
    if size != 2:
        return lax.psum(value, "tensor")
    return value + tensor_swap(value)


def send_half(value, size):
    if size != 2:
        total = lax.psum_scatter(value, "tensor", scatter_dimension=0, tiled=True)
        return total, jnp.zeros_like(total)
    me = lax.axis_index("tensor")
    halved = value.reshape(2, -1, value.shape[1])
    return choose(halved, me, 0), tensor_swap(choose(halved, 1 - me, 0))


def shards(
    tokens, lengths, norm_gain, zx_weight, bc_weight, dt_weight, conv_inner, bias_inner,
    conv_shared, bias_shared, step_bias, log_rate, skip_gain, gate_gain, out_weight, cotangent,
):
    size = lax.axis_size("tensor")
    channels = zx_weight.shape[2]
    heads = step_bias.shape[0]
    width = bc_weight.shape[1]
    inputs = tokens.astype(f32)
    norm_scale = lax.rsqrt(jnp.mean(inputs * inputs, axis=1, keepdims=True) + EPSILON)
    normed_rows = (inputs * norm_scale * norm_gain[None, :]).astype(bf16)
    step_weight = jnp.pad(dt_weight, ((0, 0), (0, LANES - heads)))
    early = jnp.concatenate([zx_weight[:, 1, :], bc_weight, step_weight], axis=1)
    late = jnp.concatenate([zx_weight[:, 0, :], out_weight], axis=1)
    weight_late = lax.all_gather(late, "dp", axis=0, tiled=True)
    half = normed_rows.shape[0] // 2
    stacked, upper_rows = lax.optimization_barrier(
        (gather_long(early), gather_other(normed_rows[:half], size))
    )
    chips, lower_rows = lax.optimization_barrier(
        (gather_x(stacked), gather_other(normed_rows[half:], size))
    )
    normed = join_pieces(normed_rows, upper_rows, lower_rows, size)
    weight = gather_cores(chips)
    spread = spread_map(heads, channels)
    rate = lanes_of(-jnp.exp(log_rate))
    skip = jnp.repeat(skip_gain, channels // heads)[None, :]
    saved = mixer_forward(
        lengths, normed, weight, conv_inner, bias_inner[None, :], conv_shared,
        bias_shared[None, :], lanes_of(step_bias), rate, skip, spread, SPAN,
    )
    gain = gate_gain[None, :]
    other, ssm, weight_late = lax.optimization_barrier(
        (gather_other(cotangent, size), saved[0], weight_late)
    )
    upstream = join_halves(cotangent, other, size)
    gate, grad, sums = gate_forward(normed, upstream, weight_late, gain, ssm, SPAN)
    sums = tensor_sum(sums, size)
    grad_gate, grad_ssm, gain_sum, branch, first = gate_norm(
        sums, gate, grad, ssm, gain, normed, upstream, weight_late, channels * size, SPAN
    )
    branch_own, branch_other = send_half(branch, size)
    count = len(chip_bits()) + 1
    first = first.reshape(count, 2, 2, -1, first.shape[1])
    blocks = grad_ssm.shape[0] // SPAN
    quarter = blocks // 4
    known = channels + width + LANES
    carry = (
        jnp.pad(gain_sum[:1], ((TAIL - 1, 0), (0, known - channels))),
        jnp.zeros((TAIL, channels), f32),
        jnp.zeros((TAIL, width), f32),
        jnp.zeros((width // 2, channels), f32),
    )
    packed = jnp.zeros((TAIL, known + normed.shape[1]), f32)

    def part(index, carry, packed):
        begin = index * quarter
        grads, carry = mixer_backward(
            lengths, grad_ssm, saved, conv_inner, conv_shared, rate, skip, spread, carry,
            (begin, begin + quarter), SPAN,
        )
        return grads, carry

    def terms_of(index, grads, sums, packed):
        return input_terms(
            grad_gate, grads, weight_late, weight, normed, norm_gain[None, :], sums, packed,
            index * quarter, SPAN,
        )

    grads3, carry = part(3, carry, packed)
    first = fold(first, 1, 2).astype(bf16)
    carry, first = lax.optimization_barrier((carry, first))
    first_gate, first_out = first[..., :channels], first[..., channels:]
    grads2, carry = part(2, carry, packed)
    terms3, packed = terms_of(3, grads3, carry[0], packed)
    terms2, packed = terms_of(2, grads2, carry[0], packed)
    carry, packed = lax.optimization_barrier((carry, packed))
    grads1, carry = part(1, carry, packed)
    terms1, packed = terms_of(1, grads1, carry[0], packed)
    first_gate = fold(first_gate, 2, 1)
    first_out = fold_chips(first_out).astype(bf16)
    send1 = pick_half(terms3, terms1, size)
    carry, first_gate, first_out, send1, branch_other = lax.optimization_barrier(
        (carry, first_gate, first_out, send1, branch_other)
    )
    other1 = gather_other(send1, size)
    part_gate = fold_chips(first_gate)
    part_out = fold(first_out, 2, 0)
    block_out = (inputs + (branch_own.astype(f32) + branch_other.astype(f32))).astype(bf16)
    grads0, carry = part(0, carry, packed)
    products = weight_products(normed, (grads0, grads1, grads2, grads3))
    parts = fold(products.reshape(count, 2, 2, -1, known), 1, 2).astype(bf16)
    terms0, packed = terms_of(0, grads0, carry[0], packed)
    parts, packed, terms0 = lax.optimization_barrier((parts, packed, terms0))
    other0 = gather_other(pick_half(terms2, terms0, size), size)
    cut = (known // (2 * LANES)) * LANES
    parts_a = fold_chips(fold(parts[..., :cut], 2, 1))
    parts_b = fold(fold_chips(parts[..., cut:]).astype(bf16), 2, 0)
    part_small = jnp.concatenate([parts_a, parts_b], axis=1)
    packed = sum_dp(packed)
    grad_normed = sum_quarters((terms0, terms1, terms2, terms3), other0, other1, size)
    packed_all = tensor_sum(packed, size)
    part_inner = part_small[:, :channels]
    part_step = part_small[:, channels + width : channels + width + heads]
    part_shared = tensor_sum(part_small[:, channels : channels + width], size)
    scaled_grad = grad_normed * norm_gain[None, :]
    grad_inputs = norm_scale * scaled_grad - inputs * norm_scale**3 * jnp.mean(
        scaled_grad * inputs, axis=1, keepdims=True
    )
    grad_tokens = (cotangent.astype(f32) + grad_inputs).astype(bf16)
    part_in = jnp.stack([part_gate, part_inner], axis=1)
    at_step = channels + width
    at_norm = at_step + LANES
    return (
        block_out,
        grad_tokens,
        packed_all[0, at_norm:],
        part_in,
        part_shared,
        part_step,
        packed[:TAPS, :channels],
        packed[TAPS, :channels],
        packed_all[:TAPS, channels:at_step],
        packed_all[TAPS, channels:at_step],
        packed[0, at_step : at_step + heads],
        packed[1, at_step : at_step + heads],
        packed[2, at_step : at_step + heads],
        packed[TAIL - 1, :channels],
        part_out,
    )


def solution(mesh):
    return jax.shard_map(
        shards,
        mesh=mesh,
        in_specs=(
            P(("dp", "tensor"), None),
            P("dp", None),
            P(),
            P("dp", None, "tensor"),
            P("dp", None),
            P("dp", "tensor"),
            P(None, "tensor"),
            P("tensor"),
            P(),
            P(),
            P("tensor"),
            P("tensor"),
            P("tensor"),
            P("tensor"),
            P("dp", "tensor"),
            P(("dp", "tensor"), None),
        ),
        out_specs=(
            P(("dp", "tensor"), None),
            P(("dp", "tensor"), None),
            P(),
            P("dp", None, "tensor"),
            P("dp", None),
            P("dp", "tensor"),
            P(None, "tensor"),
            P("tensor"),
            P(),
            P(),
            P("tensor"),
            P("tensor"),
            P("tensor"),
            P("tensor"),
            P("dp", "tensor"),
        ),
        check_vma=False,
    )
```

```python
from functools import partial

import jax
import jax.numpy as jnp
from jax import lax
from jax.experimental import pallas as pl
from jax.experimental.pallas import tpu as pltpu
from jax.sharding import PartitionSpec as P

EPSILON = 1e-05
SPAN = 256
LANES = 128
TAIL = 8
TAPS = 4
MASKED = -1e30
f32 = jnp.float32
bf16 = jnp.bfloat16
LIMIT = 60 * 1024 * 1024


def mm(left, right, dims):
    return lax.dot_general(left, right, ((dims[0], dims[1]), ((), ())), preferred_element_type=f32)


NN = ((1,), (0,))
NT = ((1,), (1,))
TN = ((0,), (0,))


def halves(value, axis):
    high = value.astype(bf16)
    low = (value - high.astype(f32)).astype(bf16)
    return jnp.concatenate([high, low], axis=axis)


def sigmoid(value):
    return 1.0 / (1.0 + jnp.exp(-value))


def softplus(value):
    return jnp.maximum(value, 0.0) + jnp.log1p(jnp.exp(-jnp.abs(value)))


def segment_at(ends, position):
    total = jnp.zeros(position.shape, jnp.int32)
    for end in ends:
        total = total + (position >= end).astype(jnp.int32)
    return total


def sequence_ends(lengths_ref):
    ends, total = [], 0
    for i in range(lengths_ref.shape[1]):
        total = total + lengths_ref[0, i]
        ends.append(total)
    return ends


def step_parts(step_raw, rate, ends, base):
    rows = step_raw.shape[0]
    step = softplus(step_raw)
    row = lax.broadcasted_iota(jnp.int32, (rows, rows), 0)
    col = lax.broadcasted_iota(jnp.int32, (rows, rows), 1)
    lower = (row >= col).astype(f32).astype(bf16)
    split = mm(lower, halves(step * rate, 1), NN)
    running = split[:, :LANES] + split[:, LANES:]
    position = base + lax.broadcasted_iota(jnp.int32, (rows, 1), 0)
    segment = segment_at(ends, position)
    before = segment_at(ends, jnp.full((1, 1), base - 1, jnp.int32))
    last = segment_at(ends, jnp.full((1, 1), base + rows - 1, jnp.int32))
    carried = ((segment == before) & (position >= rows)).astype(f32)
    matched = (segment == last).astype(f32)
    entry = jnp.exp(running) * carried
    leave = jnp.exp(running[rows - 1 :, :] - running) * matched
    return step, running, entry, leave, lower, segment, row, col


def same_rows(ends, base, rows):
    across = segment_at(ends, base + lax.broadcasted_iota(jnp.int32, (1, rows), 1))
    down = segment_at(ends, base + lax.broadcasted_iota(jnp.int32, (rows, 1), 0))
    return down == across


def rows_of(block, blocks, spot_ref, own_ref, others):
    if not others:
        return own_ref[...]
    half = blocks // 2
    local = lax.rem(block, half)
    span = own_ref.shape[0] // half
    each = half // len(others)
    value = None
    for i, ref in enumerate(others):
        at = lax.rem(local, each) * span
        piece = ref[pl.ds(pl.multiple_of(at, span), span), :]
        value = piece if i == 0 else jnp.where(local >= i * each, piece, value)
    mine = own_ref[pl.ds(pl.multiple_of(local * span, span), span), :]
    return jnp.where(block // half == spot_ref[0, 0], mine, value)


def own_specs(own, others, span):
    if not others:
        return [pl.BlockSpec((span, own.shape[1]), lambda i: (i, 0))]
    return [full(own.shape), *[full(other.shape) for other in others]]


def place_weights(spot_ref, weight_ref, sources, count):
    rows = weight_ref.shape[0] // (4 * count)
    for i, ref in enumerate(sources):
        along = spot_ref[0, 2] ^ (i % 2)
        core = spot_ref[0, 3] ^ (i // 2)
        for k in range(count):
            at = (((spot_ref[0, 1] ^ k) * 2 + along) * 2 + core) * rows
            weight_ref[pl.ds(pl.multiple_of(at, rows), rows), :] = ref[k * rows : (k + 1) * rows, :]


def split_cores(spot_ref, value_ref, keep_ref, send_ref, chips):
    rows = keep_ref.shape[0] // chips
    core = spot_ref[0, 3]
    for chip in range(chips):
        here = pl.ds(pl.multiple_of((2 * chip + core) * rows, rows), rows)
        there = pl.ds(pl.multiple_of((2 * chip + 1 - core) * rows, rows), rows)
        keep_ref[chip * rows : (chip + 1) * rows, :] = value_ref[here, :].astype(bf16)
        send_ref[chip * rows : (chip + 1) * rows, :] = value_ref[there, :].astype(bf16)


def forward_kernel(
    pieces, count, spot_ref, lengths_ref, *refs
):
    own_ref, others = refs[0], refs[1:pieces]
    sources = refs[pieces : pieces + 4]
    (
        conv_inner_ref, bias_inner_ref, conv_shared_ref, bias_shared_ref, step_bias_ref, rate_ref,
        skip_ref, spread_ref, normed_ref, weight_ref, ssm_ref, inner_ref, pre_inner_ref, shared_ref,
        pre_shared_ref, step_ref, entering_ref, inner_tail, shared_tail, state,
    ) = refs[pieces + 4 :]
    block = pl.program_id(0)
    rows = normed_ref.shape[0]
    channels = conv_inner_ref.shape[1]
    base = block * rows
    ends = sequence_ends(lengths_ref)

    @pl.when(block == 0)
    def _():
        inner_tail[0:TAIL, :] = jnp.zeros((TAIL, channels), f32)
        shared_tail[0:TAIL, :] = jnp.zeros((TAIL, shared_tail.shape[1]), f32)
        state[...] = jnp.zeros_like(state)
        place_weights(spot_ref, weight_ref, sources, count)

    @pl.when(block > 0)
    def _():
        inner_tail[0:TAIL, :] = inner_tail[rows : rows + TAIL, :]
        shared_tail[0:TAIL, :] = shared_tail[rows : rows + TAIL, :]

    normed = rows_of(block, pl.num_programs(0), spot_ref, own_ref, others)
    normed_ref[...] = normed
    small = mm(normed, weight_ref[:, channels:], NN)
    width = conv_shared_ref.shape[1]
    shared_proj = small[:, :width]
    shared_tail[TAIL : TAIL + rows, :] = shared_proj
    shared_ref[...] = shared_proj
    step_raw = small[:, width:] + step_bias_ref[...]
    step_ref[...] = step_raw
    inner_proj = mm(normed, weight_ref[:, :channels], NN)
    inner_tail[TAIL : TAIL + rows, :] = inner_proj
    inner_ref[...] = inner_proj

    step, running, entry, leave, lower, segment, row, col = step_parts(
        step_raw, rate_ref[...], ends, base
    )
    position = base + lax.broadcasted_iota(jnp.int32, (rows, 1), 0)
    keeps = [
        ((segment_at(ends, position - k) == segment) & (position >= k)).astype(f32)
        for k in range(1, TAPS)
    ]

    def conv(tail, taps_ref, bias_ref, lo, hi):
        total = bias_ref[:, lo:hi] + taps_ref[TAPS - 1 : TAPS, lo:hi] * tail[TAIL : TAIL + rows, lo:hi]
        for k in range(1, TAPS):
            shifted = tail[TAIL - k : TAIL - k + rows, lo:hi]
            total = total + taps_ref[TAPS - 1 - k : TAPS - k, lo:hi] * (shifted * keeps[k - 1])
        return total

    pre_shared = conv(shared_tail, conv_shared_ref, bias_shared_ref, 0, width)
    pre_shared_ref[...] = pre_shared
    shared = pre_shared * sigmoid(pre_shared)
    in_map = shared[:, : width // 2].astype(bf16)
    out_map = shared[:, width // 2 :].astype(bf16)
    scores = mm(out_map, in_map, NT)
    allowed = jnp.where((row >= col) & same_rows(ends, base, rows), 0.0, MASKED)
    running_t = jnp.transpose(running)
    step2, entry2, leave2 = halves(step, 1), halves(entry, 1), halves(leave, 1)
    lane = lax.broadcasted_iota(jnp.int32, (rows, LANES), 1)
    for pair in range(channels // LANES):
        lo, hi = pair * LANES, (pair + 1) * LANES
        pre = conv(inner_tail, conv_inner_ref, bias_inner_ref, lo, hi)
        pre_inner_ref[:, lo:hi] = pre
        head_in = pre * sigmoid(pre)
        spread = spread_ref[:, lo:hi]
        scaled = head_in * mm(step2, spread, NN)
        scaled_low = scaled.astype(bf16)
        entry_wide = mm(entry2, spread, NN)
        leave_wide = mm(leave2, spread, NN)
        held = state[:, lo:hi]
        entering_ref[0, :, lo:hi] = held
        carried_out = mm(out_map, held.astype(bf16), NN) * entry_wide
        parts = []
        for side in range(2):
            head = 2 * pair + side
            gap = running[:, head : head + 1] - running_t[head : head + 1, :]
            mixed = (scores * jnp.exp(gap + allowed)).astype(bf16)
            parts.append(mm(mixed, scaled_low, NN))
        intra = jnp.where(lane < LANES // 2, parts[0], parts[1])
        ssm_ref[:, lo:hi] = carried_out + intra + skip_ref[:, lo:hi] * head_in
        added = mm(in_map, (scaled * leave_wide).astype(bf16), TN)
        state[:, lo:hi] = held * entry_wide[rows - 1 :, :] + added


def full(shape):
    return pl.BlockSpec(shape, lambda *_: (0,) * len(shape))


def mixer_forward(
    spot, lengths, own, others, sources, count, conv_inner, bias_inner, conv_shared, bias_shared,
    step_bias, rate, skip, spread, span,
):
    rows = own.shape[0] * (2 if others else 1)
    model = own.shape[1]
    channels = conv_inner.shape[1]
    width = conv_shared.shape[1]
    known = channels + width + LANES
    blocks = rows // span
    by_row = lambda cols: pl.BlockSpec((span, cols), lambda i: (i, 0))
    shape = lambda cols: jax.ShapeDtypeStruct((rows, cols), f32)
    states = width // 2
    smem = pl.BlockSpec(memory_space=pltpu.SMEM)
    fixed = (conv_inner, bias_inner, conv_shared, bias_shared, step_bias, rate, skip, spread)
    return pl.pallas_call(
        partial(forward_kernel, 1 + len(others), count),
        grid=(blocks,),
        in_specs=[
            smem, smem, *own_specs(own, others, span), *[full(x.shape) for x in sources],
            *[full(x.shape) for x in fixed],
        ],
        out_specs=[
            by_row(model), full((model, known)), by_row(channels), by_row(channels),
            by_row(channels), by_row(width), by_row(width), by_row(LANES),
            pl.BlockSpec((1, states, channels), lambda i: (i, 0, 0)),
        ],
        out_shape=[
            jax.ShapeDtypeStruct((rows, model), bf16), jax.ShapeDtypeStruct((model, known), bf16),
            shape(channels), shape(channels), shape(channels), shape(width), shape(width),
            shape(LANES), jax.ShapeDtypeStruct((blocks, states, channels), f32),
        ],
        scratch_shapes=[
            pltpu.VMEM((TAIL + span, channels), f32),
            pltpu.VMEM((TAIL + span, width), f32),
            pltpu.VMEM((states, channels), f32),
        ],
        compiler_params=pltpu.CompilerParams(
            dimension_semantics=("arbitrary",), vmem_limit_bytes=LIMIT
        ),
        name="mixer_forward",
    )(spot, lengths, own, *others, *sources, *fixed)


def backward_kernel(
    first_block, total_rows, lengths_ref, upstream_ref, ssm_ref, inner_ref, pre_inner_ref, shared_ref, pre_shared_ref,
    step_ref, entering_ref, conv_inner_ref, conv_shared_ref, rate_ref, skip_ref, spread_ref,
    sums_in_ref, inner_in_ref, shared_in_ref, adjoint_in_ref,
    grads_ref, sums_ref, inner_out_ref, shared_out_ref, adjoint, inner_head, shared_head,
):
    turn = pl.program_id(0)
    block = first_block + pl.num_programs(0) - 1 - turn
    rows, channels = upstream_ref.shape
    width = conv_shared_ref.shape[1]
    base = block * rows
    ends = sequence_ends(lengths_ref)

    @pl.when(turn == 0)
    def _():
        inner_head[rows : rows + TAIL, :] = inner_in_ref[...]
        shared_head[rows : rows + TAIL, :] = shared_in_ref[...]
        adjoint[...] = adjoint_in_ref[...]
        sums_ref[...] = sums_in_ref[...]

    @pl.when(turn > 0)
    def _():
        inner_head[rows : rows + TAIL, :] = inner_head[0:TAIL, :]
        shared_head[rows : rows + TAIL, :] = shared_head[0:TAIL, :]

    step_raw = step_ref[...]
    rate = rate_ref[...]
    step, running, entry, leave, lower, segment, row, col = step_parts(step_raw, rate, ends, base)
    position = base + lax.broadcasted_iota(jnp.int32, (rows, 1), 0)
    keeps = [
        ((segment_at(ends, position + k) == segment) & (position + k < total_rows)).astype(f32)
        for k in range(1, TAPS)
    ]
    pre_shared = pre_shared_ref[...]
    shared_gate = sigmoid(pre_shared)
    shared = pre_shared * shared_gate
    half = width // 2
    in_map = shared[:, :half].astype(bf16)
    out_map = shared[:, half:].astype(bf16)
    scores_t = mm(in_map, out_map, NT)
    allowed_t = jnp.where((col >= row) & same_rows(ends, base, rows), 0.0, MASKED)
    running_t = jnp.transpose(running)
    step2, entry2, leave2 = halves(step, 1), halves(entry, 1), halves(leave, 1)
    lane = lax.broadcasted_iota(jnp.int32, (rows, LANES), 1)
    first_half = lane < LANES // 2
    grad_scores_t = jnp.zeros((rows, rows), f32)
    grad_in = jnp.zeros((rows, half), f32)
    grad_out = jnp.zeros((rows, half), f32)
    by_head = jnp.zeros((rows, LANES), f32)
    step_terms = jnp.zeros((rows, LANES), f32)
    leaving = jnp.zeros((TAIL, LANES), f32)
    for pair in range(channels // LANES):
        lo, hi = pair * LANES, (pair + 1) * LANES
        spread = spread_ref[:, lo:hi]
        step_wide = mm(step2, spread, NN)
        entry_wide = mm(entry2, spread, NN)
        leave_wide = mm(leave2, spread, NN)
        pre = pre_inner_ref[:, lo:hi]
        gate = sigmoid(pre)
        head_in = pre * gate
        skip = skip_ref[:, lo:hi]
        upstream = upstream_ref[:, lo:hi]
        upstream_low = upstream.astype(bf16)
        upstream_back = upstream_low.astype(f32)
        scaled = head_in * step_wide
        scaled_low = scaled.astype(bf16)
        scaled_back = scaled_low.astype(f32)
        held = entering_ref[0, :, lo:hi]
        held_low = held.astype(bf16)
        ahead = adjoint[:, lo:hi]
        ahead_low = ahead.astype(bf16)
        entry_up = (upstream_back * entry_wide).astype(bf16)
        grad_out = grad_out + mm(entry_up, held_low, NT)
        grad_in = grad_in + mm((scaled * leave_wide).astype(bf16), ahead_low, NT)
        grad_scaled = mm(in_map, ahead_low, NN) * leave_wide
        through = entry_wide[rows - 1 :, :]
        tail_terms = jnp.sum(scaled_back * grad_scaled, axis=0, keepdims=True) + through * jnp.sum(
            ahead * held, axis=0, keepdims=True
        )
        adjoint[:, lo:hi] = ahead * through + mm(out_map, entry_up, TN)
        parts = []
        for side in range(2):
            head = 2 * pair + side
            gap = running_t[head : head + 1, :] - running[:, head : head + 1]
            decay = jnp.exp(gap + allowed_t)
            mixed = (scores_t * decay).astype(bf16)
            parts.append(mm(mixed, upstream_low, NN))
            mine = first_half if side == 0 else jnp.logical_not(first_half)
            chosen = jnp.where(mine, scaled_back, 0.0).astype(bf16)
            grad_scores_t = grad_scores_t + mm(chosen, upstream_low, NT) * decay
        grad_scaled = grad_scaled + jnp.where(first_half, parts[0], parts[1])
        spread_one = spread[:LANES, :]
        spread_both = jnp.concatenate([spread_one, spread_one], axis=1)
        balance = upstream_back * (ssm_ref[:, lo:hi] - skip * head_in) - scaled_back * grad_scaled
        by_head = by_head + mm(halves(balance, 1), spread_both, NT)
        step_terms = step_terms + mm(halves(head_in * grad_scaled, 1), spread_both, NT)
        skip_terms = jnp.sum(upstream * head_in, axis=0, keepdims=True)
        edge = jnp.concatenate([tail_terms, skip_terms, jnp.zeros((TAIL - 2, LANES), f32)], axis=0)
        leaving = leaving + mm(halves(edge, 1), spread_both, NT)
        grad_pre = (grad_scaled * step_wide + skip * upstream) * (gate * (1.0 + pre * (1.0 - gate)))
        inner_head[0:rows, lo:hi] = grad_pre
        inner_proj = inner_ref[:, lo:hi]
        grad_proj = conv_inner_ref[TAPS - 1 : TAPS, lo:hi] * grad_pre
        sums = [None] * TAPS
        sums[TAPS - 1] = jnp.sum(grad_pre * inner_proj, axis=0, keepdims=True)
        for k in range(1, TAPS):
            moved = inner_head[k : k + rows, lo:hi] * keeps[k - 1]
            grad_proj = grad_proj + conv_inner_ref[TAPS - 1 - k : TAPS - k, lo:hi] * moved
            sums[TAPS - 1 - k] = jnp.sum(moved * inner_proj, axis=0, keepdims=True)
        grads_ref[:, lo:hi] = grad_proj.astype(bf16)
        sums.append(jnp.sum(grad_pre, axis=0, keepdims=True))
        sums.append(jnp.zeros((TAIL - len(sums), LANES), f32))
        sums_ref[:, lo:hi] += jnp.concatenate(sums, axis=0)
    grad_scores_low = grad_scores_t.astype(bf16)
    grad_out = grad_out + mm(grad_scores_low, in_map, TN)
    grad_in = grad_in + mm(grad_scores_low, out_map, NN)
    grad_shared = jnp.concatenate([grad_in, grad_out], axis=1)
    grad_pre = grad_shared * (shared_gate * (1.0 + pre_shared * (1.0 - shared_gate)))
    shared_head[0:rows, :] = grad_pre
    shared_proj = shared_ref[...]
    grad_proj = conv_shared_ref[TAPS - 1 : TAPS, :] * grad_pre
    sums = [None] * TAPS
    sums[TAPS - 1] = jnp.sum(grad_pre * shared_proj, axis=0, keepdims=True)
    for k in range(1, TAPS):
        moved = shared_head[k : k + rows, :] * keeps[k - 1]
        grad_proj = grad_proj + conv_shared_ref[TAPS - 1 - k : TAPS - k, :] * moved
        sums[TAPS - 1 - k] = jnp.sum(moved * shared_proj, axis=0, keepdims=True)
    sums.append(jnp.sum(grad_pre, axis=0, keepdims=True))
    sums.append(jnp.zeros((TAIL - len(sums), width), f32))
    sums_ref[:, channels : channels + width] += jnp.concatenate(sums, axis=0)
    split = mm(lower, halves(by_head, 1), TN)
    grad_log = split[:, :LANES] + split[:, LANES:] + leaving[0:1, :]
    grad_step = (step_terms + rate * grad_log) * sigmoid(step_raw)
    grads_ref[:, channels : channels + width] = grad_proj.astype(bf16)
    grads_ref[:, channels + width :] = grad_step.astype(bf16)
    sums_ref[:, channels + width :] += jnp.concatenate(
        [
            jnp.sum(grad_step, axis=0, keepdims=True),
            rate * jnp.sum(step * grad_log, axis=0, keepdims=True),
            leaving[1:2, :],
            jnp.zeros((TAIL - 3, LANES), f32),
        ],
        axis=0,
    )

    @pl.when(turn == pl.num_programs(0) - 1)
    def _():
        inner_out_ref[...] = inner_head[0:TAIL, :]
        shared_out_ref[...] = shared_head[0:TAIL, :]


def mixer_backward(
    lengths, upstream, saved, conv_inner, conv_shared, rate, skip, spread, carry, blocks, span
):
    ssm, inner, pre_inner, shared, pre_shared, step_raw, entering = saved
    rows, channels = upstream.shape
    width = conv_shared.shape[1]
    states = width // 2
    begin, end = blocks
    known = channels + width + LANES
    by_row = lambda cols: pl.BlockSpec((span, cols), lambda i: (end - 1 - i, 0))
    small = ((TAIL, known), (TAIL, channels), (TAIL, width), (states, channels))
    results = pl.pallas_call(
        partial(backward_kernel, begin, rows),
        grid=(end - begin,),
        in_specs=[
            pl.BlockSpec(memory_space=pltpu.SMEM),
            by_row(channels), by_row(channels), by_row(channels), by_row(channels),
            by_row(width), by_row(width), by_row(LANES),
            pl.BlockSpec((1, states, channels), lambda i: (end - 1 - i, 0, 0)),
            full(conv_inner.shape),
            full(conv_shared.shape),
            full(rate.shape),
            full(skip.shape),
            full(spread.shape),
            *[full(shape) for shape in small],
        ],
        out_specs=[
            pl.BlockSpec((span, known), lambda i: (end - begin - 1 - i, 0)),
            *[full(shape) for shape in small],
        ],
        out_shape=[
            jax.ShapeDtypeStruct(((end - begin) * span, known), bf16),
            *[jax.ShapeDtypeStruct(shape, f32) for shape in small],
        ],
        scratch_shapes=[
            pltpu.VMEM((TAIL + span, channels), f32),
            pltpu.VMEM((TAIL + span, width), f32),
        ],
        compiler_params=pltpu.CompilerParams(
            dimension_semantics=("arbitrary",), vmem_limit_bytes=LIMIT
        ),
        name="mixer_backward",
    )(
        lengths, upstream, ssm, inner, pre_inner, shared, pre_shared, step_raw, entering,
        conv_inner, conv_shared, rate, skip, spread, *carry,
    )
    return results[0], tuple(results[1:])


def gain_row(weight_ref, total_ref, columns):
    rows = weight_ref.shape[0]
    added = jnp.zeros((rows, LANES), f32)
    for lo in range(0, columns, LANES):
        added = added + weight_ref[:, lo : lo + LANES].astype(f32) * total_ref[:, lo : lo + LANES]
    return jnp.sum(jnp.transpose(added), axis=0, keepdims=True)


def product_kernel(chips, spot_ref, normed_ref, weight_ref, gain_ref, sums_ref, norm_sum_ref, *refs):
    grads, (keep_ref, send_ref, packed_ref, total) = refs[:-4], refs[-4:]
    known = sums_ref.shape[1]
    at = 0
    for i, ref in enumerate(grads):
        rows = ref.shape[0]
        added = mm(normed_ref[at : at + rows, :], ref[...], TN)
        total[...] = added if i == 0 else total[...] + added
        at += rows
    split_cores(spot_ref, total, keep_ref, send_ref, chips)
    packed_ref[:, :known] = sums_ref[...]
    packed_ref[:, known:] = norm_sum_ref[...]
    row = norm_sum_ref[0:1, :] + gain_row(weight_ref, total, known)
    packed_ref[0:1, known:] = row / gain_ref[...]


def weight_products(spot, normed, weight, gain, sums, norm_sum, grads, chips):
    known = grads[0].shape[1]
    model = normed.shape[1]
    part = jax.ShapeDtypeStruct((model // 2, known), bf16)
    vmem = pl.BlockSpec(memory_space=pltpu.VMEM)
    return pl.pallas_call(
        partial(product_kernel, chips),
        in_specs=[pl.BlockSpec(memory_space=pltpu.SMEM), *[vmem for _ in range(5 + len(grads))]],
        out_specs=[vmem, vmem, vmem],
        out_shape=[part, part, jax.ShapeDtypeStruct((TAIL, known + model), f32)],
        scratch_shapes=[pltpu.VMEM((model, known), f32)],
        compiler_params=pltpu.CompilerParams(vmem_limit_bytes=LIMIT),
        name="weight_products",
    )(spot, normed, weight, gain, sums, norm_sum, *grads)


def gate_kernel(pieces, spot_ref, normed_ref, *refs):
    own_ref, others = refs[0], refs[1:pieces]
    gate_w_ref, out_w_ref, gain_ref, ssm_ref, upstream_ref, gate_ref, grad_ref, sums_ref = refs[pieces:]
    rows, channels = ssm_ref.shape
    normed = normed_ref[...]
    upstream = rows_of(pl.program_id(0), pl.num_programs(0), spot_ref, own_ref, others)
    upstream_ref[...] = upstream
    square = jnp.zeros((rows, LANES), f32)
    cross = jnp.zeros((rows, LANES), f32)
    step = 2 * LANES
    for lo in range(0, channels, step):
        hi = lo + step
        gate = mm(normed, gate_w_ref[:, lo:hi], NN)
        grad = mm(upstream, out_w_ref[:, lo:hi], NN)
        gate_ref[:, lo:hi] = gate
        grad_ref[:, lo:hi] = grad
        gated = ssm_ref[:, lo:hi] * (gate * sigmoid(gate))
        squares = gated * gated
        crosses = grad * gain_ref[:, lo:hi] * gated
        square = square + (squares[:, :LANES] + squares[:, LANES:])
        cross = cross + (crosses[:, :LANES] + crosses[:, LANES:])
    square = jnp.sum(square, axis=1, keepdims=True)
    cross = jnp.sum(cross, axis=1, keepdims=True)
    lane = lax.broadcasted_iota(jnp.int32, (rows, LANES), 1)
    both = jnp.where(lane == 0, square, jnp.where(lane == 1, cross, 0.0))
    sums_ref[...] = jnp.transpose(both)[0:TAIL, :]


def gate_forward(spot, normed, own, others, weight, gain, ssm, span):
    rows, model = normed.shape
    channels = ssm.shape[1]
    by_row = lambda cols: pl.BlockSpec((span, cols), lambda i: (i, 0))
    return pl.pallas_call(
        partial(gate_kernel, 1 + len(others)),
        grid=(rows // span,),
        in_specs=[
            pl.BlockSpec(memory_space=pltpu.SMEM), by_row(model), *own_specs(own, others, span),
            pl.BlockSpec((model, channels), lambda i: (0, 0)),
            pl.BlockSpec((model, channels), lambda i: (0, 1)), full(gain.shape), by_row(channels),
        ],
        out_specs=[
            by_row(model), by_row(channels), by_row(channels),
            pl.BlockSpec((TAIL, span), lambda i: (0, i)),
        ],
        out_shape=[
            jax.ShapeDtypeStruct((rows, model), bf16),
            jax.ShapeDtypeStruct((rows, channels), f32),
            jax.ShapeDtypeStruct((rows, channels), f32),
            jax.ShapeDtypeStruct((TAIL, rows), f32),
        ],
        compiler_params=pltpu.CompilerParams(
            dimension_semantics=("arbitrary",), vmem_limit_bytes=LIMIT
        ),
        name="gate_forward",
    )(spot, normed, own, *others, weight, weight, gain, ssm)


def norm_kernel(full_inner, chips, split, spot_ref, sums_ref, more_ref, gate_ref, grad_ref, ssm_ref,
                gain_ref, normed_ref, upstream_ref, gate_w_ref, out_w_ref, grad_gate_ref,
                grad_ssm_ref, gain_sum_ref, keep_ref, send_ref, mine_ref, theirs_ref, norm_sum_ref,
                scaled, totals):
    rows, channels = gate_ref.shape
    block = pl.program_id(0)

    @pl.when(block == 0)
    def _():
        gain_sum_ref[...] = jnp.zeros_like(gain_sum_ref)
        totals[...] = jnp.zeros_like(totals)

    sums = sums_ref[...] + more_ref[...] if split else sums_ref[...]
    sums = jnp.transpose(jnp.concatenate([sums, jnp.zeros((LANES - TAIL, rows), f32)], axis=0))
    scale = lax.rsqrt(sums[:, 0:1] / full_inner + EPSILON)
    pull = scale * scale * scale * (sums[:, 1:2] / full_inner)
    normed_t = jnp.transpose(normed_ref[...])
    upstream_t = jnp.transpose(upstream_ref[...])
    step = 2 * LANES
    for lo in range(0, channels, step):
        hi = lo + step
        gain = gain_ref[:, lo:hi]
        gate, grad, ssm = gate_ref[:, lo:hi], grad_ref[:, lo:hi], ssm_ref[:, lo:hi]
        sig = sigmoid(gate)
        silu = gate * sig
        gated = ssm * silu
        normal = gated * scale
        scaled_low = (normal * gain).astype(bf16)
        scaled[:, lo:hi] = scaled_low
        gain_sum_ref[:, lo:hi] += jnp.broadcast_to(
            jnp.sum(grad * normal, axis=0, keepdims=True), (TAIL, step)
        )
        grad_gated = scale * (grad * gain) - gated * pull
        grad_ssm_ref[:, lo:hi] = grad_gated * silu
        grad_gate = (grad_gated * ssm * (sig * (1.0 + gate * (1.0 - sig)))).astype(bf16)
        grad_gate_ref[:, lo:hi] = grad_gate
        totals[:, lo:hi] += mm(normed_t, grad_gate, NN)
        totals[:, channels + lo : channels + hi] += mm(upstream_t, scaled_low, NN)
    branch = mm(scaled[...], out_w_ref[...], NT).astype(bf16)
    if split:
        half = pl.num_programs(0) // 2
        at = pl.ds(pl.multiple_of(lax.rem(block, half) * rows, rows), rows)

        @pl.when(block // half == spot_ref[0, 0])
        def _():
            mine_ref[at, :] = branch

        @pl.when(block // half != spot_ref[0, 0])
        def _():
            theirs_ref[at, :] = branch
    else:
        mine_ref[pl.ds(pl.multiple_of(block * rows, rows), rows), :] = branch

        @pl.when(block == 0)
        def _():
            theirs_ref[...] = jnp.zeros_like(theirs_ref)

    @pl.when(block == pl.num_programs(0) - 1)
    def _():
        split_cores(spot_ref, totals, keep_ref, send_ref, chips)
        norm_sum_ref[...] = jnp.zeros_like(norm_sum_ref)
        norm_sum_ref[0:1, :] = gain_row(gate_w_ref, totals, channels)


def gate_norm(
    spot, sums, more, gate, grad, ssm, gain, normed, upstream, weight, full_inner, chips, split, span
):
    rows, channels = gate.shape
    model = normed.shape[1]
    by_row = lambda cols: pl.BlockSpec((span, cols), lambda i: (i, 0))
    stats = pl.BlockSpec((TAIL, span), lambda i: (0, i))
    half = (model // 2, 2 * channels)
    mine = (rows // 2 if split else rows, model)
    theirs = (rows // 2 if split else TAIL * 2, model)
    return pl.pallas_call(
        partial(norm_kernel, float(full_inner), chips, split),
        grid=(rows // span,),
        in_specs=[
            pl.BlockSpec(memory_space=pltpu.SMEM), stats, stats, by_row(channels), by_row(channels),
            by_row(channels), full(gain.shape), by_row(model), by_row(model),
            pl.BlockSpec((model, channels), lambda i: (0, 0)),
            pl.BlockSpec((model, channels), lambda i: (0, 1)),
        ],
        out_specs=[
            by_row(channels), by_row(channels), full((TAIL, channels)), full(half), full(half),
            full(mine), full(theirs), full((TAIL, model)),
        ],
        out_shape=[
            jax.ShapeDtypeStruct((rows, channels), bf16),
            jax.ShapeDtypeStruct((rows, channels), f32),
            jax.ShapeDtypeStruct((TAIL, channels), f32),
            jax.ShapeDtypeStruct(half, bf16),
            jax.ShapeDtypeStruct(half, bf16),
            jax.ShapeDtypeStruct(mine, bf16),
            jax.ShapeDtypeStruct(theirs, bf16),
            jax.ShapeDtypeStruct((TAIL, model), f32),
        ],
        scratch_shapes=[
            pltpu.VMEM((span, channels), bf16),
            pltpu.VMEM((model, 2 * channels), f32),
        ],
        compiler_params=pltpu.CompilerParams(
            dimension_semantics=("arbitrary",), vmem_limit_bytes=LIMIT
        ),
        name="gate_norm",
    )(spot, sums, more, gate, grad, ssm, gain, normed, upstream, weight, weight)


def lanes_of(vector):
    return jnp.pad(vector, (0, LANES - vector.shape[0]))[None, :]


def spread_map(heads, channels):
    size = channels // heads
    row = lax.broadcasted_iota(jnp.int32, (2 * LANES, channels), 0) % LANES
    col = lax.broadcasted_iota(jnp.int32, (2 * LANES, channels), 1) // size
    return (row == col).astype(bf16)


def input_kernel(grad_gate_ref, grads_ref, gate_w_ref, weight_ref, terms_ref):
    terms = mm(grad_gate_ref[...], gate_w_ref[...], NT)
    terms = terms + mm(grads_ref[...], weight_ref[...], NT)
    terms_ref[...] = terms.astype(bf16)


def input_terms(grad_gate, grads, weight_late, weight, begin, span):
    model = weight.shape[0]
    channels = grad_gate.shape[1]
    rows, known = grads.shape
    return pl.pallas_call(
        input_kernel,
        grid=(rows // span,),
        in_specs=[
            pl.BlockSpec((span, channels), lambda i: (i + begin, 0)),
            pl.BlockSpec((span, known), lambda i: (i, 0)),
            pl.BlockSpec((model, channels), lambda i: (0, 0)), full(weight.shape),
        ],
        out_specs=pl.BlockSpec((span, model), lambda i: (i, 0)),
        out_shape=jax.ShapeDtypeStruct((rows, model), bf16),
        compiler_params=pltpu.CompilerParams(
            dimension_semantics=("arbitrary",), vmem_limit_bytes=LIMIT
        ),
        name="input_terms",
    )(grad_gate, grads, weight_late, weight)


def dp_send(value, bit):
    size = lax.axis_size("dp")
    return lax.ppermute(value, "dp", [(i, i ^ bit) for i in range(size)])


def chip_bits():
    return [4 * k for k in range(1, lax.axis_size("dp") // 4)]


def choose(stacked, index, axis):
    return lax.dynamic_index_in_dim(stacked, index, axis, keepdims=False)


def fold(parts, bit, axis):
    mine = (lax.axis_index("dp") // bit) % 2
    got = dp_send(choose(parts, 1 - mine, axis), bit)
    return choose(parts, mine, axis).astype(f32) + got.astype(f32)


def fold_chips(parts):
    place = lax.axis_index("dp") // 4
    sends = parts.astype(bf16)
    total = choose(parts, place, 0)
    got = [dp_send(choose(sends, place ^ (bit // 4), 0), bit) for bit in chip_bits()]
    for piece in got:
        total = total + piece.astype(f32)
    return total


def tensor_swap(value):
    return lax.ppermute(value, "tensor", [(0, 1), (1, 0)])


def sum_chips(value):
    bits = chip_bits()
    pieces = [value] + [dp_send(value, bit) for bit in bits]
    while len(pieces) > 1:
        pieces = [a + b for a, b in zip(pieces[0::2], pieces[1::2])]
    return pieces[0]


def gather_other(own, size):
    if size != 2:
        return lax.all_gather(own, "tensor", axis=0, tiled=True)
    return tensor_swap(own)


def join_pieces(own, top, bottom, size):
    top = top.reshape(size, -1, own.shape[1])
    bottom = bottom.reshape(size, -1, own.shape[1])
    return jnp.concatenate([top, bottom], axis=1).reshape(-1, own.shape[1])


def pick_half(lower, upper, size):
    if size != 2:
        return lower
    return jnp.where(lax.axis_index("tensor") == 0, lower, upper)


def sum_quarters(quarters, other0, other1, size):
    if size != 2:
        whole = jnp.concatenate(quarters, axis=0)
        return lax.psum_scatter(whole, "tensor", scatter_dimension=0, tiled=True).astype(f32)
    first = lax.axis_index("tensor") == 0
    lower = jnp.concatenate(quarters[:2], axis=0)
    others = jnp.concatenate([other0, other1], axis=0)
    return jnp.where(first, lower, quarters[2]).astype(f32) + others.astype(f32)


def tensor_sum(value, size):
    if size != 2:
        return lax.psum(value, "tensor")
    return value + tensor_swap(value)


def shards(
    tokens, lengths, norm_gain, zx_weight, bc_weight, dt_weight, conv_inner, bias_inner,
    conv_shared, bias_shared, step_bias, log_rate, skip_gain, gate_gain, out_weight, cotangent,
):
    size = lax.axis_size("tensor")
    split = size == 2
    me = lax.axis_index("dp")
    count = len(chip_bits()) + 1
    spot = jnp.stack([lax.axis_index("tensor"), me // 4, (me // 2) % 2, me % 2])[None, :]
    spot = spot.astype(jnp.int32)
    channels = zx_weight.shape[2]
    heads = step_bias.shape[0]
    width = bc_weight.shape[1]
    known = channels + width + LANES
    step_weight = jnp.pad(dt_weight, ((0, 0), (0, LANES - heads)))
    early = jnp.concatenate([zx_weight[:, 1, :], bc_weight, step_weight], axis=1)
    inputs = tokens.astype(f32)
    norm_scale = lax.rsqrt(jnp.mean(inputs * inputs, axis=1, keepdims=True) + EPSILON)
    normed_rows = (inputs * norm_scale * norm_gain[None, :]).astype(bf16)
    half = normed_rows.shape[0] // 2
    fixed = (
        conv_inner, bias_inner[None, :], conv_shared, bias_shared[None, :], lanes_of(step_bias),
        lanes_of(-jnp.exp(log_rate)), jnp.repeat(skip_gain, channels // heads)[None, :],
        spread_map(heads, channels),
    )
    late = jnp.concatenate([zx_weight[:, 0, :], out_weight], axis=1)
    column = jnp.concatenate([early] + [dp_send(early, bit) for bit in chip_bits()], axis=0)
    column, late, top, fixed = lax.optimization_barrier(
        (column, late, gather_other(normed_rows[:half], size), fixed)
    )
    weight_late = lax.all_gather(late, "dp", axis=0, tiled=True)
    by_core = dp_send(column, 1)
    by_x, bottom = lax.optimization_barrier(
        (dp_send(column, 2), gather_other(normed_rows[half:], size))
    )
    sources = (column, by_x, by_core, dp_send(by_x, 1))
    own, others = normed_rows, (top, bottom)
    if not split:
        own, others = join_pieces(normed_rows, top, bottom, size), ()
    normed, weight, *saved = mixer_forward(
        spot, lengths, own, others, sources, count, *fixed, SPAN
    )
    _, _, _, _, _, rate, skip, spread = fixed
    gain = gate_gain[None, :]
    other, ssm, weight_late = lax.optimization_barrier(
        (gather_other(cotangent, size), saved[0], weight_late)
    )
    own, others = (cotangent, (other,)) if split else (other, ())
    upstream, gate, grad, sums = gate_forward(
        spot, normed, own, others, weight_late, gain, ssm, SPAN
    )
    more = gather_other(sums, size) if split else sums
    sums = sums if split else lax.psum(sums, "tensor")
    chips = 2 * count
    grad_gate, grad_ssm, gain_sum, keep, send, branch_own, branch_send, norm_sum = gate_norm(
        spot, sums, more, gate, grad, ssm, gain, normed, upstream, weight_late, channels * size,
        chips, split, SPAN,
    )
    if split:
        branch_other = gather_other(branch_send, size)
    else:
        branch_own = lax.psum_scatter(branch_own, "tensor", scatter_dimension=0, tiled=True)
        branch_other = jnp.zeros_like(branch_own)
    quarter = grad_ssm.shape[0] // SPAN // 4
    carry = (
        jnp.pad(gain_sum[:1], ((TAIL - 1, 0), (0, known - channels))),
        jnp.zeros((TAIL, channels), f32),
        jnp.zeros((TAIL, width), f32),
        jnp.zeros((width // 2, channels), f32),
    )
    def back(begin, end, carry):
        return mixer_backward(
            lengths, grad_ssm, saved, conv_inner, conv_shared, rate, skip, spread, carry,
            (begin * quarter, end * quarter), SPAN,
        )

    def terms_of(begin, grads):
        return input_terms(grad_gate, grads, weight_late, weight, begin * quarter, SPAN)

    first = dp_send(send, 1)
    grads2, carry = back(2, 4, carry)
    first = (keep.astype(f32) + first.astype(f32)).astype(bf16)
    first = first.reshape(count, 2, -1, first.shape[1])
    carry, first, grads2 = lax.optimization_barrier((carry, first, grads2))
    first_gate, first_out = first[..., :channels], first[..., channels:]
    terms2 = terms_of(2, grads2)
    carry, terms2 = lax.optimization_barrier((carry, terms2))
    grads1, carry = back(1, 2, carry)
    terms1 = terms_of(1, grads1)
    first_gate = fold(first_gate, 2, 1)
    first_out = fold_chips(first_out).astype(bf16)
    send1 = pick_half(terms2[terms2.shape[0] // 2 :], terms1, size)
    carry, send1, branch_other, first_gate, first_out = lax.optimization_barrier(
        (carry, send1, branch_other, first_gate, first_out)
    )
    other1 = gather_other(send1, size) if split else send1
    block_out = (inputs + (branch_own.astype(f32) + branch_other.astype(f32))).astype(bf16)
    part_gate = fold_chips(first_gate)
    part_out = fold(first_out, 2, 0)
    grads0, carry = back(0, 1, carry)
    sums, part_gate, part_out, grads0, other1, block_out = lax.optimization_barrier(
        (carry[0], part_gate, part_out, grads0, other1, block_out)
    )
    keep, send, sums = weight_products(
        spot, normed, weight, norm_gain[None, :], sums, norm_sum, (grads0, grads1, grads2), chips
    )
    got = dp_send(send, 1)
    sums = (sums + dp_send(sums, 1)) + (dp_send(sums, 2) + dp_send(sums, 3))
    terms0 = terms_of(0, grads0)
    send0 = pick_half(terms2[: terms2.shape[0] // 2], terms0, size)
    parts = (keep.astype(f32) + got.astype(f32)).astype(bf16).reshape(count, 2, -1, known)
    parts, sums, send0 = lax.optimization_barrier((parts, sums, send0))
    other0 = gather_other(send0, size) if split else send0
    cut = (known // (2 * LANES)) * LANES
    parts_a = fold(parts[..., :cut], 2, 1)
    parts_b = fold_chips(parts[..., cut:]).astype(bf16)
    sums = sum_chips(sums)
    parts_a, parts_b, other0, sums = lax.optimization_barrier((parts_a, parts_b, other0, sums))
    shared_sums = tensor_sum(sums[:, channels:], size)
    norm_sum = shared_sums[0, known - channels :]
    grad_normed = sum_quarters((terms0, terms1, terms2), other0, other1, size)
    scaled_grad = grad_normed * norm_gain[None, :]
    grad_inputs = norm_scale * scaled_grad - inputs * norm_scale**3 * jnp.mean(
        scaled_grad * inputs, axis=1, keepdims=True
    )
    grad_tokens = (cotangent.astype(f32) + grad_inputs).astype(bf16)
    parts_a = fold_chips(parts_a)
    parts_b = fold(parts_b, 2, 0)
    part_inner = jnp.concatenate([parts_a, parts_b[:, : channels - cut]], axis=1)
    at_step = channels + width
    part_shared = tensor_sum(parts_b[:, channels - cut : at_step - cut], size)
    part_step = parts_b[:, at_step - cut : at_step - cut + heads]
    part_in = jnp.stack([part_gate, part_inner], axis=1)
    return (
        block_out,
        grad_tokens,
        norm_sum,
        part_in,
        part_shared,
        part_step,
        sums[:TAPS, :channels],
        sums[TAPS, :channels],
        shared_sums[:TAPS, :width],
        shared_sums[TAPS, :width],
        sums[0, at_step : at_step + heads],
        sums[1, at_step : at_step + heads],
        sums[2, at_step : at_step + heads],
        sums[TAIL - 1, :channels],
        part_out,
    )


def solution(mesh):
    return jax.shard_map(
        shards,
        mesh=mesh,
        in_specs=(
            P(("dp", "tensor"), None),
            P("dp", None),
            P(),
            P("dp", None, "tensor"),
            P("dp", None),
            P("dp", "tensor"),
            P(None, "tensor"),
            P("tensor"),
            P(),
            P(),
            P("tensor"),
            P("tensor"),
            P("tensor"),
            P("tensor"),
            P("dp", "tensor"),
            P(("dp", "tensor"), None),
        ),
        out_specs=(
            P(("dp", "tensor"), None),
            P(("dp", "tensor"), None),
            P(),
            P("dp", None, "tensor"),
            P("dp", None),
            P("dp", "tensor"),
            P(None, "tensor"),
            P("tensor"),
            P(),
            P(),
            P("tensor"),
            P("tensor"),
            P("tensor"),
            P("tensor"),
            P("dp", "tensor"),
        ),
        check_vma=False,
    )
```

```python
from functools import partial

import jax
import jax.numpy as jnp
from jax import lax
from jax.experimental import pallas as pl
from jax.experimental.pallas import tpu as pltpu
from jax.sharding import PartitionSpec as P

EPSILON = 1e-05
SPAN = 256
LANES = 128
TAIL = 8
TAPS = 4
MASKED = -1e30
f32 = jnp.float32
bf16 = jnp.bfloat16
LIMIT = 60 * 1024 * 1024


def mm(left, right, dims):
    return lax.dot_general(left, right, ((dims[0], dims[1]), ((), ())), preferred_element_type=f32)


NN = ((1,), (0,))
NT = ((1,), (1,))
TN = ((0,), (0,))


def halves(value, axis):
    high = value.astype(bf16)
    low = (value - high.astype(f32)).astype(bf16)
    return jnp.concatenate([high, low], axis=axis)


def sigmoid(value):
    return 1.0 / (1.0 + jnp.exp(-value))


def softplus(value):
    return jnp.maximum(value, 0.0) + jnp.log1p(jnp.exp(-jnp.abs(value)))


def segment_at(ends, position):
    total = jnp.zeros(position.shape, jnp.int32)
    for end in ends:
        total = total + (position >= end).astype(jnp.int32)
    return total


def sequence_ends(lengths_ref):
    ends, total = [], 0
    for i in range(lengths_ref.shape[1]):
        total = total + lengths_ref[0, i]
        ends.append(total)
    return ends


def step_parts(step_raw, rate, ends, base):
    rows = step_raw.shape[0]
    step = softplus(step_raw)
    row = lax.broadcasted_iota(jnp.int32, (rows, rows), 0)
    col = lax.broadcasted_iota(jnp.int32, (rows, rows), 1)
    lower = (row >= col).astype(f32).astype(bf16)
    split = mm(lower, halves(step * rate, 1), NN)
    running = split[:, :LANES] + split[:, LANES:]
    position = base + lax.broadcasted_iota(jnp.int32, (rows, 1), 0)
    segment = segment_at(ends, position)
    before = segment_at(ends, jnp.full((1, 1), base - 1, jnp.int32))
    last = segment_at(ends, jnp.full((1, 1), base + rows - 1, jnp.int32))
    carried = ((segment == before) & (position >= rows)).astype(f32)
    matched = (segment == last).astype(f32)
    entry = jnp.exp(running) * carried
    leave = jnp.exp(running[rows - 1 :, :] - running) * matched
    return step, running, entry, leave, lower, segment, row, col


def same_rows(ends, base, rows):
    across = segment_at(ends, base + lax.broadcasted_iota(jnp.int32, (1, rows), 1))
    down = segment_at(ends, base + lax.broadcasted_iota(jnp.int32, (rows, 1), 0))
    return down == across


def rows_of(block, blocks, spot_ref, own_ref, others):
    if not others:
        return own_ref[...]
    half = blocks // 2
    local = lax.rem(block, half)
    span = own_ref.shape[0] // half
    each = half // len(others)
    value = None
    for i, ref in enumerate(others):
        at = lax.rem(local, each) * span
        piece = ref[pl.ds(pl.multiple_of(at, span), span), :]
        value = piece if i == 0 else jnp.where(local >= i * each, piece, value)
    mine = own_ref[pl.ds(pl.multiple_of(local * span, span), span), :]
    return jnp.where(block // half == spot_ref[0, 0], mine, value)


def own_specs(own, others, span):
    if not others:
        return [pl.BlockSpec((span, own.shape[1]), lambda i: (i, 0))]
    return [full(own.shape), *[full(other.shape) for other in others]]


def place_weights(spot_ref, weight_ref, sources, count):
    rows = weight_ref.shape[0] // (4 * count)
    for i, ref in enumerate(sources):
        along = spot_ref[0, 2] ^ (i % 2)
        core = spot_ref[0, 3] ^ (i // 2)
        for k in range(count):
            at = (((spot_ref[0, 1] ^ k) * 2 + along) * 2 + core) * rows
            at = pl.ds(pl.multiple_of(at, rows), rows)
            weight_ref[at, :] = ref[k * rows : (k + 1) * rows, :]


def place_pairs(spot_ref, weight_ref, sources, count, lo):
    rows = weight_ref.shape[0] // (4 * count)
    for i, (ref, begin) in enumerate(sources):
        core = spot_ref[0, 3] ^ (i // count)
        for j in range(2):
            at = (((spot_ref[0, 1] ^ (i % count)) * 2 + (spot_ref[0, 2] ^ j)) * 2 + core) * rows
            at = pl.ds(pl.multiple_of(at, rows), rows)
            here = begin + j * rows
            weight_ref[at, lo : lo + ref.shape[1]] = ref[here : here + rows, :]


def split_cores(spot_ref, value_ref, keep_ref, send_ref, chips):
    rows = keep_ref.shape[0] // chips
    core = spot_ref[0, 3]
    for chip in range(chips):
        here = pl.ds(pl.multiple_of((2 * chip + core) * rows, rows), rows)
        there = pl.ds(pl.multiple_of((2 * chip + 1 - core) * rows, rows), rows)
        keep_ref[chip * rows : (chip + 1) * rows, :] = value_ref[here, :].astype(bf16)
        send_ref[chip * rows : (chip + 1) * rows, :] = value_ref[there, :].astype(bf16)


def forward_kernel(
    pieces, count, spot_ref, lengths_ref, *refs
):
    own_ref, others = refs[0], refs[1:pieces]
    sources = refs[pieces : pieces + 4]
    (
        conv_inner_ref, bias_inner_ref, conv_shared_ref, bias_shared_ref, step_bias_ref, rate_ref,
        skip_ref, spread_ref, normed_ref, weight_ref, ssm_ref, inner_ref, pre_inner_ref, shared_ref,
        pre_shared_ref, step_ref, entering_ref, inner_tail, shared_tail, state,
    ) = refs[pieces + 4 :]
    block = pl.program_id(0)
    rows = normed_ref.shape[0]
    channels = conv_inner_ref.shape[1]
    base = block * rows
    ends = sequence_ends(lengths_ref)

    @pl.when(block == 0)
    def _():
        inner_tail[0:TAIL, :] = jnp.zeros((TAIL, channels), f32)
        shared_tail[0:TAIL, :] = jnp.zeros((TAIL, shared_tail.shape[1]), f32)
        state[...] = jnp.zeros_like(state)
        place_weights(spot_ref, weight_ref, sources, count)

    @pl.when(block > 0)
    def _():
        inner_tail[0:TAIL, :] = inner_tail[rows : rows + TAIL, :]
        shared_tail[0:TAIL, :] = shared_tail[rows : rows + TAIL, :]

    normed = rows_of(block, pl.num_programs(0), spot_ref, own_ref, others)
    normed_ref[...] = normed
    small = mm(normed, weight_ref[:, channels:], NN)
    width = conv_shared_ref.shape[1]
    shared_proj = small[:, :width]
    shared_tail[TAIL : TAIL + rows, :] = shared_proj
    shared_ref[...] = shared_proj
    step_raw = small[:, width:] + step_bias_ref[...]
    step_ref[...] = step_raw
    inner_proj = mm(normed, weight_ref[:, :channels], NN)
    inner_tail[TAIL : TAIL + rows, :] = inner_proj
    inner_ref[...] = inner_proj

    step, running, entry, leave, lower, segment, row, col = step_parts(
        step_raw, rate_ref[...], ends, base
    )
    position = base + lax.broadcasted_iota(jnp.int32, (rows, 1), 0)
    keeps = [
        ((segment_at(ends, position - k) == segment) & (position >= k)).astype(f32)
        for k in range(1, TAPS)
    ]

    def conv(tail, taps_ref, bias_ref, lo, hi):
        total = bias_ref[:, lo:hi] + taps_ref[TAPS - 1 : TAPS, lo:hi] * tail[TAIL : TAIL + rows, lo:hi]
        for k in range(1, TAPS):
            shifted = tail[TAIL - k : TAIL - k + rows, lo:hi]
            total = total + taps_ref[TAPS - 1 - k : TAPS - k, lo:hi] * (shifted * keeps[k - 1])
        return total

    pre_shared = conv(shared_tail, conv_shared_ref, bias_shared_ref, 0, width)
    pre_shared_ref[...] = pre_shared
    shared = pre_shared * sigmoid(pre_shared)
    in_map = shared[:, : width // 2].astype(bf16)
    out_map = shared[:, width // 2 :].astype(bf16)
    scores = mm(out_map, in_map, NT)
    allowed = jnp.where((row >= col) & same_rows(ends, base, rows), 0.0, MASKED)
    running_t = jnp.transpose(running)
    step2, entry2, leave2 = halves(step, 1), halves(entry, 1), halves(leave, 1)
    lane = lax.broadcasted_iota(jnp.int32, (rows, LANES), 1)
    for pair in range(channels // LANES):
        lo, hi = pair * LANES, (pair + 1) * LANES
        pre = conv(inner_tail, conv_inner_ref, bias_inner_ref, lo, hi)
        pre_inner_ref[:, lo:hi] = pre
        head_in = pre * sigmoid(pre)
        spread = spread_ref[:, lo:hi]
        scaled = head_in * mm(step2, spread, NN)
        scaled_low = scaled.astype(bf16)
        entry_wide = mm(entry2, spread, NN)
        leave_wide = mm(leave2, spread, NN)
        held = state[:, lo:hi]
        entering_ref[0, :, lo:hi] = held
        carried_out = mm(out_map, held.astype(bf16), NN) * entry_wide
        parts = []
        for side in range(2):
            head = 2 * pair + side
            gap = running[:, head : head + 1] - running_t[head : head + 1, :]
            mixed = (scores * jnp.exp(gap + allowed)).astype(bf16)
            parts.append(mm(mixed, scaled_low, NN))
        intra = jnp.where(lane < LANES // 2, parts[0], parts[1])
        ssm_ref[:, lo:hi] = carried_out + intra + skip_ref[:, lo:hi] * head_in
        added = mm(in_map, (scaled * leave_wide).astype(bf16), TN)
        state[:, lo:hi] = held * entry_wide[rows - 1 :, :] + added


def full(shape):
    return pl.BlockSpec(shape, lambda *_: (0,) * len(shape))


def mixer_forward(
    spot, lengths, own, others, sources, count, conv_inner, bias_inner, conv_shared, bias_shared,
    step_bias, rate, skip, spread, span,
):
    rows = own.shape[0] * (2 if others else 1)
    model = own.shape[1]
    channels = conv_inner.shape[1]
    width = conv_shared.shape[1]
    known = channels + width + LANES
    blocks = rows // span
    by_row = lambda cols: pl.BlockSpec((span, cols), lambda i: (i, 0))
    shape = lambda cols: jax.ShapeDtypeStruct((rows, cols), f32)
    states = width // 2
    smem = pl.BlockSpec(memory_space=pltpu.SMEM)
    fixed = (conv_inner, bias_inner, conv_shared, bias_shared, step_bias, rate, skip, spread)
    return pl.pallas_call(
        partial(forward_kernel, 1 + len(others), count),
        grid=(blocks,),
        in_specs=[
            smem, smem, *own_specs(own, others, span), *[full(x.shape) for x in sources],
            *[full(x.shape) for x in fixed],
        ],
        out_specs=[
            by_row(model), full((model, known)), by_row(channels), by_row(channels),
            by_row(channels), by_row(width), by_row(width), by_row(LANES),
            pl.BlockSpec((1, states, channels), lambda i: (i, 0, 0)),
        ],
        out_shape=[
            jax.ShapeDtypeStruct((rows, model), bf16), jax.ShapeDtypeStruct((model, known), bf16),
            shape(channels), shape(channels), shape(channels), shape(width), shape(width),
            shape(LANES), jax.ShapeDtypeStruct((blocks, states, channels), f32),
        ],
        scratch_shapes=[
            pltpu.VMEM((TAIL + span, channels), f32),
            pltpu.VMEM((TAIL + span, width), f32),
            pltpu.VMEM((states, channels), f32),
        ],
        compiler_params=pltpu.CompilerParams(
            dimension_semantics=("arbitrary",), vmem_limit_bytes=LIMIT
        ),
        name="mixer_forward",
    )(spot, lengths, own, *others, *sources, *fixed)


def backward_kernel(
    first_block, total_rows, lengths_ref, upstream_ref, ssm_ref, inner_ref, pre_inner_ref, shared_ref, pre_shared_ref,
    step_ref, entering_ref, conv_inner_ref, conv_shared_ref, rate_ref, skip_ref, spread_ref,
    sums_in_ref, inner_in_ref, shared_in_ref, adjoint_in_ref,
    grads_ref, sums_ref, inner_out_ref, shared_out_ref, adjoint, inner_head, shared_head,
):
    turn = pl.program_id(0)
    block = first_block + pl.num_programs(0) - 1 - turn
    rows, channels = upstream_ref.shape
    width = conv_shared_ref.shape[1]
    base = block * rows
    ends = sequence_ends(lengths_ref)

    @pl.when(turn == 0)
    def _():
        inner_head[rows : rows + TAIL, :] = inner_in_ref[...]
        shared_head[rows : rows + TAIL, :] = shared_in_ref[...]
        adjoint[...] = adjoint_in_ref[...]
        sums_ref[...] = sums_in_ref[...]

    @pl.when(turn > 0)
    def _():
        inner_head[rows : rows + TAIL, :] = inner_head[0:TAIL, :]
        shared_head[rows : rows + TAIL, :] = shared_head[0:TAIL, :]

    step_raw = step_ref[...]
    rate = rate_ref[...]
    step, running, entry, leave, lower, segment, row, col = step_parts(step_raw, rate, ends, base)
    position = base + lax.broadcasted_iota(jnp.int32, (rows, 1), 0)
    keeps = [
        ((segment_at(ends, position + k) == segment) & (position + k < total_rows)).astype(f32)
        for k in range(1, TAPS)
    ]
    pre_shared = pre_shared_ref[...]
    shared_gate = sigmoid(pre_shared)
    shared = pre_shared * shared_gate
    half = width // 2
    in_map = shared[:, :half].astype(bf16)
    out_map = shared[:, half:].astype(bf16)
    scores_t = mm(in_map, out_map, NT)
    allowed_t = jnp.where((col >= row) & same_rows(ends, base, rows), 0.0, MASKED)
    running_t = jnp.transpose(running)
    step2, entry2, leave2 = halves(step, 1), halves(entry, 1), halves(leave, 1)
    lane = lax.broadcasted_iota(jnp.int32, (rows, LANES), 1)
    first_half = lane < LANES // 2
    grad_scores_t = jnp.zeros((rows, rows), f32)
    grad_in = jnp.zeros((rows, half), f32)
    grad_out = jnp.zeros((rows, half), f32)
    by_head = jnp.zeros((rows, LANES), f32)
    step_terms = jnp.zeros((rows, LANES), f32)
    leaving = jnp.zeros((TAIL, LANES), f32)
    for pair in range(channels // LANES):
        lo, hi = pair * LANES, (pair + 1) * LANES
        spread = spread_ref[:, lo:hi]
        step_wide = mm(step2, spread, NN)
        entry_wide = mm(entry2, spread, NN)
        leave_wide = mm(leave2, spread, NN)
        pre = pre_inner_ref[:, lo:hi]
        gate = sigmoid(pre)
        head_in = pre * gate
        skip = skip_ref[:, lo:hi]
        upstream = upstream_ref[:, lo:hi]
        upstream_low = upstream.astype(bf16)
        upstream_back = upstream_low.astype(f32)
        scaled = head_in * step_wide
        scaled_low = scaled.astype(bf16)
        scaled_back = scaled_low.astype(f32)
        held = entering_ref[0, :, lo:hi]
        held_low = held.astype(bf16)
        ahead = adjoint[:, lo:hi]
        ahead_low = ahead.astype(bf16)
        entry_up = (upstream_back * entry_wide).astype(bf16)
        grad_out = grad_out + mm(entry_up, held_low, NT)
        grad_in = grad_in + mm((scaled * leave_wide).astype(bf16), ahead_low, NT)
        grad_scaled = mm(in_map, ahead_low, NN) * leave_wide
        through = entry_wide[rows - 1 :, :]
        tail_terms = jnp.sum(scaled_back * grad_scaled, axis=0, keepdims=True) + through * jnp.sum(
            ahead * held, axis=0, keepdims=True
        )
        adjoint[:, lo:hi] = ahead * through + mm(out_map, entry_up, TN)
        parts = []
        for side in range(2):
            head = 2 * pair + side
            gap = running_t[head : head + 1, :] - running[:, head : head + 1]
            decay = jnp.exp(gap + allowed_t)
            mixed = (scores_t * decay).astype(bf16)
            parts.append(mm(mixed, upstream_low, NN))
            mine = first_half if side == 0 else jnp.logical_not(first_half)
            chosen = jnp.where(mine, scaled_back, 0.0).astype(bf16)
            grad_scores_t = grad_scores_t + mm(chosen, upstream_low, NT) * decay
        grad_scaled = grad_scaled + jnp.where(first_half, parts[0], parts[1])
        spread_one = spread[:LANES, :]
        spread_both = jnp.concatenate([spread_one, spread_one], axis=1)
        balance = upstream_back * (ssm_ref[:, lo:hi] - skip * head_in) - scaled_back * grad_scaled
        by_head = by_head + mm(halves(balance, 1), spread_both, NT)
        step_terms = step_terms + mm(halves(head_in * grad_scaled, 1), spread_both, NT)
        skip_terms = jnp.sum(upstream * head_in, axis=0, keepdims=True)
        edge = jnp.concatenate([tail_terms, skip_terms, jnp.zeros((TAIL - 2, LANES), f32)], axis=0)
        leaving = leaving + mm(halves(edge, 1), spread_both, NT)
        grad_pre = (grad_scaled * step_wide + skip * upstream) * (gate * (1.0 + pre * (1.0 - gate)))
        inner_head[0:rows, lo:hi] = grad_pre
        inner_proj = inner_ref[:, lo:hi]
        grad_proj = conv_inner_ref[TAPS - 1 : TAPS, lo:hi] * grad_pre
        sums = [None] * TAPS
        sums[TAPS - 1] = jnp.sum(grad_pre * inner_proj, axis=0, keepdims=True)
        for k in range(1, TAPS):
            moved = inner_head[k : k + rows, lo:hi] * keeps[k - 1]
            grad_proj = grad_proj + conv_inner_ref[TAPS - 1 - k : TAPS - k, lo:hi] * moved
            sums[TAPS - 1 - k] = jnp.sum(moved * inner_proj, axis=0, keepdims=True)
        grads_ref[:, lo:hi] = grad_proj.astype(bf16)
        sums.append(jnp.sum(grad_pre, axis=0, keepdims=True))
        sums.append(jnp.zeros((TAIL - len(sums), LANES), f32))
        sums_ref[:, lo:hi] += jnp.concatenate(sums, axis=0)
    grad_scores_low = grad_scores_t.astype(bf16)
    grad_out = grad_out + mm(grad_scores_low, in_map, TN)
    grad_in = grad_in + mm(grad_scores_low, out_map, NN)
    grad_shared = jnp.concatenate([grad_in, grad_out], axis=1)
    grad_pre = grad_shared * (shared_gate * (1.0 + pre_shared * (1.0 - shared_gate)))
    shared_head[0:rows, :] = grad_pre
    shared_proj = shared_ref[...]
    grad_proj = conv_shared_ref[TAPS - 1 : TAPS, :] * grad_pre
    sums = [None] * TAPS
    sums[TAPS - 1] = jnp.sum(grad_pre * shared_proj, axis=0, keepdims=True)
    for k in range(1, TAPS):
        moved = shared_head[k : k + rows, :] * keeps[k - 1]
        grad_proj = grad_proj + conv_shared_ref[TAPS - 1 - k : TAPS - k, :] * moved
        sums[TAPS - 1 - k] = jnp.sum(moved * shared_proj, axis=0, keepdims=True)
    sums.append(jnp.sum(grad_pre, axis=0, keepdims=True))
    sums.append(jnp.zeros((TAIL - len(sums), width), f32))
    sums_ref[:, channels : channels + width] += jnp.concatenate(sums, axis=0)
    split = mm(lower, halves(by_head, 1), TN)
    grad_log = split[:, :LANES] + split[:, LANES:] + leaving[0:1, :]
    grad_step = (step_terms + rate * grad_log) * sigmoid(step_raw)
    grads_ref[:, channels : channels + width] = grad_proj.astype(bf16)
    grads_ref[:, channels + width :] = grad_step.astype(bf16)
    sums_ref[:, channels + width :] += jnp.concatenate(
        [
            jnp.sum(grad_step, axis=0, keepdims=True),
            rate * jnp.sum(step * grad_log, axis=0, keepdims=True),
            leaving[1:2, :],
            jnp.zeros((TAIL - 3, LANES), f32),
        ],
        axis=0,
    )

    @pl.when(turn == pl.num_programs(0) - 1)
    def _():
        inner_out_ref[...] = inner_head[0:TAIL, :]
        shared_out_ref[...] = shared_head[0:TAIL, :]


def mixer_backward(
    lengths, upstream, saved, conv_inner, conv_shared, rate, skip, spread, carry, blocks, span
):
    ssm, inner, pre_inner, shared, pre_shared, step_raw, entering = saved
    rows, channels = upstream.shape
    width = conv_shared.shape[1]
    states = width // 2
    begin, end = blocks
    known = channels + width + LANES
    by_row = lambda cols: pl.BlockSpec((span, cols), lambda i: (end - 1 - i, 0))
    small = ((TAIL, known), (TAIL, channels), (TAIL, width), (states, channels))
    results = pl.pallas_call(
        partial(backward_kernel, begin, rows),
        grid=(end - begin,),
        in_specs=[
            pl.BlockSpec(memory_space=pltpu.SMEM),
            by_row(channels), by_row(channels), by_row(channels), by_row(channels),
            by_row(width), by_row(width), by_row(LANES),
            pl.BlockSpec((1, states, channels), lambda i: (end - 1 - i, 0, 0)),
            full(conv_inner.shape),
            full(conv_shared.shape),
            full(rate.shape),
            full(skip.shape),
            full(spread.shape),
            *[full(shape) for shape in small],
        ],
        out_specs=[
            pl.BlockSpec((span, known), lambda i: (end - begin - 1 - i, 0)),
            *[full(shape) for shape in small],
        ],
        out_shape=[
            jax.ShapeDtypeStruct(((end - begin) * span, known), bf16),
            *[jax.ShapeDtypeStruct(shape, f32) for shape in small],
        ],
        scratch_shapes=[
            pltpu.VMEM((TAIL + span, channels), f32),
            pltpu.VMEM((TAIL + span, width), f32),
        ],
        compiler_params=pltpu.CompilerParams(
            dimension_semantics=("arbitrary",), vmem_limit_bytes=LIMIT
        ),
        name="mixer_backward",
    )(
        lengths, upstream, ssm, inner, pre_inner, shared, pre_shared, step_raw, entering,
        conv_inner, conv_shared, rate, skip, spread, *carry,
    )
    return results[0], tuple(results[1:])


def gain_row(weight_ref, total_ref, columns):
    rows = weight_ref.shape[0]
    begin, end = columns
    added = jnp.zeros((rows, LANES), f32)
    for lo in range(begin, end, LANES):
        weight = weight_ref[:, lo : lo + LANES].astype(f32)
        added = added + weight * total_ref[:, lo - begin : lo - begin + LANES]
    return jnp.sum(jnp.transpose(added), axis=0, keepdims=True)


def product_kernel(chips, columns, last, spot_ref, normed_ref, weight_ref, gain_ref, sums_ref,
                   norm_sum_ref, *refs):
    grads, (keep_ref, send_ref, packed_ref, total) = refs[:-4], refs[-4:]
    lo, hi = columns
    at = 0
    for i, ref in enumerate(grads):
        rows = ref.shape[0]
        added = mm(normed_ref[at : at + rows, :], ref[:, lo:hi], TN)
        total[...] = added if i == 0 else total[...] + added
        at += rows
    split_cores(spot_ref, total, keep_ref, send_ref, chips)
    row = norm_sum_ref[0:1, :] + gain_row(weight_ref, total, columns)
    known = sums_ref.shape[1]
    if last:
        packed_ref[:, :known] = sums_ref[...]
        packed_ref[:, known:] = jnp.broadcast_to(row / gain_ref[...], norm_sum_ref.shape)
    else:
        packed_ref[...] = jnp.broadcast_to(row, norm_sum_ref.shape)


def weight_products(spot, normed, weight, gain, sums, norm_sum, grads, chips, columns, last):
    known = grads[0].shape[1]
    model = normed.shape[1]
    size = columns[1] - columns[0]
    part = jax.ShapeDtypeStruct((model // 2, size), bf16)
    vmem = pl.BlockSpec(memory_space=pltpu.VMEM)
    return pl.pallas_call(
        partial(product_kernel, chips, columns, last),
        in_specs=[pl.BlockSpec(memory_space=pltpu.SMEM), *[vmem for _ in range(5 + len(grads))]],
        out_specs=[vmem, vmem, vmem],
        out_shape=[
            part, part, jax.ShapeDtypeStruct((TAIL, known + model if last else model), f32),
        ],
        scratch_shapes=[pltpu.VMEM((model, size), f32)],
        compiler_params=pltpu.CompilerParams(vmem_limit_bytes=LIMIT),
        name="weight_products",
    )(spot, normed, weight, gain, sums, norm_sum, *grads)


def gate_kernel(pieces, count, spot_ref, normed_ref, *refs):
    own_ref, others = refs[0], refs[1:pieces]
    joined, sources = refs[pieces : pieces + 2], refs[pieces + 2 : pieces + 2 + 2 * count]
    (
        gain_ref, ssm_ref, upstream_ref, weight_ref, gate_ref, grad_ref, sums_ref
    ) = refs[pieces + 2 + 2 * count :]

    @pl.when(pl.program_id(0) == 0)
    def _():
        each = joined[0].shape[0] // count
        rows = [(ref, k * each) for ref in joined for k in range(count)]
        place_pairs(spot_ref, weight_ref, rows, count, 0)
        place_pairs(spot_ref, weight_ref, [(ref, 0) for ref in sources], count, joined[0].shape[1])

    rows, channels = ssm_ref.shape
    normed = normed_ref[...]
    upstream = rows_of(pl.program_id(0), pl.num_programs(0), spot_ref, own_ref, others)
    upstream_ref[...] = upstream
    square = jnp.zeros((rows, LANES), f32)
    cross = jnp.zeros((rows, LANES), f32)
    step = 2 * LANES
    for lo in range(0, channels, step):
        hi = lo + step
        gate = mm(normed, weight_ref[:, lo:hi], NN)
        grad = mm(upstream, weight_ref[:, channels + lo : channels + hi], NN)
        gate_ref[:, lo:hi] = gate
        grad_ref[:, lo:hi] = grad
        gated = ssm_ref[:, lo:hi] * (gate * sigmoid(gate))
        squares = gated * gated
        crosses = grad * gain_ref[:, lo:hi] * gated
        square = square + (squares[:, :LANES] + squares[:, LANES:])
        cross = cross + (crosses[:, :LANES] + crosses[:, LANES:])
    square = jnp.sum(square, axis=1, keepdims=True)
    cross = jnp.sum(cross, axis=1, keepdims=True)
    lane = lax.broadcasted_iota(jnp.int32, (rows, LANES), 1)
    both = jnp.where(lane == 0, square, jnp.where(lane == 1, cross, 0.0))
    sums_ref[...] = jnp.transpose(both)[0:TAIL, :]


def gate_forward(spot, normed, own, others, sources, count, gain, ssm, span):
    rows, model = normed.shape
    channels = ssm.shape[1]
    by_row = lambda cols: pl.BlockSpec((span, cols), lambda i: (i, 0))
    return pl.pallas_call(
        partial(gate_kernel, 1 + len(others), count),
        grid=(rows // span,),
        in_specs=[
            pl.BlockSpec(memory_space=pltpu.SMEM), by_row(model), *own_specs(own, others, span),
            *[full(x.shape) for x in sources], full(gain.shape), by_row(channels),
        ],
        out_specs=[
            by_row(model), full((model, 2 * channels)), by_row(channels), by_row(channels),
            pl.BlockSpec((TAIL, span), lambda i: (0, i)),
        ],
        out_shape=[
            jax.ShapeDtypeStruct((rows, model), bf16),
            jax.ShapeDtypeStruct((model, 2 * channels), bf16),
            jax.ShapeDtypeStruct((rows, channels), f32),
            jax.ShapeDtypeStruct((rows, channels), f32),
            jax.ShapeDtypeStruct((TAIL, rows), f32),
        ],
        compiler_params=pltpu.CompilerParams(
            dimension_semantics=("arbitrary",), vmem_limit_bytes=LIMIT
        ),
        name="gate_forward",
    )(spot, normed, own, *others, *sources, gain, ssm)


def norm_kernel(full_inner, chips, split, spot_ref, sums_ref, more_ref, gate_ref, grad_ref, ssm_ref,
                gain_ref, normed_ref, upstream_ref, gate_w_ref, out_w_ref, grad_gate_ref,
                grad_ssm_ref, gain_sum_ref, keep_ref, send_ref, mine_ref, theirs_ref, norm_sum_ref,
                scaled, totals):
    rows, channels = gate_ref.shape
    block = pl.program_id(0)

    @pl.when(block == 0)
    def _():
        gain_sum_ref[...] = jnp.zeros_like(gain_sum_ref)
        totals[...] = jnp.zeros_like(totals)

    sums = sums_ref[...] + more_ref[...] if split else sums_ref[...]
    sums = jnp.transpose(jnp.concatenate([sums, jnp.zeros((LANES - TAIL, rows), f32)], axis=0))
    scale = lax.rsqrt(sums[:, 0:1] / full_inner + EPSILON)
    pull = scale * scale * scale * (sums[:, 1:2] / full_inner)
    normed_t = jnp.transpose(normed_ref[...])
    upstream_t = jnp.transpose(upstream_ref[...])
    step = 2 * LANES
    for lo in range(0, channels, step):
        hi = lo + step
        gain = gain_ref[:, lo:hi]
        gate, grad, ssm = gate_ref[:, lo:hi], grad_ref[:, lo:hi], ssm_ref[:, lo:hi]
        sig = sigmoid(gate)
        silu = gate * sig
        gated = ssm * silu
        normal = gated * scale
        scaled_low = (normal * gain).astype(bf16)
        scaled[:, lo:hi] = scaled_low
        gain_sum_ref[TAIL - 1 : TAIL, lo:hi] += jnp.sum(grad * normal, axis=0, keepdims=True)
        grad_gated = scale * (grad * gain) - gated * pull
        grad_ssm_ref[:, lo:hi] = grad_gated * silu
        grad_gate = (grad_gated * ssm * (sig * (1.0 + gate * (1.0 - sig)))).astype(bf16)
        grad_gate_ref[:, lo:hi] = grad_gate
        totals[:, lo:hi] += mm(normed_t, grad_gate, NN)
        totals[:, channels + lo : channels + hi] += mm(upstream_t, scaled_low, NN)
    branch = mm(scaled[...], out_w_ref[...], NT).astype(bf16)
    if split:
        half = pl.num_programs(0) // 2
        at = pl.ds(pl.multiple_of(lax.rem(block, half) * rows, rows), rows)

        @pl.when(block // half == spot_ref[0, 0])
        def _():
            mine_ref[at, :] = branch

        @pl.when(block // half != spot_ref[0, 0])
        def _():
            theirs_ref[at, :] = branch
    else:
        mine_ref[pl.ds(pl.multiple_of(block * rows, rows), rows), :] = branch

        @pl.when(block == 0)
        def _():
            theirs_ref[...] = jnp.zeros_like(theirs_ref)

    @pl.when(block == pl.num_programs(0) - 1)
    def _():
        split_cores(spot_ref, totals, keep_ref, send_ref, chips)
        norm_sum_ref[...] = jnp.zeros_like(norm_sum_ref)
        norm_sum_ref[0:1, :] = gain_row(gate_w_ref, totals, (0, channels))


def gate_norm(
    spot, sums, more, gate, grad, ssm, gain, normed, upstream, weight, known, full_inner, chips, split, span
):
    rows, channels = gate.shape
    model = normed.shape[1]
    by_row = lambda cols: pl.BlockSpec((span, cols), lambda i: (i, 0))
    stats = pl.BlockSpec((TAIL, span), lambda i: (0, i))
    half = (model // 2, 2 * channels)
    mine = (rows // 2 if split else rows, model)
    theirs = (rows // 2 if split else TAIL * 2, model)
    return pl.pallas_call(
        partial(norm_kernel, float(full_inner), chips, split),
        grid=(rows // span,),
        in_specs=[
            pl.BlockSpec(memory_space=pltpu.SMEM), stats, stats, by_row(channels), by_row(channels),
            by_row(channels), full(gain.shape), by_row(model), by_row(model),
            pl.BlockSpec((model, channels), lambda i: (0, 0)),
            pl.BlockSpec((model, channels), lambda i: (0, 1)),
        ],
        out_specs=[
            by_row(channels), by_row(channels), full((TAIL, known)), full(half), full(half),
            full(mine), full(theirs), full((TAIL, model)),
        ],
        out_shape=[
            jax.ShapeDtypeStruct((rows, channels), bf16),
            jax.ShapeDtypeStruct((rows, channels), f32),
            jax.ShapeDtypeStruct((TAIL, known), f32),
            jax.ShapeDtypeStruct(half, bf16),
            jax.ShapeDtypeStruct(half, bf16),
            jax.ShapeDtypeStruct(mine, bf16),
            jax.ShapeDtypeStruct(theirs, bf16),
            jax.ShapeDtypeStruct((TAIL, model), f32),
        ],
        scratch_shapes=[
            pltpu.VMEM((span, channels), bf16),
            pltpu.VMEM((model, 2 * channels), f32),
        ],
        compiler_params=pltpu.CompilerParams(
            dimension_semantics=("arbitrary",), vmem_limit_bytes=LIMIT
        ),
        name="gate_norm",
    )(spot, sums, more, gate, grad, ssm, gain, normed, upstream, weight, weight)


def lanes_of(vector):
    return jnp.pad(vector, (0, LANES - vector.shape[0]))[None, :]


def spread_map(heads, channels):
    size = channels // heads
    row = lax.broadcasted_iota(jnp.int32, (2 * LANES, channels), 0) % LANES
    col = lax.broadcasted_iota(jnp.int32, (2 * LANES, channels), 1) // size
    return (row == col).astype(bf16)


def input_kernel(grad_gate_ref, grads_ref, gate_w_ref, weight_ref, terms_ref):
    terms = mm(grad_gate_ref[...], gate_w_ref[...], NT)
    terms = terms + mm(grads_ref[...], weight_ref[...], NT)
    terms_ref[...] = terms.astype(bf16)


def input_terms(grad_gate, grads, weight_late, weight, begin, span):
    model = weight.shape[0]
    channels = grad_gate.shape[1]
    rows, known = grads.shape
    return pl.pallas_call(
        input_kernel,
        grid=(rows // span,),
        in_specs=[
            pl.BlockSpec((span, channels), lambda i: (i + begin, 0)),
            pl.BlockSpec((span, known), lambda i: (i, 0)),
            pl.BlockSpec((model, channels), lambda i: (0, 0)), full(weight.shape),
        ],
        out_specs=pl.BlockSpec((span, model), lambda i: (i, 0)),
        out_shape=jax.ShapeDtypeStruct((rows, model), bf16),
        compiler_params=pltpu.CompilerParams(
            dimension_semantics=("arbitrary",), vmem_limit_bytes=LIMIT
        ),
        name="input_terms",
    )(grad_gate, grads, weight_late, weight)


def dp_send(value, bit):
    size = lax.axis_size("dp")
    return lax.ppermute(value, "dp", [(i, i ^ bit) for i in range(size)])


def chip_bits():
    return [4 * k for k in range(1, lax.axis_size("dp") // 4)]


def long_bits():
    bits, bit = [], 4
    while bit < lax.axis_size("dp"):
        bits.append(bit)
        bit *= 2
    return bits


def choose(stacked, index, axis):
    return lax.dynamic_index_in_dim(stacked, index, axis, keepdims=False)


def send_fold(parts, bit, axis):
    mine = (lax.axis_index("dp") // bit) % 2
    return dp_send(choose(parts, 1 - mine, axis), bit)


def keep_fold(parts, got, bit, axis):
    mine = (lax.axis_index("dp") // bit) % 2
    return choose(parts, mine, axis).astype(f32) + got.astype(f32)


def fold(parts, bit, axis):
    return keep_fold(parts, send_fold(parts, bit, axis), bit, axis)


def send_chips(parts):
    place = lax.axis_index("dp") // 4
    sends = parts.astype(bf16)
    return [dp_send(choose(sends, place ^ (bit // 4), 0), bit) for bit in chip_bits()]


def keep_chips(parts, got):
    total = choose(parts, lax.axis_index("dp") // 4, 0).astype(f32)
    for piece in got:
        total = total + piece.astype(f32)
    return total


def fold_chips(parts):
    return keep_chips(parts, send_chips(parts))


def tensor_swap(value):
    return lax.ppermute(value, "tensor", [(0, 1), (1, 0)])


def gather_other(own, size):
    if size != 2:
        return lax.all_gather(own, "tensor", axis=0, tiled=True)
    return tensor_swap(own)


def join_pieces(own, top, bottom, size):
    top = top.reshape(size, -1, own.shape[1])
    bottom = bottom.reshape(size, -1, own.shape[1])
    return jnp.concatenate([top, bottom], axis=1).reshape(-1, own.shape[1])


def pick_half(lower, upper, size):
    if size != 2:
        return lower
    return jnp.where(lax.axis_index("tensor") == 0, lower, upper)


def sum_quarters(quarters, other0, other1, size):
    if size != 2:
        whole = jnp.concatenate(quarters, axis=0)
        return lax.psum_scatter(whole, "tensor", scatter_dimension=0, tiled=True).astype(f32)
    first = lax.axis_index("tensor") == 0
    lower = jnp.concatenate(quarters[:2], axis=0)
    others = jnp.concatenate([other0, other1], axis=0)
    return jnp.where(first, lower, quarters[2]).astype(f32) + others.astype(f32)


def tensor_sum(value, size):
    if size != 2:
        return lax.psum(value, "tensor")
    return value + tensor_swap(value)


def shards(
    tokens, lengths, norm_gain, zx_weight, bc_weight, dt_weight, conv_inner, bias_inner,
    conv_shared, bias_shared, step_bias, log_rate, skip_gain, gate_gain, out_weight, cotangent,
):
    size = lax.axis_size("tensor")
    split = size == 2
    me = lax.axis_index("dp")
    count = len(chip_bits()) + 1
    spot = jnp.stack([lax.axis_index("tensor"), me // 4, (me // 2) % 2, me % 2])[None, :]
    spot = spot.astype(jnp.int32)
    channels = zx_weight.shape[2]
    heads = step_bias.shape[0]
    width = bc_weight.shape[1]
    known = channels + width + LANES
    step_weight = jnp.pad(dt_weight, ((0, 0), (0, LANES - heads)))
    early = jnp.concatenate([zx_weight[:, 1, :], bc_weight, step_weight], axis=1)
    inputs = tokens.astype(f32)
    norm_scale = lax.rsqrt(jnp.mean(inputs * inputs, axis=1, keepdims=True) + EPSILON)
    normed_rows = (inputs * norm_scale * norm_gain[None, :]).astype(bf16)
    half = normed_rows.shape[0] // 2
    fixed = (
        conv_inner, bias_inner[None, :], conv_shared, bias_shared[None, :], lanes_of(step_bias),
        lanes_of(-jnp.exp(log_rate)), jnp.repeat(skip_gain, channels // heads)[None, :],
        spread_map(heads, channels),
    )
    late = jnp.concatenate([zx_weight[:, 0, :], out_weight], axis=1)
    zeros = (
        jnp.zeros((TAIL, channels), f32), jnp.zeros((TAIL, width), f32),
        jnp.zeros((width // 2, channels), f32),
    )

    def along(value):
        return [value] + [dp_send(value, bit) for bit in chip_bits()]

    column = jnp.concatenate(along(early), axis=0)
    column, pair, top, fixed, zeros, spot = lax.optimization_barrier((
        column, jnp.concatenate([late, dp_send(late, 2)], axis=0),
        gather_other(normed_rows[:half], size), fixed, zeros, spot,
    ))
    cut_late = (2 * channels * 3 // 8) // LANES * LANES
    joined = along(pair[:, :cut_late])
    by_x, column, bottom, joined, pair = lax.optimization_barrier(
        (dp_send(column, 2), column, gather_other(normed_rows[half:], size), joined, pair)
    )
    joined = jnp.concatenate(joined, axis=0)
    pairs = along(pair[:, cut_late:])
    by_core = dp_send(column, 1)
    sources = (column, by_x, by_core, dp_send(by_x, 1))
    own, others = normed_rows, (top, bottom)
    if not split:
        own, others = join_pieces(normed_rows, top, bottom, size), ()
    normed, weight, *saved = mixer_forward(
        spot, lengths, own, others, sources, count, *fixed, SPAN
    )
    _, _, _, _, _, rate, skip, spread = fixed
    gain = gate_gain[None, :]
    other, ssm, joined_core, pairs = lax.optimization_barrier(
        (gather_other(cotangent, size), saved[0], dp_send(joined, 1), pairs)
    )
    sources = (joined, joined_core, *pairs, *[dp_send(pair, 1) for pair in pairs])
    own, others = (cotangent, (other,)) if split else (other, ())
    upstream, weight_late, gate, grad, sums = gate_forward(
        spot, normed, own, others, sources, count, gain, ssm, SPAN
    )
    more = gather_other(sums, size) if split else sums
    sums = sums if split else lax.psum(sums, "tensor")
    chips = 2 * count
    grad_gate, grad_ssm, gain_sum, keep, send, branch_own, branch_send, norm_sum = gate_norm(
        spot, sums, more, gate, grad, ssm, gain, normed, upstream, weight_late, known, channels * size,
        chips, split, SPAN,
    )
    if split:
        branch_other = gather_other(branch_send, size)
    else:
        branch_own = lax.psum_scatter(branch_own, "tensor", scatter_dimension=0, tiled=True)
        branch_other = jnp.zeros_like(branch_own)
    quarter = grad_ssm.shape[0] // SPAN // 4
    carry = (gain_sum, *zeros)

    def back(begin, end, carry):
        return mixer_backward(
            lengths, grad_ssm, saved, conv_inner, conv_shared, rate, skip, spread, carry,
            (begin * quarter, end * quarter), SPAN,
        )

    def terms_of(begin, grads):
        return input_terms(grad_gate, grads, weight_late, weight, begin * quarter, SPAN)

    first = dp_send(send, 1)
    grads2, carry = back(2, 4, carry)
    first = (keep.astype(f32) + first.astype(f32)).astype(bf16)
    first = first.reshape(count, 2, -1, first.shape[1])
    carry, first, grads2 = lax.optimization_barrier((carry, first, grads2))
    first_gate, first_out = first[..., :channels], first[..., channels:]
    terms2 = terms_of(2, grads2)
    carry, terms2 = lax.optimization_barrier((carry, terms2))
    grads1, carry = back(1, 2, carry)
    terms1 = terms_of(1, grads1)
    first_gate = fold(first_gate, 2, 1)
    first_out = fold_chips(first_out).astype(bf16)
    send1 = pick_half(terms2[terms2.shape[0] // 2 :], terms1, size)
    carry, send1, branch_other, first_gate, first_out = lax.optimization_barrier(
        (carry, send1, branch_other, first_gate, first_out)
    )
    other1 = gather_other(send1, size) if split else send1
    block_out = (inputs + (branch_own.astype(f32) + branch_other.astype(f32))).astype(bf16)
    part_gate = fold_chips(first_gate)
    part_out = fold(first_out, 2, 0)
    grads0, carry = back(0, 1, carry)
    sums, part_gate, part_out, grads0, other1, block_out = lax.optimization_barrier(
        (carry[0], part_gate, part_out, grads0, other1, block_out)
    )
    keep, send, sums = weight_products(
        spot, normed, weight, norm_gain[None, :], sums, norm_sum, (grads0, grads1, grads2), chips,
        (0, known), True,
    )
    got = dp_send(send, 1)
    terms0 = terms_of(0, grads0)
    send0 = pick_half(terms2[: terms2.shape[0] // 2], terms0, size)
    parts = (keep.astype(f32) + got.astype(f32)).astype(bf16).reshape(count, 2, -1, known)
    parts, sums, send0 = lax.optimization_barrier((parts, sums, send0))
    cut = min((known * 2 // 3) // LANES * LANES, channels)
    parts_a, parts_b = parts[..., :cut], parts[..., cut:]
    got_b = send_chips(parts_b)
    sums = sums + dp_send(sums, 1)
    got_a = send_fold(parts_a, 2, 1)
    sums = sums + dp_send(sums, 2)
    sums = sums + dp_send(sums, 4)
    send0, sums = lax.optimization_barrier((send0, sums))
    other0 = gather_other(send0, size) if split else send0
    got_a, got_b, sums = lax.optimization_barrier((got_a, got_b, sums))
    parts_a = keep_fold(parts_a, got_a, 2, 1)
    parts_b = keep_chips(parts_b, got_b).astype(bf16)
    got_a = send_chips(parts_a)
    parts_b = fold(parts_b, 2, 0)
    for bit in long_bits()[1:]:
        sums = sums + dp_send(sums, bit)
    parts_a = keep_chips(parts_a, got_a)
    shared_sums = tensor_sum(sums[:, channels:], size)
    norm_sum = shared_sums[0, known - channels :]
    grad_normed = sum_quarters((terms0, terms1, terms2), other0, other1, size)
    scaled_grad = grad_normed * norm_gain[None, :]
    grad_inputs = norm_scale * scaled_grad - inputs * norm_scale**3 * jnp.mean(
        scaled_grad * inputs, axis=1, keepdims=True
    )
    grad_tokens = (cotangent.astype(f32) + grad_inputs).astype(bf16)
    part_inner = jnp.concatenate([parts_a, parts_b[:, : channels - cut]], axis=1)
    at_step = channels + width
    part_shared = tensor_sum(parts_b[:, channels - cut : at_step - cut], size)
    part_step = parts_b[:, at_step - cut : at_step - cut + heads]
    part_in = jnp.stack([part_gate, part_inner], axis=1)
    return (
        block_out,
        grad_tokens,
        norm_sum,
        part_in,
        part_shared,
        part_step,
        sums[:TAPS, :channels],
        sums[TAPS, :channels],
        shared_sums[:TAPS, :width],
        shared_sums[TAPS, :width],
        sums[0, at_step : at_step + heads],
        sums[1, at_step : at_step + heads],
        sums[2, at_step : at_step + heads],
        sums[TAIL - 1, :channels],
        part_out,
    )


def solution(mesh):
    return jax.shard_map(
        shards,
        mesh=mesh,
        in_specs=(
            P(("dp", "tensor"), None),
            P("dp", None),
            P(),
            P("dp", None, "tensor"),
            P("dp", None),
            P("dp", "tensor"),
            P(None, "tensor"),
            P("tensor"),
            P(),
            P(),
            P("tensor"),
            P("tensor"),
            P("tensor"),
            P("tensor"),
            P("dp", "tensor"),
            P(("dp", "tensor"), None),
        ),
        out_specs=(
            P(("dp", "tensor"), None),
            P(("dp", "tensor"), None),
            P(),
            P("dp", None, "tensor"),
            P("dp", None),
            P("dp", "tensor"),
            P(None, "tensor"),
            P("tensor"),
            P(),
            P(),
            P("tensor"),
            P("tensor"),
            P("tensor"),
            P("tensor"),
            P("dp", "tensor"),
        ),
        check_vma=False,
    )
```

```python
from functools import partial

import jax
import jax.numpy as jnp
from jax import lax
from jax.experimental import pallas as pl
from jax.experimental.pallas import tpu as pltpu
from jax.sharding import PartitionSpec as P

EPSILON = 1e-05
SPAN = 256
LANES = 128
TAIL = 8
TAPS = 4
MASKED = -1e30
f32 = jnp.float32
bf16 = jnp.bfloat16
LIMIT = 60 * 1024 * 1024


def mm(left, right, dims):
    return lax.dot_general(left, right, ((dims[0], dims[1]), ((), ())), preferred_element_type=f32)


NN = ((1,), (0,))
NT = ((1,), (1,))
TN = ((0,), (0,))


def halves(value, axis):
    high = value.astype(bf16)
    low = (value - high.astype(f32)).astype(bf16)
    return jnp.concatenate([high, low], axis=axis)


def sigmoid(value):
    return 1.0 / (1.0 + jnp.exp(-value))


def softplus(value):
    return jnp.maximum(value, 0.0) + jnp.log1p(jnp.exp(-jnp.abs(value)))


def segment_at(ends, position):
    total = jnp.zeros(position.shape, jnp.int32)
    for end in ends:
        total = total + (position >= end).astype(jnp.int32)
    return total


def sequence_ends(lengths_ref):
    ends, total = [], 0
    for i in range(lengths_ref.shape[1]):
        total = total + lengths_ref[0, i]
        ends.append(total)
    return ends


def step_parts(step_raw, rate, ends, base):
    rows = step_raw.shape[0]
    step = softplus(step_raw)
    row = lax.broadcasted_iota(jnp.int32, (rows, rows), 0)
    col = lax.broadcasted_iota(jnp.int32, (rows, rows), 1)
    lower = (row >= col).astype(f32).astype(bf16)
    split = mm(lower, halves(step * rate, 1), NN)
    running = split[:, :LANES] + split[:, LANES:]
    position = base + lax.broadcasted_iota(jnp.int32, (rows, 1), 0)
    segment = segment_at(ends, position)
    before = segment_at(ends, jnp.full((1, 1), base - 1, jnp.int32))
    last = segment_at(ends, jnp.full((1, 1), base + rows - 1, jnp.int32))
    carried = ((segment == before) & (position >= rows)).astype(f32)
    matched = (segment == last).astype(f32)
    entry = jnp.exp(running) * carried
    leave = jnp.exp(running[rows - 1 :, :] - running) * matched
    return step, running, entry, leave, lower, segment, row, col


def same_rows(ends, base, rows):
    across = segment_at(ends, base + lax.broadcasted_iota(jnp.int32, (1, rows), 1))
    down = segment_at(ends, base + lax.broadcasted_iota(jnp.int32, (rows, 1), 0))
    return down == across


def rows_of(block, blocks, spot_ref, own_ref, others):
    if not others:
        return own_ref[...]
    half = blocks // 2
    local = lax.rem(block, half)
    span = own_ref.shape[0] // half
    each = half // len(others)
    value = None
    for i, ref in enumerate(others):
        at = lax.rem(local, each) * span
        piece = ref[pl.ds(pl.multiple_of(at, span), span), :]
        value = piece if i == 0 else jnp.where(local >= i * each, piece, value)
    mine = own_ref[pl.ds(pl.multiple_of(local * span, span), span), :]
    return jnp.where(block // half == spot_ref[0, 0], mine, value)


def own_specs(own, others, span):
    if not others:
        return [pl.BlockSpec((span, own.shape[1]), lambda i: (i, 0))]
    return [full(own.shape), *[full(other.shape) for other in others]]


def run_copies(copies):
    for copy in copies:
        copy.start()
    for copy in copies:
        copy.wait()


def place_weights(spot_ref, weight_ref, sources, count, done):
    rows = weight_ref.shape[0] // (4 * count)
    copies = []
    for i, ref in enumerate(sources):
        along = spot_ref[0, 2] ^ (i % 2)
        core = spot_ref[0, 3] ^ (i // 2)
        for k in range(count):
            at = (((spot_ref[0, 1] ^ k) * 2 + along) * 2 + core) * rows
            copies.append(pltpu.make_async_copy(
                ref.at[pl.ds(k * rows, rows), :],
                weight_ref.at[pl.ds(pl.multiple_of(at, rows), rows), :],
                done.at[i * count + k],
            ))
    run_copies(copies)


def place_pairs(spot_ref, weight_ref, sources, count, lo):
    rows = weight_ref.shape[0] // (4 * count)
    for i, (ref, begin) in enumerate(sources):
        core = spot_ref[0, 3] ^ (i // count)
        for j in range(2):
            at = (((spot_ref[0, 1] ^ (i % count)) * 2 + (spot_ref[0, 2] ^ j)) * 2 + core) * rows
            at = pl.ds(pl.multiple_of(at, rows), rows)
            here = begin + j * rows
            weight_ref[at, lo : lo + ref.shape[1]] = ref[here : here + rows, :]


def split_cores(spot_ref, value_ref, keep_ref, send_ref, chips):
    rows = keep_ref.shape[0] // chips
    core = spot_ref[0, 3]
    for chip in range(chips):
        here = pl.ds(pl.multiple_of((2 * chip + core) * rows, rows), rows)
        there = pl.ds(pl.multiple_of((2 * chip + 1 - core) * rows, rows), rows)
        keep_ref[chip * rows : (chip + 1) * rows, :] = value_ref[here, :].astype(bf16)
        send_ref[chip * rows : (chip + 1) * rows, :] = value_ref[there, :].astype(bf16)


def forward_kernel(
    pieces, count, spot_ref, lengths_ref, *refs
):
    own_ref, others = refs[0], refs[1:pieces]
    sources = refs[pieces : pieces + 4]
    (
        conv_inner_ref, bias_inner_ref, conv_shared_ref, bias_shared_ref, step_bias_ref, rate_ref,
        skip_ref, spread_ref, normed_ref, weight_ref, ssm_ref, inner_ref, pre_inner_ref, shared_ref,
        pre_shared_ref, step_ref, entering_ref, inner_tail, shared_tail, state, done,
    ) = refs[pieces + 4 :]
    block = pl.program_id(0)
    rows = normed_ref.shape[0]
    channels = conv_inner_ref.shape[1]
    base = block * rows
    ends = sequence_ends(lengths_ref)

    @pl.when(block == 0)
    def _():
        inner_tail[0:TAIL, :] = jnp.zeros((TAIL, channels), f32)
        shared_tail[0:TAIL, :] = jnp.zeros((TAIL, shared_tail.shape[1]), f32)
        state[...] = jnp.zeros_like(state)
        place_weights(spot_ref, weight_ref, sources, count, done)

    @pl.when(block > 0)
    def _():
        inner_tail[0:TAIL, :] = inner_tail[rows : rows + TAIL, :]
        shared_tail[0:TAIL, :] = shared_tail[rows : rows + TAIL, :]

    normed = rows_of(block, pl.num_programs(0), spot_ref, own_ref, others)
    normed_ref[...] = normed
    small = mm(normed, weight_ref[:, channels:], NN)
    width = conv_shared_ref.shape[1]
    shared_proj = small[:, :width]
    shared_tail[TAIL : TAIL + rows, :] = shared_proj
    shared_ref[...] = shared_proj
    step_raw = small[:, width:] + step_bias_ref[...]
    step_ref[...] = step_raw
    inner_proj = mm(normed, weight_ref[:, :channels], NN)
    inner_tail[TAIL : TAIL + rows, :] = inner_proj
    inner_ref[...] = inner_proj

    step, running, entry, leave, lower, segment, row, col = step_parts(
        step_raw, rate_ref[...], ends, base
    )
    position = base + lax.broadcasted_iota(jnp.int32, (rows, 1), 0)
    keeps = [
        ((segment_at(ends, position - k) == segment) & (position >= k)).astype(f32)
        for k in range(1, TAPS)
    ]
    keeps = [jnp.broadcast_to(keep, (rows, LANES)) for keep in keeps]

    def conv(tail, taps_ref, bias_ref, lo, hi):
        total = bias_ref[:, lo:hi] + taps_ref[TAPS - 1 : TAPS, lo:hi] * tail[TAIL : TAIL + rows, lo:hi]
        for k in range(1, TAPS):
            shifted = tail[TAIL - k : TAIL - k + rows, lo:hi]
            total = total + taps_ref[TAPS - 1 - k : TAPS - k, lo:hi] * (shifted * keeps[k - 1])
        return total

    pre_shared = jnp.concatenate(
        [
            conv(shared_tail, conv_shared_ref, bias_shared_ref, lo, lo + LANES)
            for lo in range(0, width, LANES)
        ],
        axis=1,
    )
    pre_shared_ref[...] = pre_shared
    shared = pre_shared * sigmoid(pre_shared)
    in_map = shared[:, : width // 2].astype(bf16)
    out_map = shared[:, width // 2 :].astype(bf16)
    scores = mm(out_map, in_map, NT)
    allowed = jnp.where((row >= col) & same_rows(ends, base, rows), 0.0, MASKED)
    running_t = jnp.transpose(running)
    step2, entry2, leave2 = halves(step, 1), halves(entry, 1), halves(leave, 1)
    lane = lax.broadcasted_iota(jnp.int32, (rows, LANES), 1)
    for pair in range(channels // LANES):
        lo, hi = pair * LANES, (pair + 1) * LANES
        pre = conv(inner_tail, conv_inner_ref, bias_inner_ref, lo, hi)
        pre_inner_ref[:, lo:hi] = pre
        head_in = pre * sigmoid(pre)
        side = (pair % 2) * LANES
        if side == 0:
            spread = spread_ref[:, lo : min(lo + 2 * LANES, channels)]
            wide = [mm(value, spread, NN) for value in (step2, entry2, leave2)]
        step_wide, entry_wide, leave_wide = [x[:, side : side + LANES] for x in wide]
        scaled = head_in * step_wide
        scaled_low = scaled.astype(bf16)
        held = state[:, lo:hi]
        entering_ref[0, :, lo:hi] = held
        carried_out = mm(out_map, held.astype(bf16), NN) * entry_wide
        parts = []
        for parity in range(2):
            head = 2 * pair + parity
            gap = running[:, head : head + 1] - running_t[head : head + 1, :]
            mixed = (scores * jnp.exp(gap + allowed)).astype(bf16)
            parts.append(mm(mixed, scaled_low, NN))
        intra = jnp.where(lane < LANES // 2, parts[0], parts[1])
        ssm_ref[:, lo:hi] = carried_out + intra + skip_ref[:, lo:hi] * head_in
        added = mm(in_map, (scaled * leave_wide).astype(bf16), TN)
        state[:, lo:hi] = held * entry_wide[rows - 1 :, :] + added


def full(shape):
    return pl.BlockSpec(shape, lambda *_: (0,) * len(shape))


def mixer_forward(
    spot, lengths, own, others, sources, count, conv_inner, bias_inner, conv_shared, bias_shared,
    step_bias, rate, skip, spread, span,
):
    rows = own.shape[0] * (2 if others else 1)
    model = own.shape[1]
    channels = conv_inner.shape[1]
    width = conv_shared.shape[1]
    known = channels + width + LANES
    blocks = rows // span
    by_row = lambda cols: pl.BlockSpec((span, cols), lambda i: (i, 0))
    shape = lambda cols: jax.ShapeDtypeStruct((rows, cols), f32)
    states = width // 2
    smem = pl.BlockSpec(memory_space=pltpu.SMEM)
    fixed = (conv_inner, bias_inner, conv_shared, bias_shared, step_bias, rate, skip, spread)
    return pl.pallas_call(
        partial(forward_kernel, 1 + len(others), count),
        grid=(blocks,),
        in_specs=[
            smem, smem, *own_specs(own, others, span),
            *[pl.BlockSpec(memory_space=pl.ANY) for _ in sources],
            *[full(x.shape) for x in fixed],
        ],
        out_specs=[
            by_row(model), full((model, known)), by_row(channels), by_row(channels),
            by_row(channels), by_row(width), by_row(width), by_row(LANES),
            pl.BlockSpec((1, states, channels), lambda i: (i, 0, 0)),
        ],
        out_shape=[
            jax.ShapeDtypeStruct((rows, model), bf16), jax.ShapeDtypeStruct((model, known), bf16),
            shape(channels), shape(channels), shape(channels), shape(width), shape(width),
            shape(LANES), jax.ShapeDtypeStruct((blocks, states, channels), f32),
        ],
        scratch_shapes=[
            pltpu.VMEM((TAIL + span, channels), f32),
            pltpu.VMEM((TAIL + span, width), f32),
            pltpu.VMEM((states, channels), f32),
            pltpu.SemaphoreType.DMA((4 * count,)),
        ],
        compiler_params=pltpu.CompilerParams(
            dimension_semantics=("arbitrary",), vmem_limit_bytes=LIMIT
        ),
        name="mixer_forward",
    )(spot, lengths, own, *others, *sources, *fixed)


def backward_kernel(
    first_block, total_rows, lengths_ref, upstream_ref, ssm_ref, inner_ref, pre_inner_ref, shared_ref, pre_shared_ref,
    step_ref, entering_ref, conv_inner_ref, conv_shared_ref, rate_ref, skip_ref, spread_ref,
    grad_gate_ref, gate_w_ref, weight_ref, sums_in_ref, inner_in_ref, shared_in_ref, adjoint_in_ref,
    grads_ref, terms_ref, sums_ref, inner_out_ref, shared_out_ref, adjoint, inner_head, shared_head,
    gate_w, weight, done,
):
    turn = pl.program_id(0)
    block = first_block + pl.num_programs(0) - 1 - turn
    rows, channels = upstream_ref.shape
    width = conv_shared_ref.shape[1]
    base = block * rows
    ends = sequence_ends(lengths_ref)

    def weight_copies():
        return (
            pltpu.make_async_copy(gate_w_ref.at[:, pl.ds(0, channels)], gate_w, done.at[0]),
            pltpu.make_async_copy(weight_ref, weight, done.at[1]),
        )

    @pl.when(turn == 0)
    def _():
        inner_head[rows : rows + TAIL, :] = inner_in_ref[...]
        shared_head[rows : rows + TAIL, :] = shared_in_ref[...]
        adjoint[...] = adjoint_in_ref[...]
        sums_ref[...] = sums_in_ref[...]
        for copy in weight_copies():
            copy.start()

    @pl.when(turn > 0)
    def _():
        inner_head[rows : rows + TAIL, :] = inner_head[0:TAIL, :]
        shared_head[rows : rows + TAIL, :] = shared_head[0:TAIL, :]

    step_raw = step_ref[...]
    rate = rate_ref[...]
    step, running, entry, leave, lower, segment, row, col = step_parts(step_raw, rate, ends, base)
    position = base + lax.broadcasted_iota(jnp.int32, (rows, 1), 0)
    keeps = [
        ((segment_at(ends, position + k) == segment) & (position + k < total_rows)).astype(f32)
        for k in range(1, TAPS)
    ]
    keeps = [jnp.broadcast_to(keep, (rows, LANES)) for keep in keeps]
    pre_shared = pre_shared_ref[...]
    shared_gate = sigmoid(pre_shared)
    shared = pre_shared * shared_gate
    half = width // 2
    in_map = shared[:, :half].astype(bf16)
    out_map = shared[:, half:].astype(bf16)
    scores_t = mm(in_map, out_map, NT)
    allowed_t = jnp.where((col >= row) & same_rows(ends, base, rows), 0.0, MASKED)
    running_t = jnp.transpose(running)
    step2, entry2, leave2 = halves(step, 1), halves(entry, 1), halves(leave, 1)
    lane = lax.broadcasted_iota(jnp.int32, (rows, LANES), 1)
    first_half = lane < LANES // 2
    grad_scores_t = jnp.zeros((rows, rows), f32)
    grad_in = jnp.zeros((rows, half), f32)
    grad_out = jnp.zeros((rows, half), f32)
    by_head = jnp.zeros((rows, LANES), f32)
    step_terms = jnp.zeros((rows, LANES), f32)
    leaving = jnp.zeros((TAIL, LANES), f32)
    for pair in range(channels // LANES):
        lo, hi = pair * LANES, (pair + 1) * LANES
        side = (pair % 2) * LANES
        if side == 0:
            spread = spread_ref[:, lo : min(lo + 2 * LANES, channels)]
            wide = [mm(value, spread, NN) for value in (step2, entry2, leave2)]
            products = []
        step_wide, entry_wide, leave_wide = [x[:, side : side + LANES] for x in wide]
        pre = pre_inner_ref[:, lo:hi]
        gate = sigmoid(pre)
        head_in = pre * gate
        skip = skip_ref[:, lo:hi]
        upstream = upstream_ref[:, lo:hi]
        upstream_low = upstream.astype(bf16)
        upstream_back = upstream_low.astype(f32)
        scaled = head_in * step_wide
        scaled_low = scaled.astype(bf16)
        scaled_back = scaled_low.astype(f32)
        held = entering_ref[0, :, lo:hi]
        held_low = held.astype(bf16)
        ahead = adjoint[:, lo:hi]
        ahead_low = ahead.astype(bf16)
        entry_up = (upstream_back * entry_wide).astype(bf16)
        grad_out = grad_out + mm(entry_up, held_low, NT)
        grad_in = grad_in + mm((scaled * leave_wide).astype(bf16), ahead_low, NT)
        grad_scaled = mm(in_map, ahead_low, NN) * leave_wide
        through = entry_wide[rows - 1 :, :]
        tail_terms = jnp.sum(scaled_back * grad_scaled, axis=0, keepdims=True) + through * jnp.sum(
            ahead * held, axis=0, keepdims=True
        )
        adjoint[:, lo:hi] = ahead * through + mm(out_map, entry_up, TN)
        parts = []
        for parity in range(2):
            head = 2 * pair + parity
            gap = running_t[head : head + 1, :] - running[:, head : head + 1]
            decay = jnp.exp(gap + allowed_t)
            mixed = (scores_t * decay).astype(bf16)
            parts.append(mm(mixed, upstream_low, NN))
            mine = first_half if parity == 0 else jnp.logical_not(first_half)
            chosen = jnp.where(mine, scaled_back, 0.0).astype(bf16)
            grad_scores_t = grad_scores_t + mm(chosen, upstream_low, NT) * decay
        grad_scaled = grad_scaled + jnp.where(first_half, parts[0], parts[1])
        spread_one = spread[:LANES, side : side + LANES]
        spread_both = jnp.concatenate([spread_one, spread_one], axis=1)
        balance = upstream_back * (ssm_ref[:, lo:hi] - skip * head_in) - scaled_back * grad_scaled
        by_head = by_head + mm(halves(balance, 1), spread_both, NT)
        products.append((head_in * grad_scaled).astype(bf16))
        if hi == channels or side > 0:
            joined = jnp.concatenate(products, axis=1)
            step_terms = step_terms + mm(joined, spread[:LANES, :], NT)
        skip_terms = jnp.sum(upstream * head_in, axis=0, keepdims=True)
        edge = jnp.concatenate([tail_terms, skip_terms, jnp.zeros((TAIL - 2, LANES), f32)], axis=0)
        leaving = leaving + mm(halves(edge, 1), spread_both, NT)
        grad_pre = (grad_scaled * step_wide + skip * upstream) * (gate * (1.0 + pre * (1.0 - gate)))
        inner_head[0:rows, lo:hi] = grad_pre
        inner_proj = inner_ref[:, lo:hi]
        grad_proj = conv_inner_ref[TAPS - 1 : TAPS, lo:hi] * grad_pre
        sums = [None] * TAPS
        sums[TAPS - 1] = jnp.sum(grad_pre * inner_proj, axis=0, keepdims=True)
        for k in range(1, TAPS):
            moved = inner_head[k : k + rows, lo:hi] * keeps[k - 1]
            grad_proj = grad_proj + conv_inner_ref[TAPS - 1 - k : TAPS - k, lo:hi] * moved
            sums[TAPS - 1 - k] = jnp.sum(moved * inner_proj, axis=0, keepdims=True)
        grads_ref[:, lo:hi] = grad_proj.astype(bf16)
        sums.append(jnp.sum(grad_pre, axis=0, keepdims=True))
        sums.append(jnp.zeros((TAIL - len(sums), LANES), f32))
        sums_ref[:, lo:hi] += jnp.concatenate(sums, axis=0)
    grad_scores_low = grad_scores_t.astype(bf16)
    grad_out = grad_out + mm(grad_scores_low, in_map, TN)
    grad_in = grad_in + mm(grad_scores_low, out_map, NN)
    grad_shared = jnp.concatenate([grad_in, grad_out], axis=1)
    grad_pre = grad_shared * (shared_gate * (1.0 + pre_shared * (1.0 - shared_gate)))
    shared_head[0:rows, :] = grad_pre
    shared_proj = shared_ref[...]
    grad_proj = conv_shared_ref[TAPS - 1 : TAPS, :] * grad_pre
    sums = [None] * TAPS
    sums[TAPS - 1] = jnp.sum(grad_pre * shared_proj, axis=0, keepdims=True)
    for k in range(1, TAPS):
        keep = jnp.concatenate([keeps[k - 1]] * (width // LANES), axis=1)
        moved = shared_head[k : k + rows, :] * keep
        grad_proj = grad_proj + conv_shared_ref[TAPS - 1 - k : TAPS - k, :] * moved
        sums[TAPS - 1 - k] = jnp.sum(moved * shared_proj, axis=0, keepdims=True)
    sums.append(jnp.sum(grad_pre, axis=0, keepdims=True))
    sums.append(jnp.zeros((TAIL - len(sums), width), f32))
    sums_ref[:, channels : channels + width] += jnp.concatenate(sums, axis=0)
    split = mm(lower, halves(by_head, 1), TN)
    grad_log = split[:, :LANES] + split[:, LANES:] + leaving[0:1, :]
    grad_step = (step_terms + rate * grad_log) * sigmoid(step_raw)
    grads_ref[:, channels : channels + width] = grad_proj.astype(bf16)
    grads_ref[:, channels + width :] = grad_step.astype(bf16)

    @pl.when(turn == 0)
    def _():
        for copy in weight_copies():
            copy.wait()

    terms = mm(grad_gate_ref[...], gate_w[...], NT) + mm(grads_ref[...], weight[...], NT)
    terms_ref[...] = terms.astype(bf16)
    sums_ref[:, channels + width :] += jnp.concatenate(
        [
            jnp.sum(grad_step, axis=0, keepdims=True),
            rate * jnp.sum(step * grad_log, axis=0, keepdims=True),
            leaving[1:2, :],
            jnp.zeros((TAIL - 3, LANES), f32),
        ],
        axis=0,
    )

    @pl.when(turn == pl.num_programs(0) - 1)
    def _():
        inner_out_ref[...] = inner_head[0:TAIL, :]
        shared_out_ref[...] = shared_head[0:TAIL, :]


def mixer_backward(
    lengths, upstream, saved, conv_inner, conv_shared, rate, skip, spread, grad_gate, weight_late,
    weight, carry, blocks, span
):
    ssm, inner, pre_inner, shared, pre_shared, step_raw, entering = saved
    rows, channels = upstream.shape
    width = conv_shared.shape[1]
    states = width // 2
    begin, end = blocks
    known = channels + width + LANES
    model = weight.shape[0]
    by_row = lambda cols: pl.BlockSpec((span, cols), lambda i: (end - 1 - i, 0))
    small = ((TAIL, known), (TAIL, channels), (TAIL, width), (states, channels))
    results = pl.pallas_call(
        partial(backward_kernel, begin, rows),
        grid=(end - begin,),
        in_specs=[
            pl.BlockSpec(memory_space=pltpu.SMEM),
            by_row(channels), by_row(channels), by_row(channels), by_row(channels),
            by_row(width), by_row(width), by_row(LANES),
            pl.BlockSpec((1, states, channels), lambda i: (end - 1 - i, 0, 0)),
            full(conv_inner.shape),
            full(conv_shared.shape),
            full(rate.shape),
            full(skip.shape),
            full(spread.shape),
            by_row(channels),
            pl.BlockSpec(memory_space=pl.ANY),
            pl.BlockSpec(memory_space=pl.ANY),
            *[full(shape) for shape in small],
        ],
        out_specs=[
            pl.BlockSpec((span, known), lambda i: (end - begin - 1 - i, 0)),
            pl.BlockSpec((span, model), lambda i: (end - begin - 1 - i, 0)),
            *[full(shape) for shape in small],
        ],
        out_shape=[
            jax.ShapeDtypeStruct(((end - begin) * span, known), bf16),
            jax.ShapeDtypeStruct(((end - begin) * span, model), bf16),
            *[jax.ShapeDtypeStruct(shape, f32) for shape in small],
        ],
        scratch_shapes=[
            pltpu.VMEM((TAIL + span, channels), f32),
            pltpu.VMEM((TAIL + span, width), f32),
            pltpu.VMEM((model, channels), bf16),
            pltpu.VMEM((model, known), bf16),
            pltpu.SemaphoreType.DMA((2,)),
        ],
        compiler_params=pltpu.CompilerParams(
            dimension_semantics=("arbitrary",), vmem_limit_bytes=LIMIT
        ),
        name="mixer_backward",
    )(
        lengths, upstream, ssm, inner, pre_inner, shared, pre_shared, step_raw, entering,
        conv_inner, conv_shared, rate, skip, spread, grad_gate, weight_late, weight, *carry,
    )
    return results[0], results[1], tuple(results[2:])


def gain_row(weight_ref, total_ref, columns):
    rows = weight_ref.shape[0]
    begin, end = columns
    added = jnp.zeros((rows, LANES), f32)
    for lo in range(begin, end, LANES):
        weight = weight_ref[:, lo : lo + LANES].astype(f32)
        added = added + weight * total_ref[:, lo - begin : lo - begin + LANES]
    return jnp.sum(jnp.transpose(added), axis=0, keepdims=True)


def product_kernel(chips, columns, last, spot_ref, normed_ref, weight_ref, gain_ref, sums_ref,
                   norm_sum_ref, *refs):
    grads, (keep_ref, send_ref, packed_ref, total) = refs[:-4], refs[-4:]
    lo, hi = columns
    at = 0
    for i, ref in enumerate(grads):
        rows = ref.shape[0]
        added = mm(normed_ref[at : at + rows, :], ref[:, lo:hi], TN)
        total[...] = added if i == 0 else total[...] + added
        at += rows
    split_cores(spot_ref, total, keep_ref, send_ref, chips)
    row = norm_sum_ref[0:1, :] + gain_row(weight_ref, total, columns)
    known = sums_ref.shape[1]
    if last:
        packed_ref[:, :known] = sums_ref[...]
        packed_ref[:, known:] = jnp.broadcast_to(row / gain_ref[...], norm_sum_ref.shape)
    else:
        packed_ref[...] = jnp.broadcast_to(row, norm_sum_ref.shape)


def weight_products(spot, normed, weight, gain, sums, norm_sum, grads, chips, columns, last):
    known = grads[0].shape[1]
    model = normed.shape[1]
    size = columns[1] - columns[0]
    part = jax.ShapeDtypeStruct((model // 2, size), bf16)
    vmem = pl.BlockSpec(memory_space=pltpu.VMEM)
    return pl.pallas_call(
        partial(product_kernel, chips, columns, last),
        in_specs=[pl.BlockSpec(memory_space=pltpu.SMEM), *[vmem for _ in range(5 + len(grads))]],
        out_specs=[vmem, vmem, vmem],
        out_shape=[
            part, part, jax.ShapeDtypeStruct((TAIL, known + model if last else model), f32),
        ],
        scratch_shapes=[pltpu.VMEM((model, size), f32)],
        compiler_params=pltpu.CompilerParams(vmem_limit_bytes=LIMIT),
        name="weight_products",
    )(spot, normed, weight, gain, sums, norm_sum, *grads)


def gate_kernel(pieces, count, spot_ref, normed_ref, *refs):
    own_ref, others = refs[0], refs[1:pieces]
    joined, sources = refs[pieces : pieces + 2], refs[pieces + 2 : pieces + 2 + 2 * count]
    (
        gain_ref, ssm_ref, upstream_ref, weight_ref, gate_ref, grad_ref, sums_ref
    ) = refs[pieces + 2 + 2 * count :]

    @pl.when(pl.program_id(0) == 0)
    def _():
        each = joined[0].shape[0] // count
        rows = [(ref, k * each) for ref in joined for k in range(count)]
        place_pairs(spot_ref, weight_ref, rows, count, 0)
        place_pairs(spot_ref, weight_ref, [(ref, 0) for ref in sources], count, joined[0].shape[1])

    rows, channels = ssm_ref.shape
    normed = normed_ref[...]
    upstream = rows_of(pl.program_id(0), pl.num_programs(0), spot_ref, own_ref, others)
    upstream_ref[...] = upstream
    square = jnp.zeros((rows, LANES), f32)
    cross = jnp.zeros((rows, LANES), f32)
    step = 2 * LANES
    for lo in range(0, channels, step):
        hi = lo + step
        gate = mm(normed, weight_ref[:, lo:hi], NN)
        grad = mm(upstream, weight_ref[:, channels + lo : channels + hi], NN)
        gate_ref[:, lo:hi] = gate
        grad_ref[:, lo:hi] = grad
        gated = ssm_ref[:, lo:hi] * (gate * sigmoid(gate))
        squares = gated * gated
        crosses = grad * gain_ref[:, lo:hi] * gated
        square = square + (squares[:, :LANES] + squares[:, LANES:])
        cross = cross + (crosses[:, :LANES] + crosses[:, LANES:])
    square = jnp.sum(square, axis=1, keepdims=True)
    cross = jnp.sum(cross, axis=1, keepdims=True)
    lane = lax.broadcasted_iota(jnp.int32, (rows, LANES), 1)
    both = jnp.where(lane == 0, square, jnp.where(lane == 1, cross, 0.0))
    sums_ref[...] = jnp.transpose(both)[0:TAIL, :]


def gate_forward(spot, normed, own, others, sources, count, gain, ssm, span):
    rows, model = normed.shape
    channels = ssm.shape[1]
    by_row = lambda cols: pl.BlockSpec((span, cols), lambda i: (i, 0))
    return pl.pallas_call(
        partial(gate_kernel, 1 + len(others), count),
        grid=(rows // span,),
        in_specs=[
            pl.BlockSpec(memory_space=pltpu.SMEM), by_row(model), *own_specs(own, others, span),
            *[full(x.shape) for x in sources], full(gain.shape), by_row(channels),
        ],
        out_specs=[
            by_row(model), full((model, 2 * channels)), by_row(channels), by_row(channels),
            pl.BlockSpec((TAIL, span), lambda i: (0, i)),
        ],
        out_shape=[
            jax.ShapeDtypeStruct((rows, model), bf16),
            jax.ShapeDtypeStruct((model, 2 * channels), bf16),
            jax.ShapeDtypeStruct((rows, channels), f32),
            jax.ShapeDtypeStruct((rows, channels), f32),
            jax.ShapeDtypeStruct((TAIL, rows), f32),
        ],
        compiler_params=pltpu.CompilerParams(
            dimension_semantics=("arbitrary",), vmem_limit_bytes=LIMIT
        ),
        name="gate_forward",
    )(spot, normed, own, *others, *sources, gain, ssm)


def norm_kernel(full_inner, chips, split, spot_ref, sums_ref, more_ref, gate_ref, grad_ref, ssm_ref,
                gain_ref, normed_ref, upstream_ref, gate_w_ref, out_w_ref, grad_gate_ref,
                grad_ssm_ref, gain_sum_ref, keep_ref, send_ref, mine_ref, theirs_ref, norm_sum_ref,
                scaled, totals):
    rows, channels = gate_ref.shape
    block = pl.program_id(0)

    @pl.when(block == 0)
    def _():
        gain_sum_ref[...] = jnp.zeros_like(gain_sum_ref)
        totals[...] = jnp.zeros_like(totals)

    sums = sums_ref[...] + more_ref[...] if split else sums_ref[...]
    sums = jnp.transpose(jnp.concatenate([sums, jnp.zeros((LANES - TAIL, rows), f32)], axis=0))
    scale = lax.rsqrt(sums[:, 0:1] / full_inner + EPSILON)
    pull = scale * scale * scale * (sums[:, 1:2] / full_inner)
    normed_t = jnp.transpose(normed_ref[...])
    upstream_t = jnp.transpose(upstream_ref[...])
    step = 2 * LANES
    for lo in range(0, channels, step):
        hi = lo + step
        gain = gain_ref[:, lo:hi]
        gate, grad, ssm = gate_ref[:, lo:hi], grad_ref[:, lo:hi], ssm_ref[:, lo:hi]
        sig = sigmoid(gate)
        silu = gate * sig
        gated = ssm * silu
        normal = gated * scale
        scaled_low = (normal * gain).astype(bf16)
        scaled[:, lo:hi] = scaled_low
        gain_sum_ref[TAIL - 1 : TAIL, lo:hi] += jnp.sum(grad * normal, axis=0, keepdims=True)
        grad_gated = scale * (grad * gain) - gated * pull
        grad_ssm_ref[:, lo:hi] = grad_gated * silu
        grad_gate = (grad_gated * ssm * (sig * (1.0 + gate * (1.0 - sig)))).astype(bf16)
        grad_gate_ref[:, lo:hi] = grad_gate
        totals[:, lo:hi] += mm(normed_t, grad_gate, NN)
        totals[:, channels + lo : channels + hi] += mm(upstream_t, scaled_low, NN)
    branch = mm(scaled[...], out_w_ref[...], NT).astype(bf16)
    if split:
        half = pl.num_programs(0) // 2
        at = pl.ds(pl.multiple_of(lax.rem(block, half) * rows, rows), rows)

        @pl.when(block // half == spot_ref[0, 0])
        def _():
            mine_ref[at, :] = branch

        @pl.when(block // half != spot_ref[0, 0])
        def _():
            theirs_ref[at, :] = branch
    else:
        mine_ref[pl.ds(pl.multiple_of(block * rows, rows), rows), :] = branch

        @pl.when(block == 0)
        def _():
            theirs_ref[...] = jnp.zeros_like(theirs_ref)

    @pl.when(block == pl.num_programs(0) - 1)
    def _():
        split_cores(spot_ref, totals, keep_ref, send_ref, chips)
        norm_sum_ref[...] = jnp.zeros_like(norm_sum_ref)
        norm_sum_ref[0:1, :] = gain_row(gate_w_ref, totals, (0, channels))


def gate_norm(
    spot, sums, more, gate, grad, ssm, gain, normed, upstream, weight, known, full_inner, chips, split, span
):
    rows, channels = gate.shape
    model = normed.shape[1]
    by_row = lambda cols: pl.BlockSpec((span, cols), lambda i: (i, 0))
    stats = pl.BlockSpec((TAIL, span), lambda i: (0, i))
    half = (model // 2, 2 * channels)
    mine = (rows // 2 if split else rows, model)
    theirs = (rows // 2 if split else TAIL * 2, model)
    return pl.pallas_call(
        partial(norm_kernel, float(full_inner), chips, split),
        grid=(rows // span,),
        in_specs=[
            pl.BlockSpec(memory_space=pltpu.SMEM), stats, stats, by_row(channels), by_row(channels),
            by_row(channels), full(gain.shape), by_row(model), by_row(model),
            pl.BlockSpec((model, channels), lambda i: (0, 0)),
            pl.BlockSpec((model, channels), lambda i: (0, 1)),
        ],
        out_specs=[
            by_row(channels), by_row(channels), full((TAIL, known)), full(half), full(half),
            full(mine), full(theirs), full((TAIL, model)),
        ],
        out_shape=[
            jax.ShapeDtypeStruct((rows, channels), bf16),
            jax.ShapeDtypeStruct((rows, channels), f32),
            jax.ShapeDtypeStruct((TAIL, known), f32),
            jax.ShapeDtypeStruct(half, bf16),
            jax.ShapeDtypeStruct(half, bf16),
            jax.ShapeDtypeStruct(mine, bf16),
            jax.ShapeDtypeStruct(theirs, bf16),
            jax.ShapeDtypeStruct((TAIL, model), f32),
        ],
        scratch_shapes=[
            pltpu.VMEM((span, channels), bf16),
            pltpu.VMEM((model, 2 * channels), f32),
        ],
        compiler_params=pltpu.CompilerParams(
            dimension_semantics=("arbitrary",), vmem_limit_bytes=LIMIT
        ),
        name="gate_norm",
    )(spot, sums, more, gate, grad, ssm, gain, normed, upstream, weight, weight)


def lanes_of(vector):
    return jnp.pad(vector, (0, LANES - vector.shape[0]))[None, :]


def spread_map(heads, channels):
    size = channels // heads
    row = lax.broadcasted_iota(jnp.int32, (2 * LANES, channels), 0) % LANES
    col = lax.broadcasted_iota(jnp.int32, (2 * LANES, channels), 1) // size
    return (row == col).astype(bf16)


def dp_send(value, bit):
    size = lax.axis_size("dp")
    return lax.ppermute(value, "dp", [(i, i ^ bit) for i in range(size)])


def chip_bits():
    return [4 * k for k in range(1, lax.axis_size("dp") // 4)]


def long_bits():
    bits, bit = [], 4
    while bit < lax.axis_size("dp"):
        bits.append(bit)
        bit *= 2
    return bits


def choose(stacked, index, axis):
    return lax.dynamic_index_in_dim(stacked, index, axis, keepdims=False)


def send_fold(parts, bit, axis):
    mine = (lax.axis_index("dp") // bit) % 2
    return dp_send(choose(parts, 1 - mine, axis), bit)


def keep_fold(parts, got, bit, axis):
    mine = (lax.axis_index("dp") // bit) % 2
    return choose(parts, mine, axis).astype(f32) + got.astype(f32)


def fold(parts, bit, axis):
    return keep_fold(parts, send_fold(parts, bit, axis), bit, axis)


def send_chips(parts):
    place = lax.axis_index("dp") // 4
    sends = parts.astype(bf16)
    return [dp_send(choose(sends, place ^ (bit // 4), 0), bit) for bit in chip_bits()]


def keep_chips(parts, got):
    total = choose(parts, lax.axis_index("dp") // 4, 0).astype(f32)
    for piece in got:
        total = total + piece.astype(f32)
    return total


def fold_chips(parts):
    return keep_chips(parts, send_chips(parts))


def tensor_swap(value):
    return lax.ppermute(value, "tensor", [(0, 1), (1, 0)])


def gather_other(own, size):
    if size != 2:
        return lax.all_gather(own, "tensor", axis=0, tiled=True)
    return tensor_swap(own)


def join_pieces(own, top, bottom, size):
    top = top.reshape(size, -1, own.shape[1])
    bottom = bottom.reshape(size, -1, own.shape[1])
    return jnp.concatenate([top, bottom], axis=1).reshape(-1, own.shape[1])


def pick_half(lower, upper, size):
    if size != 2:
        return lower
    return jnp.where(lax.axis_index("tensor") == 0, lower, upper)


def sum_quarters(quarters, other0, other1, size):
    if size != 2:
        whole = jnp.concatenate(quarters, axis=0)
        return lax.psum_scatter(whole, "tensor", scatter_dimension=0, tiled=True).astype(f32)
    first = lax.axis_index("tensor") == 0
    each = other0.shape[0]
    low, middle, high = quarters
    lower = jnp.concatenate([low, middle[:each]], axis=0)
    upper = jnp.concatenate([middle[each:], high], axis=0)
    others = jnp.concatenate([other0, other1], axis=0)
    return jnp.where(first, lower, upper).astype(f32) + others.astype(f32)


def tensor_sum(value, size):
    if size != 2:
        return lax.psum(value, "tensor")
    return value + tensor_swap(value)


def shards(
    tokens, lengths, norm_gain, zx_weight, bc_weight, dt_weight, conv_inner, bias_inner,
    conv_shared, bias_shared, step_bias, log_rate, skip_gain, gate_gain, out_weight, cotangent,
):
    size = lax.axis_size("tensor")
    split = size == 2
    me = lax.axis_index("dp")
    count = len(chip_bits()) + 1
    spot = jnp.stack([lax.axis_index("tensor"), me // 4, (me // 2) % 2, me % 2])[None, :]
    spot = spot.astype(jnp.int32)
    channels = zx_weight.shape[2]
    heads = step_bias.shape[0]
    width = bc_weight.shape[1]
    known = channels + width + LANES
    step_weight = jnp.pad(dt_weight, ((0, 0), (0, LANES - heads)))
    early = jnp.concatenate([zx_weight[:, 1, :], bc_weight, step_weight], axis=1)
    inputs = tokens.astype(f32)
    norm_scale = lax.rsqrt(jnp.mean(inputs * inputs, axis=1, keepdims=True) + EPSILON)
    normed_rows = (inputs * norm_scale * norm_gain[None, :]).astype(bf16)
    half = normed_rows.shape[0] // 2
    fixed = (
        conv_inner, bias_inner[None, :], conv_shared, bias_shared[None, :], lanes_of(step_bias),
        lanes_of(-jnp.exp(log_rate)), jnp.repeat(skip_gain, channels // heads)[None, :],
        spread_map(heads, channels),
    )
    late = jnp.concatenate([zx_weight[:, 0, :], out_weight], axis=1)
    zeros = (
        jnp.zeros((TAIL, channels), f32), jnp.zeros((TAIL, width), f32),
        jnp.zeros((width // 2, channels), f32),
    )

    def along(value):
        return [value] + [dp_send(value, bit) for bit in chip_bits()]

    column = jnp.concatenate(along(early), axis=0)
    column, pair, top, fixed, zeros, spot = lax.optimization_barrier((
        column, jnp.concatenate([late, dp_send(late, 2)], axis=0),
        gather_other(normed_rows[:half], size), fixed, zeros, spot,
    ))
    cut_late = (2 * channels * 3 // 8) // LANES * LANES
    joined = along(pair[:, :cut_late])
    by_x, column, bottom, joined, pair = lax.optimization_barrier(
        (dp_send(column, 2), column, gather_other(normed_rows[half:], size), joined, pair)
    )
    joined = jnp.concatenate(joined, axis=0)
    pairs = along(pair[:, cut_late:])
    by_core = dp_send(column, 1)
    sources = (column, by_x, by_core, dp_send(by_x, 1))
    own, others = normed_rows, (top, bottom)
    if not split:
        own, others = join_pieces(normed_rows, top, bottom, size), ()
    normed, weight, *saved = mixer_forward(
        spot, lengths, own, others, sources, count, *fixed, SPAN
    )
    _, _, _, _, _, rate, skip, spread = fixed
    gain = gate_gain[None, :]
    other, ssm, joined_core, pairs = lax.optimization_barrier(
        (gather_other(cotangent, size), saved[0], dp_send(joined, 1), pairs)
    )
    sources = (joined, joined_core, *pairs, *[dp_send(pair, 1) for pair in pairs])
    own, others = (cotangent, (other,)) if split else (other, ())
    upstream, weight_late, gate, grad, sums = gate_forward(
        spot, normed, own, others, sources, count, gain, ssm, SPAN
    )
    more = gather_other(sums, size) if split else sums
    sums = sums if split else lax.psum(sums, "tensor")
    chips = 2 * count
    grad_gate, grad_ssm, gain_sum, keep, send, branch_own, branch_send, norm_sum = gate_norm(
        spot, sums, more, gate, grad, ssm, gain, normed, upstream, weight_late, known, channels * size,
        chips, split, SPAN,
    )
    if split:
        branch_other = gather_other(branch_send, size)
    else:
        branch_own = lax.psum_scatter(branch_own, "tensor", scatter_dimension=0, tiled=True)
        branch_other = jnp.zeros_like(branch_own)
    quarter = grad_ssm.shape[0] // SPAN // 4
    carry = (gain_sum, *zeros)

    def back(begin, end, carry):
        return mixer_backward(
            lengths, grad_ssm, saved, conv_inner, conv_shared, rate, skip, spread, grad_gate,
            weight_late, weight, carry, (begin * quarter, end * quarter), SPAN,
        )

    first = dp_send(send, 1)
    grads3, terms3, carry = back(3, 4, carry)
    first = (keep.astype(f32) + first.astype(f32)).astype(bf16)
    first = first.reshape(count, 2, -1, first.shape[1])
    carry, first = lax.optimization_barrier((carry, first))
    first_gate, first_out = first[..., :channels], first[..., channels:]
    grads1, terms1, carry = back(1, 3, carry)
    first_gate = fold(first_gate, 2, 1)
    first_out = fold_chips(first_out).astype(bf16)
    each = terms3.shape[0]
    send1 = pick_half(terms3, terms1[:each], size)
    carry, send1, branch_other, first_gate, first_out = lax.optimization_barrier(
        (carry, send1, branch_other, first_gate, first_out)
    )
    other1 = gather_other(send1, size) if split else send1
    block_out = (inputs + (branch_own.astype(f32) + branch_other.astype(f32))).astype(bf16)
    part_gate = fold_chips(first_gate)
    part_out = fold(first_out, 2, 0)
    grads0, terms0, carry = back(0, 1, carry)
    send0 = pick_half(terms1[each:], terms0, size)
    sums, part_gate, part_out, grads0, other1, block_out, send0 = lax.optimization_barrier(
        (carry[0], part_gate, part_out, grads0, other1, block_out, send0)
    )
    other0 = gather_other(send0, size) if split else send0
    keep, send, sums = weight_products(
        spot, normed, weight, norm_gain[None, :], sums, norm_sum, (grads0, grads1, grads3), chips,
        (0, known), True,
    )
    each = send.shape[0] // 4
    got = [dp_send(send[i * each : (i + 1) * each], 1) for i in range(4)]
    *got, other0, sums, keep = lax.optimization_barrier((*got, other0, sums, keep))
    got = jnp.concatenate(got, axis=0)
    parts = (keep.astype(f32) + got.astype(f32)).astype(bf16).reshape(count, 2, -1, known)
    cut = min((known * 2 // 3) // LANES * LANES, channels)
    parts_a, parts_b = parts[..., :cut], parts[..., cut:]
    got_a = send_fold(parts_a, 2, 1)
    got_b = send_chips(parts_b)
    shared_sums = tensor_sum(sums[:, channels:], size)
    step_sums = sums[:, channels + width : known]
    sums = jnp.concatenate([sums[:, :channels], step_sums, shared_sums], axis=1)
    sums = sums + dp_send(sums, 1)
    sums = sums + dp_send(sums, 2)
    grad_normed = sum_quarters((terms0, terms1, terms3), other0, other1, size)
    scaled_grad = grad_normed * norm_gain[None, :]
    grad_inputs = norm_scale * scaled_grad - inputs * norm_scale**3 * jnp.mean(
        scaled_grad * inputs, axis=1, keepdims=True
    )
    grad_tokens = (cotangent.astype(f32) + grad_inputs).astype(bf16)
    got_a, got_b, sums, grad_tokens = lax.optimization_barrier((got_a, got_b, sums, grad_tokens))
    parts_a = keep_fold(parts_a, got_a, 2, 1)
    parts_b = keep_chips(parts_b, got_b).astype(bf16)
    got_a = send_chips(parts_a)
    parts_b = fold(parts_b, 2, 0)
    for bit in long_bits():
        sums = sums + dp_send(sums, bit)
    parts_a = keep_chips(parts_a, got_a)
    shared_sums = sums[:, channels + LANES :]
    norm_sum = shared_sums[0, known - channels :]
    part_inner = jnp.concatenate([parts_a, parts_b[:, : channels - cut]], axis=1)
    at_step = channels + width
    part_shared = tensor_sum(parts_b[:, channels - cut : at_step - cut], size)
    part_step = parts_b[:, at_step - cut : at_step - cut + heads]
    part_in = jnp.stack([part_gate, part_inner], axis=1)
    return (
        block_out,
        grad_tokens,
        norm_sum,
        part_in,
        part_shared,
        part_step,
        sums[:TAPS, :channels],
        sums[TAPS, :channels],
        shared_sums[:TAPS, :width],
        shared_sums[TAPS, :width],
        sums[0, channels : channels + heads],
        sums[1, channels : channels + heads],
        sums[2, channels : channels + heads],
        sums[TAIL - 1, :channels],
        part_out,
    )


def solution(mesh):
    return jax.shard_map(
        shards,
        mesh=mesh,
        in_specs=(
            P(("dp", "tensor"), None),
            P("dp", None),
            P(),
            P("dp", None, "tensor"),
            P("dp", None),
            P("dp", "tensor"),
            P(None, "tensor"),
            P("tensor"),
            P(),
            P(),
            P("tensor"),
            P("tensor"),
            P("tensor"),
            P("tensor"),
            P("dp", "tensor"),
            P(("dp", "tensor"), None),
        ),
        out_specs=(
            P(("dp", "tensor"), None),
            P(("dp", "tensor"), None),
            P(),
            P("dp", None, "tensor"),
            P("dp", None),
            P("dp", "tensor"),
            P(None, "tensor"),
            P("tensor"),
            P(),
            P(),
            P("tensor"),
            P("tensor"),
            P("tensor"),
            P("tensor"),
            P("dp", "tensor"),
        ),
        check_vma=False,
    )
```

```python
from functools import partial

import jax
import jax.numpy as jnp
from jax import lax
from jax.experimental import pallas as pl
from jax.experimental.pallas import tpu as pltpu
from jax.sharding import PartitionSpec as P

EPSILON = 1e-05
SPAN = 256
LANES = 128
TAIL = 8
TAPS = 4
MASKED = -1e30
f32 = jnp.float32
bf16 = jnp.bfloat16
LIMIT = 60 * 1024 * 1024


def mm(left, right, dims):
    return lax.dot_general(left, right, ((dims[0], dims[1]), ((), ())), preferred_element_type=f32)


NN = ((1,), (0,))
NT = ((1,), (1,))
TN = ((0,), (0,))


def halves(value, axis):
    high = value.astype(bf16)
    low = (value - high.astype(f32)).astype(bf16)
    return jnp.concatenate([high, low], axis=axis)


def sigmoid(value):
    return 1.0 / (1.0 + jnp.exp(-value))


def softplus(value):
    return jnp.maximum(value, 0.0) + jnp.log1p(jnp.exp(-jnp.abs(value)))


def segment_at(ends, position):
    total = jnp.zeros(position.shape, jnp.int32)
    for end in ends:
        total = total + (position >= end).astype(jnp.int32)
    return total


def sequence_ends(lengths_ref):
    ends, total = [], 0
    for i in range(lengths_ref.shape[1]):
        total = total + lengths_ref[0, i]
        ends.append(total)
    return ends


def step_parts(step_raw, rate, ends, base):
    rows = step_raw.shape[0]
    step = softplus(step_raw)
    row = lax.broadcasted_iota(jnp.int32, (rows, rows), 0)
    col = lax.broadcasted_iota(jnp.int32, (rows, rows), 1)
    lower = (row >= col).astype(f32).astype(bf16)
    split = mm(lower, halves(step * rate, 1), NN)
    running = split[:, :LANES] + split[:, LANES:]
    position = base + lax.broadcasted_iota(jnp.int32, (rows, 1), 0)
    segment = segment_at(ends, position)
    before = segment_at(ends, jnp.full((1, 1), base - 1, jnp.int32))
    last = segment_at(ends, jnp.full((1, 1), base + rows - 1, jnp.int32))
    carried = ((segment == before) & (position >= rows)).astype(f32)
    matched = (segment == last).astype(f32)
    entry = jnp.exp(running) * carried
    leave = jnp.exp(running[rows - 1 :, :] - running) * matched
    return step, running, entry, leave, lower, segment, row, col


def same_rows(ends, base, rows):
    across = segment_at(ends, base + lax.broadcasted_iota(jnp.int32, (1, rows), 1))
    down = segment_at(ends, base + lax.broadcasted_iota(jnp.int32, (rows, 1), 0))
    return down == across


def rows_of(block, blocks, spot_ref, own_ref, others):
    if not others:
        return own_ref[...]
    half = blocks // 2
    local = lax.rem(block, half)
    span = own_ref.shape[0] // half
    each = half // len(others)
    value = None
    for i, ref in enumerate(others):
        at = lax.rem(local, each) * span
        piece = ref[pl.ds(pl.multiple_of(at, span), span), :]
        value = piece if i == 0 else jnp.where(local >= i * each, piece, value)
    mine = own_ref[pl.ds(pl.multiple_of(local * span, span), span), :]
    return jnp.where(block // half == spot_ref[0, 0], mine, value)


def own_specs(own, others, span):
    if not others:
        return [pl.BlockSpec((span, own.shape[1]), lambda i: (i, 0))]
    return [full(own.shape), *[full(other.shape) for other in others]]


def run_copies(copies):
    for copy in copies:
        copy.start()
    for copy in copies:
        copy.wait()


def place_weights(spot_ref, weight_ref, sources, count, done):
    rows = weight_ref.shape[0] // (4 * count)
    copies = []
    for i, ref in enumerate(sources):
        along = spot_ref[0, 2] ^ (i % 2)
        core = spot_ref[0, 3] ^ (i // 2)
        for k in range(count):
            at = (((spot_ref[0, 1] ^ k) * 2 + along) * 2 + core) * rows
            copies.append(pltpu.make_async_copy(
                ref.at[pl.ds(k * rows, rows), :],
                weight_ref.at[pl.ds(pl.multiple_of(at, rows), rows), :],
                done.at[i * count + k],
            ))
    run_copies(copies)


def place_pairs(spot_ref, weight_ref, sources, count, lo):
    rows = weight_ref.shape[0] // (4 * count)
    for i, (ref, begin) in enumerate(sources):
        core = spot_ref[0, 3] ^ (i // count)
        for j in range(2):
            at = (((spot_ref[0, 1] ^ (i % count)) * 2 + (spot_ref[0, 2] ^ j)) * 2 + core) * rows
            at = pl.ds(pl.multiple_of(at, rows), rows)
            here = begin + j * rows
            weight_ref[at, lo : lo + ref.shape[1]] = ref[here : here + rows, :]


def split_cores(spot_ref, value_ref, keep_ref, send_refs, chips):
    rows = keep_ref.shape[0] // chips
    each = chips // len(send_refs)
    core = spot_ref[0, 3]
    for chip in range(chips):
        here = pl.ds(pl.multiple_of((2 * chip + core) * rows, rows), rows)
        there = pl.ds(pl.multiple_of((2 * chip + 1 - core) * rows, rows), rows)
        keep_ref[chip * rows : (chip + 1) * rows, :] = value_ref[here, :].astype(bf16)
        at = (chip % each) * rows
        send_refs[chip // each][at : at + rows, :] = value_ref[there, :].astype(bf16)


def forward_kernel(
    pieces, count, spot_ref, lengths_ref, *refs
):
    own_ref, others = refs[0], refs[1:pieces]
    sources = refs[pieces : pieces + 4]
    (
        conv_inner_ref, bias_inner_ref, conv_shared_ref, bias_shared_ref, step_bias_ref, rate_ref,
        skip_ref, spread_ref, normed_ref, weight_ref, ssm_ref, inner_ref, pre_inner_ref, shared_ref,
        pre_shared_ref, step_ref, entering_ref, inner_tail, shared_tail, state, done,
    ) = refs[pieces + 4 :]
    block = pl.program_id(0)
    rows = normed_ref.shape[0]
    channels = conv_inner_ref.shape[1]
    base = block * rows
    ends = sequence_ends(lengths_ref)

    @pl.when(block == 0)
    def _():
        inner_tail[0:TAIL, :] = jnp.zeros((TAIL, channels), f32)
        shared_tail[0:TAIL, :] = jnp.zeros((TAIL, shared_tail.shape[1]), f32)
        state[...] = jnp.zeros_like(state)
        place_weights(spot_ref, weight_ref, sources, count, done)

    @pl.when(block > 0)
    def _():
        inner_tail[0:TAIL, :] = inner_tail[rows : rows + TAIL, :]
        shared_tail[0:TAIL, :] = shared_tail[rows : rows + TAIL, :]

    normed = rows_of(block, pl.num_programs(0), spot_ref, own_ref, others)
    normed_ref[...] = normed
    small = mm(normed, weight_ref[:, channels:], NN)
    width = conv_shared_ref.shape[1]
    shared_proj = small[:, :width]
    shared_tail[TAIL : TAIL + rows, :] = shared_proj
    shared_ref[...] = shared_proj
    step_raw = small[:, width:] + step_bias_ref[...]
    step_ref[...] = step_raw
    inner_proj = mm(normed, weight_ref[:, :channels], NN)
    inner_tail[TAIL : TAIL + rows, :] = inner_proj
    inner_ref[...] = inner_proj

    step, running, entry, leave, lower, segment, row, col = step_parts(
        step_raw, rate_ref[...], ends, base
    )
    position = base + lax.broadcasted_iota(jnp.int32, (rows, 1), 0)
    keeps = [
        ((segment_at(ends, position - k) == segment) & (position >= k)).astype(f32)
        for k in range(1, TAPS)
    ]
    keeps = [jnp.broadcast_to(keep, (rows, LANES)) for keep in keeps]

    def conv(tail, taps_ref, bias_ref, lo, hi):
        total = bias_ref[:, lo:hi] + taps_ref[TAPS - 1 : TAPS, lo:hi] * tail[TAIL : TAIL + rows, lo:hi]
        for k in range(1, TAPS):
            shifted = tail[TAIL - k : TAIL - k + rows, lo:hi]
            total = total + taps_ref[TAPS - 1 - k : TAPS - k, lo:hi] * (shifted * keeps[k - 1])
        return total

    pre_shared = jnp.concatenate(
        [
            conv(shared_tail, conv_shared_ref, bias_shared_ref, lo, lo + LANES)
            for lo in range(0, width, LANES)
        ],
        axis=1,
    )
    pre_shared_ref[...] = pre_shared
    shared = pre_shared * sigmoid(pre_shared)
    in_map = shared[:, : width // 2].astype(bf16)
    out_map = shared[:, width // 2 :].astype(bf16)
    scores = mm(out_map, in_map, NT)
    allowed = jnp.where((row >= col) & same_rows(ends, base, rows), 0.0, MASKED)
    running_t = jnp.transpose(running)
    step2, entry2, leave2 = halves(step, 1), halves(entry, 1), halves(leave, 1)
    lane = lax.broadcasted_iota(jnp.int32, (rows, LANES), 1)
    for pair in range(channels // LANES):
        lo, hi = pair * LANES, (pair + 1) * LANES
        pre = conv(inner_tail, conv_inner_ref, bias_inner_ref, lo, hi)
        pre_inner_ref[:, lo:hi] = pre
        head_in = pre * sigmoid(pre)
        side = (pair % 2) * LANES
        if side == 0:
            spread = spread_ref[:, lo : min(lo + 2 * LANES, channels)]
            wide = [mm(value, spread, NN) for value in (step2, entry2, leave2)]
        step_wide, entry_wide, leave_wide = [x[:, side : side + LANES] for x in wide]
        scaled = head_in * step_wide
        scaled_low = scaled.astype(bf16)
        held = state[:, lo:hi]
        entering_ref[0, :, lo:hi] = held
        carried_out = mm(out_map, held.astype(bf16), NN) * entry_wide
        parts = []
        for parity in range(2):
            head = 2 * pair + parity
            gap = running[:, head : head + 1] - running_t[head : head + 1, :]
            mixed = (scores * jnp.exp(gap + allowed)).astype(bf16)
            parts.append(mm(mixed, scaled_low, NN))
        intra = jnp.where(lane < LANES // 2, parts[0], parts[1])
        ssm_ref[:, lo:hi] = carried_out + intra + skip_ref[:, lo:hi] * head_in
        added = mm(in_map, (scaled * leave_wide).astype(bf16), TN)
        state[:, lo:hi] = held * entry_wide[rows - 1 :, :] + added


def full(shape):
    return pl.BlockSpec(shape, lambda *_: (0,) * len(shape))


def mixer_forward(
    spot, lengths, own, others, sources, count, conv_inner, bias_inner, conv_shared, bias_shared,
    step_bias, rate, skip, spread, span,
):
    rows = own.shape[0] * (2 if others else 1)
    model = own.shape[1]
    channels = conv_inner.shape[1]
    width = conv_shared.shape[1]
    known = channels + width + LANES
    blocks = rows // span
    by_row = lambda cols: pl.BlockSpec((span, cols), lambda i: (i, 0))
    shape = lambda cols: jax.ShapeDtypeStruct((rows, cols), f32)
    states = width // 2
    smem = pl.BlockSpec(memory_space=pltpu.SMEM)
    fixed = (conv_inner, bias_inner, conv_shared, bias_shared, step_bias, rate, skip, spread)
    return pl.pallas_call(
        partial(forward_kernel, 1 + len(others), count),
        grid=(blocks,),
        in_specs=[
            smem, smem, *own_specs(own, others, span),
            *[pl.BlockSpec(memory_space=pl.ANY) for _ in sources],
            *[full(x.shape) for x in fixed],
        ],
        out_specs=[
            by_row(model), full((model, known)), by_row(channels), by_row(channels),
            by_row(channels), by_row(width), by_row(width), by_row(LANES),
            pl.BlockSpec((1, states, channels), lambda i: (i, 0, 0)),
        ],
        out_shape=[
            jax.ShapeDtypeStruct((rows, model), bf16), jax.ShapeDtypeStruct((model, known), bf16),
            shape(channels), shape(channels), shape(channels), shape(width), shape(width),
            shape(LANES), jax.ShapeDtypeStruct((blocks, states, channels), f32),
        ],
        scratch_shapes=[
            pltpu.VMEM((TAIL + span, channels), f32),
            pltpu.VMEM((TAIL + span, width), f32),
            pltpu.VMEM((states, channels), f32),
            pltpu.SemaphoreType.DMA((4 * count,)),
        ],
        compiler_params=pltpu.CompilerParams(
            dimension_semantics=("arbitrary",), vmem_limit_bytes=LIMIT
        ),
        name="mixer_forward",
    )(spot, lengths, own, *others, *sources, *fixed)


def backward_kernel(
    first_block, total_rows, lengths_ref, upstream_ref, ssm_ref, inner_ref, pre_inner_ref, shared_ref, pre_shared_ref,
    step_ref, entering_ref, conv_inner_ref, conv_shared_ref, rate_ref, skip_ref, spread_ref,
    grad_gate_ref, gate_w_ref, weight_ref, sums_in_ref, inner_in_ref, shared_in_ref, adjoint_in_ref,
    grads_ref, terms_ref, sums_ref, inner_out_ref, shared_out_ref, adjoint, inner_head, shared_head,
    gate_w, weight, done,
):
    turn = pl.program_id(0)
    block = first_block + pl.num_programs(0) - 1 - turn
    rows, channels = upstream_ref.shape
    width = conv_shared_ref.shape[1]
    base = block * rows
    ends = sequence_ends(lengths_ref)

    def weight_copies():
        return (
            pltpu.make_async_copy(gate_w_ref.at[:, pl.ds(0, channels)], gate_w, done.at[0]),
            pltpu.make_async_copy(weight_ref, weight, done.at[1]),
        )

    @pl.when(turn == 0)
    def _():
        inner_head[rows : rows + TAIL, :] = inner_in_ref[...]
        shared_head[rows : rows + TAIL, :] = shared_in_ref[...]
        adjoint[...] = adjoint_in_ref[...]
        sums_ref[...] = sums_in_ref[...]
        for copy in weight_copies():
            copy.start()

    @pl.when(turn > 0)
    def _():
        inner_head[rows : rows + TAIL, :] = inner_head[0:TAIL, :]
        shared_head[rows : rows + TAIL, :] = shared_head[0:TAIL, :]

    step_raw = step_ref[...]
    rate = rate_ref[...]
    step, running, entry, leave, lower, segment, row, col = step_parts(step_raw, rate, ends, base)
    position = base + lax.broadcasted_iota(jnp.int32, (rows, 1), 0)
    keeps = [
        ((segment_at(ends, position + k) == segment) & (position + k < total_rows)).astype(f32)
        for k in range(1, TAPS)
    ]
    keeps = [jnp.broadcast_to(keep, (rows, LANES)) for keep in keeps]
    pre_shared = pre_shared_ref[...]
    shared_gate = sigmoid(pre_shared)
    shared = pre_shared * shared_gate
    half = width // 2
    in_map = shared[:, :half].astype(bf16)
    out_map = shared[:, half:].astype(bf16)
    scores_t = mm(in_map, out_map, NT)
    allowed_t = jnp.where((col >= row) & same_rows(ends, base, rows), 0.0, MASKED)
    running_t = jnp.transpose(running)
    step2, entry2, leave2 = halves(step, 1), halves(entry, 1), halves(leave, 1)
    lane = lax.broadcasted_iota(jnp.int32, (rows, LANES), 1)
    first_half = lane < LANES // 2
    grad_scores_t = jnp.zeros((rows, rows), f32)
    grad_in = jnp.zeros((rows, half), f32)
    grad_out = jnp.zeros((rows, half), f32)
    by_head = jnp.zeros((rows, LANES), f32)
    step_terms = jnp.zeros((rows, LANES), f32)
    leaving = jnp.zeros((TAIL, LANES), f32)
    for pair in range(channels // LANES):
        lo, hi = pair * LANES, (pair + 1) * LANES
        side = (pair % 2) * LANES
        if side == 0:
            spread = spread_ref[:, lo : min(lo + 2 * LANES, channels)]
            wide = [mm(value, spread, NN) for value in (step2, entry2, leave2)]
            products = []
        step_wide, entry_wide, leave_wide = [x[:, side : side + LANES] for x in wide]
        pre = pre_inner_ref[:, lo:hi]
        gate = sigmoid(pre)
        head_in = pre * gate
        skip = skip_ref[:, lo:hi]
        upstream = upstream_ref[:, lo:hi]
        upstream_low = upstream.astype(bf16)
        upstream_back = upstream_low.astype(f32)
        scaled = head_in * step_wide
        scaled_low = scaled.astype(bf16)
        scaled_back = scaled_low.astype(f32)
        held = entering_ref[0, :, lo:hi]
        held_low = held.astype(bf16)
        ahead = adjoint[:, lo:hi]
        ahead_low = ahead.astype(bf16)
        entry_up = (upstream_back * entry_wide).astype(bf16)
        grad_out = grad_out + mm(entry_up, held_low, NT)
        grad_in = grad_in + mm((scaled * leave_wide).astype(bf16), ahead_low, NT)
        grad_scaled = mm(in_map, ahead_low, NN) * leave_wide
        through = entry_wide[rows - 1 :, :]
        tail_terms = jnp.sum(scaled_back * grad_scaled, axis=0, keepdims=True) + through * jnp.sum(
            ahead * held, axis=0, keepdims=True
        )
        adjoint[:, lo:hi] = ahead * through + mm(out_map, entry_up, TN)
        parts = []
        for parity in range(2):
            head = 2 * pair + parity
            gap = running_t[head : head + 1, :] - running[:, head : head + 1]
            decay = jnp.exp(gap + allowed_t)
            mixed = (scores_t * decay).astype(bf16)
            parts.append(mm(mixed, upstream_low, NN))
            mine = first_half if parity == 0 else jnp.logical_not(first_half)
            chosen = jnp.where(mine, scaled_back, 0.0).astype(bf16)
            grad_scores_t = grad_scores_t + mm(chosen, upstream_low, NT) * decay
        grad_scaled = grad_scaled + jnp.where(first_half, parts[0], parts[1])
        spread_one = spread[:LANES, side : side + LANES]
        spread_both = jnp.concatenate([spread_one, spread_one], axis=1)
        balance = upstream_back * (ssm_ref[:, lo:hi] - skip * head_in) - scaled_back * grad_scaled
        by_head = by_head + mm(halves(balance, 1), spread_both, NT)
        products.append((head_in * grad_scaled).astype(bf16))
        if hi == channels or side > 0:
            joined = jnp.concatenate(products, axis=1)
            step_terms = step_terms + mm(joined, spread[:LANES, :], NT)
        skip_terms = jnp.sum(upstream * head_in, axis=0, keepdims=True)
        edge = jnp.concatenate([tail_terms, skip_terms, jnp.zeros((TAIL - 2, LANES), f32)], axis=0)
        leaving = leaving + mm(halves(edge, 1), spread_both, NT)
        grad_pre = (grad_scaled * step_wide + skip * upstream) * (gate * (1.0 + pre * (1.0 - gate)))
        inner_head[0:rows, lo:hi] = grad_pre
        inner_proj = inner_ref[:, lo:hi]
        grad_proj = conv_inner_ref[TAPS - 1 : TAPS, lo:hi] * grad_pre
        sums = [None] * TAPS
        sums[TAPS - 1] = jnp.sum(grad_pre * inner_proj, axis=0, keepdims=True)
        for k in range(1, TAPS):
            moved = inner_head[k : k + rows, lo:hi] * keeps[k - 1]
            grad_proj = grad_proj + conv_inner_ref[TAPS - 1 - k : TAPS - k, lo:hi] * moved
            sums[TAPS - 1 - k] = jnp.sum(moved * inner_proj, axis=0, keepdims=True)
        grads_ref[:, lo:hi] = grad_proj.astype(bf16)
        sums.append(jnp.sum(grad_pre, axis=0, keepdims=True))
        sums.append(jnp.zeros((TAIL - len(sums), LANES), f32))
        sums_ref[:, lo:hi] += jnp.concatenate(sums, axis=0)
    grad_scores_low = grad_scores_t.astype(bf16)
    grad_out = grad_out + mm(grad_scores_low, in_map, TN)
    grad_in = grad_in + mm(grad_scores_low, out_map, NN)
    grad_shared = jnp.concatenate([grad_in, grad_out], axis=1)
    grad_pre = grad_shared * (shared_gate * (1.0 + pre_shared * (1.0 - shared_gate)))
    shared_head[0:rows, :] = grad_pre
    shared_proj = shared_ref[...]
    grad_proj = conv_shared_ref[TAPS - 1 : TAPS, :] * grad_pre
    sums = [None] * TAPS
    sums[TAPS - 1] = jnp.sum(grad_pre * shared_proj, axis=0, keepdims=True)
    for k in range(1, TAPS):
        keep = jnp.concatenate([keeps[k - 1]] * (width // LANES), axis=1)
        moved = shared_head[k : k + rows, :] * keep
        grad_proj = grad_proj + conv_shared_ref[TAPS - 1 - k : TAPS - k, :] * moved
        sums[TAPS - 1 - k] = jnp.sum(moved * shared_proj, axis=0, keepdims=True)
    sums.append(jnp.sum(grad_pre, axis=0, keepdims=True))
    sums.append(jnp.zeros((TAIL - len(sums), width), f32))
    sums_ref[:, channels : channels + width] += jnp.concatenate(sums, axis=0)
    split = mm(lower, halves(by_head, 1), TN)
    grad_log = split[:, :LANES] + split[:, LANES:] + leaving[0:1, :]
    grad_step = (step_terms + rate * grad_log) * sigmoid(step_raw)
    grads_ref[:, channels : channels + width] = grad_proj.astype(bf16)
    grads_ref[:, channels + width :] = grad_step.astype(bf16)

    @pl.when(turn == 0)
    def _():
        for copy in weight_copies():
            copy.wait()

    terms = mm(grad_gate_ref[...], gate_w[...], NT) + mm(grads_ref[...], weight[...], NT)
    terms_ref[...] = terms.astype(bf16)
    sums_ref[:, channels + width :] += jnp.concatenate(
        [
            jnp.sum(grad_step, axis=0, keepdims=True),
            rate * jnp.sum(step * grad_log, axis=0, keepdims=True),
            leaving[1:2, :],
            jnp.zeros((TAIL - 3, LANES), f32),
        ],
        axis=0,
    )

    @pl.when(turn == pl.num_programs(0) - 1)
    def _():
        inner_out_ref[...] = inner_head[0:TAIL, :]
        shared_out_ref[...] = shared_head[0:TAIL, :]


def mixer_backward(
    lengths, upstream, saved, conv_inner, conv_shared, rate, skip, spread, grad_gate, weight_late,
    weight, carry, blocks, span
):
    ssm, inner, pre_inner, shared, pre_shared, step_raw, entering = saved
    rows, channels = upstream.shape
    width = conv_shared.shape[1]
    states = width // 2
    begin, end = blocks
    known = channels + width + LANES
    model = weight.shape[0]
    by_row = lambda cols: pl.BlockSpec((span, cols), lambda i: (end - 1 - i, 0))
    small = ((TAIL, known), (TAIL, channels), (TAIL, width), (states, channels))
    results = pl.pallas_call(
        partial(backward_kernel, begin, rows),
        grid=(end - begin,),
        in_specs=[
            pl.BlockSpec(memory_space=pltpu.SMEM),
            by_row(channels), by_row(channels), by_row(channels), by_row(channels),
            by_row(width), by_row(width), by_row(LANES),
            pl.BlockSpec((1, states, channels), lambda i: (end - 1 - i, 0, 0)),
            full(conv_inner.shape),
            full(conv_shared.shape),
            full(rate.shape),
            full(skip.shape),
            full(spread.shape),
            by_row(channels),
            pl.BlockSpec(memory_space=pl.ANY),
            pl.BlockSpec(memory_space=pl.ANY),
            *[full(shape) for shape in small],
        ],
        out_specs=[
            pl.BlockSpec((span, known), lambda i: (end - begin - 1 - i, 0)),
            pl.BlockSpec((span, model), lambda i: (end - begin - 1 - i, 0)),
            *[full(shape) for shape in small],
        ],
        out_shape=[
            jax.ShapeDtypeStruct(((end - begin) * span, known), bf16),
            jax.ShapeDtypeStruct(((end - begin) * span, model), bf16),
            *[jax.ShapeDtypeStruct(shape, f32) for shape in small],
        ],
        scratch_shapes=[
            pltpu.VMEM((TAIL + span, channels), f32),
            pltpu.VMEM((TAIL + span, width), f32),
            pltpu.VMEM((model, channels), bf16),
            pltpu.VMEM((model, known), bf16),
            pltpu.SemaphoreType.DMA((2,)),
        ],
        compiler_params=pltpu.CompilerParams(
            dimension_semantics=("arbitrary",), vmem_limit_bytes=LIMIT
        ),
        name="mixer_backward",
    )(
        lengths, upstream, ssm, inner, pre_inner, shared, pre_shared, step_raw, entering,
        conv_inner, conv_shared, rate, skip, spread, grad_gate, weight_late, weight, *carry,
    )
    return results[0], results[1], tuple(results[2:])


def gain_row(weight_ref, total_ref, columns):
    rows = weight_ref.shape[0]
    begin, end = columns
    added = jnp.zeros((rows, LANES), f32)
    for lo in range(begin, end, LANES):
        weight = weight_ref[:, lo : lo + LANES].astype(f32)
        added = added + weight * total_ref[:, lo - begin : lo - begin + LANES]
    return jnp.sum(jnp.transpose(added), axis=0, keepdims=True)


def product_kernel(chips, columns, last, spot_ref, normed_ref, weight_ref, gain_ref, sums_ref,
                   norm_sum_ref, *refs):
    grads, (keep_ref, *send_refs, packed_ref, total) = refs[:-7], refs[-7:]
    lo, hi = columns
    at = 0
    for i, ref in enumerate(grads):
        rows = ref.shape[0]
        added = mm(normed_ref[at : at + rows, :], ref[:, lo:hi], TN)
        total[...] = added if i == 0 else total[...] + added
        at += rows
    split_cores(spot_ref, total, keep_ref, send_refs, chips)
    row = norm_sum_ref[0:1, :] + gain_row(weight_ref, total, columns)
    known = sums_ref.shape[1]
    if last:
        packed_ref[:, :known] = sums_ref[...]
        packed_ref[:, known:] = jnp.broadcast_to(row / gain_ref[...], norm_sum_ref.shape)
    else:
        packed_ref[...] = jnp.broadcast_to(row, norm_sum_ref.shape)


def weight_products(spot, normed, weight, gain, sums, norm_sum, grads, chips, columns, last):
    known = grads[0].shape[1]
    model = normed.shape[1]
    size = columns[1] - columns[0]
    part = jax.ShapeDtypeStruct((model // 2, size), bf16)
    piece = jax.ShapeDtypeStruct((model // 8, size), bf16)
    vmem = pl.BlockSpec(memory_space=pltpu.VMEM)
    return pl.pallas_call(
        partial(product_kernel, chips, columns, last),
        in_specs=[pl.BlockSpec(memory_space=pltpu.SMEM), *[vmem for _ in range(5 + len(grads))]],
        out_specs=[vmem] * 6,
        out_shape=[
            part, *[piece] * 4, jax.ShapeDtypeStruct((TAIL, known + model if last else model), f32),
        ],
        scratch_shapes=[pltpu.VMEM((model, size), f32)],
        compiler_params=pltpu.CompilerParams(vmem_limit_bytes=LIMIT),
        name="weight_products",
    )(spot, normed, weight, gain, sums, norm_sum, *grads)


def gate_kernel(pieces, count, spot_ref, normed_ref, *refs):
    own_ref, others = refs[0], refs[1:pieces]
    joined, sources = refs[pieces : pieces + 2], refs[pieces + 2 : pieces + 2 + 2 * count]
    (
        gain_ref, ssm_ref, upstream_ref, weight_ref, gate_ref, grad_ref, sums_ref
    ) = refs[pieces + 2 + 2 * count :]

    @pl.when(pl.program_id(0) == 0)
    def _():
        each = joined[0].shape[0] // count
        rows = [(ref, k * each) for ref in joined for k in range(count)]
        place_pairs(spot_ref, weight_ref, rows, count, 0)
        place_pairs(spot_ref, weight_ref, [(ref, 0) for ref in sources], count, joined[0].shape[1])

    rows, channels = ssm_ref.shape
    normed = normed_ref[...]
    upstream = rows_of(pl.program_id(0), pl.num_programs(0), spot_ref, own_ref, others)
    upstream_ref[...] = upstream
    square = jnp.zeros((rows, LANES), f32)
    cross = jnp.zeros((rows, LANES), f32)
    step = 2 * LANES
    for lo in range(0, channels, step):
        hi = lo + step
        gate = mm(normed, weight_ref[:, lo:hi], NN)
        grad = mm(upstream, weight_ref[:, channels + lo : channels + hi], NN)
        gate_ref[:, lo:hi] = gate
        grad_ref[:, lo:hi] = grad
        gated = ssm_ref[:, lo:hi] * (gate * sigmoid(gate))
        squares = gated * gated
        crosses = grad * gain_ref[:, lo:hi] * gated
        square = square + (squares[:, :LANES] + squares[:, LANES:])
        cross = cross + (crosses[:, :LANES] + crosses[:, LANES:])
    square = jnp.sum(square, axis=1, keepdims=True)
    cross = jnp.sum(cross, axis=1, keepdims=True)
    lane = lax.broadcasted_iota(jnp.int32, (rows, LANES), 1)
    both = jnp.where(lane == 0, square, jnp.where(lane == 1, cross, 0.0))
    sums_ref[...] = jnp.transpose(both)[0:TAIL, :]


def gate_forward(spot, normed, own, others, sources, count, gain, ssm, span):
    rows, model = normed.shape
    channels = ssm.shape[1]
    by_row = lambda cols: pl.BlockSpec((span, cols), lambda i: (i, 0))
    return pl.pallas_call(
        partial(gate_kernel, 1 + len(others), count),
        grid=(rows // span,),
        in_specs=[
            pl.BlockSpec(memory_space=pltpu.SMEM), by_row(model), *own_specs(own, others, span),
            *[full(x.shape) for x in sources], full(gain.shape), by_row(channels),
        ],
        out_specs=[
            by_row(model), full((model, 2 * channels)), by_row(channels), by_row(channels),
            pl.BlockSpec((TAIL, span), lambda i: (0, i)),
        ],
        out_shape=[
            jax.ShapeDtypeStruct((rows, model), bf16),
            jax.ShapeDtypeStruct((model, 2 * channels), bf16),
            jax.ShapeDtypeStruct((rows, channels), f32),
            jax.ShapeDtypeStruct((rows, channels), f32),
            jax.ShapeDtypeStruct((TAIL, rows), f32),
        ],
        compiler_params=pltpu.CompilerParams(
            dimension_semantics=("arbitrary",), vmem_limit_bytes=LIMIT
        ),
        name="gate_forward",
    )(spot, normed, own, *others, *sources, gain, ssm)


def norm_kernel(full_inner, chips, split, spot_ref, sums_ref, more_ref, gate_ref, grad_ref, ssm_ref,
                gain_ref, normed_ref, upstream_ref, gate_w_ref, out_w_ref, grad_gate_ref,
                grad_ssm_ref, gain_sum_ref, keep_ref, send_ref, mine_ref, theirs_ref, norm_sum_ref,
                scaled, totals):
    rows, channels = gate_ref.shape
    block = pl.program_id(0)

    @pl.when(block == 0)
    def _():
        gain_sum_ref[...] = jnp.zeros_like(gain_sum_ref)
        totals[...] = jnp.zeros_like(totals)

    sums = sums_ref[...] + more_ref[...] if split else sums_ref[...]
    sums = jnp.transpose(jnp.concatenate([sums, jnp.zeros((LANES - TAIL, rows), f32)], axis=0))
    scale = lax.rsqrt(sums[:, 0:1] / full_inner + EPSILON)
    pull = scale * scale * scale * (sums[:, 1:2] / full_inner)
    normed_t = jnp.transpose(normed_ref[...])
    upstream_t = jnp.transpose(upstream_ref[...])
    step = 2 * LANES
    for lo in range(0, channels, step):
        hi = lo + step
        gain = gain_ref[:, lo:hi]
        gate, grad, ssm = gate_ref[:, lo:hi], grad_ref[:, lo:hi], ssm_ref[:, lo:hi]
        sig = sigmoid(gate)
        silu = gate * sig
        gated = ssm * silu
        normal = gated * scale
        scaled_low = (normal * gain).astype(bf16)
        scaled[:, lo:hi] = scaled_low
        gain_sum_ref[TAIL - 1 : TAIL, lo:hi] += jnp.sum(grad * normal, axis=0, keepdims=True)
        grad_gated = scale * (grad * gain) - gated * pull
        grad_ssm_ref[:, lo:hi] = grad_gated * silu
        grad_gate = (grad_gated * ssm * (sig * (1.0 + gate * (1.0 - sig)))).astype(bf16)
        grad_gate_ref[:, lo:hi] = grad_gate
        totals[:, lo:hi] += mm(normed_t, grad_gate, NN)
        totals[:, channels + lo : channels + hi] += mm(upstream_t, scaled_low, NN)
    branch = mm(scaled[...], out_w_ref[...], NT).astype(bf16)
    if split:
        half = pl.num_programs(0) // 2
        at = pl.ds(pl.multiple_of(lax.rem(block, half) * rows, rows), rows)

        @pl.when(block // half == spot_ref[0, 0])
        def _():
            mine_ref[at, :] = branch

        @pl.when(block // half != spot_ref[0, 0])
        def _():
            theirs_ref[at, :] = branch
    else:
        mine_ref[pl.ds(pl.multiple_of(block * rows, rows), rows), :] = branch

        @pl.when(block == 0)
        def _():
            theirs_ref[...] = jnp.zeros_like(theirs_ref)

    @pl.when(block == pl.num_programs(0) - 1)
    def _():
        split_cores(spot_ref, totals, keep_ref, [send_ref], chips)
        norm_sum_ref[...] = jnp.zeros_like(norm_sum_ref)
        norm_sum_ref[0:1, :] = gain_row(gate_w_ref, totals, (0, channels))


def gate_norm(
    spot, sums, more, gate, grad, ssm, gain, normed, upstream, weight, known, full_inner, chips, split, span
):
    rows, channels = gate.shape
    model = normed.shape[1]
    by_row = lambda cols: pl.BlockSpec((span, cols), lambda i: (i, 0))
    stats = pl.BlockSpec((TAIL, span), lambda i: (0, i))
    half = (model // 2, 2 * channels)
    mine = (rows // 2 if split else rows, model)
    theirs = (rows // 2 if split else TAIL * 2, model)
    return pl.pallas_call(
        partial(norm_kernel, float(full_inner), chips, split),
        grid=(rows // span,),
        in_specs=[
            pl.BlockSpec(memory_space=pltpu.SMEM), stats, stats, by_row(channels), by_row(channels),
            by_row(channels), full(gain.shape), by_row(model), by_row(model),
            pl.BlockSpec((model, channels), lambda i: (0, 0)),
            pl.BlockSpec((model, channels), lambda i: (0, 1)),
        ],
        out_specs=[
            by_row(channels), by_row(channels), full((TAIL, known)), full(half), full(half),
            full(mine), full(theirs), full((TAIL, model)),
        ],
        out_shape=[
            jax.ShapeDtypeStruct((rows, channels), bf16),
            jax.ShapeDtypeStruct((rows, channels), f32),
            jax.ShapeDtypeStruct((TAIL, known), f32),
            jax.ShapeDtypeStruct(half, bf16),
            jax.ShapeDtypeStruct(half, bf16),
            jax.ShapeDtypeStruct(mine, bf16),
            jax.ShapeDtypeStruct(theirs, bf16),
            jax.ShapeDtypeStruct((TAIL, model), f32),
        ],
        scratch_shapes=[
            pltpu.VMEM((span, channels), bf16),
            pltpu.VMEM((model, 2 * channels), f32),
        ],
        compiler_params=pltpu.CompilerParams(
            dimension_semantics=("arbitrary",), vmem_limit_bytes=LIMIT
        ),
        name="gate_norm",
    )(spot, sums, more, gate, grad, ssm, gain, normed, upstream, weight, weight)


def lanes_of(vector):
    return jnp.pad(vector, (0, LANES - vector.shape[0]))[None, :]


def spread_map(heads, channels):
    size = channels // heads
    row = lax.broadcasted_iota(jnp.int32, (2 * LANES, channels), 0) % LANES
    col = lax.broadcasted_iota(jnp.int32, (2 * LANES, channels), 1) // size
    return (row == col).astype(bf16)


def dp_send(value, bit):
    size = lax.axis_size("dp")
    return lax.ppermute(value, "dp", [(i, i ^ bit) for i in range(size)])


def chip_bits():
    return [4 * k for k in range(1, lax.axis_size("dp") // 4)]


def long_bits():
    bits, bit = [], 4
    while bit < lax.axis_size("dp"):
        bits.append(bit)
        bit *= 2
    return bits


def choose(stacked, index, axis):
    return lax.dynamic_index_in_dim(stacked, index, axis, keepdims=False)


def send_fold(parts, bit, axis):
    mine = (lax.axis_index("dp") // bit) % 2
    return dp_send(choose(parts, 1 - mine, axis), bit)


def keep_fold(parts, got, bit, axis):
    mine = (lax.axis_index("dp") // bit) % 2
    return choose(parts, mine, axis).astype(f32) + got.astype(f32)


def fold(parts, bit, axis):
    return keep_fold(parts, send_fold(parts, bit, axis), bit, axis)


def send_chips(parts):
    place = lax.axis_index("dp") // 4
    sends = parts.astype(bf16)
    return [dp_send(choose(sends, place ^ (bit // 4), 0), bit) for bit in chip_bits()]


def keep_chips(parts, got):
    total = choose(parts, lax.axis_index("dp") // 4, 0).astype(f32)
    for piece in got:
        total = total + piece.astype(f32)
    return total


def fold_chips(parts):
    return keep_chips(parts, send_chips(parts))


def tensor_swap(value):
    return lax.ppermute(value, "tensor", [(0, 1), (1, 0)])


def gather_other(own, size):
    if size != 2:
        return lax.all_gather(own, "tensor", axis=0, tiled=True)
    return tensor_swap(own)


def join_pieces(own, top, bottom, size):
    top = top.reshape(size, -1, own.shape[1])
    bottom = bottom.reshape(size, -1, own.shape[1])
    return jnp.concatenate([top, bottom], axis=1).reshape(-1, own.shape[1])


def pick_half(lower, upper, size):
    if size != 2:
        return lower
    return jnp.where(lax.axis_index("tensor") == 0, lower, upper)


def sum_quarters(quarters, other0, other1, size):
    if size != 2:
        whole = jnp.concatenate(quarters, axis=0)
        return lax.psum_scatter(whole, "tensor", scatter_dimension=0, tiled=True).astype(f32)
    first = lax.axis_index("tensor") == 0
    each = other0.shape[0]
    low, middle, high = quarters
    lower = jnp.concatenate([low, middle[:each]], axis=0)
    upper = jnp.concatenate([middle[each:], high], axis=0)
    others = jnp.concatenate([other0, other1], axis=0)
    return jnp.where(first, lower, upper).astype(f32) + others.astype(f32)


def tensor_sum(value, size):
    if size != 2:
        return lax.psum(value, "tensor")
    return value + tensor_swap(value)


def shards(
    tokens, lengths, norm_gain, zx_weight, bc_weight, dt_weight, conv_inner, bias_inner,
    conv_shared, bias_shared, step_bias, log_rate, skip_gain, gate_gain, out_weight, cotangent,
):
    size = lax.axis_size("tensor")
    split = size == 2
    me = lax.axis_index("dp")
    count = len(chip_bits()) + 1
    spot = jnp.stack([lax.axis_index("tensor"), me // 4, (me // 2) % 2, me % 2])[None, :]
    spot = spot.astype(jnp.int32)
    channels = zx_weight.shape[2]
    heads = step_bias.shape[0]
    width = bc_weight.shape[1]
    known = channels + width + LANES
    step_weight = jnp.pad(dt_weight, ((0, 0), (0, LANES - heads)))
    early = jnp.concatenate([zx_weight[:, 1, :], bc_weight, step_weight], axis=1)
    inputs = tokens.astype(f32)
    norm_scale = lax.rsqrt(jnp.mean(inputs * inputs, axis=1, keepdims=True) + EPSILON)
    normed_rows = (inputs * norm_scale * norm_gain[None, :]).astype(bf16)
    half = normed_rows.shape[0] // 2
    fixed = (
        conv_inner, bias_inner[None, :], conv_shared, bias_shared[None, :], lanes_of(step_bias),
        lanes_of(-jnp.exp(log_rate)), jnp.repeat(skip_gain, channels // heads)[None, :],
        spread_map(heads, channels),
    )
    late = jnp.concatenate([zx_weight[:, 0, :], out_weight], axis=1)
    zeros = (
        jnp.zeros((TAIL, channels), f32), jnp.zeros((TAIL, width), f32),
        jnp.zeros((width // 2, channels), f32),
    )

    def along(value):
        return [value] + [dp_send(value, bit) for bit in chip_bits()]

    column = jnp.concatenate(along(early), axis=0)
    column, pair, top, fixed, zeros, spot = lax.optimization_barrier((
        column, jnp.concatenate([late, dp_send(late, 2)], axis=0),
        gather_other(normed_rows[:half], size), fixed, zeros, spot,
    ))
    cut_late = (2 * channels * 3 // 8) // LANES * LANES
    joined = along(pair[:, :cut_late])
    by_x, column, bottom, joined, pair = lax.optimization_barrier(
        (dp_send(column, 2), column, gather_other(normed_rows[half:], size), joined, pair)
    )
    joined = jnp.concatenate(joined, axis=0)
    pairs = along(pair[:, cut_late:])
    by_core = dp_send(column, 1)
    sources = (column, by_x, by_core, dp_send(by_x, 1))
    own, others = normed_rows, (top, bottom)
    if not split:
        own, others = join_pieces(normed_rows, top, bottom, size), ()
    normed, weight, *saved = mixer_forward(
        spot, lengths, own, others, sources, count, *fixed, SPAN
    )
    _, _, _, _, _, rate, skip, spread = fixed
    gain = gate_gain[None, :]
    other, ssm, joined_core, pairs = lax.optimization_barrier(
        (gather_other(cotangent, size), saved[0], dp_send(joined, 1), pairs)
    )
    sources = (joined, joined_core, *pairs, *[dp_send(pair, 1) for pair in pairs])
    own, others = (cotangent, (other,)) if split else (other, ())
    upstream, weight_late, gate, grad, sums = gate_forward(
        spot, normed, own, others, sources, count, gain, ssm, SPAN
    )
    more = gather_other(sums, size) if split else sums
    sums = sums if split else lax.psum(sums, "tensor")
    chips = 2 * count
    grad_gate, grad_ssm, gain_sum, keep, send, branch_own, branch_send, norm_sum = gate_norm(
        spot, sums, more, gate, grad, ssm, gain, normed, upstream, weight_late, known, channels * size,
        chips, split, SPAN,
    )
    if split:
        branch_other = gather_other(branch_send, size)
    else:
        branch_own = lax.psum_scatter(branch_own, "tensor", scatter_dimension=0, tiled=True)
        branch_other = jnp.zeros_like(branch_own)
    quarter = grad_ssm.shape[0] // SPAN // 4
    carry = (gain_sum, *zeros)

    def back(begin, end, carry):
        return mixer_backward(
            lengths, grad_ssm, saved, conv_inner, conv_shared, rate, skip, spread, grad_gate,
            weight_late, weight, carry, (begin * quarter, end * quarter), SPAN,
        )

    first = dp_send(send, 1)
    grads3, terms3, carry = back(3, 4, carry)
    first = (keep.astype(f32) + first.astype(f32)).astype(bf16)
    first = first.reshape(count, 2, -1, first.shape[1])
    carry, first = lax.optimization_barrier((carry, first))
    first_gate, first_out = first[..., :channels], first[..., channels:]
    grads1, terms1, carry = back(1, 3, carry)
    first_gate = fold(first_gate, 2, 1)
    first_out = fold_chips(first_out).astype(bf16)
    each = terms3.shape[0]
    send1 = pick_half(terms3, terms1[:each], size)
    carry, send1, branch_other, first_gate, first_out = lax.optimization_barrier(
        (carry, send1, branch_other, first_gate, first_out)
    )
    other1 = gather_other(send1, size) if split else send1
    block_out = (inputs + (branch_own.astype(f32) + branch_other.astype(f32))).astype(bf16)
    part_gate = fold_chips(first_gate)
    part_out = fold(first_out, 2, 0)
    grads0, terms0, carry = back(0, 1, carry)
    sums, part_gate, part_out, grads0, other1, block_out, terms0 = lax.optimization_barrier(
        (carry[0], part_gate, part_out, grads0, other1, block_out, terms0)
    )
    send0 = pick_half(terms1[each:], terms0, size)
    send0, grads0 = lax.optimization_barrier((send0, grads0))
    other0 = gather_other(send0, size) if split else send0
    keep, *send, sums = weight_products(
        spot, normed, weight, norm_gain[None, :], sums, norm_sum, (grads0, grads1, grads3), chips,
        (0, known), True,
    )
    got = [dp_send(piece, 1) for piece in send]
    *got, other0, sums, keep = lax.optimization_barrier((*got, other0, sums, keep))
    got = jnp.concatenate(got, axis=0)
    parts = (keep.astype(f32) + got.astype(f32)).astype(bf16).reshape(count, 2, -1, known)
    cut = min((known * 2 // 3) // LANES * LANES, channels)
    parts_a, parts_b = parts[..., :cut], parts[..., cut:]
    got_a = send_fold(parts_a, 2, 1)
    got_b = send_chips(parts_b)
    shared_sums = tensor_sum(sums[:, channels:], size)
    step_sums = sums[:, channels + width : known]
    shared_sums, other0 = lax.optimization_barrier((shared_sums, other0))
    sums = jnp.concatenate([sums[:, :channels], step_sums, shared_sums], axis=1)
    sums = sums + dp_send(sums, 1)
    sums = sums + dp_send(sums, 2)
    grad_normed = sum_quarters((terms0, terms1, terms3), other0, other1, size)
    scaled_grad = grad_normed * norm_gain[None, :]
    grad_inputs = norm_scale * scaled_grad - inputs * norm_scale**3 * jnp.mean(
        scaled_grad * inputs, axis=1, keepdims=True
    )
    grad_tokens = (cotangent.astype(f32) + grad_inputs).astype(bf16)
    got_a, got_b, sums, grad_tokens = lax.optimization_barrier((got_a, got_b, sums, grad_tokens))
    parts_a = keep_fold(parts_a, got_a, 2, 1)
    parts_b = keep_chips(parts_b, got_b).astype(bf16)
    got_a = send_chips(parts_a)
    parts_b = fold(parts_b, 2, 0)
    for bit in long_bits():
        sums = sums + dp_send(sums, bit)
    parts_a = keep_chips(parts_a, got_a)
    shared_sums = sums[:, channels + LANES :]
    norm_sum = shared_sums[0, known - channels :]
    part_inner = jnp.concatenate([parts_a, parts_b[:, : channels - cut]], axis=1)
    at_step = channels + width
    part_shared = tensor_sum(parts_b[:, channels - cut : at_step - cut], size)
    part_step = parts_b[:, at_step - cut : at_step - cut + heads]
    part_in = jnp.stack([part_gate, part_inner], axis=1)
    return (
        block_out,
        grad_tokens,
        norm_sum,
        part_in,
        part_shared,
        part_step,
        sums[:TAPS, :channels],
        sums[TAPS, :channels],
        shared_sums[:TAPS, :width],
        shared_sums[TAPS, :width],
        sums[0, channels : channels + heads],
        sums[1, channels : channels + heads],
        sums[2, channels : channels + heads],
        sums[TAIL - 1, :channels],
        part_out,
    )


def solution(mesh):
    return jax.shard_map(
        shards,
        mesh=mesh,
        in_specs=(
            P(("dp", "tensor"), None),
            P("dp", None),
            P(),
            P("dp", None, "tensor"),
            P("dp", None),
            P("dp", "tensor"),
            P(None, "tensor"),
            P("tensor"),
            P(),
            P(),
            P("tensor"),
            P("tensor"),
            P("tensor"),
            P("tensor"),
            P("dp", "tensor"),
            P(("dp", "tensor"), None),
        ),
        out_specs=(
            P(("dp", "tensor"), None),
            P(("dp", "tensor"), None),
            P(),
            P("dp", None, "tensor"),
            P("dp", None),
            P("dp", "tensor"),
            P(None, "tensor"),
            P("tensor"),
            P(),
            P(),
            P("tensor"),
            P("tensor"),
            P("tensor"),
            P("tensor"),
            P("dp", "tensor"),
        ),
        check_vma=False,
    )
```

```python
from functools import partial

import jax
import jax.numpy as jnp
from jax import lax
from jax.experimental import pallas as pl
from jax.experimental.pallas import tpu as pltpu
from jax.sharding import PartitionSpec as P

EPSILON = 1e-05
SPAN = 256
LANES = 128
TAIL = 8
TAPS = 4
MASKED = -1e30
f32 = jnp.float32
bf16 = jnp.bfloat16
LIMIT = 60 * 1024 * 1024


def mm(left, right, dims):
    return lax.dot_general(left, right, ((dims[0], dims[1]), ((), ())), preferred_element_type=f32)


NN = ((1,), (0,))
NT = ((1,), (1,))
TN = ((0,), (0,))


def halves(value, axis):
    high = value.astype(bf16)
    low = (value - high.astype(f32)).astype(bf16)
    return jnp.concatenate([high, low], axis=axis)


def sigmoid(value):
    return 1.0 / (1.0 + jnp.exp(-value))


def softplus(value):
    return jnp.maximum(value, 0.0) + jnp.log1p(jnp.exp(-jnp.abs(value)))


def segment_at(ends, position):
    total = jnp.zeros(position.shape, jnp.int32)
    for end in ends:
        total = total + (position >= end).astype(jnp.int32)
    return total


def sequence_ends(lengths_ref):
    ends, total = [], 0
    for i in range(lengths_ref.shape[1]):
        total = total + lengths_ref[0, i]
        ends.append(total)
    return ends


def step_parts(step_raw, rate, ends, base):
    rows = step_raw.shape[0]
    step = softplus(step_raw)
    row = lax.broadcasted_iota(jnp.int32, (rows, rows), 0)
    col = lax.broadcasted_iota(jnp.int32, (rows, rows), 1)
    lower = (row >= col).astype(f32).astype(bf16)
    split = mm(lower, halves(step * rate, 1), NN)
    running = split[:, :LANES] + split[:, LANES:]
    position = base + lax.broadcasted_iota(jnp.int32, (rows, 1), 0)
    segment = segment_at(ends, position)
    before = segment_at(ends, jnp.full((1, 1), base - 1, jnp.int32))
    last = segment_at(ends, jnp.full((1, 1), base + rows - 1, jnp.int32))
    carried = ((segment == before) & (position >= rows)).astype(f32)
    matched = (segment == last).astype(f32)
    entry = jnp.exp(running) * carried
    leave = jnp.exp(running[rows - 1 :, :] - running) * matched
    return step, running, entry, leave, lower, segment, row, col


def same_rows(ends, base, rows):
    across = segment_at(ends, base + lax.broadcasted_iota(jnp.int32, (1, rows), 1))
    down = segment_at(ends, base + lax.broadcasted_iota(jnp.int32, (rows, 1), 0))
    return down == across


def rows_of(block, blocks, spot_ref, own_ref, others):
    if not others:
        return own_ref[...]
    half = blocks // 2
    local = lax.rem(block, half)
    span = own_ref.shape[0] // half
    each = half // len(others)
    value = None
    for i, ref in enumerate(others):
        at = lax.rem(local, each) * span
        piece = ref[pl.ds(pl.multiple_of(at, span), span), :]
        value = piece if i == 0 else jnp.where(local >= i * each, piece, value)
    mine = own_ref[pl.ds(pl.multiple_of(local * span, span), span), :]
    return jnp.where(block // half == spot_ref[0, 0], mine, value)


def own_specs(own, others, span):
    if not others:
        return [pl.BlockSpec((span, own.shape[1]), lambda i: (i, 0))]
    return [full(own.shape), *[full(other.shape) for other in others]]


def run_copies(copies):
    for copy in copies:
        copy.start()
    for copy in copies:
        copy.wait()


def place_weights(spot_ref, weight_ref, sources, count, done):
    rows = weight_ref.shape[0] // (4 * count)
    copies = []
    for i, ref in enumerate(sources):
        along = spot_ref[0, 2] ^ (i % 2)
        core = spot_ref[0, 3] ^ (i // 2)
        for k in range(count):
            at = (((spot_ref[0, 1] ^ k) * 2 + along) * 2 + core) * rows
            copies.append(pltpu.make_async_copy(
                ref.at[pl.ds(k * rows, rows), :],
                weight_ref.at[pl.ds(pl.multiple_of(at, rows), rows), :],
                done.at[i * count + k],
            ))
    run_copies(copies)


def place_pairs(spot_ref, weight_ref, sources, count, lo):
    rows = weight_ref.shape[0] // (4 * count)
    for i, (ref, begin) in enumerate(sources):
        core = spot_ref[0, 3] ^ (i // count)
        for j in range(2):
            at = (((spot_ref[0, 1] ^ (i % count)) * 2 + (spot_ref[0, 2] ^ j)) * 2 + core) * rows
            at = pl.ds(pl.multiple_of(at, rows), rows)
            here = begin + j * rows
            weight_ref[at, lo : lo + ref.shape[1]] = ref[here : here + rows, :]


def split_cores(spot_ref, value_ref, keep_ref, send_refs, chips):
    rows = keep_ref.shape[0] // chips
    each = chips // len(send_refs)
    core = spot_ref[0, 3]
    for chip in range(chips):
        here = pl.ds(pl.multiple_of((2 * chip + core) * rows, rows), rows)
        there = pl.ds(pl.multiple_of((2 * chip + 1 - core) * rows, rows), rows)
        keep_ref[chip * rows : (chip + 1) * rows, :] = value_ref[here, :].astype(bf16)
        at = (chip % each) * rows
        send_refs[chip // each][at : at + rows, :] = value_ref[there, :].astype(bf16)


def forward_kernel(
    pieces, count, spot_ref, lengths_ref, *refs
):
    own_ref, others = refs[0], refs[1:pieces]
    sources = refs[pieces : pieces + 4]
    (
        conv_inner_ref, bias_inner_ref, conv_shared_ref, bias_shared_ref, step_bias_ref, rate_ref,
        skip_ref, spread_ref, normed_ref, weight_ref, ssm_ref, inner_ref, pre_inner_ref, shared_ref,
        pre_shared_ref, step_ref, entering_ref, inner_tail, shared_tail, state, done,
    ) = refs[pieces + 4 :]
    block = pl.program_id(0)
    rows = normed_ref.shape[0]
    channels = conv_inner_ref.shape[1]
    base = block * rows
    ends = sequence_ends(lengths_ref)

    @pl.when(block == 0)
    def _():
        inner_tail[0:TAIL, :] = jnp.zeros((TAIL, channels), f32)
        shared_tail[0:TAIL, :] = jnp.zeros((TAIL, shared_tail.shape[1]), f32)
        state[...] = jnp.zeros_like(state)
        place_weights(spot_ref, weight_ref, sources, count, done)

    @pl.when(block > 0)
    def _():
        inner_tail[0:TAIL, :] = inner_tail[rows : rows + TAIL, :]
        shared_tail[0:TAIL, :] = shared_tail[rows : rows + TAIL, :]

    normed = rows_of(block, pl.num_programs(0), spot_ref, own_ref, others)
    normed_ref[...] = normed
    small = mm(normed, weight_ref[:, channels:], NN)
    width = conv_shared_ref.shape[1]
    shared_proj = small[:, :width]
    shared_tail[TAIL : TAIL + rows, :] = shared_proj
    shared_ref[...] = shared_proj
    step_raw = small[:, width:] + step_bias_ref[...]
    step_ref[...] = step_raw
    inner_proj = mm(normed, weight_ref[:, :channels], NN)
    inner_tail[TAIL : TAIL + rows, :] = inner_proj
    inner_ref[...] = inner_proj

    step, running, entry, leave, lower, segment, row, col = step_parts(
        step_raw, rate_ref[...], ends, base
    )
    position = base + lax.broadcasted_iota(jnp.int32, (rows, 1), 0)
    keeps = [
        ((segment_at(ends, position - k) == segment) & (position >= k)).astype(f32)
        for k in range(1, TAPS)
    ]
    keeps = [jnp.broadcast_to(keep, (rows, LANES)) for keep in keeps]

    def conv(tail, taps_ref, bias_ref, lo, hi):
        total = bias_ref[:, lo:hi] + taps_ref[TAPS - 1 : TAPS, lo:hi] * tail[TAIL : TAIL + rows, lo:hi]
        for k in range(1, TAPS):
            shifted = tail[TAIL - k : TAIL - k + rows, lo:hi]
            total = total + taps_ref[TAPS - 1 - k : TAPS - k, lo:hi] * (shifted * keeps[k - 1])
        return total

    pre_shared = jnp.concatenate(
        [
            conv(shared_tail, conv_shared_ref, bias_shared_ref, lo, lo + LANES)
            for lo in range(0, width, LANES)
        ],
        axis=1,
    )
    pre_shared_ref[...] = pre_shared
    shared = pre_shared * sigmoid(pre_shared)
    in_map = shared[:, : width // 2].astype(bf16)
    out_map = shared[:, width // 2 :].astype(bf16)
    scores = mm(out_map, in_map, NT)
    in_map_t = jnp.transpose(in_map)
    allowed = jnp.where((row >= col) & same_rows(ends, base, rows), 0.0, MASKED)
    running_t = jnp.transpose(running)
    factors = jnp.concatenate([halves(x, 1) for x in (step, entry, leave)], axis=0)
    lane = lax.broadcasted_iota(jnp.int32, (rows, LANES), 1)
    for pair in range(channels // LANES):
        lo, hi = pair * LANES, (pair + 1) * LANES
        pre = conv(inner_tail, conv_inner_ref, bias_inner_ref, lo, hi)
        pre_inner_ref[:, lo:hi] = pre
        head_in = pre * sigmoid(pre)
        side = (pair % 2) * LANES
        if side == 0:
            spread = spread_ref[:, lo : min(lo + 2 * LANES, channels)]
            wide = mm(factors, spread, NN)
        step_wide, entry_wide, leave_wide = [
            wide[i * rows : (i + 1) * rows, side : side + LANES] for i in range(3)
        ]
        scaled = head_in * step_wide
        scaled_low = scaled.astype(bf16)
        held = state[:, lo:hi]
        entering_ref[0, :, lo:hi] = held
        carried_out = mm(out_map, held.astype(bf16), NN) * entry_wide
        parts = []
        for parity in range(2):
            head = 2 * pair + parity
            gap = running[:, head : head + 1] - running_t[head : head + 1, :]
            parts.append((scores * jnp.exp(gap + allowed)).astype(bf16))
        both = mm(jnp.concatenate(parts, axis=0), scaled_low, NN)
        intra = jnp.where(lane < LANES // 2, both[:rows], both[rows:])
        ssm_ref[:, lo:hi] = carried_out + intra + skip_ref[:, lo:hi] * head_in
        added = mm(in_map_t, (scaled * leave_wide).astype(bf16), NN)
        state[:, lo:hi] = held * entry_wide[rows - 1 :, :] + added


def full(shape):
    return pl.BlockSpec(shape, lambda *_: (0,) * len(shape))


def mixer_forward(
    spot, lengths, own, others, sources, count, conv_inner, bias_inner, conv_shared, bias_shared,
    step_bias, rate, skip, spread, span,
):
    rows = own.shape[0] * (2 if others else 1)
    model = own.shape[1]
    channels = conv_inner.shape[1]
    width = conv_shared.shape[1]
    known = channels + width + LANES
    blocks = rows // span
    by_row = lambda cols: pl.BlockSpec((span, cols), lambda i: (i, 0))
    shape = lambda cols: jax.ShapeDtypeStruct((rows, cols), f32)
    states = width // 2
    smem = pl.BlockSpec(memory_space=pltpu.SMEM)
    fixed = (conv_inner, bias_inner, conv_shared, bias_shared, step_bias, rate, skip, spread)
    return pl.pallas_call(
        partial(forward_kernel, 1 + len(others), count),
        grid=(blocks,),
        in_specs=[
            smem, smem, *own_specs(own, others, span),
            *[pl.BlockSpec(memory_space=pl.ANY) for _ in sources],
            *[full(x.shape) for x in fixed],
        ],
        out_specs=[
            by_row(model), full((model, known)), by_row(channels), by_row(channels),
            by_row(channels), by_row(width), by_row(width), by_row(LANES),
            pl.BlockSpec((1, states, channels), lambda i: (i, 0, 0)),
        ],
        out_shape=[
            jax.ShapeDtypeStruct((rows, model), bf16), jax.ShapeDtypeStruct((model, known), bf16),
            shape(channels), shape(channels), shape(channels), shape(width), shape(width),
            shape(LANES), jax.ShapeDtypeStruct((blocks, states, channels), f32),
        ],
        scratch_shapes=[
            pltpu.VMEM((TAIL + span, channels), f32),
            pltpu.VMEM((TAIL + span, width), f32),
            pltpu.VMEM((states, channels), f32),
            pltpu.SemaphoreType.DMA((4 * count,)),
        ],
        compiler_params=pltpu.CompilerParams(
            dimension_semantics=("arbitrary",), vmem_limit_bytes=LIMIT
        ),
        name="mixer_forward",
    )(spot, lengths, own, *others, *sources, *fixed)


def backward_kernel(
    first_block, total_rows, lengths_ref, upstream_ref, ssm_ref, inner_ref, pre_inner_ref,
    shared_ref, pre_shared_ref, step_ref, entering_ref, conv_inner_ref, conv_shared_ref, rate_ref, skip_ref, spread_ref,
    grad_gate_ref, gate_w_ref, weight_ref, sums_in_ref, *refs,
):
    carried_in, refs = refs[:-11], refs[-11:]
    (
        grads_ref, terms_ref, sums_ref, inner_out_ref, shared_out_ref, adjoint, inner_head,
        shared_head, gate_w, weight, done,
    ) = refs
    turn = pl.program_id(0)
    block = first_block + pl.num_programs(0) - 1 - turn
    rows, channels = upstream_ref.shape
    width = conv_shared_ref.shape[1]
    base = block * rows
    ends = sequence_ends(lengths_ref)

    def weight_copies():
        return (
            pltpu.make_async_copy(gate_w_ref.at[:, pl.ds(0, channels)], gate_w, done.at[0]),
            pltpu.make_async_copy(weight_ref, weight, done.at[1]),
        )

    @pl.when(turn == 0)
    def _():
        if carried_in:
            inner_head[rows : rows + TAIL, :] = carried_in[0][...]
            shared_head[rows : rows + TAIL, :] = carried_in[1][...]
            adjoint[...] = carried_in[2][...]
        else:
            inner_head[rows : rows + TAIL, :] = jnp.zeros((TAIL, channels), f32)
            shared_head[rows : rows + TAIL, :] = jnp.zeros((TAIL, width), f32)
            adjoint[...] = jnp.zeros_like(adjoint)
        sums_ref[...] = sums_in_ref[...]
        for copy in weight_copies():
            copy.start()

    @pl.when(turn > 0)
    def _():
        inner_head[rows : rows + TAIL, :] = inner_head[0:TAIL, :]
        shared_head[rows : rows + TAIL, :] = shared_head[0:TAIL, :]

    step_raw = step_ref[...]
    rate = rate_ref[...]
    step, running, entry, leave, lower, segment, row, col = step_parts(step_raw, rate, ends, base)
    position = base + lax.broadcasted_iota(jnp.int32, (rows, 1), 0)
    keeps = [
        ((segment_at(ends, position + k) == segment) & (position + k < total_rows)).astype(f32)
        for k in range(1, TAPS)
    ]
    keeps = [jnp.broadcast_to(keep, (rows, LANES)) for keep in keeps]
    pre_shared = pre_shared_ref[...]
    shared_gate = sigmoid(pre_shared)
    shared = pre_shared * shared_gate
    half = width // 2
    in_map = shared[:, :half].astype(bf16)
    out_map = shared[:, half:].astype(bf16)
    scores_t = mm(in_map, out_map, NT)
    out_map_t = jnp.transpose(out_map)
    allowed_t = jnp.where((col >= row) & same_rows(ends, base, rows), 0.0, MASKED)
    running_t = jnp.transpose(running)
    factors = jnp.concatenate([halves(x, 1) for x in (step, entry, leave)], axis=0)
    lane = lax.broadcasted_iota(jnp.int32, (rows, LANES), 1)
    first_half = lane < LANES // 2
    grad_scores_t = jnp.zeros((rows, rows), f32)
    grad_in = jnp.zeros((rows, half), f32)
    grad_out = jnp.zeros((rows, half), f32)
    by_head = jnp.zeros((rows + TAIL, LANES), f32)
    step_terms = jnp.zeros((rows, LANES), f32)
    for pair in range(channels // LANES):
        lo, hi = pair * LANES, (pair + 1) * LANES
        side = (pair % 2) * LANES
        if side == 0:
            spread = spread_ref[:, lo : min(lo + 2 * LANES, channels)]
            wide = mm(factors, spread, NN)
            products = []
        step_wide, entry_wide, leave_wide = [
            wide[i * rows : (i + 1) * rows, side : side + LANES] for i in range(3)
        ]
        pre = pre_inner_ref[:, lo:hi]
        gate = sigmoid(pre)
        head_in = pre * gate
        skip = skip_ref[:, lo:hi]
        upstream = upstream_ref[:, lo:hi]
        upstream_low = upstream.astype(bf16)
        upstream_back = upstream_low.astype(f32)
        scaled = head_in * step_wide
        scaled_low = scaled.astype(bf16)
        scaled_back = scaled_low.astype(f32)
        held = entering_ref[0, :, lo:hi]
        held_low = held.astype(bf16)
        ahead = adjoint[:, lo:hi]
        ahead_low = ahead.astype(bf16)
        entry_up = (upstream_back * entry_wide).astype(bf16)
        grad_out = grad_out + mm(entry_up, held_low, NT)
        grad_in = grad_in + mm((scaled * leave_wide).astype(bf16), ahead_low, NT)
        grad_scaled = mm(in_map, ahead_low, NN) * leave_wide
        through = entry_wide[rows - 1 :, :]
        tail_terms = jnp.sum(scaled_back * grad_scaled, axis=0, keepdims=True) + through * jnp.sum(
            ahead * held, axis=0, keepdims=True
        )
        adjoint[:, lo:hi] = ahead * through + mm(out_map_t, entry_up, NN)
        parts, decays, chosen = [], [], []
        for parity in range(2):
            head = 2 * pair + parity
            gap = running_t[head : head + 1, :] - running[:, head : head + 1]
            decays.append(jnp.exp(gap + allowed_t))
            parts.append((scores_t * decays[parity]).astype(bf16))
            mine = first_half if parity == 0 else jnp.logical_not(first_half)
            chosen.append(jnp.where(mine, scaled_back, 0.0).astype(bf16))
        both = mm(jnp.concatenate(parts, axis=0), upstream_low, NN)
        pulled = mm(jnp.concatenate(chosen, axis=0), upstream_low, NT)
        grad_scores_t = grad_scores_t + (pulled[:rows] * decays[0] + pulled[rows:] * decays[1])
        grad_scaled = grad_scaled + jnp.where(first_half, both[:rows], both[rows:])
        spread_one = spread[:LANES, side : side + LANES]
        spread_both = jnp.concatenate([spread_one, spread_one], axis=1)
        balance = upstream_back * (ssm_ref[:, lo:hi] - skip * head_in) - scaled_back * grad_scaled
        products.append((head_in * grad_scaled).astype(bf16))
        if hi == channels or side > 0:
            joined = jnp.concatenate(products, axis=1)
            step_terms = step_terms + mm(joined, spread[:LANES, :], NT)
        skip_terms = jnp.sum(upstream * head_in, axis=0, keepdims=True)
        edge = jnp.concatenate([tail_terms, skip_terms, jnp.zeros((TAIL - 2, LANES), f32)], axis=0)
        by_head = by_head + mm(
            halves(jnp.concatenate([balance, edge], axis=0), 1), spread_both, NT
        )
        grad_pre = (grad_scaled * step_wide + skip * upstream) * (gate * (1.0 + pre * (1.0 - gate)))
        inner_head[0:rows, lo:hi] = grad_pre
        inner_proj = inner_ref[:, lo:hi]
        grad_proj = conv_inner_ref[TAPS - 1 : TAPS, lo:hi] * grad_pre
        sums = [None] * TAPS
        sums[TAPS - 1] = jnp.sum(grad_pre * inner_proj, axis=0, keepdims=True)
        for k in range(1, TAPS):
            moved = inner_head[k : k + rows, lo:hi] * keeps[k - 1]
            grad_proj = grad_proj + conv_inner_ref[TAPS - 1 - k : TAPS - k, lo:hi] * moved
            sums[TAPS - 1 - k] = jnp.sum(moved * inner_proj, axis=0, keepdims=True)
        grads_ref[:, lo:hi] = grad_proj.astype(bf16)
        sums.append(jnp.sum(grad_pre, axis=0, keepdims=True))
        sums.append(jnp.zeros((TAIL - len(sums), LANES), f32))
        sums_ref[:, lo:hi] += jnp.concatenate(sums, axis=0)
    grad_scores_low = grad_scores_t.astype(bf16)
    grad_out = grad_out + mm(grad_scores_low, in_map, TN)
    grad_in = grad_in + mm(grad_scores_low, out_map, NN)
    grad_shared = jnp.concatenate([grad_in, grad_out], axis=1)
    grad_pre = grad_shared * (shared_gate * (1.0 + pre_shared * (1.0 - shared_gate)))
    shared_head[0:rows, :] = grad_pre
    shared_proj = shared_ref[...]
    grad_proj = conv_shared_ref[TAPS - 1 : TAPS, :] * grad_pre
    sums = [None] * TAPS
    sums[TAPS - 1] = jnp.sum(grad_pre * shared_proj, axis=0, keepdims=True)
    for k in range(1, TAPS):
        keep = jnp.concatenate([keeps[k - 1]] * (width // LANES), axis=1)
        moved = shared_head[k : k + rows, :] * keep
        grad_proj = grad_proj + conv_shared_ref[TAPS - 1 - k : TAPS - k, :] * moved
        sums[TAPS - 1 - k] = jnp.sum(moved * shared_proj, axis=0, keepdims=True)
    sums.append(jnp.sum(grad_pre, axis=0, keepdims=True))
    sums.append(jnp.zeros((TAIL - len(sums), width), f32))
    sums_ref[:, channels : channels + width] += jnp.concatenate(sums, axis=0)
    leaving = by_head[rows:]
    split = mm(lower, halves(by_head[:rows], 1), TN)
    grad_log = split[:, :LANES] + split[:, LANES:] + leaving[0:1, :]
    grad_step = (step_terms + rate * grad_log) * sigmoid(step_raw)
    grads_ref[:, channels : channels + width] = grad_proj.astype(bf16)
    grads_ref[:, channels + width :] = grad_step.astype(bf16)

    @pl.when(turn == 0)
    def _():
        for copy in weight_copies():
            copy.wait()

    terms = mm(grad_gate_ref[...], gate_w[...], NT) + mm(grads_ref[...], weight[...], NT)
    terms_ref[...] = terms.astype(bf16)
    sums_ref[:, channels + width :] += jnp.concatenate(
        [
            jnp.sum(grad_step, axis=0, keepdims=True),
            rate * jnp.sum(step * grad_log, axis=0, keepdims=True),
            leaving[1:2, :],
            jnp.zeros((TAIL - 3, LANES), f32),
        ],
        axis=0,
    )

    @pl.when(turn == pl.num_programs(0) - 1)
    def _():
        inner_out_ref[...] = inner_head[0:TAIL, :]
        shared_out_ref[...] = shared_head[0:TAIL, :]


def mixer_backward(
    lengths, upstream, saved, conv_inner, conv_shared, rate, skip, spread, grad_gate, weight_late,
    weight, carry, blocks, span
):
    ssm, inner, pre_inner, shared, pre_shared, step_raw, entering = saved
    rows, channels = upstream.shape
    width = conv_shared.shape[1]
    states = width // 2
    begin, end = blocks
    known = channels + width + LANES
    model = weight.shape[0]
    by_row = lambda cols: pl.BlockSpec((span, cols), lambda i: (end - 1 - i, 0))
    small = ((TAIL, known), (TAIL, channels), (TAIL, width), (states, channels))
    results = pl.pallas_call(
        partial(backward_kernel, begin, rows),
        grid=(end - begin,),
        in_specs=[
            pl.BlockSpec(memory_space=pltpu.SMEM),
            by_row(channels), by_row(channels), by_row(channels), by_row(channels),
            by_row(width), by_row(width), by_row(LANES),
            pl.BlockSpec((1, states, channels), lambda i: (end - 1 - i, 0, 0)),
            full(conv_inner.shape),
            full(conv_shared.shape),
            full(rate.shape),
            full(skip.shape),
            full(spread.shape),
            by_row(channels),
            pl.BlockSpec(memory_space=pl.ANY),
            pl.BlockSpec(memory_space=pl.ANY),
            *[full(x.shape) for x in carry],
        ],
        out_specs=[
            pl.BlockSpec((span, known), lambda i: (end - begin - 1 - i, 0)),
            pl.BlockSpec((span, model), lambda i: (end - begin - 1 - i, 0)),
            *[full(shape) for shape in small],
        ],
        out_shape=[
            jax.ShapeDtypeStruct(((end - begin) * span, known), bf16),
            jax.ShapeDtypeStruct(((end - begin) * span, model), bf16),
            *[jax.ShapeDtypeStruct(shape, f32) for shape in small],
        ],
        scratch_shapes=[
            pltpu.VMEM((TAIL + span, channels), f32),
            pltpu.VMEM((TAIL + span, width), f32),
            pltpu.VMEM((model, channels), bf16),
            pltpu.VMEM((model, known), bf16),
            pltpu.SemaphoreType.DMA((2,)),
        ],
        compiler_params=pltpu.CompilerParams(
            dimension_semantics=("arbitrary",), vmem_limit_bytes=LIMIT
        ),
        name="mixer_backward",
    )(
        lengths, upstream, ssm, inner, pre_inner, shared, pre_shared, step_raw, entering,
        conv_inner, conv_shared, rate, skip, spread, grad_gate, weight_late, weight, *carry,
    )
    return results[0], results[1], tuple(results[2:])


def gain_row(weight_ref, total_ref, columns):
    rows = weight_ref.shape[0]
    begin, end = columns
    added = jnp.zeros((rows, LANES), f32)
    for lo in range(begin, end, LANES):
        weight = weight_ref[:, lo : lo + LANES].astype(f32)
        added = added + weight * total_ref[:, lo - begin : lo - begin + LANES]
    return jnp.sum(jnp.transpose(added), axis=0, keepdims=True)


def product_kernel(chips, columns, spot_ref, normed_ref, weight_ref, gain_ref, sums_ref,
                   norm_sum_ref, *refs):
    grads, (keep_ref, *send_refs, heads_ref, shared_ref, total) = refs[:-8], refs[-8:]
    lo, hi = columns
    at = 0
    for i, ref in enumerate(grads):
        rows = ref.shape[0]
        added = mm(normed_ref[at : at + rows, :], ref[:, lo:hi], TN)
        total[...] = added if i == 0 else total[...] + added
        at += rows
    split_cores(spot_ref, total, keep_ref, send_refs, chips)
    row = norm_sum_ref[0:1, :] + gain_row(weight_ref, total, columns)
    width = shared_ref.shape[1] - norm_sum_ref.shape[1]
    inner = heads_ref.shape[1] - LANES
    heads_ref[:, :inner] = sums_ref[:, :inner]
    heads_ref[:, inner:] = sums_ref[:, inner + width :]
    shared_ref[:, :width] = sums_ref[:, inner : inner + width]
    shared_ref[:, width:] = jnp.broadcast_to(row / gain_ref[...], norm_sum_ref.shape)


def weight_products(spot, normed, weight, gain, sums, norm_sum, grads, chips, width):
    known = grads[0].shape[1]
    model = normed.shape[1]
    size = known
    part = jax.ShapeDtypeStruct((model // 2, size), bf16)
    piece = jax.ShapeDtypeStruct((model // 8, size), bf16)
    vmem = pl.BlockSpec(memory_space=pltpu.VMEM)
    return pl.pallas_call(
        partial(product_kernel, chips, (0, known)),
        in_specs=[pl.BlockSpec(memory_space=pltpu.SMEM), *[vmem for _ in range(5 + len(grads))]],
        out_specs=[vmem] * 7,
        out_shape=[
            part, *[piece] * 4, jax.ShapeDtypeStruct((TAIL, known - width), f32),
            jax.ShapeDtypeStruct((TAIL, width + model), f32),
        ],
        scratch_shapes=[pltpu.VMEM((model, size), f32)],
        compiler_params=pltpu.CompilerParams(vmem_limit_bytes=LIMIT),
        name="weight_products",
    )(spot, normed, weight, gain, sums, norm_sum, *grads)


def gate_kernel(pieces, count, spot_ref, normed_ref, *refs):
    own_ref, others = refs[0], refs[1:pieces]
    joined, sources = refs[pieces : pieces + 2], refs[pieces + 2 : pieces + 2 + 2 * count]
    (
        gain_ref, ssm_ref, upstream_ref, weight_ref, gate_ref, grad_ref, sums_ref
    ) = refs[pieces + 2 + 2 * count :]

    @pl.when(pl.program_id(0) == 0)
    def _():
        each = joined[0].shape[0] // count
        rows = [(ref, k * each) for ref in joined for k in range(count)]
        place_pairs(spot_ref, weight_ref, rows, count, 0)
        place_pairs(spot_ref, weight_ref, [(ref, 0) for ref in sources], count, joined[0].shape[1])

    rows, channels = ssm_ref.shape
    normed = normed_ref[...]
    upstream = rows_of(pl.program_id(0), pl.num_programs(0), spot_ref, own_ref, others)
    upstream_ref[...] = upstream
    square = jnp.zeros((rows, LANES), f32)
    cross = jnp.zeros((rows, LANES), f32)
    step = 2 * LANES
    for lo in range(0, channels, step):
        hi = lo + step
        gate = mm(normed, weight_ref[:, lo:hi], NN)
        grad = mm(upstream, weight_ref[:, channels + lo : channels + hi], NN)
        gate_ref[:, lo:hi] = gate
        grad_ref[:, lo:hi] = grad
        gated = ssm_ref[:, lo:hi] * (gate * sigmoid(gate))
        squares = gated * gated
        crosses = grad * gain_ref[:, lo:hi] * gated
        square = square + (squares[:, :LANES] + squares[:, LANES:])
        cross = cross + (crosses[:, :LANES] + crosses[:, LANES:])
    square = jnp.sum(square, axis=1, keepdims=True)
    cross = jnp.sum(cross, axis=1, keepdims=True)
    lane = lax.broadcasted_iota(jnp.int32, (rows, LANES), 1)
    both = jnp.where(lane == 0, square, jnp.where(lane == 1, cross, 0.0))
    sums_ref[...] = jnp.transpose(both)[0:TAIL, :]


def gate_forward(spot, normed, own, others, sources, count, gain, ssm, span):
    rows, model = normed.shape
    channels = ssm.shape[1]
    by_row = lambda cols: pl.BlockSpec((span, cols), lambda i: (i, 0))
    return pl.pallas_call(
        partial(gate_kernel, 1 + len(others), count),
        grid=(rows // span,),
        in_specs=[
            pl.BlockSpec(memory_space=pltpu.SMEM), by_row(model), *own_specs(own, others, span),
            *[full(x.shape) for x in sources], full(gain.shape), by_row(channels),
        ],
        out_specs=[
            by_row(model), full((model, 2 * channels)), by_row(channels), by_row(channels),
            pl.BlockSpec((TAIL, span), lambda i: (0, i)),
        ],
        out_shape=[
            jax.ShapeDtypeStruct((rows, model), bf16),
            jax.ShapeDtypeStruct((model, 2 * channels), bf16),
            jax.ShapeDtypeStruct((rows, channels), f32),
            jax.ShapeDtypeStruct((rows, channels), f32),
            jax.ShapeDtypeStruct((TAIL, rows), f32),
        ],
        compiler_params=pltpu.CompilerParams(
            dimension_semantics=("arbitrary",), vmem_limit_bytes=LIMIT
        ),
        name="gate_forward",
    )(spot, normed, own, *others, *sources, gain, ssm)


def norm_kernel(full_inner, chips, split, spot_ref, sums_ref, more_ref, gate_ref, grad_ref, ssm_ref,
                gain_ref, normed_ref, upstream_ref, gate_w_ref, out_w_ref, grad_gate_ref,
                grad_ssm_ref, gain_sum_ref, keep_ref, send_ref, mine_ref, theirs_ref, norm_sum_ref,
                scaled, totals):
    rows, channels = gate_ref.shape
    block = pl.program_id(0)

    @pl.when(block == 0)
    def _():
        gain_sum_ref[...] = jnp.zeros_like(gain_sum_ref)
        totals[...] = jnp.zeros_like(totals)

    sums = sums_ref[...] + more_ref[...] if split else sums_ref[...]
    sums = jnp.transpose(jnp.concatenate([sums, jnp.zeros((LANES - TAIL, rows), f32)], axis=0))
    scale = lax.rsqrt(sums[:, 0:1] / full_inner + EPSILON)
    pull = scale * scale * scale * (sums[:, 1:2] / full_inner)
    normed_t = jnp.transpose(normed_ref[...])
    upstream_t = jnp.transpose(upstream_ref[...])
    step = 2 * LANES
    for lo in range(0, channels, step):
        hi = lo + step
        gain = gain_ref[:, lo:hi]
        gate, grad, ssm = gate_ref[:, lo:hi], grad_ref[:, lo:hi], ssm_ref[:, lo:hi]
        sig = sigmoid(gate)
        silu = gate * sig
        gated = ssm * silu
        normal = gated * scale
        scaled_low = (normal * gain).astype(bf16)
        scaled[:, lo:hi] = scaled_low
        gain_sum_ref[TAIL - 1 : TAIL, lo:hi] += jnp.sum(grad * normal, axis=0, keepdims=True)
        grad_gated = scale * (grad * gain) - gated * pull
        grad_ssm_ref[:, lo:hi] = grad_gated * silu
        grad_gate = (grad_gated * ssm * (sig * (1.0 + gate * (1.0 - sig)))).astype(bf16)
        grad_gate_ref[:, lo:hi] = grad_gate
        totals[:, lo:hi] += mm(normed_t, grad_gate, NN)
        totals[:, channels + lo : channels + hi] += mm(upstream_t, scaled_low, NN)
    branch = mm(scaled[...], out_w_ref[...], NT).astype(bf16)
    if split:
        half = pl.num_programs(0) // 2
        at = pl.ds(pl.multiple_of(lax.rem(block, half) * rows, rows), rows)

        @pl.when(block // half == spot_ref[0, 0])
        def _():
            mine_ref[at, :] = branch

        @pl.when(block // half != spot_ref[0, 0])
        def _():
            theirs_ref[at, :] = branch
    else:
        mine_ref[pl.ds(pl.multiple_of(block * rows, rows), rows), :] = branch

        @pl.when(block == 0)
        def _():
            theirs_ref[...] = jnp.zeros_like(theirs_ref)

    @pl.when(block == pl.num_programs(0) - 1)
    def _():
        split_cores(spot_ref, totals, keep_ref, [send_ref], chips)
        norm_sum_ref[...] = jnp.zeros_like(norm_sum_ref)
        norm_sum_ref[0:1, :] = gain_row(gate_w_ref, totals, (0, channels))


def gate_norm(
    spot, sums, more, gate, grad, ssm, gain, normed, upstream, weight, known, full_inner, chips, split, span
):
    rows, channels = gate.shape
    model = normed.shape[1]
    by_row = lambda cols: pl.BlockSpec((span, cols), lambda i: (i, 0))
    stats = pl.BlockSpec((TAIL, span), lambda i: (0, i))
    half = (model // 2, 2 * channels)
    mine = (rows // 2 if split else rows, model)
    theirs = (rows // 2 if split else TAIL * 2, model)
    return pl.pallas_call(
        partial(norm_kernel, float(full_inner), chips, split),
        grid=(rows // span,),
        in_specs=[
            pl.BlockSpec(memory_space=pltpu.SMEM), stats, stats, by_row(channels), by_row(channels),
            by_row(channels), full(gain.shape), by_row(model), by_row(model),
            pl.BlockSpec((model, channels), lambda i: (0, 0)),
            pl.BlockSpec((model, channels), lambda i: (0, 1)),
        ],
        out_specs=[
            by_row(channels), by_row(channels), full((TAIL, known)), full(half), full(half),
            full(mine), full(theirs), full((TAIL, model)),
        ],
        out_shape=[
            jax.ShapeDtypeStruct((rows, channels), bf16),
            jax.ShapeDtypeStruct((rows, channels), f32),
            jax.ShapeDtypeStruct((TAIL, known), f32),
            jax.ShapeDtypeStruct(half, bf16),
            jax.ShapeDtypeStruct(half, bf16),
            jax.ShapeDtypeStruct(mine, bf16),
            jax.ShapeDtypeStruct(theirs, bf16),
            jax.ShapeDtypeStruct((TAIL, model), f32),
        ],
        scratch_shapes=[
            pltpu.VMEM((span, channels), bf16),
            pltpu.VMEM((model, 2 * channels), f32),
        ],
        compiler_params=pltpu.CompilerParams(
            dimension_semantics=("arbitrary",), vmem_limit_bytes=LIMIT
        ),
        name="gate_norm",
    )(spot, sums, more, gate, grad, ssm, gain, normed, upstream, weight, weight)


def lanes_of(vector):
    return jnp.pad(vector, (0, LANES - vector.shape[0]))[None, :]


def spread_map(heads, channels):
    size = channels // heads
    row = lax.broadcasted_iota(jnp.int32, (2 * LANES, channels), 0) % LANES
    col = lax.broadcasted_iota(jnp.int32, (2 * LANES, channels), 1) // size
    return (row == col).astype(bf16)


def dp_send(value, bit):
    size = lax.axis_size("dp")
    return lax.ppermute(value, "dp", [(i, i ^ bit) for i in range(size)])


def chip_bits():
    return [4 * k for k in range(1, lax.axis_size("dp") // 4)]


def long_bits():
    bits, bit = [], 4
    while bit < lax.axis_size("dp"):
        bits.append(bit)
        bit *= 2
    return bits


def choose(stacked, index, axis):
    return lax.dynamic_index_in_dim(stacked, index, axis, keepdims=False)


def send_fold(parts, bit, axis):
    mine = (lax.axis_index("dp") // bit) % 2
    return dp_send(choose(parts, 1 - mine, axis), bit)


def keep_fold(parts, got, bit, axis):
    mine = (lax.axis_index("dp") // bit) % 2
    return choose(parts, mine, axis).astype(f32) + got.astype(f32)


def fold(parts, bit, axis):
    return keep_fold(parts, send_fold(parts, bit, axis), bit, axis)


def send_chips(parts):
    place = lax.axis_index("dp") // 4
    sends = parts.astype(bf16)
    return [dp_send(choose(sends, place ^ (bit // 4), 0), bit) for bit in chip_bits()]


def keep_chips(parts, got):
    total = choose(parts, lax.axis_index("dp") // 4, 0).astype(f32)
    for piece in got:
        total = total + piece.astype(f32)
    return total


def fold_chips(parts):
    return keep_chips(parts, send_chips(parts))


def tensor_swap(value):
    return lax.ppermute(value, "tensor", [(0, 1), (1, 0)])


def gather_other(own, size):
    if size != 2:
        return lax.all_gather(own, "tensor", axis=0, tiled=True)
    return tensor_swap(own)


def join_pieces(own, top, bottom, size):
    top = top.reshape(size, -1, own.shape[1])
    bottom = bottom.reshape(size, -1, own.shape[1])
    return jnp.concatenate([top, bottom], axis=1).reshape(-1, own.shape[1])


def pick_half(lower, upper, size):
    if size != 2:
        return lower
    return jnp.where(lax.axis_index("tensor") == 0, lower, upper)


def sum_quarters(quarters, other0, other1, size):
    if size != 2:
        whole = jnp.concatenate(quarters, axis=0)
        return lax.psum_scatter(whole, "tensor", scatter_dimension=0, tiled=True).astype(f32)
    first = lax.axis_index("tensor") == 0
    each = other0.shape[0]
    low, middle, high = quarters
    lower = jnp.concatenate([low, middle[:each]], axis=0)
    upper = jnp.concatenate([middle[each:], high], axis=0)
    others = jnp.concatenate([other0, other1], axis=0)
    return jnp.where(first, lower, upper).astype(f32) + others.astype(f32)


def tensor_sum(value, size):
    if size != 2:
        return lax.psum(value, "tensor")
    return value + tensor_swap(value)


def shards(
    tokens, lengths, norm_gain, zx_weight, bc_weight, dt_weight, conv_inner, bias_inner,
    conv_shared, bias_shared, step_bias, log_rate, skip_gain, gate_gain, out_weight, cotangent,
):
    size = lax.axis_size("tensor")
    split = size == 2
    me = lax.axis_index("dp")
    count = len(chip_bits()) + 1
    spot = jnp.stack([lax.axis_index("tensor"), me // 4, (me // 2) % 2, me % 2])[None, :]
    spot = spot.astype(jnp.int32)
    channels = zx_weight.shape[2]
    heads = step_bias.shape[0]
    width = bc_weight.shape[1]
    known = channels + width + LANES
    step_weight = jnp.pad(dt_weight, ((0, 0), (0, LANES - heads)))
    early = jnp.concatenate([zx_weight[:, 1, :], bc_weight, step_weight], axis=1)
    inputs = tokens.astype(f32)
    norm_scale = lax.rsqrt(jnp.mean(inputs * inputs, axis=1, keepdims=True) + EPSILON)
    normed_rows = (inputs * norm_scale * norm_gain[None, :]).astype(bf16)
    half = normed_rows.shape[0] // 2
    fixed = (
        conv_inner, bias_inner[None, :], conv_shared, bias_shared[None, :], lanes_of(step_bias),
        lanes_of(-jnp.exp(log_rate)), jnp.repeat(skip_gain, channels // heads)[None, :],
        spread_map(heads, channels),
    )
    late = jnp.concatenate([zx_weight[:, 0, :], out_weight], axis=1)
    def along(value):
        return [value] + [dp_send(value, bit) for bit in chip_bits()]

    column = jnp.concatenate(along(early), axis=0)
    column, pair, top, fixed, spot = lax.optimization_barrier((
        column, jnp.concatenate([late, dp_send(late, 2)], axis=0),
        gather_other(normed_rows[:half], size), fixed, spot,
    ))
    cut_late = (2 * channels * 3 // 8) // LANES * LANES
    joined = along(pair[:, :cut_late])
    by_x, column, bottom, joined, pair = lax.optimization_barrier(
        (dp_send(column, 2), column, gather_other(normed_rows[half:], size), joined, pair)
    )
    joined = jnp.concatenate(joined, axis=0)
    pairs = along(pair[:, cut_late:])
    by_core = dp_send(column, 1)
    sources = (column, by_x, by_core, dp_send(by_x, 1))
    own, others = normed_rows, (top, bottom)
    if not split:
        own, others = join_pieces(normed_rows, top, bottom, size), ()
    normed, weight, *saved = mixer_forward(
        spot, lengths, own, others, sources, count, *fixed, SPAN
    )
    _, _, _, _, _, rate, skip, spread = fixed
    gain = gate_gain[None, :]
    other, ssm, joined_core, pairs = lax.optimization_barrier(
        (gather_other(cotangent, size), saved[0], dp_send(joined, 1), pairs)
    )
    sources = (joined, joined_core, *pairs, *[dp_send(pair, 1) for pair in pairs])
    own, others = (cotangent, (other,)) if split else (other, ())
    upstream, weight_late, gate, grad, sums = gate_forward(
        spot, normed, own, others, sources, count, gain, ssm, SPAN
    )
    more = gather_other(sums, size) if split else sums
    sums = sums if split else lax.psum(sums, "tensor")
    chips = 2 * count
    grad_gate, grad_ssm, gain_sum, keep, send, branch_own, branch_send, norm_sum = gate_norm(
        spot, sums, more, gate, grad, ssm, gain, normed, upstream, weight_late, known, channels * size,
        chips, split, SPAN,
    )
    if split:
        branch_other = gather_other(branch_send, size)
    else:
        branch_own = lax.psum_scatter(branch_own, "tensor", scatter_dimension=0, tiled=True)
        branch_other = jnp.zeros_like(branch_own)
    quarter = grad_ssm.shape[0] // SPAN // 4
    carry = (gain_sum,)

    def back(begin, end, carry):
        return mixer_backward(
            lengths, grad_ssm, saved, conv_inner, conv_shared, rate, skip, spread, grad_gate,
            weight_late, weight, carry, (begin * quarter, end * quarter), SPAN,
        )

    first = dp_send(send, 1)
    grads3, terms3, carry = back(3, 4, carry)
    first = (keep.astype(f32) + first.astype(f32)).astype(bf16)
    first = first.reshape(count, 2, -1, first.shape[1])
    carry, first = lax.optimization_barrier((carry, first))
    first_gate, first_out = first[..., :channels], first[..., channels:]
    grads1, terms1, carry = back(1, 3, carry)
    first_gate = fold(first_gate, 2, 1)
    first_out = fold_chips(first_out).astype(bf16)
    each = terms3.shape[0]
    send1 = pick_half(terms3, terms1[:each], size)
    carry, send1, branch_other, first_gate, first_out = lax.optimization_barrier(
        (carry, send1, branch_other, first_gate, first_out)
    )
    other1 = gather_other(send1, size) if split else send1
    part_gate = fold_chips(first_gate)
    part_out = fold(first_out, 2, 0)
    grads0, terms0, carry = back(0, 1, carry)
    sums, part_gate, part_out, grads0, other1, terms0 = lax.optimization_barrier(
        (carry[0], part_gate, part_out, grads0, other1, terms0)
    )
    send0 = pick_half(terms1[each:], terms0, size)
    send0, grads0 = lax.optimization_barrier((send0, grads0))
    other0 = gather_other(send0, size) if split else send0
    keep, *send, sums, shared_sums = weight_products(
        spot, normed, weight, norm_gain[None, :], sums, norm_sum, (grads0, grads1, grads3), chips,
        width,
    )
    got = [dp_send(piece, 1) for piece in send]
    *got, other0, sums, shared_sums, keep = lax.optimization_barrier(
        (*got, other0, sums, shared_sums, keep)
    )
    got = jnp.concatenate(got, axis=0)
    parts = (keep.astype(f32) + got.astype(f32)).astype(bf16).reshape(count, 2, -1, known)
    cut = min((known * 2 // 3) // LANES * LANES, channels)
    parts_a, parts_b = parts[..., :cut], parts[..., cut:]
    got_a = send_fold(parts_a, 2, 1)
    got_b = send_chips(parts_b)
    shared_sums = tensor_sum(shared_sums, size)
    shared_sums, other0 = lax.optimization_barrier((shared_sums, other0))
    sums = jnp.concatenate([sums, shared_sums], axis=1)
    sums = sums + dp_send(sums, 1)
    sums = sums + dp_send(sums, 2)
    grad_normed = sum_quarters((terms0, terms1, terms3), other0, other1, size)
    scaled_grad = grad_normed * norm_gain[None, :]
    grad_inputs = norm_scale * scaled_grad - inputs * norm_scale**3 * jnp.mean(
        scaled_grad * inputs, axis=1, keepdims=True
    )
    grad_tokens = (cotangent.astype(f32) + grad_inputs).astype(bf16)
    got_a, got_b, sums, grad_tokens, branch_other = lax.optimization_barrier(
        (got_a, got_b, sums, grad_tokens, branch_other)
    )
    block_out = (inputs + (branch_own.astype(f32) + branch_other.astype(f32))).astype(bf16)
    parts_a = keep_fold(parts_a, got_a, 2, 1)
    parts_b = keep_chips(parts_b, got_b).astype(bf16)
    got_a = send_chips(parts_a)
    parts_b = fold(parts_b, 2, 0)
    for bit in long_bits():
        sums = sums + dp_send(sums, bit)
    parts_a = keep_chips(parts_a, got_a)
    shared_sums = sums[:, channels + LANES :]
    norm_sum = shared_sums[0, width:]
    part_inner = jnp.concatenate([parts_a, parts_b[:, : channels - cut]], axis=1)
    at_step = channels + width
    part_shared = tensor_sum(parts_b[:, channels - cut : at_step - cut], size)
    part_step = parts_b[:, at_step - cut : at_step - cut + heads]
    part_in = jnp.stack([part_gate, part_inner], axis=1)
    return (
        block_out,
        grad_tokens,
        norm_sum,
        part_in,
        part_shared,
        part_step,
        sums[:TAPS, :channels],
        sums[TAPS, :channels],
        shared_sums[:TAPS, :width],
        shared_sums[TAPS, :width],
        sums[0, channels : channels + heads],
        sums[1, channels : channels + heads],
        sums[2, channels : channels + heads],
        sums[TAIL - 1, :channels],
        part_out,
    )


def solution(mesh):
    return jax.shard_map(
        shards,
        mesh=mesh,
        in_specs=(
            P(("dp", "tensor"), None),
            P("dp", None),
            P(),
            P("dp", None, "tensor"),
            P("dp", None),
            P("dp", "tensor"),
            P(None, "tensor"),
            P("tensor"),
            P(),
            P(),
            P("tensor"),
            P("tensor"),
            P("tensor"),
            P("tensor"),
            P("dp", "tensor"),
            P(("dp", "tensor"), None),
        ),
        out_specs=(
            P(("dp", "tensor"), None),
            P(("dp", "tensor"), None),
            P(),
            P("dp", None, "tensor"),
            P("dp", None),
            P("dp", "tensor"),
            P(None, "tensor"),
            P("tensor"),
            P(),
            P(),
            P("tensor"),
            P("tensor"),
            P("tensor"),
            P("tensor"),
            P("dp", "tensor"),
        ),
        check_vma=False,
    )
```

```python
from functools import partial

import jax
import jax.numpy as jnp
from jax import lax
from jax.experimental import pallas as pl
from jax.experimental.pallas import tpu as pltpu
from jax.sharding import PartitionSpec as P

EPSILON = 1e-05
SPAN = 256
LANES = 128
TAIL = 8
TAPS = 4
MASKED = -1e30
f32 = jnp.float32
bf16 = jnp.bfloat16
LIMIT = 60 * 1024 * 1024


def mm(left, right, dims):
    return lax.dot_general(left, right, ((dims[0], dims[1]), ((), ())), preferred_element_type=f32)


NN = ((1,), (0,))
NT = ((1,), (1,))
TN = ((0,), (0,))


def halves(value, axis):
    high = value.astype(bf16)
    low = (value - high.astype(f32)).astype(bf16)
    return jnp.concatenate([high, low], axis=axis)


def sigmoid(value):
    return 1.0 / (1.0 + jnp.exp(-value))


def softplus(value):
    return jnp.maximum(value, 0.0) + jnp.log1p(jnp.exp(-jnp.abs(value)))


def segment_at(ends, position):
    total = jnp.zeros(position.shape, jnp.int32)
    for end in ends:
        total = total + (position >= end).astype(jnp.int32)
    return total


def sequence_ends(lengths_ref):
    ends, total = [], 0
    for i in range(lengths_ref.shape[1]):
        total = total + lengths_ref[0, i]
        ends.append(total)
    return ends


def step_parts(step_raw, rate, ends, base):
    rows = step_raw.shape[0]
    step = softplus(step_raw)
    row = lax.broadcasted_iota(jnp.int32, (rows, rows), 0)
    col = lax.broadcasted_iota(jnp.int32, (rows, rows), 1)
    lower = (row >= col).astype(f32).astype(bf16)
    split = mm(lower, halves(step * rate, 1), NN)
    running = split[:, :LANES] + split[:, LANES:]
    position = base + lax.broadcasted_iota(jnp.int32, (rows, 1), 0)
    segment = segment_at(ends, position)
    before = segment_at(ends, jnp.full((1, 1), base - 1, jnp.int32))
    last = segment_at(ends, jnp.full((1, 1), base + rows - 1, jnp.int32))
    carried = ((segment == before) & (position >= rows)).astype(f32)
    matched = (segment == last).astype(f32)
    entry = jnp.exp(running) * carried
    leave = jnp.exp(running[rows - 1 :, :] - running) * matched
    return step, running, entry, leave, lower, segment, row, col


def same_rows(ends, base, rows):
    across = segment_at(ends, base + lax.broadcasted_iota(jnp.int32, (1, rows), 1))
    down = segment_at(ends, base + lax.broadcasted_iota(jnp.int32, (rows, 1), 0))
    return down == across


def rows_of(block, blocks, spot_ref, own_ref, others):
    if not others:
        return own_ref[...]
    half = blocks // 2
    local = lax.rem(block, half)
    span = own_ref.shape[0] // half
    each = half // len(others)
    value = None
    for i, ref in enumerate(others):
        at = lax.rem(local, each) * span
        piece = ref[pl.ds(pl.multiple_of(at, span), span), :]
        value = piece if i == 0 else jnp.where(local >= i * each, piece, value)
    mine = own_ref[pl.ds(pl.multiple_of(local * span, span), span), :]
    return jnp.where(block // half == spot_ref[0, 0], mine, value)


def own_specs(own, others, span):
    if not others:
        return [pl.BlockSpec((span, own.shape[1]), lambda i: (i, 0))]
    return [full(own.shape), *[full(other.shape) for other in others]]


def run_copies(copies):
    for copy in copies:
        copy.start()
    for copy in copies:
        copy.wait()


def place_weights(spot_ref, weight_ref, sources, count, done):
    rows = weight_ref.shape[0] // (4 * count)
    copies = []
    for i, ref in enumerate(sources):
        along = spot_ref[0, 2] ^ (i % 2)
        core = spot_ref[0, 3] ^ (i // 2)
        for k in range(count):
            at = (((spot_ref[0, 1] ^ k) * 2 + along) * 2 + core) * rows
            copies.append(pltpu.make_async_copy(
                ref.at[pl.ds(k * rows, rows), :],
                weight_ref.at[pl.ds(pl.multiple_of(at, rows), rows), :],
                done.at[i * count + k],
            ))
    run_copies(copies)


def place_columns(spot_ref, weight_ref, sources, count):
    rows = weight_ref.shape[0] // (4 * count)
    for i, ref in enumerate(sources):
        along = spot_ref[0, 2] ^ (i % 2)
        core = spot_ref[0, 3] ^ (i // 2)
        for k in range(count):
            at = (((spot_ref[0, 1] ^ k) * 2 + along) * 2 + core) * rows
            at = pl.ds(pl.multiple_of(at, rows), rows)
            weight_ref[at, : ref.shape[1]] = ref[k * rows : (k + 1) * rows, :]


def place_pairs(spot_ref, weight_ref, sources, count, lo):
    rows = weight_ref.shape[0] // (4 * count)
    for i, (ref, begin) in enumerate(sources):
        core = spot_ref[0, 3] ^ (i // count)
        for j in range(2):
            at = (((spot_ref[0, 1] ^ (i % count)) * 2 + (spot_ref[0, 2] ^ j)) * 2 + core) * rows
            at = pl.ds(pl.multiple_of(at, rows), rows)
            here = begin + j * rows
            weight_ref[at, lo : lo + ref.shape[1]] = ref[here : here + rows, :]


def split_cores(spot_ref, value_ref, keep_ref, send_refs, chips):
    rows = keep_ref.shape[0] // chips
    each = chips // len(send_refs)
    core = spot_ref[0, 3]
    for chip in range(chips):
        here = pl.ds(pl.multiple_of((2 * chip + core) * rows, rows), rows)
        there = pl.ds(pl.multiple_of((2 * chip + 1 - core) * rows, rows), rows)
        keep_ref[chip * rows : (chip + 1) * rows, :] = value_ref[here, :].astype(bf16)
        at = (chip % each) * rows
        send_refs[chip // each][at : at + rows, :] = value_ref[there, :].astype(bf16)


def forward_kernel(
    pieces, count, spot_ref, lengths_ref, *refs
):
    own_ref, others = refs[0], refs[1:pieces]
    sources = refs[pieces : pieces + 4]
    (
        conv_inner_ref, bias_inner_ref, conv_shared_ref, bias_shared_ref, step_bias_ref, rate_ref,
        skip_ref, spread_ref, normed_ref, weight_ref, ssm_ref, inner_ref, pre_inner_ref, shared_ref,
        pre_shared_ref, step_ref, entering_ref, inner_tail, shared_tail, state, done,
    ) = refs[pieces + 4 :]
    block = pl.program_id(0)
    rows = normed_ref.shape[0]
    channels = conv_inner_ref.shape[1]
    base = block * rows
    ends = sequence_ends(lengths_ref)

    @pl.when(block == 0)
    def _():
        inner_tail[0:TAIL, :] = jnp.zeros((TAIL, channels), f32)
        shared_tail[0:TAIL, :] = jnp.zeros((TAIL, shared_tail.shape[1]), f32)
        state[...] = jnp.zeros_like(state)
        place_weights(spot_ref, weight_ref, sources, count, done)

    @pl.when(block > 0)
    def _():
        inner_tail[0:TAIL, :] = inner_tail[rows : rows + TAIL, :]
        shared_tail[0:TAIL, :] = shared_tail[rows : rows + TAIL, :]

    normed = rows_of(block, pl.num_programs(0), spot_ref, own_ref, others)
    normed_ref[...] = normed
    small = mm(normed, weight_ref[:, channels:], NN)
    width = conv_shared_ref.shape[1]
    shared_proj = small[:, :width]
    shared_tail[TAIL : TAIL + rows, :] = shared_proj
    shared_ref[...] = shared_proj
    step_raw = small[:, width:] + step_bias_ref[...]
    step_ref[...] = step_raw
    inner_proj = mm(normed, weight_ref[:, :channels], NN)
    inner_tail[TAIL : TAIL + rows, :] = inner_proj
    inner_ref[...] = inner_proj

    step, running, entry, leave, lower, segment, row, col = step_parts(
        step_raw, rate_ref[...], ends, base
    )
    position = base + lax.broadcasted_iota(jnp.int32, (rows, 1), 0)
    keeps = [
        ((segment_at(ends, position - k) == segment) & (position >= k)).astype(f32)
        for k in range(1, TAPS)
    ]
    keeps = [jnp.broadcast_to(keep, (rows, LANES)) for keep in keeps]

    def conv(tail, taps_ref, bias_ref, lo, hi):
        total = bias_ref[:, lo:hi] + taps_ref[TAPS - 1 : TAPS, lo:hi] * tail[TAIL : TAIL + rows, lo:hi]
        for k in range(1, TAPS):
            shifted = tail[TAIL - k : TAIL - k + rows, lo:hi]
            total = total + taps_ref[TAPS - 1 - k : TAPS - k, lo:hi] * (shifted * keeps[k - 1])
        return total

    pre_shared = jnp.concatenate(
        [
            conv(shared_tail, conv_shared_ref, bias_shared_ref, lo, lo + LANES)
            for lo in range(0, width, LANES)
        ],
        axis=1,
    )
    pre_shared_ref[...] = pre_shared
    shared = pre_shared * sigmoid(pre_shared)
    in_map = shared[:, : width // 2].astype(bf16)
    out_map = shared[:, width // 2 :].astype(bf16)
    scores = mm(out_map, in_map, NT)
    in_map_t = jnp.transpose(in_map)
    allowed = jnp.where((row >= col) & same_rows(ends, base, rows), 0.0, MASKED)
    running_t = jnp.transpose(running)
    factors = jnp.concatenate([halves(x, 1) for x in (step, entry, leave)], axis=0)
    lane = lax.broadcasted_iota(jnp.int32, (rows, LANES), 1)
    for pair in range(channels // LANES):
        lo, hi = pair * LANES, (pair + 1) * LANES
        pre = conv(inner_tail, conv_inner_ref, bias_inner_ref, lo, hi)
        pre_inner_ref[:, lo:hi] = pre
        head_in = pre * sigmoid(pre)
        side = (pair % 2) * LANES
        if side == 0:
            spread = spread_ref[:, lo : min(lo + 2 * LANES, channels)]
            wide = mm(factors, spread, NN)
        step_wide, entry_wide, leave_wide = [
            wide[i * rows : (i + 1) * rows, side : side + LANES] for i in range(3)
        ]
        scaled = head_in * step_wide
        scaled_low = scaled.astype(bf16)
        held = state[:, lo:hi]
        entering_ref[0, :, lo:hi] = held
        carried_out = mm(out_map, held.astype(bf16), NN) * entry_wide
        parts = []
        for parity in range(2):
            head = 2 * pair + parity
            gap = running[:, head : head + 1] - running_t[head : head + 1, :]
            parts.append((scores * jnp.exp(gap + allowed)).astype(bf16))
        both = mm(jnp.concatenate(parts, axis=0), scaled_low, NN)
        intra = jnp.where(lane < LANES // 2, both[:rows], both[rows:])
        ssm_ref[:, lo:hi] = carried_out + intra + skip_ref[:, lo:hi] * head_in
        added = mm(in_map_t, (scaled * leave_wide).astype(bf16), NN)
        state[:, lo:hi] = held * entry_wide[rows - 1 :, :] + added


def full(shape):
    return pl.BlockSpec(shape, lambda *_: (0,) * len(shape))


def mixer_forward(
    spot, lengths, own, others, sources, count, conv_inner, bias_inner, conv_shared, bias_shared,
    step_bias, rate, skip, spread, span,
):
    rows = own.shape[0] * (2 if others else 1)
    model = own.shape[1]
    channels = conv_inner.shape[1]
    width = conv_shared.shape[1]
    known = channels + width + LANES
    blocks = rows // span
    by_row = lambda cols: pl.BlockSpec((span, cols), lambda i: (i, 0))
    shape = lambda cols: jax.ShapeDtypeStruct((rows, cols), f32)
    states = width // 2
    smem = pl.BlockSpec(memory_space=pltpu.SMEM)
    fixed = (conv_inner, bias_inner, conv_shared, bias_shared, step_bias, rate, skip, spread)
    return pl.pallas_call(
        partial(forward_kernel, 1 + len(others), count),
        grid=(blocks,),
        in_specs=[
            smem, smem, *own_specs(own, others, span),
            *[pl.BlockSpec(memory_space=pl.ANY) for _ in sources],
            *[full(x.shape) for x in fixed],
        ],
        out_specs=[
            by_row(model), full((model, known)), by_row(channels), by_row(channels),
            by_row(channels), by_row(width), by_row(width), by_row(LANES),
            pl.BlockSpec((1, states, channels), lambda i: (i, 0, 0)),
        ],
        out_shape=[
            jax.ShapeDtypeStruct((rows, model), bf16), jax.ShapeDtypeStruct((model, known), bf16),
            shape(channels), shape(channels), shape(channels), shape(width), shape(width),
            shape(LANES), jax.ShapeDtypeStruct((blocks, states, channels), f32),
        ],
        scratch_shapes=[
            pltpu.VMEM((TAIL + span, channels), f32),
            pltpu.VMEM((TAIL + span, width), f32),
            pltpu.VMEM((states, channels), f32),
            pltpu.SemaphoreType.DMA((4 * count,)),
        ],
        compiler_params=pltpu.CompilerParams(
            dimension_semantics=("arbitrary",), vmem_limit_bytes=LIMIT
        ),
        name="mixer_forward",
    )(spot, lengths, own, *others, *sources, *fixed)


def backward_kernel(
    first_block, total_rows, lengths_ref, upstream_ref, ssm_ref, inner_ref, pre_inner_ref,
    shared_ref, pre_shared_ref, step_ref, entering_ref, conv_inner_ref, conv_shared_ref, rate_ref, skip_ref, spread_ref,
    grad_gate_ref, gate_w_ref, weight_ref, sums_in_ref, *refs,
):
    carried_in, refs = refs[:-11], refs[-11:]
    (
        grads_ref, terms_ref, sums_ref, inner_out_ref, shared_out_ref, adjoint, inner_head,
        shared_head, gate_w, weight, done,
    ) = refs
    turn = pl.program_id(0)
    block = first_block + pl.num_programs(0) - 1 - turn
    rows, channels = upstream_ref.shape
    width = conv_shared_ref.shape[1]
    base = block * rows
    ends = sequence_ends(lengths_ref)

    def weight_copies():
        return (
            pltpu.make_async_copy(gate_w_ref.at[:, pl.ds(0, channels)], gate_w, done.at[0]),
            pltpu.make_async_copy(weight_ref, weight, done.at[1]),
        )

    @pl.when(turn == 0)
    def _():
        if carried_in:
            inner_head[rows : rows + TAIL, :] = carried_in[0][...]
            shared_head[rows : rows + TAIL, :] = carried_in[1][...]
            adjoint[...] = carried_in[2][...]
        else:
            inner_head[rows : rows + TAIL, :] = jnp.zeros((TAIL, channels), f32)
            shared_head[rows : rows + TAIL, :] = jnp.zeros((TAIL, width), f32)
            adjoint[...] = jnp.zeros_like(adjoint)
        sums_ref[...] = sums_in_ref[...]
        for copy in weight_copies():
            copy.start()

    @pl.when(turn > 0)
    def _():
        inner_head[rows : rows + TAIL, :] = inner_head[0:TAIL, :]
        shared_head[rows : rows + TAIL, :] = shared_head[0:TAIL, :]

    step_raw = step_ref[...]
    rate = rate_ref[...]
    step, running, entry, leave, lower, segment, row, col = step_parts(step_raw, rate, ends, base)
    position = base + lax.broadcasted_iota(jnp.int32, (rows, 1), 0)
    keeps = [
        ((segment_at(ends, position + k) == segment) & (position + k < total_rows)).astype(f32)
        for k in range(1, TAPS)
    ]
    keeps = [jnp.broadcast_to(keep, (rows, LANES)) for keep in keeps]
    pre_shared = pre_shared_ref[...]
    shared_gate = sigmoid(pre_shared)
    shared = pre_shared * shared_gate
    half = width // 2
    in_map = shared[:, :half].astype(bf16)
    out_map = shared[:, half:].astype(bf16)
    scores_t = mm(in_map, out_map, NT)
    out_map_t = jnp.transpose(out_map)
    allowed_t = jnp.where((col >= row) & same_rows(ends, base, rows), 0.0, MASKED)
    running_t = jnp.transpose(running)
    factors = jnp.concatenate([halves(x, 1) for x in (step, entry, leave)], axis=0)
    lane = lax.broadcasted_iota(jnp.int32, (rows, LANES), 1)
    first_half = lane < LANES // 2
    grad_scores_t = jnp.zeros((rows, rows), f32)
    grad_in = jnp.zeros((rows, half), f32)
    grad_out = jnp.zeros((rows, half), f32)
    by_head = jnp.zeros((rows + TAIL, LANES), f32)
    step_terms = jnp.zeros((rows, LANES), f32)
    for pair in range(channels // LANES):
        lo, hi = pair * LANES, (pair + 1) * LANES
        side = (pair % 2) * LANES
        if side == 0:
            spread = spread_ref[:, lo : min(lo + 2 * LANES, channels)]
            wide = mm(factors, spread, NN)
            products = []
        step_wide, entry_wide, leave_wide = [
            wide[i * rows : (i + 1) * rows, side : side + LANES] for i in range(3)
        ]
        pre = pre_inner_ref[:, lo:hi]
        gate = sigmoid(pre)
        head_in = pre * gate
        skip = skip_ref[:, lo:hi]
        upstream = upstream_ref[:, lo:hi]
        upstream_low = upstream.astype(bf16)
        upstream_back = upstream_low.astype(f32)
        scaled = head_in * step_wide
        scaled_low = scaled.astype(bf16)
        scaled_back = scaled_low.astype(f32)
        held = entering_ref[0, :, lo:hi]
        held_low = held.astype(bf16)
        ahead = adjoint[:, lo:hi]
        ahead_low = ahead.astype(bf16)
        entry_up = (upstream_back * entry_wide).astype(bf16)
        grad_out = grad_out + mm(entry_up, held_low, NT)
        grad_in = grad_in + mm((scaled * leave_wide).astype(bf16), ahead_low, NT)
        grad_scaled = mm(in_map, ahead_low, NN) * leave_wide
        through = entry_wide[rows - 1 :, :]
        tail_terms = jnp.sum(scaled_back * grad_scaled, axis=0, keepdims=True) + through * jnp.sum(
            ahead * held, axis=0, keepdims=True
        )
        adjoint[:, lo:hi] = ahead * through + mm(out_map_t, entry_up, NN)
        parts, decays, chosen = [], [], []
        for parity in range(2):
            head = 2 * pair + parity
            gap = running_t[head : head + 1, :] - running[:, head : head + 1]
            decays.append(jnp.exp(gap + allowed_t))
            parts.append((scores_t * decays[parity]).astype(bf16))
            mine = first_half if parity == 0 else jnp.logical_not(first_half)
            chosen.append(jnp.where(mine, scaled_back, 0.0).astype(bf16))
        both = mm(jnp.concatenate(parts, axis=0), upstream_low, NN)
        pulled = mm(jnp.concatenate(chosen, axis=0), upstream_low, NT)
        grad_scores_t = grad_scores_t + (pulled[:rows] * decays[0] + pulled[rows:] * decays[1])
        grad_scaled = grad_scaled + jnp.where(first_half, both[:rows], both[rows:])
        spread_one = spread[:LANES, side : side + LANES]
        spread_both = jnp.concatenate([spread_one, spread_one], axis=1)
        balance = upstream_back * (ssm_ref[:, lo:hi] - skip * head_in) - scaled_back * grad_scaled
        products.append((head_in * grad_scaled).astype(bf16))
        if hi == channels or side > 0:
            joined = jnp.concatenate(products, axis=1)
            step_terms = step_terms + mm(joined, spread[:LANES, :], NT)
        skip_terms = jnp.sum(upstream * head_in, axis=0, keepdims=True)
        edge = jnp.concatenate([tail_terms, skip_terms, jnp.zeros((TAIL - 2, LANES), f32)], axis=0)
        by_head = by_head + mm(
            halves(jnp.concatenate([balance, edge], axis=0), 1), spread_both, NT
        )
        grad_pre = (grad_scaled * step_wide + skip * upstream) * (gate * (1.0 + pre * (1.0 - gate)))
        inner_head[0:rows, lo:hi] = grad_pre
        inner_proj = inner_ref[:, lo:hi]
        grad_proj = conv_inner_ref[TAPS - 1 : TAPS, lo:hi] * grad_pre
        sums = [None] * TAPS
        sums[TAPS - 1] = jnp.sum(grad_pre * inner_proj, axis=0, keepdims=True)
        for k in range(1, TAPS):
            moved = inner_head[k : k + rows, lo:hi] * keeps[k - 1]
            grad_proj = grad_proj + conv_inner_ref[TAPS - 1 - k : TAPS - k, lo:hi] * moved
            sums[TAPS - 1 - k] = jnp.sum(moved * inner_proj, axis=0, keepdims=True)
        grads_ref[:, lo:hi] = grad_proj.astype(bf16)
        sums.append(jnp.sum(grad_pre, axis=0, keepdims=True))
        sums.append(jnp.zeros((TAIL - len(sums), LANES), f32))
        sums_ref[:, lo:hi] += jnp.concatenate(sums, axis=0)
    grad_scores_low = grad_scores_t.astype(bf16)
    grad_out = grad_out + mm(grad_scores_low, in_map, TN)
    grad_in = grad_in + mm(grad_scores_low, out_map, NN)
    grad_shared = jnp.concatenate([grad_in, grad_out], axis=1)
    grad_pre = grad_shared * (shared_gate * (1.0 + pre_shared * (1.0 - shared_gate)))
    shared_head[0:rows, :] = grad_pre
    shared_proj = shared_ref[...]
    grad_proj = conv_shared_ref[TAPS - 1 : TAPS, :] * grad_pre
    sums = [None] * TAPS
    sums[TAPS - 1] = jnp.sum(grad_pre * shared_proj, axis=0, keepdims=True)
    for k in range(1, TAPS):
        keep = jnp.concatenate([keeps[k - 1]] * (width // LANES), axis=1)
        moved = shared_head[k : k + rows, :] * keep
        grad_proj = grad_proj + conv_shared_ref[TAPS - 1 - k : TAPS - k, :] * moved
        sums[TAPS - 1 - k] = jnp.sum(moved * shared_proj, axis=0, keepdims=True)
    sums.append(jnp.sum(grad_pre, axis=0, keepdims=True))
    sums.append(jnp.zeros((TAIL - len(sums), width), f32))
    sums_ref[:, channels : channels + width] += jnp.concatenate(sums, axis=0)
    leaving = by_head[rows:]
    split = mm(lower, halves(by_head[:rows], 1), TN)
    grad_log = split[:, :LANES] + split[:, LANES:] + leaving[0:1, :]
    grad_step = (step_terms + rate * grad_log) * sigmoid(step_raw)
    grads_ref[:, channels : channels + width] = grad_proj.astype(bf16)
    grads_ref[:, channels + width :] = grad_step.astype(bf16)

    @pl.when(turn == 0)
    def _():
        for copy in weight_copies():
            copy.wait()

    terms = mm(grad_gate_ref[...], gate_w[...], NT) + mm(grads_ref[...], weight[...], NT)
    terms_ref[...] = terms.astype(bf16)
    sums_ref[:, channels + width :] += jnp.concatenate(
        [
            jnp.sum(grad_step, axis=0, keepdims=True),
            rate * jnp.sum(step * grad_log, axis=0, keepdims=True),
            leaving[1:2, :],
            jnp.zeros((TAIL - 3, LANES), f32),
        ],
        axis=0,
    )

    @pl.when(turn == pl.num_programs(0) - 1)
    def _():
        inner_out_ref[...] = inner_head[0:TAIL, :]
        shared_out_ref[...] = shared_head[0:TAIL, :]


def mixer_backward(
    lengths, upstream, saved, conv_inner, conv_shared, rate, skip, spread, grad_gate, weight_late,
    weight, carry, blocks, span
):
    ssm, inner, pre_inner, shared, pre_shared, step_raw, entering = saved
    rows, channels = upstream.shape
    width = conv_shared.shape[1]
    states = width // 2
    begin, end = blocks
    known = channels + width + LANES
    model = weight.shape[0]
    by_row = lambda cols: pl.BlockSpec((span, cols), lambda i: (end - 1 - i, 0))
    small = ((TAIL, known), (TAIL, channels), (TAIL, width), (states, channels))
    results = pl.pallas_call(
        partial(backward_kernel, begin, rows),
        grid=(end - begin,),
        in_specs=[
            pl.BlockSpec(memory_space=pltpu.SMEM),
            by_row(channels), by_row(channels), by_row(channels), by_row(channels),
            by_row(width), by_row(width), by_row(LANES),
            pl.BlockSpec((1, states, channels), lambda i: (end - 1 - i, 0, 0)),
            full(conv_inner.shape),
            full(conv_shared.shape),
            full(rate.shape),
            full(skip.shape),
            full(spread.shape),
            by_row(channels),
            pl.BlockSpec(memory_space=pl.ANY),
            pl.BlockSpec(memory_space=pl.ANY),
            *[full(x.shape) for x in carry],
        ],
        out_specs=[
            pl.BlockSpec((span, known), lambda i: (end - begin - 1 - i, 0)),
            pl.BlockSpec((span, model), lambda i: (end - begin - 1 - i, 0)),
            *[full(shape) for shape in small],
        ],
        out_shape=[
            jax.ShapeDtypeStruct(((end - begin) * span, known), bf16),
            jax.ShapeDtypeStruct(((end - begin) * span, model), bf16),
            *[jax.ShapeDtypeStruct(shape, f32) for shape in small],
        ],
        scratch_shapes=[
            pltpu.VMEM((TAIL + span, channels), f32),
            pltpu.VMEM((TAIL + span, width), f32),
            pltpu.VMEM((model, channels), bf16),
            pltpu.VMEM((model, known), bf16),
            pltpu.SemaphoreType.DMA((2,)),
        ],
        compiler_params=pltpu.CompilerParams(
            dimension_semantics=("arbitrary",), vmem_limit_bytes=LIMIT
        ),
        name="mixer_backward",
    )(
        lengths, upstream, ssm, inner, pre_inner, shared, pre_shared, step_raw, entering,
        conv_inner, conv_shared, rate, skip, spread, grad_gate, weight_late, weight, *carry,
    )
    return results[0], results[1], tuple(results[2:])


def gain_row(weight_ref, total_ref, columns):
    rows = weight_ref.shape[0]
    begin, end = columns
    added = jnp.zeros((rows, LANES), f32)
    for lo in range(begin, end, LANES):
        weight = weight_ref[:, lo : lo + LANES].astype(f32)
        added = added + weight * total_ref[:, lo - begin : lo - begin + LANES]
    return jnp.sum(jnp.transpose(added), axis=0, keepdims=True)


def product_kernel(chips, columns, spot_ref, normed_ref, weight_ref, gain_ref, sums_ref,
                   norm_sum_ref, *refs):
    grads, (keep_ref, *send_refs, heads_ref, shared_ref, total) = refs[:-8], refs[-8:]
    lo, hi = columns
    at = 0
    for i, ref in enumerate(grads):
        rows = ref.shape[0]
        added = mm(normed_ref[at : at + rows, :], ref[:, lo:hi], TN)
        total[...] = added if i == 0 else total[...] + added
        at += rows
    split_cores(spot_ref, total, keep_ref, send_refs, chips)
    row = norm_sum_ref[0:1, :] + gain_row(weight_ref, total, columns)
    width = shared_ref.shape[1] - norm_sum_ref.shape[1]
    inner = heads_ref.shape[1] - LANES
    heads_ref[:, :inner] = sums_ref[:, :inner]
    heads_ref[:, inner:] = sums_ref[:, inner + width :]
    shared_ref[:, :width] = sums_ref[:, inner : inner + width]
    shared_ref[:, width:] = jnp.broadcast_to(row / gain_ref[...], norm_sum_ref.shape)


def weight_products(spot, normed, weight, gain, sums, norm_sum, grads, chips, width):
    known = grads[0].shape[1]
    model = normed.shape[1]
    size = known
    part = jax.ShapeDtypeStruct((model // 2, size), bf16)
    piece = jax.ShapeDtypeStruct((model // 8, size), bf16)
    vmem = pl.BlockSpec(memory_space=pltpu.VMEM)
    return pl.pallas_call(
        partial(product_kernel, chips, (0, known)),
        in_specs=[pl.BlockSpec(memory_space=pltpu.SMEM), *[vmem for _ in range(5 + len(grads))]],
        out_specs=[vmem] * 7,
        out_shape=[
            part, *[piece] * 4, jax.ShapeDtypeStruct((TAIL, known - width), f32),
            jax.ShapeDtypeStruct((TAIL, width + model), f32),
        ],
        scratch_shapes=[pltpu.VMEM((model, size), f32)],
        compiler_params=pltpu.CompilerParams(vmem_limit_bytes=LIMIT),
        name="weight_products",
    )(spot, normed, weight, gain, sums, norm_sum, *grads)


def gate_kernel(pieces, count, spot_ref, normed_ref, *refs):
    own_ref, others = refs[0], refs[1:pieces]
    columns, sources = refs[pieces : pieces + 4], refs[pieces + 4 : pieces + 4 + 2 * count]
    (
        gain_ref, ssm_ref, upstream_ref, weight_ref, gate_ref, grad_ref, sums_ref
    ) = refs[pieces + 4 + 2 * count :]

    @pl.when(pl.program_id(0) == 0)
    def _():
        place_columns(spot_ref, weight_ref, columns, count)
        place_pairs(spot_ref, weight_ref, [(ref, 0) for ref in sources], count, columns[0].shape[1])

    rows, channels = ssm_ref.shape
    normed = normed_ref[...]
    upstream = rows_of(pl.program_id(0), pl.num_programs(0), spot_ref, own_ref, others)
    upstream_ref[...] = upstream
    square = jnp.zeros((rows, LANES), f32)
    cross = jnp.zeros((rows, LANES), f32)
    step = 2 * LANES
    for lo in range(0, channels, step):
        hi = lo + step
        gate = mm(normed, weight_ref[:, lo:hi], NN)
        grad = mm(upstream, weight_ref[:, channels + lo : channels + hi], NN)
        gate_ref[:, lo:hi] = gate
        grad_ref[:, lo:hi] = grad
        gated = ssm_ref[:, lo:hi] * (gate * sigmoid(gate))
        squares = gated * gated
        crosses = grad * gain_ref[:, lo:hi] * gated
        square = square + (squares[:, :LANES] + squares[:, LANES:])
        cross = cross + (crosses[:, :LANES] + crosses[:, LANES:])
    square = jnp.sum(square, axis=1, keepdims=True)
    cross = jnp.sum(cross, axis=1, keepdims=True)
    lane = lax.broadcasted_iota(jnp.int32, (rows, LANES), 1)
    both = jnp.where(lane == 0, square, jnp.where(lane == 1, cross, 0.0))
    sums_ref[...] = jnp.transpose(both)[0:TAIL, :]


def gate_forward(spot, normed, own, others, sources, count, gain, ssm, span):
    rows, model = normed.shape
    channels = ssm.shape[1]
    by_row = lambda cols: pl.BlockSpec((span, cols), lambda i: (i, 0))
    return pl.pallas_call(
        partial(gate_kernel, 1 + len(others), count),
        grid=(rows // span,),
        in_specs=[
            pl.BlockSpec(memory_space=pltpu.SMEM), by_row(model), *own_specs(own, others, span),
            *[full(x.shape) for x in sources], full(gain.shape), by_row(channels),
        ],
        out_specs=[
            by_row(model), full((model, 2 * channels)), by_row(channels), by_row(channels),
            pl.BlockSpec((TAIL, span), lambda i: (0, i)),
        ],
        out_shape=[
            jax.ShapeDtypeStruct((rows, model), bf16),
            jax.ShapeDtypeStruct((model, 2 * channels), bf16),
            jax.ShapeDtypeStruct((rows, channels), f32),
            jax.ShapeDtypeStruct((rows, channels), f32),
            jax.ShapeDtypeStruct((TAIL, rows), f32),
        ],
        compiler_params=pltpu.CompilerParams(
            dimension_semantics=("arbitrary",), vmem_limit_bytes=LIMIT
        ),
        name="gate_forward",
    )(spot, normed, own, *others, *sources, gain, ssm)


def norm_kernel(full_inner, chips, split, spot_ref, sums_ref, more_ref, gate_ref, grad_ref, ssm_ref,
                gain_ref, normed_ref, upstream_ref, gate_w_ref, out_w_ref, grad_gate_ref,
                grad_ssm_ref, gain_sum_ref, keep_ref, send_ref, mine_ref, theirs_ref, norm_sum_ref,
                scaled, totals):
    rows, channels = gate_ref.shape
    block = pl.program_id(0)

    @pl.when(block == 0)
    def _():
        gain_sum_ref[...] = jnp.zeros_like(gain_sum_ref)
        totals[...] = jnp.zeros_like(totals)

    sums = sums_ref[...] + more_ref[...] if split else sums_ref[...]
    sums = jnp.transpose(jnp.concatenate([sums, jnp.zeros((LANES - TAIL, rows), f32)], axis=0))
    scale = lax.rsqrt(sums[:, 0:1] / full_inner + EPSILON)
    pull = scale * scale * scale * (sums[:, 1:2] / full_inner)
    normed_t = jnp.transpose(normed_ref[...])
    upstream_t = jnp.transpose(upstream_ref[...])
    step = 2 * LANES
    for lo in range(0, channels, step):
        hi = lo + step
        gain = gain_ref[:, lo:hi]
        gate, grad, ssm = gate_ref[:, lo:hi], grad_ref[:, lo:hi], ssm_ref[:, lo:hi]
        sig = sigmoid(gate)
        silu = gate * sig
        gated = ssm * silu
        normal = gated * scale
        scaled_low = (normal * gain).astype(bf16)
        scaled[:, lo:hi] = scaled_low
        gain_sum_ref[TAIL - 1 : TAIL, lo:hi] += jnp.sum(grad * normal, axis=0, keepdims=True)
        grad_gated = scale * (grad * gain) - gated * pull
        grad_ssm_ref[:, lo:hi] = grad_gated * silu
        grad_gate = (grad_gated * ssm * (sig * (1.0 + gate * (1.0 - sig)))).astype(bf16)
        grad_gate_ref[:, lo:hi] = grad_gate
        totals[:, lo:hi] += mm(normed_t, grad_gate, NN)
        totals[:, channels + lo : channels + hi] += mm(upstream_t, scaled_low, NN)
    branch = mm(scaled[...], out_w_ref[...], NT).astype(bf16)
    if split:
        half = pl.num_programs(0) // 2
        at = pl.ds(pl.multiple_of(lax.rem(block, half) * rows, rows), rows)

        @pl.when(block // half == spot_ref[0, 0])
        def _():
            mine_ref[at, :] = branch

        @pl.when(block // half != spot_ref[0, 0])
        def _():
            theirs_ref[at, :] = branch
    else:
        mine_ref[pl.ds(pl.multiple_of(block * rows, rows), rows), :] = branch

        @pl.when(block == 0)
        def _():
            theirs_ref[...] = jnp.zeros_like(theirs_ref)

    @pl.when(block == pl.num_programs(0) - 1)
    def _():
        split_cores(spot_ref, totals, keep_ref, [send_ref], chips)
        norm_sum_ref[...] = jnp.zeros_like(norm_sum_ref)
        norm_sum_ref[0:1, :] = gain_row(gate_w_ref, totals, (0, channels))


def gate_norm(
    spot, sums, more, gate, grad, ssm, gain, normed, upstream, weight, known, full_inner, chips, split, span
):
    rows, channels = gate.shape
    model = normed.shape[1]
    by_row = lambda cols: pl.BlockSpec((span, cols), lambda i: (i, 0))
    stats = pl.BlockSpec((TAIL, span), lambda i: (0, i))
    half = (model // 2, 2 * channels)
    mine = (rows // 2 if split else rows, model)
    theirs = (rows // 2 if split else TAIL * 2, model)
    return pl.pallas_call(
        partial(norm_kernel, float(full_inner), chips, split),
        grid=(rows // span,),
        in_specs=[
            pl.BlockSpec(memory_space=pltpu.SMEM), stats, stats, by_row(channels), by_row(channels),
            by_row(channels), full(gain.shape), by_row(model), by_row(model),
            pl.BlockSpec((model, channels), lambda i: (0, 0)),
            pl.BlockSpec((model, channels), lambda i: (0, 1)),
        ],
        out_specs=[
            by_row(channels), by_row(channels), full((TAIL, known)), full(half), full(half),
            full(mine), full(theirs), full((TAIL, model)),
        ],
        out_shape=[
            jax.ShapeDtypeStruct((rows, channels), bf16),
            jax.ShapeDtypeStruct((rows, channels), f32),
            jax.ShapeDtypeStruct((TAIL, known), f32),
            jax.ShapeDtypeStruct(half, bf16),
            jax.ShapeDtypeStruct(half, bf16),
            jax.ShapeDtypeStruct(mine, bf16),
            jax.ShapeDtypeStruct(theirs, bf16),
            jax.ShapeDtypeStruct((TAIL, model), f32),
        ],
        scratch_shapes=[
            pltpu.VMEM((span, channels), bf16),
            pltpu.VMEM((model, 2 * channels), f32),
        ],
        compiler_params=pltpu.CompilerParams(
            dimension_semantics=("arbitrary",), vmem_limit_bytes=LIMIT
        ),
        name="gate_norm",
    )(spot, sums, more, gate, grad, ssm, gain, normed, upstream, weight, weight)


def output_kernel(width, sums_ref, more_ref, *out_refs):
    sums = sums_ref[...] + more_ref[...]
    inner = out_refs[0].shape[1]
    heads = out_refs[4].shape[1]
    shared = inner + LANES
    parts = (
        sums[:TAPS, :inner], sums[TAPS : TAPS + 1, :inner], sums[:TAPS, shared : shared + width],
        sums[TAPS : TAPS + 1, shared : shared + width], sums[0:1, inner : inner + LANES][:, :heads],
        sums[1:2, inner : inner + LANES][:, :heads], sums[2:3, inner : inner + LANES][:, :heads],
        sums[TAIL - 1 :, :inner], sums[0:1, shared + width :],
    )
    for ref, part in zip(out_refs, parts):
        ref[...] = part


def sums_outputs(sums, more, channels, width, heads):
    model = sums.shape[1] - channels - LANES - width
    shapes = [
        (TAPS, channels), (1, channels), (TAPS, width), (1, width), (1, heads), (1, heads),
        (1, heads), (1, channels), (1, model),
    ]
    vmem = pl.BlockSpec(memory_space=pltpu.VMEM)
    return pl.pallas_call(
        partial(output_kernel, width),
        in_specs=[vmem, vmem],
        out_specs=[vmem] * len(shapes),
        out_shape=[jax.ShapeDtypeStruct(shape, f32) for shape in shapes],
        name="sums_outputs",
    )(sums, more)


def lanes_of(vector):
    return jnp.pad(vector, (0, LANES - vector.shape[0]))[None, :]


def spread_map(heads, channels):
    size = channels // heads
    row = lax.broadcasted_iota(jnp.int32, (2 * LANES, channels), 0) % LANES
    col = lax.broadcasted_iota(jnp.int32, (2 * LANES, channels), 1) // size
    return (row == col).astype(bf16)


def dp_send(value, bit):
    size = lax.axis_size("dp")
    return lax.ppermute(value, "dp", [(i, i ^ bit) for i in range(size)])


def chip_bits():
    return [4 * k for k in range(1, lax.axis_size("dp") // 4)]


def long_bits():
    bits, bit = [], 4
    while bit < lax.axis_size("dp"):
        bits.append(bit)
        bit *= 2
    return bits


def choose(stacked, index, axis):
    return lax.dynamic_index_in_dim(stacked, index, axis, keepdims=False)


def send_fold(parts, bit, axis):
    mine = (lax.axis_index("dp") // bit) % 2
    return dp_send(choose(parts, 1 - mine, axis), bit)


def keep_fold(parts, got, bit, axis):
    mine = (lax.axis_index("dp") // bit) % 2
    return choose(parts, mine, axis).astype(f32) + got.astype(f32)


def fold(parts, bit, axis):
    return keep_fold(parts, send_fold(parts, bit, axis), bit, axis)


def send_chips(parts):
    place = lax.axis_index("dp") // 4
    sends = parts.astype(bf16)
    return [dp_send(choose(sends, place ^ (bit // 4), 0), bit) for bit in chip_bits()]


def keep_chips(parts, got):
    total = choose(parts, lax.axis_index("dp") // 4, 0).astype(f32)
    for piece in got:
        total = total + piece.astype(f32)
    return total


def fold_chips(parts):
    return keep_chips(parts, send_chips(parts))


def tensor_swap(value):
    return lax.ppermute(value, "tensor", [(0, 1), (1, 0)])


def gather_other(own, size):
    if size != 2:
        return lax.all_gather(own, "tensor", axis=0, tiled=True)
    return tensor_swap(own)


def join_pieces(own, top, bottom, size):
    top = top.reshape(size, -1, own.shape[1])
    bottom = bottom.reshape(size, -1, own.shape[1])
    return jnp.concatenate([top, bottom], axis=1).reshape(-1, own.shape[1])


def pick_half(lower, upper, size):
    if size != 2:
        return lower
    return jnp.where(lax.axis_index("tensor") == 0, lower, upper)


def sum_quarters(quarters, other0, other1, size):
    if size != 2:
        whole = jnp.concatenate(quarters, axis=0)
        return lax.psum_scatter(whole, "tensor", scatter_dimension=0, tiled=True).astype(f32)
    first = lax.axis_index("tensor") == 0
    each = other0.shape[0]
    low, middle, high = quarters
    lower = jnp.concatenate([low, middle[:each]], axis=0)
    upper = jnp.concatenate([middle[each:], high], axis=0)
    others = jnp.concatenate([other0, other1], axis=0)
    return jnp.where(first, lower, upper).astype(f32) + others.astype(f32)


def tensor_sum(value, size):
    if size != 2:
        return lax.psum(value, "tensor")
    return value + tensor_swap(value)


def shards(
    tokens, lengths, norm_gain, zx_weight, bc_weight, dt_weight, conv_inner, bias_inner,
    conv_shared, bias_shared, step_bias, log_rate, skip_gain, gate_gain, out_weight, cotangent,
):
    size = lax.axis_size("tensor")
    split = size == 2
    me = lax.axis_index("dp")
    count = len(chip_bits()) + 1
    spot = jnp.stack([lax.axis_index("tensor"), me // 4, (me // 2) % 2, me % 2])[None, :]
    spot = spot.astype(jnp.int32)
    channels = zx_weight.shape[2]
    heads = step_bias.shape[0]
    width = bc_weight.shape[1]
    known = channels + width + LANES
    step_weight = jnp.pad(dt_weight, ((0, 0), (0, LANES - heads)))
    early = jnp.concatenate([zx_weight[:, 1, :], bc_weight, step_weight], axis=1)
    inputs = tokens.astype(f32)
    norm_scale = lax.rsqrt(jnp.mean(inputs * inputs, axis=1, keepdims=True) + EPSILON)
    normed_rows = (inputs * norm_scale * norm_gain[None, :]).astype(bf16)
    half = normed_rows.shape[0] // 2
    fixed = (
        conv_inner, bias_inner[None, :], conv_shared, bias_shared[None, :], lanes_of(step_bias),
        lanes_of(-jnp.exp(log_rate)), jnp.repeat(skip_gain, channels // heads)[None, :],
        spread_map(heads, channels),
    )
    def along(value):
        return [value] + [dp_send(value, bit) for bit in chip_bits()]

    column = jnp.concatenate(along(early), axis=0)
    column, pair, top, fixed, spot = lax.optimization_barrier((
        column, jnp.concatenate([out_weight, dp_send(out_weight, 2)], axis=0),
        gather_other(normed_rows[:half], size), fixed, spot,
    ))
    by_x, column, bottom, gate_column, pair, late_rows = lax.optimization_barrier((
        dp_send(column, 2), column, gather_other(normed_rows[half:], size),
        along(zx_weight[:, 0, :]), pair, cotangent,
    ))
    gate_column = jnp.concatenate(gate_column, axis=0)
    pairs = along(pair)
    by_core = dp_send(column, 1)
    sources = (column, by_x, by_core, dp_send(by_x, 1))
    own, others = normed_rows, (top, bottom)
    if not split:
        own, others = join_pieces(normed_rows, top, bottom, size), ()
    normed, weight, *saved = mixer_forward(
        spot, lengths, own, others, sources, count, *fixed, SPAN
    )
    _, _, _, _, _, rate, skip, spread = fixed
    gain = gate_gain[None, :]
    other, ssm, gate_x, gate_column, pairs = lax.optimization_barrier((
        gather_other(late_rows, size), saved[0], dp_send(gate_column, 2), gate_column, pairs,
    ))
    sources = (
        gate_column, gate_x, dp_send(gate_column, 1), dp_send(gate_x, 1), *pairs,
        *[dp_send(pair, 1) for pair in pairs],
    )
    own, others = (cotangent, (other,)) if split else (other, ())
    upstream, weight_late, gate, grad, sums = gate_forward(
        spot, normed, own, others, sources, count, gain, ssm, SPAN
    )
    more = gather_other(sums, size) if split else sums
    sums = sums if split else lax.psum(sums, "tensor")
    chips = 2 * count
    grad_gate, grad_ssm, gain_sum, keep, send, branch_own, branch_send, norm_sum = gate_norm(
        spot, sums, more, gate, grad, ssm, gain, normed, upstream, weight_late, known, channels * size,
        chips, split, SPAN,
    )
    if split:
        branch_other = gather_other(branch_send, size)
    else:
        branch_own = lax.psum_scatter(branch_own, "tensor", scatter_dimension=0, tiled=True)
        branch_other = jnp.zeros_like(branch_own)
    quarter = grad_ssm.shape[0] // SPAN // 4
    carry = (gain_sum,)

    def back(begin, end, carry):
        return mixer_backward(
            lengths, grad_ssm, saved, conv_inner, conv_shared, rate, skip, spread, grad_gate,
            weight_late, weight, carry, (begin * quarter, end * quarter), SPAN,
        )

    first = dp_send(send, 1)
    grads3, terms3, carry = back(3, 4, carry)
    first = (keep.astype(f32) + first.astype(f32)).astype(bf16)
    first = first.reshape(count, 2, -1, first.shape[1])
    carry, first = lax.optimization_barrier((carry, first))
    first_gate, first_out = first[..., :channels], first[..., channels:]
    grads1, terms1, carry = back(1, 3, carry)
    first_gate = fold(first_gate, 2, 1)
    first_out = fold_chips(first_out).astype(bf16)
    each = terms3.shape[0]
    send1 = pick_half(terms3, terms1[:each], size)
    carry, send1, branch_other, first_gate, first_out = lax.optimization_barrier(
        (carry, send1, branch_other, first_gate, first_out)
    )
    other1 = gather_other(send1, size) if split else send1
    part_gate = fold_chips(first_gate)
    part_out = fold(first_out, 2, 0)
    grads0, terms0, carry = back(0, 1, carry)
    sums, part_gate, part_out, grads0, other1, terms0 = lax.optimization_barrier(
        (carry[0], part_gate, part_out, grads0, other1, terms0)
    )
    send0 = pick_half(terms1[each:], terms0, size)
    send0, grads0 = lax.optimization_barrier((send0, grads0))
    other0 = gather_other(send0, size) if split else send0
    keep, *send, sums, shared_sums = weight_products(
        spot, normed, weight, norm_gain[None, :], sums, norm_sum, (grads0, grads1, grads3), chips,
        width,
    )
    got = [dp_send(piece, 1) for piece in send]
    *got, other0, sums, shared_sums, keep = lax.optimization_barrier(
        (*got, other0, sums, shared_sums, keep)
    )
    got = jnp.concatenate(got, axis=0)
    parts = (keep.astype(f32) + got.astype(f32)).astype(bf16).reshape(count, 2, -1, known)
    cut = min((known * 2 // 3) // LANES * LANES, channels)
    parts_a, parts_b = parts[..., :cut], parts[..., cut:]
    got_a = send_fold(parts_a, 2, 1)
    got_b = send_chips(parts_b)
    shared_sums = tensor_sum(shared_sums, size)
    shared_sums, other0 = lax.optimization_barrier((shared_sums, other0))
    sums = jnp.concatenate([sums, shared_sums], axis=1)
    sums = sums + dp_send(sums, 1)
    sums = sums + dp_send(sums, 2)
    grad_normed = sum_quarters((terms0, terms1, terms3), other0, other1, size)
    scaled_grad = grad_normed * norm_gain[None, :]
    grad_inputs = norm_scale * scaled_grad - inputs * norm_scale**3 * jnp.mean(
        scaled_grad * inputs, axis=1, keepdims=True
    )
    grad_tokens = (cotangent.astype(f32) + grad_inputs).astype(bf16)
    got_a, got_b, sums, grad_tokens, branch_other = lax.optimization_barrier(
        (got_a, got_b, sums, grad_tokens, branch_other)
    )
    block_out = (inputs + (branch_own.astype(f32) + branch_other.astype(f32))).astype(bf16)
    parts_a = keep_fold(parts_a, got_a, 2, 1)
    parts_b = keep_chips(parts_b, got_b).astype(bf16)
    got_a = send_chips(parts_a)
    parts_b = fold(parts_b, 2, 0)
    for bit in long_bits()[:-1]:
        sums = sums + dp_send(sums, bit)
    smalls = sums_outputs(sums, dp_send(sums, long_bits()[-1]), channels, width, heads)
    parts_a = keep_chips(parts_a, got_a)
    part_inner = jnp.concatenate([parts_a, parts_b[:, : channels - cut]], axis=1)
    at_step = channels + width
    part_shared = tensor_sum(parts_b[:, channels - cut : at_step - cut], size)
    part_step = parts_b[:, at_step - cut : at_step - cut + heads]
    part_in = jnp.stack([part_gate, part_inner], axis=1)
    return (
        block_out,
        grad_tokens,
        smalls[8][0],
        part_in,
        part_shared,
        part_step,
        smalls[0],
        smalls[1][0],
        smalls[2],
        smalls[3][0],
        smalls[4][0],
        smalls[5][0],
        smalls[6][0],
        smalls[7][0],
        part_out,
    )


def solution(mesh):
    return jax.shard_map(
        shards,
        mesh=mesh,
        in_specs=(
            P(("dp", "tensor"), None),
            P("dp", None),
            P(),
            P("dp", None, "tensor"),
            P("dp", None),
            P("dp", "tensor"),
            P(None, "tensor"),
            P("tensor"),
            P(),
            P(),
            P("tensor"),
            P("tensor"),
            P("tensor"),
            P("tensor"),
            P("dp", "tensor"),
            P(("dp", "tensor"), None),
        ),
        out_specs=(
            P(("dp", "tensor"), None),
            P(("dp", "tensor"), None),
            P(),
            P("dp", None, "tensor"),
            P("dp", None),
            P("dp", "tensor"),
            P(None, "tensor"),
            P("tensor"),
            P(),
            P(),
            P("tensor"),
            P("tensor"),
            P("tensor"),
            P("tensor"),
            P("dp", "tensor"),
        ),
        check_vma=False,
    )
```

```python
from functools import partial

import jax
import jax.numpy as jnp
from jax import lax
from jax.experimental import pallas as pl
from jax.experimental.pallas import tpu as pltpu
from jax.sharding import PartitionSpec as P

EPSILON = 1e-05
SPAN = 256
LANES = 128
TAIL = 8
TAPS = 4
MASKED = -1e30
f32 = jnp.float32
bf16 = jnp.bfloat16
LIMIT = 60 * 1024 * 1024


def mm(left, right, dims):
    return lax.dot_general(left, right, ((dims[0], dims[1]), ((), ())), preferred_element_type=f32)


NN = ((1,), (0,))
NT = ((1,), (1,))
TN = ((0,), (0,))


def halves(value, axis):
    high = value.astype(bf16)
    low = (value - high.astype(f32)).astype(bf16)
    return jnp.concatenate([high, low], axis=axis)


def sigmoid(value):
    return 1.0 / (1.0 + jnp.exp(-value))


def softplus(value):
    return jnp.maximum(value, 0.0) + jnp.log1p(jnp.exp(-jnp.abs(value)))


def segment_at(ends, position):
    total = jnp.zeros(position.shape, jnp.int32)
    for end in ends:
        total = total + (position >= end).astype(jnp.int32)
    return total


def sequence_ends(lengths_ref):
    ends, total = [], 0
    for i in range(lengths_ref.shape[1]):
        total = total + lengths_ref[0, i]
        ends.append(total)
    return ends


def step_parts(step_raw, rate, ends, base):
    rows = step_raw.shape[0]
    step = softplus(step_raw)
    row = lax.broadcasted_iota(jnp.int32, (rows, rows), 0)
    col = lax.broadcasted_iota(jnp.int32, (rows, rows), 1)
    lower = (row >= col).astype(f32).astype(bf16)
    split = mm(lower, halves(step * rate, 1), NN)
    running = split[:, :LANES] + split[:, LANES:]
    position = base + lax.broadcasted_iota(jnp.int32, (rows, 1), 0)
    segment = segment_at(ends, position)
    before = segment_at(ends, jnp.full((1, 1), base - 1, jnp.int32))
    last = segment_at(ends, jnp.full((1, 1), base + rows - 1, jnp.int32))
    carried = ((segment == before) & (position >= rows)).astype(f32)
    matched = (segment == last).astype(f32)
    entry = jnp.exp(running) * carried
    leave = jnp.exp(running[rows - 1 :, :] - running) * matched
    return step, running, entry, leave, lower, segment, row, col


def same_rows(ends, base, rows):
    across = segment_at(ends, base + lax.broadcasted_iota(jnp.int32, (1, rows), 1))
    down = segment_at(ends, base + lax.broadcasted_iota(jnp.int32, (rows, 1), 0))
    return down == across


def rows_of(block, blocks, spot_ref, own_ref, others):
    if not others:
        return own_ref[...]
    half = blocks // 2
    local = lax.rem(block, half)
    span = own_ref.shape[0] // half
    each = half // len(others)
    value = None
    for i, ref in enumerate(others):
        at = lax.rem(local, each) * span
        piece = ref[pl.ds(pl.multiple_of(at, span), span), :]
        value = piece if i == 0 else jnp.where(local >= i * each, piece, value)
    mine = own_ref[pl.ds(pl.multiple_of(local * span, span), span), :]
    return jnp.where(block // half == spot_ref[0, 0], mine, value)


def own_specs(own, others, span):
    if not others:
        return [pl.BlockSpec((span, own.shape[1]), lambda i: (i, 0))]
    return [full(own.shape), *[full(other.shape) for other in others]]


def run_copies(copies):
    for copy in copies:
        copy.start()
    for copy in copies:
        copy.wait()


def place_weights(spot_ref, weight_ref, sources, count, done):
    rows = weight_ref.shape[0] // (4 * count)
    copies = []
    for i, ref in enumerate(sources):
        along = spot_ref[0, 2] ^ (i % 2)
        core = spot_ref[0, 3] ^ (i // 2)
        for k in range(count):
            at = (((spot_ref[0, 1] ^ k) * 2 + along) * 2 + core) * rows
            copies.append(pltpu.make_async_copy(
                ref.at[pl.ds(k * rows, rows), :],
                weight_ref.at[pl.ds(pl.multiple_of(at, rows), rows), :],
                done.at[i * count + k],
            ))
    run_copies(copies)


def place_columns(spot_ref, weight_ref, sources, count):
    rows = weight_ref.shape[0] // (4 * count)
    for i, ref in enumerate(sources):
        along = spot_ref[0, 2] ^ (i % 2)
        core = spot_ref[0, 3] ^ (i // 2)
        for k in range(count):
            at = (((spot_ref[0, 1] ^ k) * 2 + along) * 2 + core) * rows
            at = pl.ds(pl.multiple_of(at, rows), rows)
            weight_ref[at, : ref.shape[1]] = ref[k * rows : (k + 1) * rows, :]


def place_pairs(spot_ref, weight_ref, sources, count, lo):
    rows = weight_ref.shape[0] // (4 * count)
    for i, (ref, begin) in enumerate(sources):
        core = spot_ref[0, 3] ^ (i // count)
        for j in range(2):
            at = (((spot_ref[0, 1] ^ (i % count)) * 2 + (spot_ref[0, 2] ^ j)) * 2 + core) * rows
            at = pl.ds(pl.multiple_of(at, rows), rows)
            here = begin + j * rows
            weight_ref[at, lo : lo + ref.shape[1]] = ref[here : here + rows, :]


def split_cores(spot_ref, value_ref, keep_ref, send_refs, chips):
    rows = keep_ref.shape[0] // chips
    each = chips // len(send_refs)
    core = spot_ref[0, 3]
    for chip in range(chips):
        here = pl.ds(pl.multiple_of((2 * chip + core) * rows, rows), rows)
        there = pl.ds(pl.multiple_of((2 * chip + 1 - core) * rows, rows), rows)
        keep_ref[chip * rows : (chip + 1) * rows, :] = value_ref[here, :].astype(bf16)
        at = (chip % each) * rows
        send_refs[chip // each][at : at + rows, :] = value_ref[there, :].astype(bf16)


def forward_kernel(
    pieces, count, spot_ref, lengths_ref, *refs
):
    own_ref, others = refs[0], refs[1:pieces]
    sources = refs[pieces : pieces + 4]
    (
        conv_inner_ref, bias_inner_ref, conv_shared_ref, bias_shared_ref, step_bias_ref, rate_ref,
        skip_ref, spread_ref, normed_ref, weight_ref, ssm_ref, inner_ref, pre_inner_ref, shared_ref,
        pre_shared_ref, step_ref, entering_ref, inner_tail, shared_tail, state, done,
    ) = refs[pieces + 4 :]
    block = pl.program_id(0)
    rows = normed_ref.shape[0]
    channels = conv_inner_ref.shape[1]
    base = block * rows
    ends = sequence_ends(lengths_ref)

    @pl.when(block == 0)
    def _():
        inner_tail[0:TAIL, :] = jnp.zeros((TAIL, channels), f32)
        shared_tail[0:TAIL, :] = jnp.zeros((TAIL, shared_tail.shape[1]), f32)
        state[...] = jnp.zeros_like(state)
        place_weights(spot_ref, weight_ref, sources, count, done)

    @pl.when(block > 0)
    def _():
        inner_tail[0:TAIL, :] = inner_tail[rows : rows + TAIL, :]
        shared_tail[0:TAIL, :] = shared_tail[rows : rows + TAIL, :]

    normed = rows_of(block, pl.num_programs(0), spot_ref, own_ref, others)
    normed_ref[...] = normed
    small = mm(normed, weight_ref[:, channels:], NN)
    width = conv_shared_ref.shape[1]
    shared_proj = small[:, :width]
    shared_tail[TAIL : TAIL + rows, :] = shared_proj
    shared_ref[...] = shared_proj
    step_raw = small[:, width:] + step_bias_ref[...]
    step_ref[...] = step_raw
    inner_proj = mm(normed, weight_ref[:, :channels], NN)
    inner_tail[TAIL : TAIL + rows, :] = inner_proj
    inner_ref[...] = inner_proj

    step, running, entry, leave, lower, segment, row, col = step_parts(
        step_raw, rate_ref[...], ends, base
    )
    position = base + lax.broadcasted_iota(jnp.int32, (rows, 1), 0)
    keeps = [
        ((segment_at(ends, position - k) == segment) & (position >= k)).astype(f32)
        for k in range(1, TAPS)
    ]
    keeps = [jnp.broadcast_to(keep, (rows, LANES)) for keep in keeps]

    def conv(tail, taps_ref, bias_ref, lo, hi):
        total = bias_ref[:, lo:hi] + taps_ref[TAPS - 1 : TAPS, lo:hi] * tail[TAIL : TAIL + rows, lo:hi]
        for k in range(1, TAPS):
            shifted = tail[TAIL - k : TAIL - k + rows, lo:hi]
            total = total + taps_ref[TAPS - 1 - k : TAPS - k, lo:hi] * (shifted * keeps[k - 1])
        return total

    pre_shared = jnp.concatenate(
        [
            conv(shared_tail, conv_shared_ref, bias_shared_ref, lo, lo + LANES)
            for lo in range(0, width, LANES)
        ],
        axis=1,
    )
    pre_shared_ref[...] = pre_shared
    shared = pre_shared * sigmoid(pre_shared)
    in_map = shared[:, : width // 2].astype(bf16)
    out_map = shared[:, width // 2 :].astype(bf16)
    scores = mm(out_map, in_map, NT)
    in_map_t = jnp.transpose(in_map)
    allowed = jnp.where((row >= col) & same_rows(ends, base, rows), 0.0, MASKED)
    running_t = jnp.transpose(running)
    factors = jnp.concatenate([halves(x, 1) for x in (step, entry, leave)], axis=0)
    lane = lax.broadcasted_iota(jnp.int32, (rows, LANES), 1)
    for pair in range(channels // LANES):
        lo, hi = pair * LANES, (pair + 1) * LANES
        pre = conv(inner_tail, conv_inner_ref, bias_inner_ref, lo, hi)
        pre_inner_ref[:, lo:hi] = pre
        head_in = pre * sigmoid(pre)
        side = (pair % 2) * LANES
        if side == 0:
            spread = spread_ref[:, lo : min(lo + 2 * LANES, channels)]
            wide = mm(factors, spread, NN)
        step_wide, entry_wide, leave_wide = [
            wide[i * rows : (i + 1) * rows, side : side + LANES] for i in range(3)
        ]
        scaled = head_in * step_wide
        scaled_low = scaled.astype(bf16)
        held = state[:, lo:hi]
        entering_ref[0, :, lo:hi] = held
        carried_out = mm(out_map, held.astype(bf16), NN) * entry_wide
        parts = []
        for parity in range(2):
            head = 2 * pair + parity
            gap = running[:, head : head + 1] - running_t[head : head + 1, :]
            parts.append((scores * jnp.exp(gap + allowed)).astype(bf16))
        both = mm(jnp.concatenate(parts, axis=0), scaled_low, NN)
        intra = jnp.where(lane < LANES // 2, both[:rows], both[rows:])
        ssm_ref[:, lo:hi] = carried_out + intra + skip_ref[:, lo:hi] * head_in
        added = mm(in_map_t, (scaled * leave_wide).astype(bf16), NN)
        state[:, lo:hi] = held * entry_wide[rows - 1 :, :] + added


def full(shape):
    return pl.BlockSpec(shape, lambda *_: (0,) * len(shape))


def mixer_forward(
    spot, lengths, own, others, sources, count, conv_inner, bias_inner, conv_shared, bias_shared,
    step_bias, rate, skip, spread, span,
):
    rows = own.shape[0] * (2 if others else 1)
    model = own.shape[1]
    channels = conv_inner.shape[1]
    width = conv_shared.shape[1]
    known = channels + width + LANES
    blocks = rows // span
    by_row = lambda cols: pl.BlockSpec((span, cols), lambda i: (i, 0))
    shape = lambda cols: jax.ShapeDtypeStruct((rows, cols), f32)
    states = width // 2
    smem = pl.BlockSpec(memory_space=pltpu.SMEM)
    fixed = (conv_inner, bias_inner, conv_shared, bias_shared, step_bias, rate, skip, spread)
    return pl.pallas_call(
        partial(forward_kernel, 1 + len(others), count),
        grid=(blocks,),
        in_specs=[
            smem, smem, *own_specs(own, others, span),
            *[pl.BlockSpec(memory_space=pl.ANY) for _ in sources],
            *[full(x.shape) for x in fixed],
        ],
        out_specs=[
            by_row(model), full((model, known)), by_row(channels), by_row(channels),
            by_row(channels), by_row(width), by_row(width), by_row(LANES),
            pl.BlockSpec((1, states, channels), lambda i: (i, 0, 0)),
        ],
        out_shape=[
            jax.ShapeDtypeStruct((rows, model), bf16), jax.ShapeDtypeStruct((model, known), bf16),
            shape(channels), shape(channels), shape(channels), shape(width), shape(width),
            shape(LANES), jax.ShapeDtypeStruct((blocks, states, channels), f32),
        ],
        scratch_shapes=[
            pltpu.VMEM((TAIL + span, channels), f32),
            pltpu.VMEM((TAIL + span, width), f32),
            pltpu.VMEM((states, channels), f32),
            pltpu.SemaphoreType.DMA((4 * count,)),
        ],
        compiler_params=pltpu.CompilerParams(
            dimension_semantics=("arbitrary",), vmem_limit_bytes=LIMIT
        ),
        name="mixer_forward",
    )(spot, lengths, own, *others, *sources, *fixed)


def backward_kernel(
    first_block, total_rows, first_call, sending, lengths_ref, upstream_ref, ssm_ref, inner_ref, pre_inner_ref,
    shared_ref, pre_shared_ref, step_ref, entering_ref, conv_inner_ref, conv_shared_ref, rate_ref, skip_ref, spread_ref,
    grad_gate_ref, gate_w_ref, weight_ref, sums_in_ref, *refs,
):
    inputs = 5 if sending else 0 if first_call else 3
    carried_in, refs = refs[:inputs], refs[inputs:]
    if sending:
        send_ref = refs[6]
        refs = refs[:6] + refs[7:]
    (
        grads_ref, terms_ref, sums_ref, inner_out_ref, shared_out_ref, adjoint, inner_head,
        shared_head, gate_w, weight, done,
    ) = refs
    turn = pl.program_id(0)
    block = first_block + pl.num_programs(0) - 1 - turn
    rows, channels = upstream_ref.shape
    width = conv_shared_ref.shape[1]
    base = block * rows
    ends = sequence_ends(lengths_ref)

    def weight_copies():
        return (
            pltpu.make_async_copy(gate_w_ref.at[:, pl.ds(0, channels)], gate_w, done.at[0]),
            pltpu.make_async_copy(weight_ref, weight, done.at[1]),
        )

    @pl.when(turn == 0)
    def _():
        if carried_in:
            inner_head[rows : rows + TAIL, :] = carried_in[0][...]
            shared_head[rows : rows + TAIL, :] = carried_in[1][...]
            adjoint[...] = carried_in[2][...]
        else:
            inner_head[rows : rows + TAIL, :] = jnp.zeros((TAIL, channels), f32)
            shared_head[rows : rows + TAIL, :] = jnp.zeros((TAIL, width), f32)
            adjoint[...] = jnp.zeros_like(adjoint)
        sums_ref[...] = sums_in_ref[...]
        for copy in weight_copies():
            copy.start()

    @pl.when(turn > 0)
    def _():
        inner_head[rows : rows + TAIL, :] = inner_head[0:TAIL, :]
        shared_head[rows : rows + TAIL, :] = shared_head[0:TAIL, :]

    step_raw = step_ref[...]
    rate = rate_ref[...]
    step, running, entry, leave, lower, segment, row, col = step_parts(step_raw, rate, ends, base)
    position = base + lax.broadcasted_iota(jnp.int32, (rows, 1), 0)
    keeps = [
        ((segment_at(ends, position + k) == segment) & (position + k < total_rows)).astype(f32)
        for k in range(1, TAPS)
    ]
    keeps = [jnp.broadcast_to(keep, (rows, LANES)) for keep in keeps]
    pre_shared = pre_shared_ref[...]
    shared_gate = sigmoid(pre_shared)
    shared = pre_shared * shared_gate
    half = width // 2
    in_map = shared[:, :half].astype(bf16)
    out_map = shared[:, half:].astype(bf16)
    scores_t = mm(in_map, out_map, NT)
    out_map_t = jnp.transpose(out_map)
    allowed_t = jnp.where((col >= row) & same_rows(ends, base, rows), 0.0, MASKED)
    running_t = jnp.transpose(running)
    factors = jnp.concatenate([halves(x, 1) for x in (step, entry, leave)], axis=0)
    lane = lax.broadcasted_iota(jnp.int32, (rows, LANES), 1)
    first_half = lane < LANES // 2
    grad_scores_t = jnp.zeros((rows, rows), f32)
    grad_in = jnp.zeros((rows, half), f32)
    grad_out = jnp.zeros((rows, half), f32)
    by_head = jnp.zeros((rows + TAIL, LANES), f32)
    step_terms = jnp.zeros((rows, LANES), f32)
    for pair in range(channels // LANES):
        lo, hi = pair * LANES, (pair + 1) * LANES
        side = (pair % 2) * LANES
        if side == 0:
            spread = spread_ref[:, lo : min(lo + 2 * LANES, channels)]
            wide = mm(factors, spread, NN)
            products = []
        step_wide, entry_wide, leave_wide = [
            wide[i * rows : (i + 1) * rows, side : side + LANES] for i in range(3)
        ]
        pre = pre_inner_ref[:, lo:hi]
        gate = sigmoid(pre)
        head_in = pre * gate
        skip = skip_ref[:, lo:hi]
        upstream = upstream_ref[:, lo:hi]
        upstream_low = upstream.astype(bf16)
        upstream_back = upstream_low.astype(f32)
        scaled = head_in * step_wide
        scaled_low = scaled.astype(bf16)
        scaled_back = scaled_low.astype(f32)
        held = entering_ref[0, :, lo:hi]
        held_low = held.astype(bf16)
        ahead = adjoint[:, lo:hi]
        ahead_low = ahead.astype(bf16)
        entry_up = (upstream_back * entry_wide).astype(bf16)
        grad_out = grad_out + mm(entry_up, held_low, NT)
        grad_in = grad_in + mm((scaled * leave_wide).astype(bf16), ahead_low, NT)
        grad_scaled = mm(in_map, ahead_low, NN) * leave_wide
        through = entry_wide[rows - 1 :, :]
        tail_terms = jnp.sum(scaled_back * grad_scaled, axis=0, keepdims=True) + through * jnp.sum(
            ahead * held, axis=0, keepdims=True
        )
        adjoint[:, lo:hi] = ahead * through + mm(out_map_t, entry_up, NN)
        parts, decays, chosen = [], [], []
        for parity in range(2):
            head = 2 * pair + parity
            gap = running_t[head : head + 1, :] - running[:, head : head + 1]
            decays.append(jnp.exp(gap + allowed_t))
            parts.append((scores_t * decays[parity]).astype(bf16))
            mine = first_half if parity == 0 else jnp.logical_not(first_half)
            chosen.append(jnp.where(mine, scaled_back, 0.0).astype(bf16))
        both = mm(jnp.concatenate(parts, axis=0), upstream_low, NN)
        pulled = mm(jnp.concatenate(chosen, axis=0), upstream_low, NT)
        grad_scores_t = grad_scores_t + (pulled[:rows] * decays[0] + pulled[rows:] * decays[1])
        grad_scaled = grad_scaled + jnp.where(first_half, both[:rows], both[rows:])
        spread_one = spread[:LANES, side : side + LANES]
        spread_both = jnp.concatenate([spread_one, spread_one], axis=1)
        balance = upstream_back * (ssm_ref[:, lo:hi] - skip * head_in) - scaled_back * grad_scaled
        products.append((head_in * grad_scaled).astype(bf16))
        if hi == channels or side > 0:
            joined = jnp.concatenate(products, axis=1)
            step_terms = step_terms + mm(joined, spread[:LANES, :], NT)
        skip_terms = jnp.sum(upstream * head_in, axis=0, keepdims=True)
        edge = jnp.concatenate([tail_terms, skip_terms, jnp.zeros((TAIL - 2, LANES), f32)], axis=0)
        by_head = by_head + mm(
            halves(jnp.concatenate([balance, edge], axis=0), 1), spread_both, NT
        )
        grad_pre = (grad_scaled * step_wide + skip * upstream) * (gate * (1.0 + pre * (1.0 - gate)))
        inner_head[0:rows, lo:hi] = grad_pre
        inner_proj = inner_ref[:, lo:hi]
        grad_proj = conv_inner_ref[TAPS - 1 : TAPS, lo:hi] * grad_pre
        sums = [None] * TAPS
        sums[TAPS - 1] = jnp.sum(grad_pre * inner_proj, axis=0, keepdims=True)
        for k in range(1, TAPS):
            moved = inner_head[k : k + rows, lo:hi] * keeps[k - 1]
            grad_proj = grad_proj + conv_inner_ref[TAPS - 1 - k : TAPS - k, lo:hi] * moved
            sums[TAPS - 1 - k] = jnp.sum(moved * inner_proj, axis=0, keepdims=True)
        grads_ref[:, lo:hi] = grad_proj.astype(bf16)
        sums.append(jnp.sum(grad_pre, axis=0, keepdims=True))
        sums.append(jnp.zeros((TAIL - len(sums), LANES), f32))
        sums_ref[:, lo:hi] += jnp.concatenate(sums, axis=0)
    grad_scores_low = grad_scores_t.astype(bf16)
    grad_out = grad_out + mm(grad_scores_low, in_map, TN)
    grad_in = grad_in + mm(grad_scores_low, out_map, NN)
    grad_shared = jnp.concatenate([grad_in, grad_out], axis=1)
    grad_pre = grad_shared * (shared_gate * (1.0 + pre_shared * (1.0 - shared_gate)))
    shared_head[0:rows, :] = grad_pre
    shared_proj = shared_ref[...]
    grad_proj = conv_shared_ref[TAPS - 1 : TAPS, :] * grad_pre
    sums = [None] * TAPS
    sums[TAPS - 1] = jnp.sum(grad_pre * shared_proj, axis=0, keepdims=True)
    for k in range(1, TAPS):
        keep = jnp.concatenate([keeps[k - 1]] * (width // LANES), axis=1)
        moved = shared_head[k : k + rows, :] * keep
        grad_proj = grad_proj + conv_shared_ref[TAPS - 1 - k : TAPS - k, :] * moved
        sums[TAPS - 1 - k] = jnp.sum(moved * shared_proj, axis=0, keepdims=True)
    sums.append(jnp.sum(grad_pre, axis=0, keepdims=True))
    sums.append(jnp.zeros((TAIL - len(sums), width), f32))
    sums_ref[:, channels : channels + width] += jnp.concatenate(sums, axis=0)
    leaving = by_head[rows:]
    split = mm(lower, halves(by_head[:rows], 1), TN)
    grad_log = split[:, :LANES] + split[:, LANES:] + leaving[0:1, :]
    grad_step = (step_terms + rate * grad_log) * sigmoid(step_raw)
    grads_ref[:, channels : channels + width] = grad_proj.astype(bf16)
    grads_ref[:, channels + width :] = grad_step.astype(bf16)

    @pl.when(turn == 0)
    def _():
        for copy in weight_copies():
            copy.wait()

    terms = mm(grad_gate_ref[...], gate_w[...], NT) + mm(grads_ref[...], weight[...], NT)
    terms_ref[...] = terms.astype(bf16)
    if sending:
        spot_ref, earlier_ref = carried_in[3:]

        @pl.when(turn == pl.num_programs(0) - 1)
        def _():
            send_ref[...] = jnp.where(spot_ref[0, 0] == 0, earlier_ref[...], terms.astype(bf16))

    sums_ref[:, channels + width :] += jnp.concatenate(
        [
            jnp.sum(grad_step, axis=0, keepdims=True),
            rate * jnp.sum(step * grad_log, axis=0, keepdims=True),
            leaving[1:2, :],
            jnp.zeros((TAIL - 3, LANES), f32),
        ],
        axis=0,
    )

    @pl.when(turn == pl.num_programs(0) - 1)
    def _():
        inner_out_ref[...] = inner_head[0:TAIL, :]
        shared_out_ref[...] = shared_head[0:TAIL, :]


def mixer_backward(
    lengths, upstream, saved, conv_inner, conv_shared, rate, skip, spread, grad_gate, weight_late,
    weight, carry, blocks, span, spot=None, earlier=None
):
    ssm, inner, pre_inner, shared, pre_shared, step_raw, entering = saved
    rows, channels = upstream.shape
    width = conv_shared.shape[1]
    states = width // 2
    begin, end = blocks
    known = channels + width + LANES
    model = weight.shape[0]
    by_row = lambda cols: pl.BlockSpec((span, cols), lambda i: (end - 1 - i, 0))
    extra, extra_specs = (), ()
    if earlier is not None:
        last = earlier.shape[0] // span - 1
        extra = (spot, earlier)
        extra_specs = (
            pl.BlockSpec(memory_space=pltpu.SMEM), pl.BlockSpec((span, model), lambda i: (last, 0)),
        )
    small = ((TAIL, known), (TAIL, channels), (TAIL, width), (states, channels))
    results = pl.pallas_call(
        partial(backward_kernel, begin, rows, len(carry) == 1, earlier is not None),
        grid=(end - begin,),
        in_specs=[
            pl.BlockSpec(memory_space=pltpu.SMEM),
            by_row(channels), by_row(channels), by_row(channels), by_row(channels),
            by_row(width), by_row(width), by_row(LANES),
            pl.BlockSpec((1, states, channels), lambda i: (end - 1 - i, 0, 0)),
            full(conv_inner.shape),
            full(conv_shared.shape),
            full(rate.shape),
            full(skip.shape),
            full(spread.shape),
            by_row(channels),
            pl.BlockSpec(memory_space=pl.ANY),
            pl.BlockSpec(memory_space=pl.ANY),
            *[full(x.shape) for x in carry],
            *extra_specs,
        ],
        out_specs=[
            pl.BlockSpec((span, known), lambda i: (end - begin - 1 - i, 0)),
            pl.BlockSpec((span, model), lambda i: (end - begin - 1 - i, 0)),
            *[full(shape) for shape in small],
            *([full((span, model))] if extra else []),
        ],
        out_shape=[
            jax.ShapeDtypeStruct(((end - begin) * span, known), bf16),
            jax.ShapeDtypeStruct(((end - begin) * span, model), bf16),
            *[jax.ShapeDtypeStruct(shape, f32) for shape in small],
            *([jax.ShapeDtypeStruct((span, model), bf16)] if extra else []),
        ],
        scratch_shapes=[
            pltpu.VMEM((TAIL + span, channels), f32),
            pltpu.VMEM((TAIL + span, width), f32),
            pltpu.VMEM((model, channels), bf16),
            pltpu.VMEM((model, known), bf16),
            pltpu.SemaphoreType.DMA((2,)),
        ],
        compiler_params=pltpu.CompilerParams(
            dimension_semantics=("arbitrary",), vmem_limit_bytes=LIMIT
        ),
        name="mixer_backward",
    )(
        lengths, upstream, ssm, inner, pre_inner, shared, pre_shared, step_raw, entering,
        conv_inner, conv_shared, rate, skip, spread, grad_gate, weight_late, weight, *carry,
        *extra,
    )
    return results[0], results[1], tuple(results[2:6]), *results[6:]


def gain_row(weight_ref, total_ref, columns):
    rows = weight_ref.shape[0]
    begin, end = columns
    added = jnp.zeros((rows, LANES), f32)
    for lo in range(begin, end, LANES):
        weight = weight_ref[:, lo : lo + LANES].astype(f32)
        added = added + weight * total_ref[:, lo - begin : lo - begin + LANES]
    return jnp.sum(jnp.transpose(added), axis=0, keepdims=True)


def product_kernel(chips, columns, spot_ref, normed_ref, weight_ref, gain_ref, sums_ref,
                   norm_sum_ref, *refs):
    grads, (keep_ref, *send_refs, heads_ref, shared_ref, total) = refs[:-8], refs[-8:]
    lo, hi = columns
    at = 0
    for i, ref in enumerate(grads):
        rows = ref.shape[0]
        added = mm(normed_ref[at : at + rows, :], ref[:, lo:hi], TN)
        total[...] = added if i == 0 else total[...] + added
        at += rows
    split_cores(spot_ref, total, keep_ref, send_refs, chips)
    row = norm_sum_ref[0:1, :] + gain_row(weight_ref, total, columns)
    width = shared_ref.shape[1] - norm_sum_ref.shape[1]
    inner = heads_ref.shape[1] - LANES
    heads_ref[:, :inner] = sums_ref[:, :inner]
    heads_ref[:, inner:] = sums_ref[:, inner + width :]
    shared_ref[:, :width] = sums_ref[:, inner : inner + width]
    shared_ref[:, width:] = jnp.broadcast_to(row / gain_ref[...], norm_sum_ref.shape)


def weight_products(spot, normed, weight, gain, sums, norm_sum, grads, chips, width):
    known = grads[0].shape[1]
    model = normed.shape[1]
    size = known
    part = jax.ShapeDtypeStruct((model // 2, size), bf16)
    piece = jax.ShapeDtypeStruct((model // 8, size), bf16)
    vmem = pl.BlockSpec(memory_space=pltpu.VMEM)
    return pl.pallas_call(
        partial(product_kernel, chips, (0, known)),
        in_specs=[pl.BlockSpec(memory_space=pltpu.SMEM), *[vmem for _ in range(5 + len(grads))]],
        out_specs=[vmem] * 7,
        out_shape=[
            part, *[piece] * 4, jax.ShapeDtypeStruct((TAIL, known - width), f32),
            jax.ShapeDtypeStruct((TAIL, width + model), f32),
        ],
        scratch_shapes=[pltpu.VMEM((model, size), f32)],
        compiler_params=pltpu.CompilerParams(vmem_limit_bytes=LIMIT),
        name="weight_products",
    )(spot, normed, weight, gain, sums, norm_sum, *grads)


def gate_kernel(pieces, count, spot_ref, normed_ref, *refs):
    own_ref, others = refs[0], refs[1:pieces]
    columns, sources = refs[pieces : pieces + 4], refs[pieces + 4 : pieces + 4 + 2 * count]
    (
        gain_ref, ssm_ref, upstream_ref, weight_ref, gate_ref, grad_ref, sums_ref
    ) = refs[pieces + 4 + 2 * count :]

    @pl.when(pl.program_id(0) == 0)
    def _():
        place_columns(spot_ref, weight_ref, columns, count)
        place_pairs(spot_ref, weight_ref, [(ref, 0) for ref in sources], count, columns[0].shape[1])

    rows, channels = ssm_ref.shape
    normed = normed_ref[...]
    upstream = rows_of(pl.program_id(0), pl.num_programs(0), spot_ref, own_ref, others)
    upstream_ref[...] = upstream
    square = jnp.zeros((rows, LANES), f32)
    cross = jnp.zeros((rows, LANES), f32)
    step = 2 * LANES
    for lo in range(0, channels, step):
        hi = lo + step
        gate = mm(normed, weight_ref[:, lo:hi], NN)
        grad = mm(upstream, weight_ref[:, channels + lo : channels + hi], NN)
        gate_ref[:, lo:hi] = gate
        grad_ref[:, lo:hi] = grad
        gated = ssm_ref[:, lo:hi] * (gate * sigmoid(gate))
        squares = gated * gated
        crosses = grad * gain_ref[:, lo:hi] * gated
        square = square + (squares[:, :LANES] + squares[:, LANES:])
        cross = cross + (crosses[:, :LANES] + crosses[:, LANES:])
    square = jnp.sum(square, axis=1, keepdims=True)
    cross = jnp.sum(cross, axis=1, keepdims=True)
    lane = lax.broadcasted_iota(jnp.int32, (rows, LANES), 1)
    both = jnp.where(lane == 0, square, jnp.where(lane == 1, cross, 0.0))
    sums_ref[...] = jnp.transpose(both)[0:TAIL, :]


def gate_forward(spot, normed, own, others, sources, count, gain, ssm, span):
    rows, model = normed.shape
    channels = ssm.shape[1]
    by_row = lambda cols: pl.BlockSpec((span, cols), lambda i: (i, 0))
    return pl.pallas_call(
        partial(gate_kernel, 1 + len(others), count),
        grid=(rows // span,),
        in_specs=[
            pl.BlockSpec(memory_space=pltpu.SMEM), by_row(model), *own_specs(own, others, span),
            *[full(x.shape) for x in sources], full(gain.shape), by_row(channels),
        ],
        out_specs=[
            by_row(model), full((model, 2 * channels)), by_row(channels), by_row(channels),
            pl.BlockSpec((TAIL, span), lambda i: (0, i)),
        ],
        out_shape=[
            jax.ShapeDtypeStruct((rows, model), bf16),
            jax.ShapeDtypeStruct((model, 2 * channels), bf16),
            jax.ShapeDtypeStruct((rows, channels), f32),
            jax.ShapeDtypeStruct((rows, channels), f32),
            jax.ShapeDtypeStruct((TAIL, rows), f32),
        ],
        compiler_params=pltpu.CompilerParams(
            dimension_semantics=("arbitrary",), vmem_limit_bytes=LIMIT
        ),
        name="gate_forward",
    )(spot, normed, own, *others, *sources, gain, ssm)


def norm_kernel(full_inner, chips, split, spot_ref, sums_ref, more_ref, gate_ref, grad_ref, ssm_ref,
                gain_ref, normed_ref, upstream_ref, gate_w_ref, out_w_ref, grad_gate_ref,
                grad_ssm_ref, gain_sum_ref, keep_ref, send_ref, mine_ref, theirs_ref, norm_sum_ref,
                scaled, totals):
    rows, channels = gate_ref.shape
    block = pl.program_id(0)

    @pl.when(block == 0)
    def _():
        gain_sum_ref[...] = jnp.zeros_like(gain_sum_ref)
        totals[...] = jnp.zeros_like(totals)

    sums = sums_ref[...] + more_ref[...] if split else sums_ref[...]
    sums = jnp.transpose(jnp.concatenate([sums, jnp.zeros((LANES - TAIL, rows), f32)], axis=0))
    scale = lax.rsqrt(sums[:, 0:1] / full_inner + EPSILON)
    pull = scale * scale * scale * (sums[:, 1:2] / full_inner)
    normed_t = jnp.transpose(normed_ref[...])
    upstream_t = jnp.transpose(upstream_ref[...])
    step = 2 * LANES
    for lo in range(0, channels, step):
        hi = lo + step
        gain = gain_ref[:, lo:hi]
        gate, grad, ssm = gate_ref[:, lo:hi], grad_ref[:, lo:hi], ssm_ref[:, lo:hi]
        sig = sigmoid(gate)
        silu = gate * sig
        gated = ssm * silu
        normal = gated * scale
        scaled_low = (normal * gain).astype(bf16)
        scaled[:, lo:hi] = scaled_low
        gain_sum_ref[TAIL - 1 : TAIL, lo:hi] += jnp.sum(grad * normal, axis=0, keepdims=True)
        grad_gated = scale * (grad * gain) - gated * pull
        grad_ssm_ref[:, lo:hi] = grad_gated * silu
        grad_gate = (grad_gated * ssm * (sig * (1.0 + gate * (1.0 - sig)))).astype(bf16)
        grad_gate_ref[:, lo:hi] = grad_gate
        totals[:, lo:hi] += mm(normed_t, grad_gate, NN)
        totals[:, channels + lo : channels + hi] += mm(upstream_t, scaled_low, NN)
    branch = mm(scaled[...], out_w_ref[...], NT).astype(bf16)
    if split:
        half = pl.num_programs(0) // 2
        at = pl.ds(pl.multiple_of(lax.rem(block, half) * rows, rows), rows)

        @pl.when(block // half == spot_ref[0, 0])
        def _():
            mine_ref[at, :] = branch

        @pl.when(block // half != spot_ref[0, 0])
        def _():
            theirs_ref[at, :] = branch
    else:
        mine_ref[pl.ds(pl.multiple_of(block * rows, rows), rows), :] = branch

        @pl.when(block == 0)
        def _():
            theirs_ref[...] = jnp.zeros_like(theirs_ref)

    @pl.when(block == pl.num_programs(0) - 1)
    def _():
        split_cores(spot_ref, totals, keep_ref, [send_ref], chips)
        norm_sum_ref[...] = jnp.zeros_like(norm_sum_ref)
        norm_sum_ref[0:1, :] = gain_row(gate_w_ref, totals, (0, channels))


def gate_norm(
    spot, sums, more, gate, grad, ssm, gain, normed, upstream, weight, known, full_inner, chips, split, span
):
    rows, channels = gate.shape
    model = normed.shape[1]
    by_row = lambda cols: pl.BlockSpec((span, cols), lambda i: (i, 0))
    stats = pl.BlockSpec((TAIL, span), lambda i: (0, i))
    half = (model // 2, 2 * channels)
    mine = (rows // 2 if split else rows, model)
    theirs = (rows // 2 if split else TAIL * 2, model)
    return pl.pallas_call(
        partial(norm_kernel, float(full_inner), chips, split),
        grid=(rows // span,),
        in_specs=[
            pl.BlockSpec(memory_space=pltpu.SMEM), stats, stats, by_row(channels), by_row(channels),
            by_row(channels), full(gain.shape), by_row(model), by_row(model),
            pl.BlockSpec((model, channels), lambda i: (0, 0)),
            pl.BlockSpec((model, channels), lambda i: (0, 1)),
        ],
        out_specs=[
            by_row(channels), by_row(channels), full((TAIL, known)), full(half), full(half),
            full(mine), full(theirs), full((TAIL, model)),
        ],
        out_shape=[
            jax.ShapeDtypeStruct((rows, channels), bf16),
            jax.ShapeDtypeStruct((rows, channels), f32),
            jax.ShapeDtypeStruct((TAIL, known), f32),
            jax.ShapeDtypeStruct(half, bf16),
            jax.ShapeDtypeStruct(half, bf16),
            jax.ShapeDtypeStruct(mine, bf16),
            jax.ShapeDtypeStruct(theirs, bf16),
            jax.ShapeDtypeStruct((TAIL, model), f32),
        ],
        scratch_shapes=[
            pltpu.VMEM((span, channels), bf16),
            pltpu.VMEM((model, 2 * channels), f32),
        ],
        compiler_params=pltpu.CompilerParams(
            dimension_semantics=("arbitrary",), vmem_limit_bytes=LIMIT
        ),
        name="gate_norm",
    )(spot, sums, more, gate, grad, ssm, gain, normed, upstream, weight, weight)


def output_kernel(width, sums_ref, more_ref, *out_refs):
    sums = sums_ref[...] + more_ref[...]
    inner = out_refs[0].shape[1]
    heads = out_refs[4].shape[1]
    shared = inner + LANES
    parts = (
        sums[:TAPS, :inner], sums[TAPS : TAPS + 1, :inner], sums[:TAPS, shared : shared + width],
        sums[TAPS : TAPS + 1, shared : shared + width], sums[0:1, inner : inner + LANES][:, :heads],
        sums[1:2, inner : inner + LANES][:, :heads], sums[2:3, inner : inner + LANES][:, :heads],
        sums[TAIL - 1 :, :inner], sums[0:1, shared + width :],
    )
    for ref, part in zip(out_refs, parts):
        ref[...] = part


def sums_outputs(sums, more, channels, width, heads):
    model = sums.shape[1] - channels - LANES - width
    shapes = [
        (TAPS, channels), (1, channels), (TAPS, width), (1, width), (1, heads), (1, heads),
        (1, heads), (1, channels), (1, model),
    ]
    vmem = pl.BlockSpec(memory_space=pltpu.VMEM)
    return pl.pallas_call(
        partial(output_kernel, width),
        in_specs=[vmem, vmem],
        out_specs=[vmem] * len(shapes),
        out_shape=[jax.ShapeDtypeStruct(shape, f32) for shape in shapes],
        name="sums_outputs",
    )(sums, more)


def lanes_of(vector):
    return jnp.pad(vector, (0, LANES - vector.shape[0]))[None, :]


def spread_map(heads, channels):
    size = channels // heads
    row = lax.broadcasted_iota(jnp.int32, (2 * LANES, channels), 0) % LANES
    col = lax.broadcasted_iota(jnp.int32, (2 * LANES, channels), 1) // size
    return (row == col).astype(bf16)


def dp_send(value, bit):
    size = lax.axis_size("dp")
    return lax.ppermute(value, "dp", [(i, i ^ bit) for i in range(size)])


def chip_bits():
    return [4 * k for k in range(1, lax.axis_size("dp") // 4)]


def long_bits():
    bits, bit = [], 4
    while bit < lax.axis_size("dp"):
        bits.append(bit)
        bit *= 2
    return bits


def choose(stacked, index, axis):
    return lax.dynamic_index_in_dim(stacked, index, axis, keepdims=False)


def send_fold(parts, bit, axis):
    mine = (lax.axis_index("dp") // bit) % 2
    return dp_send(choose(parts, 1 - mine, axis), bit)


def keep_fold(parts, got, bit, axis):
    mine = (lax.axis_index("dp") // bit) % 2
    return choose(parts, mine, axis).astype(f32) + got.astype(f32)


def fold(parts, bit, axis):
    return keep_fold(parts, send_fold(parts, bit, axis), bit, axis)


def send_chips(parts):
    place = lax.axis_index("dp") // 4
    sends = parts.astype(bf16)
    return [dp_send(choose(sends, place ^ (bit // 4), 0), bit) for bit in chip_bits()]


def keep_chips(parts, got):
    total = choose(parts, lax.axis_index("dp") // 4, 0).astype(f32)
    for piece in got:
        total = total + piece.astype(f32)
    return total


def fold_chips(parts):
    return keep_chips(parts, send_chips(parts))


def tensor_swap(value):
    return lax.ppermute(value, "tensor", [(0, 1), (1, 0)])


def gather_other(own, size):
    if size != 2:
        return lax.all_gather(own, "tensor", axis=0, tiled=True)
    return tensor_swap(own)


def join_pieces(own, top, bottom, size):
    top = top.reshape(size, -1, own.shape[1])
    bottom = bottom.reshape(size, -1, own.shape[1])
    return jnp.concatenate([top, bottom], axis=1).reshape(-1, own.shape[1])


def pick_half(lower, upper, size):
    if size != 2:
        return lower
    return jnp.where(lax.axis_index("tensor") == 0, lower, upper)


def sum_quarters(quarters, other0, other1, size):
    if size != 2:
        whole = jnp.concatenate(quarters, axis=0)
        return lax.psum_scatter(whole, "tensor", scatter_dimension=0, tiled=True).astype(f32)
    first = lax.axis_index("tensor") == 0
    each = other0.shape[0]
    low, middle, high = quarters
    lower = jnp.concatenate([low, middle[:each]], axis=0)
    upper = jnp.concatenate([middle[each:], high], axis=0)
    others = jnp.concatenate([other0, other1], axis=0)
    return jnp.where(first, lower, upper).astype(f32) + others.astype(f32)


def tensor_sum(value, size):
    if size != 2:
        return lax.psum(value, "tensor")
    return value + tensor_swap(value)


def shards(
    tokens, lengths, norm_gain, zx_weight, bc_weight, dt_weight, conv_inner, bias_inner,
    conv_shared, bias_shared, step_bias, log_rate, skip_gain, gate_gain, out_weight, cotangent,
):
    size = lax.axis_size("tensor")
    split = size == 2
    me = lax.axis_index("dp")
    count = len(chip_bits()) + 1
    spot = jnp.stack([lax.axis_index("tensor"), me // 4, (me // 2) % 2, me % 2])[None, :]
    spot = spot.astype(jnp.int32)
    channels = zx_weight.shape[2]
    heads = step_bias.shape[0]
    width = bc_weight.shape[1]
    known = channels + width + LANES
    step_weight = jnp.pad(dt_weight, ((0, 0), (0, LANES - heads)))
    early = jnp.concatenate([zx_weight[:, 1, :], bc_weight, step_weight], axis=1)
    inputs = tokens.astype(f32)
    norm_scale = lax.rsqrt(jnp.mean(inputs * inputs, axis=1, keepdims=True) + EPSILON)
    normed_rows = (inputs * norm_scale * norm_gain[None, :]).astype(bf16)
    half = normed_rows.shape[0] // 2
    fixed = (
        conv_inner, bias_inner[None, :], conv_shared, bias_shared[None, :], lanes_of(step_bias),
        lanes_of(-jnp.exp(log_rate)), jnp.repeat(skip_gain, channels // heads)[None, :],
        spread_map(heads, channels),
    )
    def along(value):
        return [value] + [dp_send(value, bit) for bit in chip_bits()]

    column = jnp.concatenate(along(early), axis=0)
    column, pair, top, fixed, spot = lax.optimization_barrier((
        column, jnp.concatenate([out_weight, dp_send(out_weight, 2)], axis=0),
        gather_other(normed_rows[:half], size), fixed, spot,
    ))
    by_x, column, bottom, gate_column, pair, late_rows = lax.optimization_barrier((
        dp_send(column, 2), column, gather_other(normed_rows[half:], size),
        along(zx_weight[:, 0, :]), pair, cotangent,
    ))
    gate_column = jnp.concatenate(gate_column, axis=0)
    pairs = along(pair)
    by_core = dp_send(column, 1)
    sources = (column, by_x, by_core, dp_send(by_x, 1))
    own, others = normed_rows, (top, bottom)
    if not split:
        own, others = join_pieces(normed_rows, top, bottom, size), ()
    normed, weight, *saved = mixer_forward(
        spot, lengths, own, others, sources, count, *fixed, SPAN
    )
    _, _, _, _, _, rate, skip, spread = fixed
    gain = gate_gain[None, :]
    other, ssm, gate_x, gate_column, pairs = lax.optimization_barrier((
        gather_other(late_rows, size), saved[0], dp_send(gate_column, 2), gate_column, pairs,
    ))
    sources = (
        gate_column, gate_x, dp_send(gate_column, 1), dp_send(gate_x, 1), *pairs,
        *[dp_send(pair, 1) for pair in pairs],
    )
    own, others = (cotangent, (other,)) if split else (other, ())
    upstream, weight_late, gate, grad, sums = gate_forward(
        spot, normed, own, others, sources, count, gain, ssm, SPAN
    )
    more = gather_other(sums, size) if split else sums
    sums = sums if split else lax.psum(sums, "tensor")
    chips = 2 * count
    grad_gate, grad_ssm, gain_sum, keep, send, branch_own, branch_send, norm_sum = gate_norm(
        spot, sums, more, gate, grad, ssm, gain, normed, upstream, weight_late, known, channels * size,
        chips, split, SPAN,
    )
    if split:
        branch_other = gather_other(branch_send, size)
    else:
        branch_own = lax.psum_scatter(branch_own, "tensor", scatter_dimension=0, tiled=True)
        branch_other = jnp.zeros_like(branch_own)
    quarter = grad_ssm.shape[0] // SPAN // 4
    carry = (gain_sum,)

    fused = split and quarter == 1

    def back(begin, end, carry, earlier=None):
        return mixer_backward(
            lengths, grad_ssm, saved, conv_inner, conv_shared, rate, skip, spread, grad_gate,
            weight_late, weight, carry, (begin * quarter, end * quarter), SPAN, spot,
            earlier if fused else None,
        )

    first = dp_send(send, 1)
    grads3, terms3, carry = back(3, 4, carry)
    first = (keep.astype(f32) + first.astype(f32)).astype(bf16)
    first = first.reshape(count, 2, -1, first.shape[1])
    carry, first = lax.optimization_barrier((carry, first))
    first_gate, first_out = first[..., :channels], first[..., channels:]
    grads1, terms1, carry, *ready = back(1, 3, carry, terms3)
    first_gate = fold(first_gate, 2, 1)
    first_out = fold_chips(first_out).astype(bf16)
    each = terms3.shape[0]
    send1 = ready[0] if fused else pick_half(terms3, terms1[:each], size)
    carry, send1, branch_other, first_gate, first_out = lax.optimization_barrier(
        (carry, send1, branch_other, first_gate, first_out)
    )
    other1 = gather_other(send1, size) if split else send1
    part_gate = fold_chips(first_gate)
    part_out = fold(first_out, 2, 0)
    grads0, terms0, carry, *ready = back(0, 1, carry, terms1)
    sums, part_gate, part_out, grads0, other1, terms0 = lax.optimization_barrier(
        (carry[0], part_gate, part_out, grads0, other1, terms0)
    )
    send0 = ready[0] if fused else pick_half(terms1[each:], terms0, size)
    send0, grads0 = lax.optimization_barrier((send0, grads0))
    other0 = gather_other(send0, size) if split else send0
    keep, *send, sums, shared_sums = weight_products(
        spot, normed, weight, norm_gain[None, :], sums, norm_sum, (grads0, grads1, grads3), chips,
        width,
    )
    got = [dp_send(piece, 1) for piece in send]
    *got, other0, sums, shared_sums, keep = lax.optimization_barrier(
        (*got, other0, sums, shared_sums, keep)
    )
    got = jnp.concatenate(got, axis=0)
    parts = (keep.astype(f32) + got.astype(f32)).astype(bf16).reshape(count, 2, -1, known)
    cut = min((known * 2 // 3) // LANES * LANES, channels)
    parts_a, parts_b = parts[..., :cut], parts[..., cut:]
    got_a = send_fold(parts_a, 2, 1)
    got_b = send_chips(parts_b)
    shared_sums = tensor_sum(shared_sums, size)
    shared_sums, other0 = lax.optimization_barrier((shared_sums, other0))
    sums = jnp.concatenate([sums, shared_sums], axis=1)
    sums = sums + dp_send(sums, 1)
    sums = sums + dp_send(sums, 2)
    grad_normed = sum_quarters((terms0, terms1, terms3), other0, other1, size)
    scaled_grad = grad_normed * norm_gain[None, :]
    grad_inputs = norm_scale * scaled_grad - inputs * norm_scale**3 * jnp.mean(
        scaled_grad * inputs, axis=1, keepdims=True
    )
    grad_tokens = (cotangent.astype(f32) + grad_inputs).astype(bf16)
    got_a, got_b, sums, grad_tokens, branch_other = lax.optimization_barrier(
        (got_a, got_b, sums, grad_tokens, branch_other)
    )
    block_out = (inputs + (branch_own.astype(f32) + branch_other.astype(f32))).astype(bf16)
    parts_a = keep_fold(parts_a, got_a, 2, 1)
    parts_b = keep_chips(parts_b, got_b).astype(bf16)
    got_a = send_chips(parts_a)
    parts_b = fold(parts_b, 2, 0)
    for bit in long_bits()[:-1]:
        sums = sums + dp_send(sums, bit)
    smalls = sums_outputs(sums, dp_send(sums, long_bits()[-1]), channels, width, heads)
    parts_a = keep_chips(parts_a, got_a)
    part_inner = jnp.concatenate([parts_a, parts_b[:, : channels - cut]], axis=1)
    at_step = channels + width
    part_shared = tensor_sum(parts_b[:, channels - cut : at_step - cut], size)
    part_step = parts_b[:, at_step - cut : at_step - cut + heads]
    part_in = jnp.stack([part_gate, part_inner], axis=1)
    return (
        block_out,
        grad_tokens,
        smalls[8][0],
        part_in,
        part_shared,
        part_step,
        smalls[0],
        smalls[1][0],
        smalls[2],
        smalls[3][0],
        smalls[4][0],
        smalls[5][0],
        smalls[6][0],
        smalls[7][0],
        part_out,
    )


def solution(mesh):
    return jax.shard_map(
        shards,
        mesh=mesh,
        in_specs=(
            P(("dp", "tensor"), None),
            P("dp", None),
            P(),
            P("dp", None, "tensor"),
            P("dp", None),
            P("dp", "tensor"),
            P(None, "tensor"),
            P("tensor"),
            P(),
            P(),
            P("tensor"),
            P("tensor"),
            P("tensor"),
            P("tensor"),
            P("dp", "tensor"),
            P(("dp", "tensor"), None),
        ),
        out_specs=(
            P(("dp", "tensor"), None),
            P(("dp", "tensor"), None),
            P(),
            P("dp", None, "tensor"),
            P("dp", None),
            P("dp", "tensor"),
            P(None, "tensor"),
            P("tensor"),
            P(),
            P(),
            P("tensor"),
            P("tensor"),
            P("tensor"),
            P("tensor"),
            P("dp", "tensor"),
        ),
        check_vma=False,
    )
```
